32 devices in a mesh: dp: 16 (over z, y, x), tensor: 2 (over core).
Axes of the slice: x: 2, y: 2, z: 4, core: 2. Of those that a mesh axis runs over, the one named last changes fastest.
Arguments:
- tubes: bfloat16 [32, 1568, 1536], P('dp', None, 'tensor'), may hold values from -20 to 20
- tube_order: int32 [32, 1568], P('dp'), may hold values from 0 to 1567, each once within a row
- clip_mask: int32 [32], P('dp'), may hold values from 0 to 1, as said below
- enc_weights: float32 [2, 9984, 768], P('tensor', 'dp')
- dec_weights: float32 [2, 3456, 384], P('tensor', 'dp')
- vec_split: float32 [2, 6528], P('tensor'), may hold values from -2 to 2
- vec_shared: float32 [14976], replicated
- enc_moment: float32 [2, 9984, 768], P('tensor', 'dp'), may hold values from -7.361117e-05 to 7.361117e-05
- dec_moment: float32 [2, 3456, 384], P('tensor', 'dp'), may hold values from -0.024537056 to 0.024537056
- split_moment: float32 [2, 6528], P('tensor'), may hold values from -0.00073611166 to 0.00073611166
- shared_moment: float32 [14976], replicated, may hold values from -0.00073611166 to 0.00073611166
- enc_error: bfloat16 [16, 2, 9984, 768], P('dp', 'tensor'), may hold values from -7.343292e-05 to 7.343292e-05
- dec_error: bfloat16 [16, 2, 3456, 384], P('dp', 'tensor'), may hold values from -7.343292e-05 to 7.343292e-05
- factors: float32 [2, 8, 1152], P('tensor'), may hold values from -5 to 5
Outputs:
- loss_sum: float32 [], replicated
- loss_weight: float32 [], replicated
- enc_weights_new: float32 [2, 9984, 768], P('tensor', 'dp')
- enc_moment_new: float32 [2, 9984, 768], P('tensor', 'dp')
- enc_error_new: bfloat16 [16, 2, 9984, 768], P('dp', 'tensor')
- dec_weights_new: float32 [2, 3456, 384], P('tensor', 'dp')
- dec_moment_new: float32 [2, 3456, 384], P('tensor', 'dp')
- dec_error_new: bfloat16 [16, 2, 3456, 384], P('dp', 'tensor')
- factors_new: float32 [2, 8, 1152], P('tensor')
- vec_split_new: float32 [2, 6528], P('tensor')
- split_moment_new: float32 [2, 6528], P('tensor')
- vec_shared_new: float32 [14976], replicated
- shared_moment_new: float32 [14976], replicated
The draws below stay inside these ranges and needn't reach their ends.
Inputs may be any that keep to these rules, and one draw needn't show every extreme that they name: `tube_order`: each row is a permutation of the 1568 tubes. `clip_mask`: clip 0 is always counted.
All inputs are finite; a program needn't handle non-finite values.
Results may differ from the reference program's by a relative error of at most 0.014.
Values may be sent and summed in bfloat16 or wider, within the bound.
A program may use at most 384 MiB of HBM per device.

```python
import math
import jax
import jax.numpy as jnp
from jax import lax

D = 768
HEAD_DIM = 64
FF = 3072
DD = 384
DFF = 1536
PIX = 1536
TUBES = 1568
VIS = 160
MASKED = 1408
RANK = 8
CLIPS_DEV = 2
GROUPS = 2
WORKERS = 16
CLIPS = 32
ENC_ROWS = 9984
DEC_ROWS = 3456
SPLIT_LEN = 6528
SHARED_LEN = 14976


def row_scale(count, widths, scales):
    row = jnp.arange(count)
    result = jnp.zeros((count,), jnp.float32)
    start = 0
    for width, value in zip(widths, scales):
        result = jnp.where((row >= start) & (row < start + width), value, result)
        start = start + width
    return result


def draw_tubes(key, part):
    key = jax.random.fold_in(key, 19)
    column = jnp.arange(PIX).astype(jnp.float32) / (PIX - 1)
    noise = jnp.clip(jax.random.normal(key, (CLIPS, TUBES, PIX), jnp.float32), -6.0, 6.0)
    scale = jnp.exp(column * math.log(3.0))
    return (noise * scale[None, None, :]).astype(jnp.bfloat16)


def draw_enc_weights(key, part):
    key = jax.random.fold_in(key, 11)
    noise = jax.random.normal(key, (GROUPS, ENC_ROWS, D), jnp.float32)
    layer_widths = [D // GROUPS, FF // GROUPS, 3 * D // GROUPS, FF // GROUPS]
    layer_scales = [3.0 * D ** (-0.5), 2.0 * FF ** (-0.5), D ** (-0.5), D ** (-0.5)]
    scale = row_scale(ENC_ROWS, [PIX // GROUPS] + layer_widths * 2, [PIX ** (-0.5)] + layer_scales * 2)
    return noise * scale[None, :, None]


def draw_dec_weights(key, part):
    key = jax.random.fold_in(key, 12)
    noise = jax.random.normal(key, (GROUPS, DEC_ROWS, DD), jnp.float32)
    scale = row_scale(DEC_ROWS, [D // GROUPS, DD // GROUPS, DFF // GROUPS, 3 * DD // GROUPS, DFF // GROUPS, PIX // GROUPS], [D ** (-0.5), 3.0 * DD ** (-0.5), 2.0 * DFF ** (-0.5), DD ** (-0.5), DD ** (-0.5), DD ** (-0.5)])
    return noise * scale[None, :, None]


def draw_dec_moment(key, part):
    key = jax.random.fold_in(key, 23)
    noise_key, row_key, column_key = jax.random.split(key, 3)
    unit = 1.0 / (PIX * (MASKED * CLIPS_DEV) ** 0.5)
    noise = jnp.clip(jax.random.normal(noise_key, (GROUPS, DEC_ROWS, DD), jnp.float32), -5.0, 5.0)
    top_factor = 10.0
    base_scale = 20.0
    row_factor = jnp.exp(jax.random.uniform(row_key, (GROUPS, DEC_ROWS, 1), jnp.float32, 0.0, 1.0) * math.log(top_factor))
    column_factor = jnp.exp(jax.random.uniform(column_key, (1, 1, DD), jnp.float32, -1.0, 1.0) * math.log(2.0))
    return noise * row_factor * column_factor * (base_scale * unit)


def flattened_vector_rows(key, rows, width, gain_rows, first_scale):
    first_key, second_key = jax.random.split(key)
    noise = jax.random.normal(first_key, (rows, width), jnp.float32)
    spread = jax.random.uniform(second_key, (rows, width), jnp.float32, -1.0, 1.0)
    row = jnp.arange(rows)[:, None]
    is_gain = jnp.zeros((rows, 1), jnp.bool_)
    for index in gain_rows:
        is_gain = is_gain | (row == index)
    scale = jnp.where(row == 0, first_scale, 0.3)
    return jnp.where(is_gain, 1.0 + 0.3 * spread, scale * noise).reshape(-1)


def draw_vec_shared(key, part):
    key = jax.random.fold_in(key, 13)
    wide_key, narrow_key = jax.random.split(key)
    wide = flattened_vector_rows(wide_key, 15, D, [1, 4, 7, 10, 13], 0.3)
    narrow = flattened_vector_rows(narrow_key, 9, DD, [1, 4, 7], 1.0)
    return jnp.concatenate([wide, narrow])


def draw_clip_mask(key, part):
    key = jax.random.fold_in(key, 17)
    flags = (jax.random.randint(key, (CLIPS,), 0, 4) > 0).astype(jnp.int32)
    return flags.at[0].set(1)


def level_of(stream_key, dims, cuts, low, top_value):
    level = 1.0
    for axis_at, blocks in cuts:
        draws = jax.random.uniform(jax.random.fold_in(jax.random.fold_in(stream_key, 6), axis_at), (blocks,), jnp.float32, low / len(cuts), top_value / len(cuts))
        level = level * jnp.repeat(jnp.exp(draws), dims[axis_at] // blocks).reshape((-1,) + (1,) * (len(dims) - 1 - axis_at))
    return level


def scatter_about(own_key, shape, scale, reach, cuts=(), kind=jnp.bfloat16):
    drawn = jax.random.normal(own_key, shape, jnp.float32) * scale
    if len(cuts) > 0:
        drawn = level_of(own_key, shape, cuts, -0.22, 0.18) * drawn
    return jnp.clip(drawn, min=-reach, max=reach).astype(kind)


def setup_inputs(seed: int = 0) -> dict:
    arg_keys = jax.random.split(jax.random.key(seed), 15)
    tubes = draw_tubes(jax.random.fold_in(arg_keys[14], 71), 0)
    tube_order = jax.vmap(lambda own: jax.random.permutation(own, TUBES))(jax.random.split(arg_keys[1], CLIPS)).reshape((CLIPS, TUBES)).astype(jnp.int32)
    clip_mask = draw_clip_mask(jax.random.fold_in(arg_keys[14], 71), 0)
    enc_weights = draw_enc_weights(jax.random.fold_in(arg_keys[14], 71), 0)
    dec_weights = draw_dec_weights(jax.random.fold_in(arg_keys[14], 71), 0)
    vec_split = scatter_about(arg_keys[5], (GROUPS, SPLIT_LEN), 0.3, 2.0, ((0, 2),), jnp.float32)
    vec_shared = draw_vec_shared(jax.random.fold_in(arg_keys[14], 71), 0)
    enc_moment = scatter_about(arg_keys[7], (GROUPS, ENC_ROWS, D), (1.0 / (PIX * (MASKED * CLIPS_DEV) ** 0.5)), 7.361116877291352e-05, ((0, 2), (1, 16)), jnp.float32)
    dec_moment = draw_dec_moment(jax.random.fold_in(arg_keys[14], 71), 0)
    split_moment = scatter_about(arg_keys[9], (GROUPS, SPLIT_LEN), (10.0 / (PIX * (MASKED * CLIPS_DEV) ** 0.5)), 0.00073611166, ((0, 2),), jnp.float32)
    shared_moment = scatter_about(arg_keys[10], (SHARED_LEN,), (10.0 / (PIX * (MASKED * CLIPS_DEV) ** 0.5)), 0.00073611166, (), jnp.float32)
    enc_error = scatter_about(arg_keys[11], (WORKERS, GROUPS, ENC_ROWS, D), (1.0 / (PIX * (MASKED * CLIPS_DEV) ** 0.5)), 7.343292236328125e-05, ((0, 16), (1, 2)))
    dec_error = scatter_about(arg_keys[12], (WORKERS, GROUPS, DEC_ROWS, DD), (1.0 / (PIX * (MASKED * CLIPS_DEV) ** 0.5)), 7.343292236328125e-05, ((0, 16), (1, 2)))
    factors = scatter_about(arg_keys[13], (GROUPS, RANK, D + DD), 1.0, 5.0, ((0, 2),), jnp.float32)
    return dict(tubes=tubes, tube_order=tube_order, clip_mask=clip_mask, enc_weights=enc_weights, dec_weights=dec_weights, vec_split=vec_split, vec_shared=vec_shared, enc_moment=enc_moment, dec_moment=dec_moment, split_moment=split_moment, shared_moment=shared_moment, enc_error=enc_error, dec_error=dec_error, factors=factors)


@jax.custom_vjp
def low(v):
    return lax.optimization_barrier(v.astype(jnp.bfloat16)).astype(jnp.float32)

@jax.custom_vjp
def low_back(v):
    return v

def low_keep(v):
    return (low(v), None)

def low_pass(kept, grad):
    return (grad,)

def back_keep(v):
    return (v, None)

def back_low(kept, grad):
    return (low(grad),)
low.defvjp(low_keep, low_pass)
low_back.defvjp(back_keep, back_low)
highest_precision = lax.Precision.HIGHEST
norm_eps = 1e-06
momentum_keep = 0.9
step_rate = 1000.0

def matmul(left, right):
    return jnp.dot(left, right, precision=highest_precision)

def layer_norm(stream, gain, shift):
    center = stream - lax.optimization_barrier(jnp.mean(stream, -1, keepdims=True))
    spread = lax.optimization_barrier(jnp.mean(center * center, -1, keepdims=True))
    return center * lax.rsqrt(spread + norm_eps) * gain + shift

def sinusoid(width):
    place = jnp.arange(TUBES).astype(jnp.float32)[:, None]
    column = jnp.arange(width)
    rate = jnp.exp(-(2 * (column // 2)).astype(jnp.float32) * (math.log(10000.0) / width))
    angle = place * rate[None, :]
    return jnp.where(column % 2 == 0, jnp.sin(angle), jnp.cos(angle))

def unpack_rows(block, widths):
    pieces = []
    start = 0
    for width in widths:
        pieces.append(block[:, start:start + width, :].reshape(GROUPS * width, block.shape[2]))
        start = start + width
    return pieces

def unpack_vector(vector, widths):
    pieces = []
    start = 0
    for width in widths:
        pieces.append(vector[..., start:start + width].reshape(-1))
        start = start + width
    return pieces

def layer(stream, mats, vecs):
    w_query, w_key, w_value, w_out, w_up, w_down = mats
    length = stream.shape[0]
    heads = w_query.shape[1] // HEAD_DIM
    normed = low(layer_norm(stream, vecs[0], vecs[1]))
    query = low(low_back(matmul(normed, w_query) + vecs[2])).reshape(length, heads, HEAD_DIM)
    keys = low(low_back(matmul(normed, w_key))).reshape(length, heads, HEAD_DIM)
    values = low(low_back(matmul(normed, w_value) + vecs[3])).reshape(length, heads, HEAD_DIM)
    scores = low_back(jnp.einsum('qhd,khd->hqk', query, keys, precision=highest_precision) * HEAD_DIM ** (-0.5))
    probs = low(jax.nn.softmax(scores, axis=-1))
    mixed = jnp.einsum('hqk,khd->qhd', probs, values, precision=highest_precision).reshape(length, heads * HEAD_DIM)
    mixed = low(low_back(mixed))
    stream = stream + low_back(matmul(mixed, w_out) + vecs[4])
    second = low(layer_norm(stream, vecs[5], vecs[6]))
    before = low_back(matmul(second, w_up) + vecs[7])
    active = low(jax.nn.gelu(before, approximate=False))
    return stream + low_back(matmul(active, w_down) + vecs[8])

def forward(enc, dec, vsplit, vshared, pixels, order, counted):
    layer_widths = [D // GROUPS, FF // GROUPS, D // GROUPS, D // GROUPS, D // GROUPS, FF // GROUPS]
    enc_pieces = unpack_rows(low(enc), [PIX // GROUPS] + layer_widths * 2)
    embed = enc_pieces[0]
    proj, d_out, d_down, d_query, d_key, d_value, d_up, head_rows = unpack_rows(low(dec), [D // GROUPS, DD // GROUPS, DFF // GROUPS, DD // GROUPS, DD // GROUPS, DD // GROUPS, DFF // GROUPS, PIX // GROUPS])
    split_parts = unpack_vector(vsplit, [D // GROUPS, D // GROUPS, FF // GROUPS] * 2 + [DD // GROUPS, DD // GROUPS, DFF // GROUPS, PIX // GROUPS])
    shared = [vshared[index * D:(index + 1) * D] for index in range(15)] + [vshared[15 * D + index * DD:15 * D + (index + 1) * DD] for index in range(9)]
    enc_layers = []
    for index in range(2):
        e_out, e_down, e_query, e_key, e_value, e_up = enc_pieces[1 + 6 * index:7 + 6 * index]
        base = 6 * index
        mats = (e_query.T, e_key.T, e_value.T, e_out, e_up.T, e_down)
        vecs = (shared[1 + base], shared[2 + base], split_parts[3 * index], split_parts[3 * index + 1], shared[3 + base], shared[4 + base], shared[5 + base], split_parts[3 * index + 2], shared[6 + base])
        enc_layers.append((mats, vecs))
    dec_mats = (d_query.T, d_key.T, d_value.T, d_out, d_up.T, d_down)
    dec_vecs = (shared[16], shared[17], split_parts[6], split_parts[7], shared[18], shared[19], shared[20], split_parts[8], shared[21])
    pos_enc = sinusoid(D)
    pos_dec = sinusoid(DD)
    total = jnp.zeros((), jnp.float32)
    for clip in range(CLIPS_DEV):
        visible = order[clip, :VIS]
        masked = order[clip, VIS:]
        stream = low_back(matmul(pixels[clip][visible], embed) + shared[0] + pos_enc[visible])
        for mats, vecs in enc_layers:
            stream = layer(stream, mats, vecs)
        normed = low(layer_norm(stream, shared[13], shared[14]))
        latent = low_back(matmul(normed, proj))
        stream = jnp.concatenate([latent + pos_dec[visible], shared[15][None, :] + pos_dec[masked]], 0)
        stream = layer(stream, dec_mats, dec_vecs)
        normed = low(layer_norm(stream, shared[22], shared[23]))[VIS:]
        guess = low_back(matmul(normed, head_rows.T) + split_parts[9])
        target_pix = pixels[clip][masked]
        center = lax.optimization_barrier(jnp.mean(target_pix, -1, keepdims=True))
        square = lax.optimization_barrier(jnp.mean(target_pix * target_pix, -1, keepdims=True))
        target = (target_pix - center) * lax.rsqrt(square - center * center + norm_eps)
        total = total + counted[clip] * jnp.sum((guess - target) ** 2) / PIX
    return total

def orthonormal(left):
    gram = jnp.einsum('rx,sx->rs', left, left, precision=highest_precision)
    return lax.linalg.triangular_solve(jnp.linalg.cholesky(gram), left, left_side=True, lower=True)

def compress(grads, error, start, weights, moment):
    combined = grads + error.astype(jnp.float32)
    left = jnp.einsum('grc,wgxc->grx', start, combined, precision=highest_precision)
    basis_matrix = jax.vmap(orthonormal)(left)
    refreshed_factor = jnp.einsum('grx,wgxc->grc', basis_matrix, combined, precision=highest_precision) / WORKERS
    approximation_product = jnp.einsum('yju,yja->yua', basis_matrix, refreshed_factor, precision=highest_precision)
    moment_new = momentum_keep * moment + approximation_product
    return (weights - step_rate * moment_new, moment_new, (combined - approximation_product[None]).astype(jnp.bfloat16), refreshed_factor)

def reference(tubes, tube_order, clip_mask, enc_weights, dec_weights, vec_split, vec_shared, enc_moment, dec_moment, split_moment, shared_moment, enc_error, dec_error, factors):
    counted = clip_mask.astype(jnp.float32)
    weight = MASKED * jnp.sum(counted)
    pixels = tubes.astype(jnp.float32).reshape(WORKERS, CLIPS_DEV, TUBES, PIX)
    orders = tube_order.reshape(WORKERS, CLIPS_DEV, TUBES)
    masks = counted.reshape(WORKERS, CLIPS_DEV)

    def worker(inputs):
        pix, order, mask = inputs

        def objective(enc, dec, vsplit, vshared):
            loss = forward(enc, dec, vsplit, vshared, pix, order, mask)
            return (WORKERS * loss / weight, loss)
        value, back, loss = jax.vjp(objective, enc_weights, dec_weights, vec_split, vec_shared, has_aux=True)
        grads = back(jnp.ones_like(value))
        return (loss,) + tuple(grads)
    losses, g_enc, g_dec, g_split, g_shared = lax.map(worker, (pixels, orders, masks))
    enc_new, enc_mom, enc_err, enc_fac = compress(g_enc, enc_error, factors[:, :, :D], enc_weights, enc_moment)
    dec_new, dec_mom, dec_err, dec_fac = compress(g_dec, dec_error, factors[:, :, D:], dec_weights, dec_moment)
    split_mom = momentum_keep * split_moment + lax.optimization_barrier(jnp.sum(g_split, 0)) / WORKERS
    shared_mom = momentum_keep * shared_moment + lax.optimization_barrier(jnp.sum(g_shared, 0)) / WORKERS
    return (jnp.sum(losses), weight, enc_new, enc_mom, enc_err, dec_new, dec_mom, dec_err, jnp.concatenate([enc_fac, dec_fac], 2), vec_split - step_rate * split_mom, split_mom, vec_shared - step_rate * shared_mom, shared_mom)
```

```python
import math

import jax
import jax.numpy as jnp
from jax import lax
from jax.experimental import pallas as pl
from jax.experimental.pallas import tpu as pltpu
from jax.sharding import PartitionSpec as P

D = 768
HEAD_DIM = 64
FF = 3072
DD = 384
DFF = 1536
PIX = 1536
TUBES = 1568
VIS = 160
MASKED = 1408
RANK = 8

f32 = jnp.float32
bf16 = jnp.bfloat16
highest_precision = lax.Precision.HIGHEST
norm_eps = 1e-06
momentum_keep = 0.9
step_rate = 1000.0
LOG2E = 1.4426950408889634
SCORE = HEAD_DIM ** (-0.5)
BIG_VMEM = 56 << 20


def nn(left, right):
    return lax.dot_general(left, right, (((1,), (0,)), ((), ())), preferred_element_type=f32)


def nt(left, right):
    return lax.dot_general(left, right, (((1,), (1,)), ((), ())), preferred_element_type=f32)


def tn(left, right):
    return lax.dot_general(left, right, (((0,), (0,)), ((), ())), preferred_element_type=f32)


def col_sum(value):
    return jnp.sum(value, 0, keepdims=True)


def norm_parts(stream):
    center = stream - jnp.mean(stream, -1, keepdims=True)
    rate = lax.rsqrt(jnp.mean(center * center, -1, keepdims=True) + norm_eps)
    return center * rate, rate


def norm_back(grad, gain, unit, rate):
    grad_unit = grad * gain
    return rate * (
        grad_unit
        - jnp.mean(grad_unit, -1, keepdims=True)
        - unit * jnp.mean(grad_unit * unit, -1, keepdims=True)
    )


def gelu_pair(before):
    cdf_tail = jnp.exp(-0.5 * before * before)
    size = jnp.abs(before) * (2.0 ** -0.5)
    t = 1.0 / (1.0 + 0.3275911 * size)
    poly = t * (
        0.254829592 + t * (-0.284496736 + t * (1.421413741 + t * (-1.453152027 + t * 1.061405429)))
    )
    tail = 0.5 * poly * cdf_tail
    cdf = jnp.where(before < 0, tail, 1.0 - tail)
    return before * cdf, cdf + before * cdf_tail * (1.0 / math.sqrt(2.0 * math.pi))


def split3(value):
    high = value.astype(bf16)
    rest = value - high.astype(f32)
    middle = rest.astype(bf16)
    low = (rest - middle.astype(f32)).astype(bf16)
    return jnp.concatenate([high, middle, low], 0)


def fold3(value):
    rows = value.shape[0] // 3
    return value[:rows] + value[rows : 2 * rows] + value[2 * rows :]


def sinusoid_at(place, width):
    column = jnp.arange(width)
    rate = jnp.exp(-(2 * (column // 2)).astype(f32) * (math.log(10000.0) / width))
    angle = place.astype(f32)[:, None] * rate[None, :]
    return jnp.where(column % 2 == 0, jnp.sin(angle), jnp.cos(angle))


def params(**more):
    return pltpu.CompilerParams(vmem_limit_bytes=BIG_VMEM, **more)


def whole(shape):
    return pl.BlockSpec(shape, lambda *_: (0,) * len(shape))


PICK_ROWS = 224


def pick_kernel(order_ref, tubes_ref, out_ref):
    column = lax.broadcasted_iota(jnp.int32, (1, TUBES), 1)
    hot = jnp.where(order_ref[0] == column, 1.0, 0.0).astype(bf16)
    out_ref[0] = nn(hot, tubes_ref[0]).astype(bf16)


def pick(order, tubes):
    clips, _, width = tubes.shape
    return pl.pallas_call(
        pick_kernel,
        grid=(clips, TUBES // PICK_ROWS),
        in_specs=[
            pl.BlockSpec((1, PICK_ROWS, 1), lambda c, i: (c, i, 0)),
            pl.BlockSpec((1, TUBES, width), lambda c, i: (c, 0, 0)),
        ],
        out_specs=pl.BlockSpec((1, PICK_ROWS, width), lambda c, i: (c, i, 0)),
        out_shape=jax.ShapeDtypeStruct(tubes.shape, bf16),
        compiler_params=params(),
        name="pick_tubes",
    )(order[:, :, None], tubes)


QKV_ROWS = 392


def qkv_kernel(x_ref, g_ref, b_ref, w_ref, bias_ref, h_ref, qkv_ref):
    unit, _ = norm_parts(x_ref[...])
    h = (unit * g_ref[...] + b_ref[...]).astype(bf16)
    h_ref[...] = h
    qkv_ref[...] = (nt(h, w_ref[...]) + bias_ref[...]).astype(bf16)


def decoder_qkv(x, gain, shift, weights, bias):
    rows = lambda width: pl.BlockSpec((QKV_ROWS, width), lambda i: (i, 0))
    return pl.pallas_call(
        qkv_kernel,
        grid=(TUBES // QKV_ROWS,),
        in_specs=[
            rows(DD),
            whole((1, DD)),
            whole((1, DD)),
            whole((3 * DD, DD)),
            whole((1, 3 * DD)),
        ],
        out_specs=[rows(DD), rows(3 * DD)],
        out_shape=[
            jax.ShapeDtypeStruct((TUBES, DD), bf16),
            jax.ShapeDtypeStruct((TUBES, 3 * DD), bf16),
        ],
        compiler_params=params(),
        name="decoder_qkv",
    )(x, gain, shift, weights, bias)


FWD_ROWS = 392
BWD_ROWS = 256
PAIRS = DD // 128


def half_lane(index):
    return lax.broadcasted_iota(jnp.int32, (1, 128), 1) // HEAD_DIM == index


def attend_kernel(q_ref, k_ref, v_ref, o_ref, lse_ref):
    q = q_ref[...]
    k = k_ref[...]
    v_one = jnp.concatenate([v_ref[...], jnp.ones((TUBES, 128), bf16)], 1)
    mixed, logs = [], []
    for head in range(2):
        scores = nt(jnp.where(half_lane(head), q, jnp.zeros_like(q)), k)
        top = jnp.max(scores, 1, keepdims=True)
        expo = jnp.exp2((scores - top) * (SCORE * LOG2E)).astype(bf16)
        both = nn(expo, v_one)
        total = both[:, 128:]
        mixed.append(both[:, :128] / total)
        logs.append(top * (SCORE * LOG2E) + jnp.log2(total))
    o_ref[...] = jnp.where(half_lane(0), mixed[0], mixed[1])
    lse_ref[0] = jnp.where(half_lane(0), logs[0], logs[1])


def attend(qkv):
    return pl.pallas_call(
        attend_kernel,
        grid=(PAIRS, TUBES // FWD_ROWS),
        in_specs=[
            pl.BlockSpec((FWD_ROWS, 128), lambda p, i: (i, p)),
            pl.BlockSpec((TUBES, 128), lambda p, i: (0, PAIRS + p)),
            pl.BlockSpec((TUBES, 128), lambda p, i: (0, 2 * PAIRS + p)),
        ],
        out_specs=[
            pl.BlockSpec((FWD_ROWS, 128), lambda p, i: (i, p)),
            pl.BlockSpec((1, FWD_ROWS, 128), lambda p, i: (p, i, 0)),
        ],
        out_shape=[
            jax.ShapeDtypeStruct((TUBES, DD), f32),
            jax.ShapeDtypeStruct((PAIRS, TUBES, 128), f32),
        ],
        compiler_params=params(),
        name="attend",
    )(qkv, qkv, qkv)


def attend_back_kernel(
    q_ref, k_ref, v_ref, o_ref, do_ref, lse_ref, dq_ref, dk_ref, dv_ref, k_turned, dk_sum, dv_sum
):
    step = pl.program_id(1)

    @pl.when(step == 0)
    def _():
        k_turned[...] = k_ref[...].T
        dk_sum[...] = jnp.zeros_like(dk_sum)
        dv_sum[...] = jnp.zeros_like(dv_sum)

    valid = lax.broadcasted_iota(jnp.int32, (BWD_ROWS, 1), 0) + step * BWD_ROWS < TUBES
    zero = jnp.zeros((), bf16)
    q = jnp.where(valid, q_ref[...], zero)
    grad = jnp.where(valid, do_ref[...], zero)
    dots = jnp.where(valid, o_ref[...], 0.0) * grad.astype(f32)
    logs = jnp.where(valid, lse_ref[0], 0.0).T
    select = (
        lax.broadcasted_iota(jnp.int32, (8, 128), 1) // HEAD_DIM
        == lax.broadcasted_iota(jnp.int32, (8, 128), 0)
    ).astype(f32)
    row_total = lax.dot_general(
        select, dots, (((1,), (1,)), ((), ())), precision=highest_precision,
        preferred_element_type=f32,
    )
    k = k_ref[...]
    v = v_ref[...]
    turned = []
    for head in range(2):
        mask = half_lane(head)
        q_head = jnp.where(mask, q, zero)
        grad_head = jnp.where(mask, grad, zero)
        low = head * HEAD_DIM
        probs = jnp.exp2(nt(k, q_head) * (SCORE * LOG2E) - logs[low : low + 1])
        grad_scores = (probs * (nt(v, grad_head) - row_total[head : head + 1])).astype(bf16)
        dv_sum[...] += nn(probs.astype(bf16), grad_head)
        dk_sum[...] += nn(grad_scores, q_head)
        turned.append(nn(k_turned[low : low + HEAD_DIM], grad_scores))
    dq_ref[...] = (jnp.concatenate(turned, 0).T * SCORE).astype(bf16)

    @pl.when(step == pl.num_programs(1) - 1)
    def _():
        dk_ref[...] = (dk_sum[...] * SCORE).astype(bf16)
        dv_ref[...] = dv_sum[...].astype(bf16)


def attend_back(qkv, mixed, grad_mixed, logs):
    some = pl.BlockSpec((BWD_ROWS, 128), lambda p, i: (i, p))
    full = pl.BlockSpec((TUBES, 128), lambda p, i: (0, p))
    return pl.pallas_call(
        attend_back_kernel,
        grid=(PAIRS, pl.cdiv(TUBES, BWD_ROWS)),
        in_specs=[
            some,
            pl.BlockSpec((TUBES, 128), lambda p, i: (0, PAIRS + p)),
            pl.BlockSpec((TUBES, 128), lambda p, i: (0, 2 * PAIRS + p)),
            some,
            some,
            pl.BlockSpec((1, BWD_ROWS, 128), lambda p, i: (p, i, 0)),
        ],
        out_specs=[some, full, full],
        out_shape=[jax.ShapeDtypeStruct((TUBES, DD), bf16)] * 3,
        scratch_shapes=[
            pltpu.VMEM((128, TUBES), bf16),
            pltpu.VMEM((TUBES, 128), f32),
            pltpu.VMEM((TUBES, 128), f32),
        ],
        compiler_params=params(),
        name="attend_back",
    )(qkv, qkv, qkv, mixed, grad_mixed, logs)


TOKEN_ROWS = 224
CHUNK = 384
CHUNKS = DFF // CHUNK


def token_kernel(
    a_ref, x_ref, pix_ref, scal_ref, vec_ref, bu_ref, bh_ref, wo_ref, wd_ref, wu_ref, wh_ref,
    da_ref, dx1_ref,
    g_wo_ref, g_wd_ref, g_wu_ref, g_wh_ref, gvec_ref, gbu_ref, gbh_ref, loss_ref,
    slope,
):
    step = pl.program_id(0)
    sums = (g_wo_ref, g_wd_ref, g_wu_ref, g_wh_ref, gvec_ref, gbu_ref, gbh_ref, loss_ref)

    @pl.when(step == 0)
    def _():
        for ref in sums:
            ref[...] = jnp.zeros_like(ref)

    bo, g2, b2, bd, gf, sf = (vec_ref[index : index + 1] for index in range(6))
    a = a_ref[...].astype(bf16)
    x1 = x_ref[...] + (nn(a, wo_ref[...]) + bo)
    unit2, rate2 = norm_parts(x1)
    h2 = (unit2 * g2 + b2).astype(bf16)
    out = x1 + bd
    active = []
    for chunk in range(CHUNKS):
        part = pl.ds(chunk * CHUNK, CHUNK)
        value, slope_part = gelu_pair(nt(h2, wu_ref[part]) + bu_ref[:, part])
        slope[:, part] = slope_part
        active.append(value.astype(bf16))
        out = out + nn(active[-1], wd_ref[part])
    unit_f, rate_f = norm_parts(out)
    final = (unit_f * gf + sf).astype(bf16)
    pixels = [pix_ref[:, pl.ds(chunk * CHUNK, CHUNK)].astype(f32) for chunk in range(CHUNKS)]
    center = sum(jnp.sum(part, 1, keepdims=True) for part in pixels) * (1.0 / PIX)
    square = sum(jnp.sum(part * part, 1, keepdims=True) for part in pixels) * (1.0 / PIX)
    spread = lax.rsqrt(square - center * center + norm_eps)
    row = lax.broadcasted_iota(jnp.int32, (TOKEN_ROWS, 1), 0) + step * TOKEN_ROWS
    counted = jnp.where(row >= VIS, scal_ref[0:1, 0:1], 0.0)
    rate = jnp.where(row >= VIS, scal_ref[1:2, 0:1], 0.0)
    grad_final = jnp.zeros((TOKEN_ROWS, DD), f32)
    for chunk in range(CHUNKS):
        part = pl.ds(chunk * CHUNK, CHUNK)
        target = (pixels[chunk] - center) * spread
        miss = nt(final, wh_ref[part]) + bh_ref[:, part] - target
        loss_ref[:, part] += col_sum(counted * miss * miss)
        grad_guess = (rate * miss).astype(bf16)
        gbh_ref[:, part] += col_sum(grad_guess.astype(f32))
        g_wh_ref[part] += tn(grad_guess, final)
        grad_final = grad_final + nn(grad_guess, wh_ref[part])
    grad_out = norm_back(grad_final, gf, unit_f, rate_f)
    out_low = grad_out.astype(bf16)
    grad_h2 = jnp.zeros((TOKEN_ROWS, DD), f32)
    for chunk in range(CHUNKS):
        part = pl.ds(chunk * CHUNK, CHUNK)
        g_wd_ref[part] += tn(active[chunk], out_low)
        grad_before = (slope[:, part] * nt(out_low, wd_ref[part])).astype(bf16)
        gbu_ref[:, part] += col_sum(grad_before.astype(f32))
        g_wu_ref[part] += tn(grad_before, h2)
        grad_h2 = grad_h2 + nn(grad_before, wu_ref[part])
    grad_x1 = grad_out + norm_back(grad_h2, g2, unit2, rate2)
    x1_low = grad_x1.astype(bf16)
    g_wo_ref[...] += tn(a, x1_low)
    da_ref[...] = nt(x1_low, wo_ref[...]).astype(bf16)
    dx1_ref[...] = grad_x1
    gvec_ref[0:1] += col_sum(x1_low.astype(f32))
    gvec_ref[1:2] += col_sum(grad_h2 * unit2)
    gvec_ref[2:3] += col_sum(grad_h2)
    gvec_ref[3:4] += col_sum(out_low.astype(f32))
    gvec_ref[4:5] += col_sum(grad_final * unit_f)
    gvec_ref[5:6] += col_sum(grad_final)


def decoder_tokens(mixed, x, pixels, scal, vecs, bu, bh, wo, wd, wu, wh):
    rows = lambda width: pl.BlockSpec((TOKEN_ROWS, width), lambda i: (i, 0))
    sums = [(DD, DD), (DFF, DD), (DFF, DD), (PIX, DD), (8, DD), (1, DFF), (1, PIX), (1, PIX)]
    return pl.pallas_call(
        token_kernel,
        grid=(TUBES // TOKEN_ROWS,),
        in_specs=[
            rows(DD),
            rows(DD),
            rows(PIX),
            whole((8, 128)),
            whole((8, DD)),
            whole((1, DFF)),
            whole((1, PIX)),
            whole((DD, DD)),
            whole((DFF, DD)),
            whole((DFF, DD)),
            whole((PIX, DD)),
        ],
        out_specs=[rows(DD), rows(DD)] + [whole(shape) for shape in sums],
        out_shape=[
            jax.ShapeDtypeStruct((TUBES, DD), bf16),
            jax.ShapeDtypeStruct((TUBES, DD), f32),
        ]
        + [jax.ShapeDtypeStruct(shape, f32) for shape in sums],
        scratch_shapes=[pltpu.VMEM((TOKEN_ROWS, DFF), f32)],
        compiler_params=params(),
        name="decoder_tokens",
    )(mixed, x, pixels, scal, vecs, bu, bh, wo, wd, wu, wh)


def qkv_back_kernel(
    dq_ref, dk_ref, dv_ref, h_ref, x_ref, dx1_ref, g_ref, w_ref,
    dx_ref, gw_ref, gvec_ref,
):
    step = pl.program_id(0)

    @pl.when(step == 0)
    def _():
        gw_ref[...] = jnp.zeros_like(gw_ref)
        gvec_ref[...] = jnp.zeros_like(gvec_ref)

    h = h_ref[...]
    grads = (dq_ref[...], dk_ref[...], dv_ref[...])
    grad_h = jnp.zeros((QKV_ROWS, DD), f32)
    for index, grad in enumerate(grads):
        part = pl.ds(index * DD, DD)
        gw_ref[part] += tn(grad, h)
        grad_h = grad_h + nn(grad, w_ref[part])
    unit, rate = norm_parts(x_ref[...])
    grad_x = dx1_ref[...] + norm_back(grad_h, g_ref[...], unit, rate)
    dx_ref[...] = grad_x
    row = lax.broadcasted_iota(jnp.int32, (QKV_ROWS, 1), 0) + step * QKV_ROWS
    gvec_ref[0:1] += col_sum(grads[0].astype(f32))
    gvec_ref[1:2] += col_sum(grads[2].astype(f32))
    gvec_ref[2:3] += col_sum(grad_h * unit)
    gvec_ref[3:4] += col_sum(grad_h)
    gvec_ref[4:5] += col_sum(jnp.where(row >= VIS, grad_x, 0.0))


def decoder_qkv_back(dq, dk, dv, h, x, dx1, gain, weights):
    rows = lambda width: pl.BlockSpec((QKV_ROWS, width), lambda i: (i, 0))
    return pl.pallas_call(
        qkv_back_kernel,
        grid=(TUBES // QKV_ROWS,),
        in_specs=[rows(DD)] * 6 + [whole((1, DD)), whole((3 * DD, DD))],
        out_specs=[rows(DD), whole((3 * DD, DD)), whole((8, DD))],
        out_shape=[
            jax.ShapeDtypeStruct((TUBES, DD), f32),
            jax.ShapeDtypeStruct((3 * DD, DD), f32),
            jax.ShapeDtypeStruct((8, DD), f32),
        ],
        compiler_params=params(),
        name="decoder_qkv_back",
    )(dq, dk, dv, h, x, dx1, gain, weights)


HALF = D // 2
HALF_FF = FF // 2
LAYER_ROWS = 4 * HALF + 2 * HALF_FF
AT_O, AT_D, AT_Q, AT_U = 0, HALF, HALF + HALF_FF, HALF + HALF_FF + 3 * HALF
STAGES = ((AT_Q, 3 * HALF), (AT_O, HALF), (AT_U, HALF_FF), (AT_D, HALF_FF))


def stage_copies(sources, start, held, sems):
    return [
        [
            pltpu.make_async_copy(
                sources[group].at[pl.ds(start + at, size)],
                held.at[group, pl.ds(at, size)],
                sems.at[group, stage],
            )
            for group in range(2)
        ]
        for stage, (at, size) in enumerate(STAGES)
    ]


def encoder_kernel(
    start, x_ref, vec_ref, bqkv_ref, bu_ref, own_ref, other_ref,
    out_ref, h_ref, qkv_ref, a_ref, x1_ref, h2_ref, u_ref, slope_ref,
    held, sems,
):
    copies = stage_copies((own_ref, other_ref), start, held, sems)
    for stage in copies:
        for copy in stage:
            copy.start()

    def wait(stage):
        for copy in copies[stage]:
            copy.wait()

    g1, b1, bo, g2, b2, bd = (vec_ref[index : index + 1] for index in range(6))
    x = x_ref[...]
    unit, _ = norm_parts(x)
    h = (unit * g1 + b1).astype(bf16)
    h_ref[...] = h
    wait(0)
    for kind in range(3):
        for group in range(2):
            part = pl.ds((2 * kind + group) * HALF, HALF)
            rows = pl.ds(AT_Q + kind * HALF, HALF)
            qkv_ref[:, part] = (nt(h, held[group, rows]) + bqkv_ref[:, part]).astype(bf16)
    for pair in range(D // 128):
        q, k, v = (qkv_ref[:, pl.ds(kind * D + pair * 128, 128)] for kind in range(3))
        v_one = jnp.concatenate([v, jnp.ones((VIS, 128), bf16)], 1)
        mixed = []
        for head in range(2):
            scores = nt(jnp.where(half_lane(head), q, jnp.zeros_like(q)), k)
            top = jnp.max(scores, 1, keepdims=True)
            expo = jnp.exp2((scores - top) * (SCORE * LOG2E)).astype(bf16)
            both = nn(expo, v_one)
            mixed.append(both[:, :128] / both[:, 128:])
        a_ref[:, pl.ds(pair * 128, 128)] = jnp.where(half_lane(0), mixed[0], mixed[1]).astype(bf16)
    wait(1)
    x1 = x + bo
    for group in range(2):
        x1 = x1 + nn(a_ref[:, pl.ds(group * HALF, HALF)], held[group, pl.ds(AT_O, HALF)])
    x1_ref[...] = x1
    unit2, _ = norm_parts(x1)
    h2 = (unit2 * g2 + b2).astype(bf16)
    h2_ref[...] = h2
    wait(2)
    wait(3)
    out = x1 + bd
    for group in range(2):
        for chunk in range(HALF_FF // CHUNK):
            part = pl.ds(group * HALF_FF + chunk * CHUNK, CHUNK)
            before = nt(h2, held[group, pl.ds(AT_U + chunk * CHUNK, CHUNK)]) + bu_ref[:, part]
            value, slope = gelu_pair(before)
            slope_ref[:, part] = slope
            active = value.astype(bf16)
            u_ref[:, part] = active
            out = out + nn(active, held[group, pl.ds(AT_D + chunk * CHUNK, CHUNK)])
    out_ref[...] = out


def any_spec():
    return pl.BlockSpec(memory_space=pl.ANY)


def encoder_layer(start, x, vecs, bqkv, bu, own, other, name):
    shapes = [
        ((VIS, D), f32),
        ((VIS, D), bf16),
        ((VIS, 3 * D), bf16),
        ((VIS, D), bf16),
        ((VIS, D), f32),
        ((VIS, D), bf16),
        ((VIS, FF), bf16),
        ((VIS, FF), f32),
    ]
    return pl.pallas_call(
        lambda *refs: encoder_kernel(start, *refs),
        in_specs=[pl.BlockSpec(memory_space=pltpu.VMEM)] * 4 + [any_spec()] * 2,
        out_specs=[pl.BlockSpec(memory_space=pltpu.VMEM)] * len(shapes),
        out_shape=[jax.ShapeDtypeStruct(shape, kind) for shape, kind in shapes],
        scratch_shapes=[
            pltpu.VMEM((2, LAYER_ROWS, D), bf16),
            pltpu.SemaphoreType.DMA((2, len(STAGES))),
        ],
        compiler_params=params(),
        name=name,
    )(x, vecs, bqkv, bu, own, other)


def encoder_back_kernel(
    start, dout_ref, x_ref, vec_ref, qkv_ref, a_ref, x1_ref, u_ref, slope_ref, own_ref, other_ref,
    dx_ref, left_ref, low_ref, gvec_ref, gbu_ref, gbq_ref,
    held, sems, da, dqkv,
):
    copies = stage_copies((own_ref, other_ref), start, held, sems)
    for stage in (3, 2, 1, 0):
        for copy in copies[stage]:
            copy.start()

    def wait(stage):
        for copy in copies[stage]:
            copy.wait()

    g1, b1, bo, g2, b2, bd = (vec_ref[index : index + 1] for index in range(6))
    grad_out = dout_ref[...]
    out_low = grad_out.astype(bf16)
    low_ref[1] = out_low
    unit2, rate2 = norm_parts(x1_ref[...])
    grad_h2 = jnp.zeros((VIS, D), f32)
    wait(3)
    wait(2)
    for group in range(2):
        for chunk in range(HALF_FF // CHUNK):
            part = pl.ds(group * HALF_FF + chunk * CHUNK, CHUNK)
            grad_active = nt(out_low, held[group, pl.ds(AT_D + chunk * CHUNK, CHUNK)])
            grad_before = (slope_ref[:, part] * grad_active).astype(bf16)
            left_ref[group, :, pl.ds(AT_U + chunk * CHUNK, CHUNK)] = grad_before
            left_ref[group, :, pl.ds(AT_D + chunk * CHUNK, CHUNK)] = u_ref[:, part]
            gbu_ref[:, part] = col_sum(grad_before.astype(f32))
            grad_h2 = grad_h2 + nn(grad_before, held[group, pl.ds(AT_U + chunk * CHUNK, CHUNK)])
    grad_x1 = grad_out + norm_back(grad_h2, g2, unit2, rate2)
    x1_low = grad_x1.astype(bf16)
    low_ref[0] = x1_low
    wait(1)
    for group in range(2):
        part = pl.ds(group * HALF, HALF)
        da[:, part] = nt(x1_low, held[group, pl.ds(AT_O, HALF)]).astype(bf16)
        left_ref[group, :, pl.ds(AT_O, HALF)] = a_ref[:, part]
    zero = jnp.zeros((), bf16)
    for pair in range(D // 128):
        lanes = pl.ds(pair * 128, 128)
        q, k, v = (qkv_ref[:, pl.ds(kind * D + pair * 128, 128)] for kind in range(3))
        grad = da[:, lanes]
        dq = dk = dv = jnp.zeros((VIS, 128), f32)
        for head in range(2):
            mask = half_lane(head)
            q_head = jnp.where(mask, q, zero)
            grad_head = jnp.where(mask, grad, zero)
            scores = nt(q_head, k) * SCORE
            expo = jnp.exp(scores - jnp.max(scores, 1, keepdims=True))
            probs = expo / jnp.sum(expo, 1, keepdims=True)
            grad_probs = nt(grad_head, v)
            row_total = jnp.sum(probs * grad_probs, 1, keepdims=True)
            grad_scores = (probs * (grad_probs - row_total)).astype(bf16)
            dv = dv + tn(probs.astype(bf16), grad_head)
            dk = dk + tn(grad_scores, q_head)
            dq = dq + nn(grad_scores, jnp.where(mask, k, zero))
        dqkv[:, lanes] = (dq * SCORE).astype(bf16)
        dqkv[:, pl.ds(D + pair * 128, 128)] = (dk * SCORE).astype(bf16)
        dqkv[:, pl.ds(2 * D + pair * 128, 128)] = dv.astype(bf16)
    wait(0)
    grad_h = jnp.zeros((VIS, D), f32)
    for kind in range(3):
        for group in range(2):
            grad = dqkv[:, pl.ds((2 * kind + group) * HALF, HALF)]
            rows = pl.ds(AT_Q + kind * HALF, HALF)
            left_ref[group, :, rows] = grad
            grad_h = grad_h + nn(grad, held[group, rows])
    unit, rate = norm_parts(x_ref[...])
    dx_ref[...] = grad_x1 + norm_back(grad_h, g1, unit, rate)
    gbq_ref[0:1] = col_sum(dqkv[:, pl.ds(0, D)].astype(f32))
    gbq_ref[1:2] = col_sum(dqkv[:, pl.ds(2 * D, D)].astype(f32))
    gvec_ref[0:1] = col_sum(grad_h * unit)
    gvec_ref[1:2] = col_sum(grad_h)
    gvec_ref[2:3] = col_sum(x1_low.astype(f32))
    gvec_ref[3:4] = col_sum(grad_h2 * unit2)
    gvec_ref[4:5] = col_sum(grad_h2)
    gvec_ref[5:6] = col_sum(out_low.astype(f32))
    gvec_ref[6:8] = jnp.zeros((2, D), f32)


def encoder_layer_back(start, grad, x, vecs, kept, own, other, name):
    _, h, qkv, a, x1, h2, u, slope = kept
    shapes = [
        ((VIS, D), f32),
        ((2, VIS, LAYER_ROWS), bf16),
        ((2, VIS, D), bf16),
        ((8, D), f32),
        ((1, FF), f32),
        ((2, D), f32),
    ]
    dx, left, low, gvec, gbu, gbq = pl.pallas_call(
        lambda *refs: encoder_back_kernel(start, *refs),
        in_specs=[pl.BlockSpec(memory_space=pltpu.VMEM)] * 8 + [any_spec()] * 2,
        out_specs=[pl.BlockSpec(memory_space=pltpu.VMEM)] * len(shapes),
        out_shape=[jax.ShapeDtypeStruct(shape, kind) for shape, kind in shapes],
        scratch_shapes=[
            pltpu.VMEM((2, LAYER_ROWS, D), bf16),
            pltpu.SemaphoreType.DMA((2, len(STAGES))),
            pltpu.VMEM((VIS, D), bf16),
            pltpu.VMEM((VIS, 3 * D), bf16),
        ],
        compiler_params=params(),
        name=name,
    )(grad, x, vecs, qkv, a, x1, u, slope, own, other)
    right = jnp.concatenate([low, h[None], h2[None]], 0)
    return dx, left, right, gvec, gbu, gbq


ROWS = 384
ENC_BLOCKS = (D + 2 * LAYER_ROWS) // ROWS
PER_LAYER = LAYER_ROWS // ROWS
RIGHTS = 9


def right_of(block):
    inner = lax.rem(jnp.maximum(block - 2, 0), PER_LAYER)
    layer = jnp.maximum(block - 2, 0) // PER_LAYER
    kind = jnp.where(inner < 1, 1, jnp.where(inner < 5, 2, jnp.where(inner < 8, 3, 4)))
    return jnp.where(block < 2, 0, kind + 4 * layer)


def left_factor_kernel(start_ref, left_ref, right_ref, error_part_ref, out_ref):
    start = split3(start_ref[...])
    total = error_part_ref[...]
    for clip in range(2):
        inner = fold3(nt(start, right_ref[clip, 0]))
        total = total + fold3(nn(split3(inner), left_ref[clip]))
    out_ref[...] = total


def left_factor(start, left, right, error_part):
    return pl.pallas_call(
        left_factor_kernel,
        grid=(ENC_BLOCKS,),
        in_specs=[
            whole((RANK, D)),
            pl.BlockSpec((2, VIS, ROWS), lambda j: (0, 0, j)),
            pl.BlockSpec((2, 1, VIS, D), lambda j: (0, right_of(j), 0, 0)),
            pl.BlockSpec((RANK, ROWS), lambda j: (0, j)),
        ],
        out_specs=pl.BlockSpec((RANK, ROWS), lambda j: (0, j)),
        out_shape=jax.ShapeDtypeStruct((RANK, ENC_BLOCKS * ROWS), f32),
        compiler_params=params(),
        name="left_factor",
    )(start, left, right, error_part)


def error_factor_kernel(start_ref, error_ref, out_ref):
    out_ref[...] = fold3(nt(split3(start_ref[...]), error_ref[...]))


def error_factor(start, error):
    rows, width = error.shape
    return pl.pallas_call(
        error_factor_kernel,
        grid=(rows // ROWS,),
        in_specs=[whole((RANK, width)), pl.BlockSpec((ROWS, width), lambda j: (j, 0))],
        out_specs=pl.BlockSpec((RANK, ROWS), lambda j: (0, j)),
        out_shape=jax.ShapeDtypeStruct((RANK, rows), f32),
        compiler_params=params(),
        name="error_factor",
    )(start, error)


def right_factor_kernel(basis_ref, left_ref, right_ref, error_ref, out_ref):
    @pl.when(pl.program_id(0) == 0)
    def _():
        out_ref[...] = jnp.zeros_like(out_ref)

    basis = split3(basis_ref[...])
    total = fold3(nn(basis, error_ref[...]))
    for clip in range(2):
        inner = fold3(nt(basis, left_ref[clip]))
        total = total + fold3(nn(split3(inner), right_ref[clip, 0]))
    out_ref[...] += total


def right_factor(basis, left, right, error):
    return pl.pallas_call(
        right_factor_kernel,
        grid=(ENC_BLOCKS,),
        in_specs=[
            pl.BlockSpec((RANK, ROWS), lambda j: (0, j)),
            pl.BlockSpec((2, VIS, ROWS), lambda j: (0, 0, j)),
            pl.BlockSpec((2, 1, VIS, D), lambda j: (0, right_of(j), 0, 0)),
            pl.BlockSpec((ROWS, D), lambda j: (j, 0)),
        ],
        out_specs=whole((RANK, D)),
        out_shape=jax.ShapeDtypeStruct((RANK, D), f32),
        compiler_params=params(),
        name="right_factor",
    )(basis, left, right, error)


def residue_kernel(basis_ref, factor_ref, left_ref, right_ref, error_ref, out_ref):
    total = error_ref[...].astype(f32)
    total = total - tn(*low_pairs(basis_ref[...], factor_ref[...]))
    for clip in range(2):
        total = total + tn(left_ref[clip], right_ref[clip, 0])
    out_ref[...] = total.astype(bf16)


def low_pairs(basis, factor):
    basis3 = split3(basis)
    factor3 = split3(factor)
    high, middle = basis3[:RANK], basis3[RANK : 2 * RANK]
    return (
        jnp.concatenate([high, high, middle, jnp.zeros_like(high)], 0),
        jnp.concatenate([factor3[: 2 * RANK], factor3[:RANK], jnp.zeros_like(factor3[:RANK])], 0),
    )


def residue(basis, factor, left, right, error):
    return pl.pallas_call(
        residue_kernel,
        grid=(ENC_BLOCKS,),
        in_specs=[
            pl.BlockSpec((RANK, ROWS), lambda j: (0, j)),
            whole((RANK, D)),
            pl.BlockSpec((2, VIS, ROWS), lambda j: (0, 0, j)),
            pl.BlockSpec((2, 1, VIS, D), lambda j: (0, right_of(j), 0, 0)),
            pl.BlockSpec((ROWS, D), lambda j: (j, 0)),
        ],
        out_specs=pl.BlockSpec((ROWS, D), lambda j: (j, 0)),
        out_shape=jax.ShapeDtypeStruct((ENC_BLOCKS * ROWS, D), bf16),
        compiler_params=params(),
        name="residue",
    )(basis, factor, left, right, error)


def basis_kernel(enc_ref, dec_ref, enc_out, dec_out):
    place = lax.broadcasted_iota(jnp.int32, (RANK, 1), 0)
    for ref, out in ((enc_ref, enc_out), (dec_ref, dec_out)):
        left = ref[...]
        gram = lax.dot_general(
            left, left, (((1,), (1,)), ((), ())), precision=highest_precision,
            preferred_element_type=f32,
        )
        for index in range(RANK):
            scale = lax.rsqrt(gram[index : index + 1, index : index + 1])
            column = gram[:, index : index + 1] * scale
            below = jnp.where(place > index, column, 0.0)
            pivot = left[index : index + 1] * scale
            left = jnp.where(place == index, pivot, left - below * pivot)
            gram = gram - below * (gram[index : index + 1] * scale)
        out[...] = left


def orthonormal(enc_left, dec_left):
    return pl.pallas_call(
        basis_kernel,
        in_specs=[pl.BlockSpec(memory_space=pltpu.VMEM)] * 2,
        out_specs=[pl.BlockSpec(memory_space=pltpu.VMEM)] * 2,
        out_shape=[jax.ShapeDtypeStruct(enc_left.shape, f32), jax.ShapeDtypeStruct(dec_left.shape, f32)],
        compiler_params=params(),
        name="orthonormal",
    )(enc_left, dec_left)


def cut(block, widths):
    pieces = []
    start = 0
    for width in widths:
        pieces.append(block[start : start + width])
        start = start + width
    return pieces


def swap(value):
    return lax.ppermute(value, "tensor", [(0, 1), (1, 0)])


def per_device(
    tubes,
    tube_order,
    clip_mask,
    enc_weights,
    dec_weights,
    vec_split,
    vec_shared,
    enc_moment,
    dec_moment,
    split_moment,
    shared_moment,
    enc_error,
    dec_error,
    factors,
):
    workers = lax.axis_size("dp")
    half = lax.axis_index("tensor")
    worker_index = lax.axis_index("dp")
    dec_own = lax.all_gather(dec_weights[0].astype(bf16), "dp", axis=0, tiled=True)
    enc_own = lax.all_gather(enc_weights[0].astype(bf16), "dp", axis=0, tiled=True)
    dec_other = swap(dec_own)
    enc_other = swap(enc_own)
    counted_all = clip_mask.astype(f32)
    loss_weight = MASKED * lax.psum(jnp.sum(counted_all), "dp")

    mine = lambda both: lax.dynamic_index_in_dim(both, half, 0, keepdims=False)
    theirs = lambda both: lax.dynamic_index_in_dim(both, 1 - half, 0, keepdims=False)
    order = mine(tube_order)
    counted = mine(counted_all)
    picked = pick(tube_order, tubes)
    picked_mine = mine(picked)
    picked_theirs = theirs(picked)
    pixels = jnp.concatenate([picked_mine, swap(picked_theirs)], 1)

    split_own = vec_split[0]
    split_other = swap(split_own)
    split_widths = [HALF, HALF, HALF_FF] * 2 + [DD // 2, DD // 2, DFF // 2, PIX // 2]
    split_parts = [
        jnp.concatenate(pair)[None]
        for pair in zip(cut(split_own, split_widths), cut(split_other, split_widths))
    ]
    shared = cut(vec_shared, [D] * 15 + [DD] * 9)
    dec_widths = [D // 2, DD // 2, DFF // 2, 3 * DD // 2, DFF // 2, PIX // 2]
    own_parts = cut(dec_own, dec_widths)
    other_parts = cut(dec_other, dec_widths)
    proj = jnp.where(
        half == 0,
        jnp.concatenate([own_parts[0], other_parts[0]], 0),
        jnp.concatenate([other_parts[0], own_parts[0]], 0),
    )
    d_out, d_down, d_up, head_rows = (
        jnp.concatenate([own_parts[index], other_parts[index]], 0) for index in (1, 2, 4, 5)
    )
    kinds = lambda block: block.reshape(3, DD // 2, DD)
    d_qkv = jnp.concatenate([kinds(own_parts[3]), kinds(other_parts[3])], 1).reshape(3 * DD, DD)

    visible = order[:VIS]
    pos_enc = sinusoid_at(visible, D)
    pos_dec = sinusoid_at(order, DD)

    embed = jnp.concatenate([enc_own[:D], enc_other[:D]], 0)
    stream = nn(pixels[:VIS], embed) + shared[0] + pos_enc
    kept = []
    enc_vecs = []
    for layer in range(2):
        base = 1 + 6 * layer
        vecs = jnp.concatenate(
            [jnp.stack(shared[base : base + 6]), jnp.zeros((2, D), f32)], 0
        )
        bq, bv, bu = split_parts[3 * layer : 3 * layer + 3]
        bqkv = jnp.concatenate([bq, jnp.zeros_like(bq), bv], 1)
        result = encoder_layer(
            D + layer * LAYER_ROWS, stream, vecs, bqkv, bu, enc_own, enc_other, f"encoder_{layer}"
        )
        kept.append((stream, result))
        enc_vecs.append(vecs)
        stream = result[0]
    unit_e, rate_e = norm_parts(stream)
    enc_normed = (unit_e * shared[13] + shared[14]).astype(bf16)
    latent = nn(enc_normed, proj)

    dec_start = pos_dec + jnp.concatenate(
        [latent, jnp.broadcast_to(shared[15][None], (MASKED, DD))], 0
    )
    bq, bv, bu, bh = split_parts[6:]
    h, qkv = decoder_qkv(
        dec_start, shared[16][None], shared[17][None], d_qkv,
        jnp.concatenate([bq, jnp.zeros_like(bq), bv], 1),
    )
    mixed, logs = attend(qkv)
    scal = jnp.broadcast_to(
        jnp.stack([counted, 2.0 * workers / (PIX * loss_weight) * counted] + [counted] * 6)[:, None],
        (8, 128),
    )
    dec_vecs = jnp.stack([shared[index] for index in (18, 19, 20, 21, 22, 23, 22, 23)])
    (
        grad_mixed, grad_middle, g_out, g_down, g_up, g_head, g_vec, g_bu, g_bh, loss_lanes
    ) = decoder_tokens(
        mixed, dec_start, pixels, scal, dec_vecs, bu, bh, d_out, d_down, d_up, head_rows
    )
    dq, dk, dv = attend_back(qkv, mixed, grad_mixed, logs)
    grad_start, g_qkv, g_vec1 = decoder_qkv_back(
        dq, dk, dv, h, dec_start, grad_middle, shared[16][None], d_qkv
    )
    latent_low = grad_start[:VIS].astype(bf16)
    g_proj = tn(enc_normed, latent_low)
    grad_normed = nt(latent_low, proj)
    grad = norm_back(grad_normed, shared[13], unit_e, rate_e)

    proj_parts = g_proj.reshape(2, D // 2, DD)
    halves = lambda block, index: cut(block, [block.shape[0] // 2] * 2)[index]

    def dec_half(index):
        g_kinds = g_qkv.reshape(3, 2, DD // 2, DD)[:, index].reshape(3 * DD // 2, DD)
        first = mine(proj_parts) if index == 0 else theirs(proj_parts)
        return jnp.concatenate(
            [first, halves(g_out, index), halves(g_down, index), g_kinds, halves(g_up, index),
             halves(g_head, index)],
            0,
        )

    dec_comb = dec_half(0) + swap(dec_half(1)) + dec_error[0, 0].astype(f32)

    lefts = [None, None]
    rights = [None, None]
    enc_vec_grads = [None, None]
    for layer in (1, 0):
        source, result = kept[layer]
        grad, lefts[layer], rights[layer], g_vecs, g_hidden, g_qv = encoder_layer_back(
            D + layer * LAYER_ROWS, grad, source, enc_vecs[layer], result, enc_own, enc_other,
            f"encoder_back_{layer}",
        )
        enc_vec_grads[layer] = (g_vecs, g_hidden, g_qv)
    embed_low = grad.astype(bf16)
    left = jnp.stack(
        [
            jnp.concatenate([picked_mine[:VIS], lefts[0][0], lefts[1][0]], 1),
            jnp.concatenate([picked_theirs[:VIS], swap(lefts[0][1]), swap(lefts[1][1])], 1),
        ]
    )
    right_mine = jnp.concatenate([embed_low[None]] + rights, 0)
    right = jnp.stack(
        [
            right_mine,
            jnp.concatenate([swap(embed_low)[None]] + [swap(value) for value in rights], 0),
        ]
    )

    def split_half(index):
        pieces = []
        for layer in range(2):
            _, g_hidden, g_qv = enc_vec_grads[layer]
            pieces += [
                cut(g_qv[0], [HALF] * 2)[index],
                cut(g_qv[1], [HALF] * 2)[index],
                cut(g_hidden[0], [HALF_FF] * 2)[index],
            ]
        pieces += [
            cut(g_vec1[0], [DD // 2] * 2)[index],
            cut(g_vec1[1], [DD // 2] * 2)[index],
            cut(g_bu[0], [DFF // 2] * 2)[index],
            cut(g_bh[0], [PIX // 2] * 2)[index],
        ]
        return jnp.concatenate(pieces)

    shared_grad = jnp.concatenate(
        [jnp.sum(embed_low.astype(f32), 0)]
        + [enc_vec_grads[layer][0][:6].reshape(-1) for layer in range(2)]
        + [jnp.sum(grad_normed * unit_e, 0), jnp.sum(grad_normed, 0)]
        + [g_vec1[4], g_vec1[2], g_vec1[3], g_vec[:6].reshape(-1)]
    )
    loss_part = jnp.sum(loss_lanes) / PIX
    sent = jnp.concatenate([split_half(1), shared_grad, loss_part[None]])
    local = jnp.concatenate([split_half(0), shared_grad, loss_part[None]])
    vec_local = local + swap(sent)

    enc_error_part = error_factor(factors[0, :, :D], enc_error[0, 0])
    enc_left = left_factor(factors[0, :, :D], left, right, enc_error_part)
    dec_left = jnp.einsum("rc,xc->rx", factors[0, :, D:], dec_comb, precision=highest_precision)
    enc_left, dec_left, vec_sum = lax.psum((enc_left, dec_left, vec_local), "dp")
    enc_basis, dec_basis = orthonormal(enc_left, dec_left)
    enc_rows = enc_basis.shape[1] // workers
    dec_rows = dec_basis.shape[1] // workers
    enc_owned = lax.dynamic_slice_in_dim(enc_basis, worker_index * enc_rows, enc_rows, 1)
    dec_owned = lax.dynamic_slice_in_dim(dec_basis, worker_index * dec_rows, dec_rows, 1)
    enc_right, dec_right = lax.psum(
        (
            right_factor(enc_basis, left, right, enc_error[0, 0]),
            jnp.einsum("rx,xc->rc", dec_basis, dec_comb, precision=highest_precision),
        ),
        "dp",
    )
    enc_right = enc_right / workers
    dec_right = dec_right / workers
    enc_error_new = residue(enc_basis, enc_right, left, right, enc_error[0, 0])
    dec_error_new = (
        dec_comb - jnp.einsum("rx,rc->xc", dec_basis, dec_right, precision=highest_precision)
    ).astype(bf16)
    enc_mom = momentum_keep * enc_moment[0] + jnp.einsum(
        "rx,rc->xc", enc_owned, enc_right, precision=highest_precision
    )
    dec_mom = momentum_keep * dec_moment[0] + jnp.einsum(
        "rx,rc->xc", dec_owned, dec_right, precision=highest_precision
    )
    split_len = split_own.shape[0]
    split_mom = momentum_keep * split_moment[0] + vec_sum[:split_len] / workers
    shared_mom = momentum_keep * shared_moment + vec_sum[split_len:-1] / workers
    return (
        vec_sum[-1],
        loss_weight,
        (enc_weights[0] - step_rate * enc_mom)[None],
        enc_mom[None],
        enc_error_new[None, None],
        (dec_weights[0] - step_rate * dec_mom)[None],
        dec_mom[None],
        dec_error_new[None, None],
        jnp.concatenate([enc_right, dec_right], 1)[None],
        (vec_split[0] - step_rate * split_mom)[None],
        split_mom[None],
        vec_shared - step_rate * shared_mom,
        shared_mom,
    )


def solution(mesh):
    placed = (
        P("dp", None, "tensor"),
        P("dp", None),
        P("dp"),
        P("tensor", "dp", None),
        P("tensor", "dp", None),
        P("tensor", None),
        P(),
        P("tensor", "dp", None),
        P("tensor", "dp", None),
        P("tensor", None),
        P(),
        P("dp", "tensor", None, None),
        P("dp", "tensor", None, None),
        P("tensor", None, None),
    )
    return jax.shard_map(
        per_device,
        mesh=mesh,
        in_specs=placed,
        out_specs=(
            P(),
            P(),
            P("tensor", "dp", None),
            P("tensor", "dp", None),
            P("dp", "tensor", None, None),
            P("tensor", "dp", None),
            P("tensor", "dp", None),
            P("dp", "tensor", None, None),
            P("tensor", None, None),
            P("tensor", None),
            P("tensor", None),
            P(),
            P(),
        ),
        check_vma=False,
    )
```

```python
import math

import jax
import jax.numpy as jnp
from jax import lax
from jax.experimental import pallas as pl
from jax.experimental.pallas import tpu as pltpu
from jax.sharding import PartitionSpec as P

D = 768
HEAD_DIM = 64
FF = 3072
DD = 384
DFF = 1536
PIX = 1536
TUBES = 1568
VIS = 160
MASKED = 1408
RANK = 8

f32 = jnp.float32
bf16 = jnp.bfloat16
highest_precision = lax.Precision.HIGHEST
norm_eps = 1e-06
momentum_keep = 0.9
step_rate = 1000.0
LOG2E = 1.4426950408889634
SCORE = HEAD_DIM ** (-0.5)
BIG_VMEM = 56 << 20


def nn(left, right):
    return lax.dot_general(left, right, (((1,), (0,)), ((), ())), preferred_element_type=f32)


def nt(left, right):
    return lax.dot_general(left, right, (((1,), (1,)), ((), ())), preferred_element_type=f32)


def tn(left, right):
    return lax.dot_general(left, right, (((0,), (0,)), ((), ())), preferred_element_type=f32)


def col_sum(value):
    return jnp.sum(value, 0, keepdims=True)


def norm_parts(stream):
    center = stream - jnp.mean(stream, -1, keepdims=True)
    rate = lax.rsqrt(jnp.mean(center * center, -1, keepdims=True) + norm_eps)
    return center * rate, rate


def norm_back(grad, gain, unit, rate):
    grad_unit = grad * gain
    return rate * (
        grad_unit
        - jnp.mean(grad_unit, -1, keepdims=True)
        - unit * jnp.mean(grad_unit * unit, -1, keepdims=True)
    )


def gelu_pair(before):
    cdf_tail = jnp.exp(-0.5 * before * before)
    size = jnp.abs(before) * (2.0 ** -0.5)
    t = 1.0 / (1.0 + 0.3275911 * size)
    poly = t * (
        0.254829592 + t * (-0.284496736 + t * (1.421413741 + t * (-1.453152027 + t * 1.061405429)))
    )
    tail = 0.5 * poly * cdf_tail
    cdf = jnp.where(before < 0, tail, 1.0 - tail)
    return before * cdf, cdf + before * cdf_tail * (1.0 / math.sqrt(2.0 * math.pi))


def split3(value):
    high = value.astype(bf16)
    rest = value - high.astype(f32)
    middle = rest.astype(bf16)
    low = (rest - middle.astype(f32)).astype(bf16)
    return jnp.concatenate([high, middle, low], 0)


def fold3(value):
    rows = value.shape[0] // 3
    return value[:rows] + value[rows : 2 * rows] + value[2 * rows :]


def sinusoid_at(place, width):
    column = jnp.arange(width)
    rate = jnp.exp(-(2 * (column // 2)).astype(f32) * (math.log(10000.0) / width))
    angle = place.astype(f32)[:, None] * rate[None, :]
    return jnp.where(column % 2 == 0, jnp.sin(angle), jnp.cos(angle))


def params(**more):
    return pltpu.CompilerParams(vmem_limit_bytes=BIG_VMEM, **more)


def whole(shape):
    return pl.BlockSpec(shape, lambda *_: (0,) * len(shape))


def any_spec():
    return pl.BlockSpec(memory_space=pl.ANY)


def vmem_spec():
    return pl.BlockSpec(memory_space=pltpu.VMEM)


PICK_ROWS = 224


def pick_kernel(order_ref, tubes_ref, out_ref):
    column = lax.broadcasted_iota(jnp.int32, (1, TUBES), 1)
    hot = jnp.where(order_ref[0] == column, 1.0, 0.0).astype(bf16)
    out_ref[0] = nn(hot, tubes_ref[0]).astype(bf16)


def pick(order, tubes):
    clips, _, width = tubes.shape
    return pl.pallas_call(
        pick_kernel,
        grid=(clips, TUBES // PICK_ROWS),
        in_specs=[
            pl.BlockSpec((1, PICK_ROWS, 1), lambda c, i: (c, i, 0)),
            pl.BlockSpec((1, TUBES, width), lambda c, i: (c, 0, 0)),
        ],
        out_specs=pl.BlockSpec((1, PICK_ROWS, width), lambda c, i: (c, i, 0)),
        out_shape=jax.ShapeDtypeStruct(tubes.shape, bf16),
        compiler_params=params(),
        name="pick_tubes",
    )(order[:, :, None], tubes)


QKV_ROWS = 392


def qkv_kernel(pos_ref, latent_ref, vec_ref, w_ref, bias_ref, x_ref, h_ref, qkv_ref):
    token, gain, shift = (vec_ref[index : index + 1] for index in range(3))
    hidden = jnp.broadcast_to(token, (QKV_ROWS, DD))
    shown = jnp.concatenate([latent_ref[...], hidden[VIS:]], 0)
    x = pos_ref[...] + jnp.where(pl.program_id(0) == 0, shown, hidden)
    x_ref[...] = x
    unit, _ = norm_parts(x)
    h = (unit * gain + shift).astype(bf16)
    h_ref[...] = h
    qkv_ref[...] = (nt(h, w_ref[...]) + bias_ref[...]).astype(bf16)


def decoder_qkv(pos, latent, vecs, weights, bias):
    rows = lambda width: pl.BlockSpec((QKV_ROWS, width), lambda i: (i, 0))
    return pl.pallas_call(
        qkv_kernel,
        grid=(TUBES // QKV_ROWS,),
        in_specs=[
            rows(DD),
            whole((VIS, DD)),
            whole((8, DD)),
            whole((3 * DD, DD)),
            whole((1, 3 * DD)),
        ],
        out_specs=[rows(DD), rows(DD), rows(3 * DD)],
        out_shape=[
            jax.ShapeDtypeStruct((TUBES, DD), f32),
            jax.ShapeDtypeStruct((TUBES, DD), bf16),
            jax.ShapeDtypeStruct((TUBES, 3 * DD), bf16),
        ],
        compiler_params=params(),
        name="decoder_qkv",
    )(pos, latent, vecs, weights, bias)


FWD_ROWS = 392
BWD_ROWS = 256
PAIRS = DD // 128


def half_lane(index):
    return lax.broadcasted_iota(jnp.int32, (1, 128), 1) // HEAD_DIM == index


def attend_kernel(q_ref, k_ref, v_ref, o_ref, lse_ref):
    q = q_ref[...]
    k = k_ref[...]
    v_one = jnp.concatenate([v_ref[...], jnp.ones((TUBES, 128), bf16)], 1)
    mixed, logs = [], []
    for head in range(2):
        scores = nt(jnp.where(half_lane(head), q, jnp.zeros_like(q)), k)
        top = jnp.max(scores, 1, keepdims=True)
        expo = jnp.exp2((scores - top) * (SCORE * LOG2E)).astype(bf16)
        both = nn(expo, v_one)
        total = both[:, 128:]
        mixed.append(both[:, :128] / total)
        logs.append(top * (SCORE * LOG2E) + jnp.log2(total))
    o_ref[...] = jnp.where(half_lane(0), mixed[0], mixed[1])
    lse_ref[0] = jnp.where(half_lane(0), logs[0], logs[1])


def attend(qkv):
    return pl.pallas_call(
        attend_kernel,
        grid=(PAIRS, TUBES // FWD_ROWS),
        in_specs=[
            pl.BlockSpec((FWD_ROWS, 128), lambda p, i: (i, p)),
            pl.BlockSpec((TUBES, 128), lambda p, i: (0, PAIRS + p)),
            pl.BlockSpec((TUBES, 128), lambda p, i: (0, 2 * PAIRS + p)),
        ],
        out_specs=[
            pl.BlockSpec((FWD_ROWS, 128), lambda p, i: (i, p)),
            pl.BlockSpec((1, FWD_ROWS, 128), lambda p, i: (p, i, 0)),
        ],
        out_shape=[
            jax.ShapeDtypeStruct((TUBES, DD), f32),
            jax.ShapeDtypeStruct((PAIRS, TUBES, 128), f32),
        ],
        compiler_params=params(),
        name="attend",
    )(qkv, qkv, qkv)


def attend_back_kernel(
    q_ref, k_ref, v_ref, o_ref, do_ref, lse_ref, dq_ref, dk_ref, dv_ref, k_turned, dk_sum, dv_sum
):
    step = pl.program_id(1)

    @pl.when(step == 0)
    def _():
        k_turned[...] = k_ref[...].T
        dk_sum[...] = jnp.zeros_like(dk_sum)
        dv_sum[...] = jnp.zeros_like(dv_sum)

    valid = lax.broadcasted_iota(jnp.int32, (BWD_ROWS, 1), 0) + step * BWD_ROWS < TUBES
    zero = jnp.zeros((), bf16)
    q = jnp.where(valid, q_ref[...], zero)
    grad = jnp.where(valid, do_ref[...], zero)
    dots = jnp.where(valid, o_ref[...], 0.0) * grad.astype(f32)
    logs = jnp.where(valid, lse_ref[0], 0.0).T
    select = (
        lax.broadcasted_iota(jnp.int32, (8, 128), 1) // HEAD_DIM
        == lax.broadcasted_iota(jnp.int32, (8, 128), 0)
    ).astype(f32)
    row_total = lax.dot_general(
        select, dots, (((1,), (1,)), ((), ())), precision=highest_precision,
        preferred_element_type=f32,
    )
    k = k_ref[...]
    v = v_ref[...]
    turned = []
    for head in range(2):
        mask = half_lane(head)
        q_head = jnp.where(mask, q, zero)
        grad_head = jnp.where(mask, grad, zero)
        low = head * HEAD_DIM
        probs = jnp.exp2(nt(k, q_head) * (SCORE * LOG2E) - logs[low : low + 1])
        grad_scores = (probs * (nt(v, grad_head) - row_total[head : head + 1])).astype(bf16)
        dv_sum[...] += nn(probs.astype(bf16), grad_head)
        dk_sum[...] += nn(grad_scores, q_head)
        turned.append(nn(k_turned[low : low + HEAD_DIM], grad_scores))
    dq_ref[...] = (jnp.concatenate(turned, 0).T * SCORE).astype(bf16)

    @pl.when(step == pl.num_programs(1) - 1)
    def _():
        dk_ref[...] = (dk_sum[...] * SCORE).astype(bf16)
        dv_ref[...] = dv_sum[...].astype(bf16)


def attend_back(qkv, mixed, grad_mixed, logs):
    some = pl.BlockSpec((BWD_ROWS, 128), lambda p, i: (i, p))
    full = pl.BlockSpec((TUBES, 128), lambda p, i: (0, p))
    return pl.pallas_call(
        attend_back_kernel,
        grid=(PAIRS, pl.cdiv(TUBES, BWD_ROWS)),
        in_specs=[
            some,
            pl.BlockSpec((TUBES, 128), lambda p, i: (0, PAIRS + p)),
            pl.BlockSpec((TUBES, 128), lambda p, i: (0, 2 * PAIRS + p)),
            some,
            some,
            pl.BlockSpec((1, BWD_ROWS, 128), lambda p, i: (p, i, 0)),
        ],
        out_specs=[some, full, full],
        out_shape=[jax.ShapeDtypeStruct((TUBES, DD), bf16)] * 3,
        scratch_shapes=[
            pltpu.VMEM((128, TUBES), bf16),
            pltpu.VMEM((TUBES, 128), f32),
            pltpu.VMEM((TUBES, 128), f32),
        ],
        compiler_params=params(),
        name="attend_back",
    )(qkv, qkv, qkv, mixed, grad_mixed, logs)


TOKEN_ROWS = 224
CHUNK = 384
DEC_O = D // 2
DEC_D = DEC_O + DD // 2
DEC_Q = DEC_D + DFF // 2
DEC_U = DEC_Q + 3 * DD // 2
DEC_H = DEC_U + DFF // 2
DEC_ROWS = DEC_H + PIX // 2
CHUNKS = DFF // CHUNK


def token_kernel(
    a_ref, x_ref, pix_ref, scal_ref, vec_ref, bu_ref, bh_ref, wo_ref, wd_ref, wu_ref, wh_ref,
    da_ref, dx1_ref,
    grads_ref, gvec_ref, gbu_ref, gbh_ref, loss_ref,
    slope,
):
    step = pl.program_id(0)
    sums = (grads_ref, gvec_ref, gbu_ref, gbh_ref, loss_ref)

    @pl.when(step == 0)
    def _():
        for ref in sums:
            ref[...] = jnp.zeros_like(ref)

    bo, g2, b2, bd, gf, sf = (vec_ref[index : index + 1] for index in range(6))
    a = a_ref[...].astype(bf16)
    x1 = x_ref[...] + (nn(a, wo_ref[...]) + bo)
    unit2, rate2 = norm_parts(x1)
    h2 = (unit2 * g2 + b2).astype(bf16)
    out = x1 + bd
    active = []
    for chunk in range(CHUNKS):
        part = pl.ds(chunk * CHUNK, CHUNK)
        value, slope_part = gelu_pair(nt(h2, wu_ref[part]) + bu_ref[:, part])
        slope[:, part] = slope_part
        active.append(value.astype(bf16))
        out = out + nn(active[-1], wd_ref[part])
    unit_f, rate_f = norm_parts(out)
    final = (unit_f * gf + sf).astype(bf16)
    pixels = [pix_ref[:, pl.ds(chunk * CHUNK, CHUNK)].astype(f32) for chunk in range(CHUNKS)]
    center = sum(jnp.sum(part, 1, keepdims=True) for part in pixels) * (1.0 / PIX)
    square = sum(jnp.sum(part * part, 1, keepdims=True) for part in pixels) * (1.0 / PIX)
    spread = lax.rsqrt(square - center * center + norm_eps)
    row = lax.broadcasted_iota(jnp.int32, (TOKEN_ROWS, 1), 0) + step * TOKEN_ROWS
    counted = jnp.where(row >= VIS, scal_ref[0:1, 0:1], 0.0)
    rate = jnp.where(row >= VIS, scal_ref[1:2, 0:1], 0.0)
    grad_final = jnp.zeros((TOKEN_ROWS, DD), f32)
    for chunk in range(CHUNKS):
        part = pl.ds(chunk * CHUNK, CHUNK)
        target = (pixels[chunk] - center) * spread
        miss = nt(final, wh_ref[part]) + bh_ref[:, part] - target
        loss_ref[:, part] += col_sum(counted * miss * miss)
        grad_guess = (rate * miss).astype(bf16)
        gbh_ref[:, part] += col_sum(grad_guess.astype(f32))
        grads_ref[chunk // 2, pl.ds(DEC_H + (chunk % 2) * CHUNK, CHUNK)] += tn(grad_guess, final)
        grad_final = grad_final + nn(grad_guess, wh_ref[part])
    grad_out = norm_back(grad_final, gf, unit_f, rate_f)
    out_low = grad_out.astype(bf16)
    grad_h2 = jnp.zeros((TOKEN_ROWS, DD), f32)
    for chunk in range(CHUNKS):
        part = pl.ds(chunk * CHUNK, CHUNK)
        grads_ref[chunk // 2, pl.ds(DEC_D + (chunk % 2) * CHUNK, CHUNK)] += tn(
            active[chunk], out_low
        )
        grad_before = (slope[:, part] * nt(out_low, wd_ref[part])).astype(bf16)
        gbu_ref[:, part] += col_sum(grad_before.astype(f32))
        grads_ref[chunk // 2, pl.ds(DEC_U + (chunk % 2) * CHUNK, CHUNK)] += tn(grad_before, h2)
        grad_h2 = grad_h2 + nn(grad_before, wu_ref[part])
    grad_x1 = grad_out + norm_back(grad_h2, g2, unit2, rate2)
    x1_low = grad_x1.astype(bf16)
    g_out = tn(a, x1_low)
    for group in range(2):
        grads_ref[group, pl.ds(DEC_O, DD // 2)] += g_out[group * DD // 2 : (group + 1) * DD // 2]
    da_ref[...] = nt(x1_low, wo_ref[...]).astype(bf16)
    dx1_ref[...] = grad_x1
    gvec_ref[0:1] += col_sum(x1_low.astype(f32))
    gvec_ref[1:2] += col_sum(grad_h2 * unit2)
    gvec_ref[2:3] += col_sum(grad_h2)
    gvec_ref[3:4] += col_sum(out_low.astype(f32))
    gvec_ref[4:5] += col_sum(grad_final * unit_f)
    gvec_ref[5:6] += col_sum(grad_final)


def decoder_tokens(mixed, x, pixels, scal, vecs, bu, bh, wo, wd, wu, wh):
    rows = lambda width: pl.BlockSpec((TOKEN_ROWS, width), lambda i: (i, 0))
    sums = [(2, DEC_ROWS, DD), (8, DD), (1, DFF), (1, PIX), (1, PIX)]
    return pl.pallas_call(
        token_kernel,
        grid=(TUBES // TOKEN_ROWS,),
        in_specs=[
            rows(DD),
            rows(DD),
            rows(PIX),
            whole((8, 128)),
            whole((8, DD)),
            whole((1, DFF)),
            whole((1, PIX)),
            whole((DD, DD)),
            whole((DFF, DD)),
            whole((DFF, DD)),
            whole((PIX, DD)),
        ],
        out_specs=[rows(DD), rows(DD)] + [whole(shape) for shape in sums],
        out_shape=[
            jax.ShapeDtypeStruct((TUBES, DD), bf16),
            jax.ShapeDtypeStruct((TUBES, DD), f32),
        ]
        + [jax.ShapeDtypeStruct(shape, f32) for shape in sums],
        scratch_shapes=[pltpu.VMEM((TOKEN_ROWS, DFF), f32)],
        compiler_params=params(),
        name="decoder_tokens",
    )(mixed, x, pixels, scal, vecs, bu, bh, wo, wd, wu, wh)


def qkv_back_kernel(
    half_ref, dq_ref, dk_ref, dv_ref, h_ref, x_ref, dx1_ref, vec_ref, w_ref, normed_ref, _,
    latent_ref, grads_ref, gvec_ref,
    g_qkv, g_proj, sems,
):
    step = pl.program_id(0)

    @pl.when(step == 0)
    def _():
        g_qkv[...] = jnp.zeros_like(g_qkv)
        gvec_ref[...] = jnp.zeros_like(gvec_ref)

    h = h_ref[...]
    grads = (dq_ref[...], dk_ref[...], dv_ref[...])
    grad_h = jnp.zeros((QKV_ROWS, DD), f32)
    for index, grad in enumerate(grads):
        g_both = tn(grad, h)
        for group in range(2):
            rows = pl.ds(index * DD // 2, DD // 2)
            g_qkv[group, rows] += g_both[group * DD // 2 : (group + 1) * DD // 2]
        grad_h = grad_h + nn(grad, w_ref[pl.ds(index * DD, DD)])
    unit, rate = norm_parts(x_ref[...])
    grad_x = dx1_ref[...] + norm_back(grad_h, vec_ref[1:2], unit, rate)
    row = lax.broadcasted_iota(jnp.int32, (QKV_ROWS, 1), 0) + step * QKV_ROWS
    gvec_ref[0:1] += col_sum(grads[0].astype(f32))
    gvec_ref[1:2] += col_sum(grads[2].astype(f32))
    gvec_ref[2:3] += col_sum(grad_h * unit)
    gvec_ref[3:4] += col_sum(grad_h)
    gvec_ref[4:5] += col_sum(jnp.where(row >= VIS, grad_x, 0.0))

    @pl.when(step == 0)
    def _():
        latent = grad_x[:VIS].astype(bf16)
        latent_ref[...] = latent
        both = tn(normed_ref[...], latent)
        g_proj[0] = both[: D // 2]
        g_proj[1] = both[D // 2 :]

    @pl.when(step == pl.num_programs(0) - 1)
    def _():
        half = half_ref[0]
        copies = [
            pltpu.make_async_copy(g_qkv, grads_ref.at[:, pl.ds(DEC_Q, 3 * DD // 2)], sems.at[0]),
            pltpu.make_async_copy(
                g_proj.at[half], grads_ref.at[0, pl.ds(0, D // 2)], sems.at[1]
            ),
            pltpu.make_async_copy(
                g_proj.at[1 - half], grads_ref.at[1, pl.ds(0, D // 2)], sems.at[2]
            ),
        ]
        for copy in copies:
            copy.start()
        for copy in copies:
            copy.wait()


def decoder_qkv_back(half, dq, dk, dv, h, x, dx1, vecs, weights, normed, grads):
    rows = lambda width: pl.BlockSpec((QKV_ROWS, width), lambda i: (i, 0))
    return pl.pallas_call(
        qkv_back_kernel,
        grid=(TUBES // QKV_ROWS,),
        in_specs=[pl.BlockSpec(memory_space=pltpu.SMEM)]
        + [rows(DD)] * 6
        + [whole((8, DD)), whole((3 * DD, DD)), whole((VIS, D)), any_spec()],
        out_specs=[whole((VIS, DD)), any_spec(), whole((8, DD))],
        out_shape=[
            jax.ShapeDtypeStruct((VIS, DD), bf16),
            jax.ShapeDtypeStruct((2, DEC_ROWS, DD), f32),
            jax.ShapeDtypeStruct((8, DD), f32),
        ],
        scratch_shapes=[
            pltpu.VMEM((2, 3 * DD // 2, DD), f32),
            pltpu.VMEM((2, D // 2, DD), f32),
            pltpu.SemaphoreType.DMA((3,)),
        ],
        input_output_aliases={10: 1},
        compiler_params=params(),
        name="decoder_qkv_back",
    )(half, dq, dk, dv, h, x, dx1, vecs, weights, normed, grads)


HALF = D // 2
HALF_FF = FF // 2
LAYER_ROWS = 4 * HALF + 2 * HALF_FF
AT_O, AT_D, AT_Q, AT_U = 0, HALF, HALF + HALF_FF, HALF + HALF_FF + 3 * HALF
STAGES = ((AT_Q, 3 * HALF), (AT_O, HALF), (AT_U, HALF_FF), (AT_D, HALF_FF))


def stage_copies(sources, start, held, sems):
    return [
        [
            pltpu.make_async_copy(
                sources[group].at[pl.ds(start + at, size)],
                held.at[group, pl.ds(at, size)],
                sems.at[group, stage],
            )
            for group in range(2)
        ]
        for stage, (at, size) in enumerate(STAGES)
    ]


def encoder_kernel(start, last, x_ref, vec_ref, bqkv_ref, bu_ref, own_ref, other_ref, *refs):
    if last:
        proj_ref, *refs = refs
        normed_ref, latent_ref = refs[8:10]
    out_ref, h_ref, qkv_ref, a_ref, x1_ref, h2_ref, u_ref, slope_ref = refs[:8]
    held, sems = refs[-2:]
    copies = stage_copies((own_ref, other_ref), start, held, sems)
    for stage in copies:
        for copy in stage:
            copy.start()

    def wait(stage):
        for copy in copies[stage]:
            copy.wait()

    g1, b1, bo, g2, b2, bd = (vec_ref[index : index + 1] for index in range(6))
    x = x_ref[...]
    unit, _ = norm_parts(x)
    h = (unit * g1 + b1).astype(bf16)
    h_ref[...] = h
    wait(0)
    for kind in range(3):
        for group in range(2):
            part = pl.ds((2 * kind + group) * HALF, HALF)
            rows = pl.ds(AT_Q + kind * HALF, HALF)
            qkv_ref[:, part] = (nt(h, held[group, rows]) + bqkv_ref[:, part]).astype(bf16)
    for pair in range(D // 128):
        q, k, v = (qkv_ref[:, pl.ds(kind * D + pair * 128, 128)] for kind in range(3))
        v_one = jnp.concatenate([v, jnp.ones((VIS, 128), bf16)], 1)
        mixed = []
        for head in range(2):
            scores = nt(jnp.where(half_lane(head), q, jnp.zeros_like(q)), k)
            top = jnp.max(scores, 1, keepdims=True)
            expo = jnp.exp2((scores - top) * (SCORE * LOG2E)).astype(bf16)
            both = nn(expo, v_one)
            mixed.append(both[:, :128] / both[:, 128:])
        a_ref[:, pl.ds(pair * 128, 128)] = jnp.where(half_lane(0), mixed[0], mixed[1]).astype(bf16)
    wait(1)
    x1 = x + bo
    for group in range(2):
        x1 = x1 + nn(a_ref[:, pl.ds(group * HALF, HALF)], held[group, pl.ds(AT_O, HALF)])
    x1_ref[...] = x1
    unit2, _ = norm_parts(x1)
    h2 = (unit2 * g2 + b2).astype(bf16)
    h2_ref[...] = h2
    wait(2)
    wait(3)
    out = x1 + bd
    for group in range(2):
        for chunk in range(HALF_FF // CHUNK):
            part = pl.ds(group * HALF_FF + chunk * CHUNK, CHUNK)
            before = nt(h2, held[group, pl.ds(AT_U + chunk * CHUNK, CHUNK)]) + bu_ref[:, part]
            value, slope = gelu_pair(before)
            slope_ref[:, part] = slope
            active = value.astype(bf16)
            u_ref[:, part] = active
            out = out + nn(active, held[group, pl.ds(AT_D + chunk * CHUNK, CHUNK)])
    out_ref[...] = out
    if last:
        unit3, _ = norm_parts(out)
        normed = (unit3 * vec_ref[6:7] + vec_ref[7:8]).astype(bf16)
        normed_ref[...] = normed
        latent_ref[...] = nn(normed, proj_ref[...])


def encoder_layer(start, x, vecs, bqkv, bu, own, other, name, proj=None):
    shapes = [
        ((VIS, D), f32),
        ((VIS, D), bf16),
        ((VIS, 3 * D), bf16),
        ((VIS, D), bf16),
        ((VIS, D), f32),
        ((VIS, D), bf16),
        ((VIS, FF), bf16),
        ((VIS, FF), f32),
    ]
    last = proj is not None
    more = ()
    if last:
        more = (proj,)
        shapes += [((VIS, D), bf16), ((VIS, DD), f32)]
    return pl.pallas_call(
        lambda *refs: encoder_kernel(start, last, *refs),
        in_specs=[vmem_spec()] * 4 + [any_spec()] * 2 + [vmem_spec()] * len(more),
        out_specs=[vmem_spec()] * len(shapes),
        out_shape=[jax.ShapeDtypeStruct(shape, kind) for shape, kind in shapes],
        scratch_shapes=[
            pltpu.VMEM((2, LAYER_ROWS, D), bf16),
            pltpu.SemaphoreType.DMA((2, len(STAGES))),
        ],
        compiler_params=params(),
        name=name,
    )(x, vecs, bqkv, bu, own, other, *more)


RIGHT_AT = LAYER_ROWS


def encoder_back_kernel(start, last, *refs):
    (
        grad_ref, x_ref, vec_ref, h_ref, qkv_ref, a_ref, x1_ref, h2_ref, u_ref, slope_ref,
        start_ref, own_ref, other_ref, extra_ref,
    ) = refs[:14]
    refs = refs[14:]
    if last:
        out_ref, proj_ref, *refs = refs
    dx_ref, mine_ref, other_pack_ref, left_ref, gvec_ref, gbu_ref, gbq_ref = refs[:7]
    held, sems, da, dqkv = refs[7:]
    packs = (mine_ref, other_pack_ref)
    copies = stage_copies((own_ref, other_ref), start, held, sems)
    for stage in (3, 2, 1, 0):
        for copy in copies[stage]:
            copy.start()

    def wait(stage):
        for copy in copies[stage]:
            copy.wait()

    g1, b1, bo, g2, b2, bd = (vec_ref[index : index + 1] for index in range(6))
    gvec_ref[6:8] = jnp.zeros((2, D), f32)
    if last:
        unit3, rate3 = norm_parts(out_ref[...])
        grad_normed = nt(grad_ref[...], proj_ref[...])
        grad_out = norm_back(grad_normed, vec_ref[6:7], unit3, rate3)
        gvec_ref[6:7] = col_sum(grad_normed * unit3)
        gvec_ref[7:8] = col_sum(grad_normed)
    else:
        grad_out = grad_ref[...]
    out_low = grad_out.astype(bf16)
    unit2, rate2 = norm_parts(x1_ref[...])
    grad_h2 = jnp.zeros((VIS, D), f32)
    wait(3)
    wait(2)
    for group in range(2):
        for chunk in range(HALF_FF // CHUNK):
            part = pl.ds(group * HALF_FF + chunk * CHUNK, CHUNK)
            grad_active = nt(out_low, held[group, pl.ds(AT_D + chunk * CHUNK, CHUNK)])
            grad_before = (slope_ref[:, part] * grad_active).astype(bf16)
            packs[group][:, pl.ds(AT_U + chunk * CHUNK, CHUNK)] = grad_before
            packs[group][:, pl.ds(AT_D + chunk * CHUNK, CHUNK)] = u_ref[:, part]
            gbu_ref[:, part] = col_sum(grad_before.astype(f32))
            grad_h2 = grad_h2 + nn(grad_before, held[group, pl.ds(AT_U + chunk * CHUNK, CHUNK)])
    grad_x1 = grad_out + norm_back(grad_h2, g2, unit2, rate2)
    x1_low = grad_x1.astype(bf16)
    wait(1)
    for group in range(2):
        part = pl.ds(group * HALF, HALF)
        da[:, part] = nt(x1_low, held[group, pl.ds(AT_O, HALF)]).astype(bf16)
        packs[group][:, pl.ds(AT_O, HALF)] = a_ref[:, part]
    zero = jnp.zeros((), bf16)
    for pair in range(D // 128):
        lanes = pl.ds(pair * 128, 128)
        q, k, v = (qkv_ref[:, pl.ds(kind * D + pair * 128, 128)] for kind in range(3))
        grad = da[:, lanes]
        dq = dk = dv = jnp.zeros((VIS, 128), f32)
        for head in range(2):
            mask = half_lane(head)
            q_head = jnp.where(mask, q, zero)
            grad_head = jnp.where(mask, grad, zero)
            scores = nt(q_head, k) * SCORE
            expo = jnp.exp(scores - jnp.max(scores, 1, keepdims=True))
            probs = expo / jnp.sum(expo, 1, keepdims=True)
            grad_probs = nt(grad_head, v)
            row_total = jnp.sum(probs * grad_probs, 1, keepdims=True)
            grad_scores = (probs * (grad_probs - row_total)).astype(bf16)
            dv = dv + tn(probs.astype(bf16), grad_head)
            dk = dk + tn(grad_scores, q_head)
            dq = dq + nn(grad_scores, jnp.where(mask, k, zero))
        dqkv[:, lanes] = (dq * SCORE).astype(bf16)
        dqkv[:, pl.ds(D + pair * 128, 128)] = (dk * SCORE).astype(bf16)
        dqkv[:, pl.ds(2 * D + pair * 128, 128)] = dv.astype(bf16)
    wait(0)
    grad_h = jnp.zeros((VIS, D), f32)
    for kind in range(3):
        for group in range(2):
            grad = dqkv[:, pl.ds((2 * kind + group) * HALF, HALF)]
            rows = pl.ds(AT_Q + kind * HALF, HALF)
            packs[group][:, rows] = grad
            grad_h = grad_h + nn(grad, held[group, rows])
    unit, rate = norm_parts(x_ref[...])
    grad_x = grad_x1 + norm_back(grad_h, g1, unit, rate)
    dx_ref[...] = grad_x
    gbq_ref[0:1] = col_sum(dqkv[:, pl.ds(0, D)].astype(f32))
    gbq_ref[1:2] = col_sum(dqkv[:, pl.ds(2 * D, D)].astype(f32))
    gvec_ref[0:1] = col_sum(grad_h * unit)
    gvec_ref[1:2] = col_sum(grad_h)
    gvec_ref[2:3] = col_sum(x1_low.astype(f32))
    gvec_ref[3:4] = col_sum(grad_h2 * unit2)
    gvec_ref[4:5] = col_sum(grad_h2)
    gvec_ref[5:6] = col_sum(out_low.astype(f32))
    rights = [x1_low, out_low, h_ref[...], h2_ref[...]]
    spans = [(AT_O, HALF, 0), (AT_D, HALF_FF, 0), (AT_Q, 3 * HALF, 0), (AT_U, HALF_FF, 0)]
    if not last:
        embed_low = grad_x.astype(bf16)
        rights.append(embed_low)
        gvec_ref[6:7] = col_sum(embed_low.astype(f32))
    starts = jnp.concatenate([split3(start_ref[0]), split3(start_ref[1])], 0)
    before = 0 if last else D
    for index, right in enumerate(rights):
        for pack in packs:
            pack[:, pl.ds(RIGHT_AT + index * D, D)] = right
        inner = nt(starts, right)
        for group in range(2):
            parts = split3(fold3(inner[3 * RANK * group : 3 * RANK * (group + 1)]))
            if index == 4:
                value = fold3(nn(parts, extra_ref[:, pl.ds(group * D, D)]))
                left_ref[group, :, pl.ds(0, D)] = value
            else:
                at, size, _ = spans[index]
                value = fold3(nn(parts, packs[group][:, pl.ds(at, size)]))
                left_ref[group, :, pl.ds(before + at, size)] = value


def encoder_layer_back(start, grad, source, vecs, kept, starts, own, other, extra, name, last=()):
    width = RIGHT_AT + (4 if last else 5) * D
    shapes = [
        ((VIS, D), f32),
        ((VIS, width), bf16),
        ((VIS, width), bf16),
        ((2, RANK, LAYER_ROWS if last else D + LAYER_ROWS), f32),
        ((8, D), f32),
        ((1, FF), f32),
        ((2, D), f32),
    ]
    _, h, qkv, a, x1, h2, u, slope = kept[:8]
    return pl.pallas_call(
        lambda *refs: encoder_back_kernel(start, bool(last), *refs),
        in_specs=[vmem_spec()] * 11 + [any_spec()] * 2 + [vmem_spec()] * (1 + len(last)),
        out_specs=[vmem_spec()] * len(shapes),
        out_shape=[jax.ShapeDtypeStruct(shape, kind) for shape, kind in shapes],
        scratch_shapes=[
            pltpu.VMEM((2, LAYER_ROWS, D), bf16),
            pltpu.SemaphoreType.DMA((2, len(STAGES))),
            pltpu.VMEM((VIS, D), bf16),
            pltpu.VMEM((VIS, 3 * D), bf16),
        ],
        compiler_params=params(),
        name=name,
    )(grad, source, vecs, h, qkv, a, x1, h2, u, slope, starts, own, other, extra, *last)


ROWS = 768
HALF_ROWS = ROWS // 2
ENC_ROWS = D + 2 * LAYER_ROWS
ENC_BLOCKS = ENC_ROWS // ROWS
PER_LAYER = LAYER_ROWS // ROWS


def kinds_of(inner):
    first = jnp.where(inner < 1, 0, jnp.where(inner < 3, 1, jnp.where(inner < 4, 2, 3)))
    first = jnp.where(inner == 2, 1, first)
    second = jnp.where(inner < 2, 1, jnp.where(inner < 4, 2, 3))
    return jnp.where(inner == 3, 2, first), second


def pack_specs():
    pixel = pl.BlockSpec((VIS, D), lambda j: (0, 0))
    specs = []
    for layer in range(2):
        inner = lambda j, layer=layer: jnp.clip(j - 1 - layer * PER_LAYER, 0, PER_LAYER - 1)
        at = RIGHT_AT // D
        specs.append(pl.BlockSpec((VIS, ROWS), lambda j, inner=inner: (0, inner(j))))
        for side in range(2):
            specs.append(
                pl.BlockSpec(
                    (VIS, D), lambda j, inner=inner, side=side: (0, at + kinds_of(inner(j))[side])
                )
            )
    embed = pl.BlockSpec((VIS, D), lambda j: (0, RIGHT_AT // D + 4))
    return [pixel, embed] + specs


def by_segment(refs, run):
    step = pl.program_id(0)
    count = len(refs) // 2
    mine, theirs = refs[:count], refs[count:]

    @pl.when(step == 0)
    def _():
        run((mine[0], theirs[0]), (mine[1], theirs[1]), (mine[1], theirs[1]))

    for layer in range(2):
        low = 1 + layer * PER_LAYER

        @pl.when(jnp.logical_and(step >= low, step < low + PER_LAYER))
        def _(at=2 + 3 * layer):
            run(*((mine[at + index], theirs[at + index]) for index in range(3)))


def error_factor_kernel(start_ref, error_ref, out_ref):
    turned = nt(error_ref[...], split3(start_ref[...]))
    out_ref[...] = fold3(turned.T)


def error_factor(start, error):
    rows, width = error.shape
    return pl.pallas_call(
        error_factor_kernel,
        grid=(rows // HALF_ROWS,),
        in_specs=[whole((RANK, width)), pl.BlockSpec((HALF_ROWS, width), lambda j: (j, 0))],
        out_specs=pl.BlockSpec((RANK, HALF_ROWS), lambda j: (0, j)),
        out_shape=jax.ShapeDtypeStruct((RANK, rows), f32),
        compiler_params=params(),
        name="error_factor",
    )(start, error)


def right_factor_kernel(basis_ref, error_ref, *refs):
    out_ref = refs[-1]

    @pl.when(pl.program_id(0) == 0)
    def _():
        out_ref[...] = jnp.zeros_like(out_ref)

    basis = split3(basis_ref[...])
    out_ref[...] += fold3(nn(basis, error_ref[...]))

    def run(left, first, second):
        total = jnp.zeros((3 * RANK, D), f32)
        for clip in range(2):
            for side, right in ((0, first), (1, second)):
                lanes = pl.ds(side * HALF_ROWS, HALF_ROWS)
                inner = fold3(nt(basis[:, side * HALF_ROWS : (side + 1) * HALF_ROWS],
                                 left[clip][:, lanes]))
                total = total + nn(split3(inner), right[clip][...])
        out_ref[...] += fold3(total)

    by_segment(refs[:-1], run)


def right_factor(basis, error, mine, theirs):
    return pl.pallas_call(
        right_factor_kernel,
        grid=(ENC_BLOCKS,),
        in_specs=[
            pl.BlockSpec((RANK, ROWS), lambda j: (0, j)),
            pl.BlockSpec((ROWS, D), lambda j: (j, 0)),
        ]
        + pack_specs() * 2,
        out_specs=whole((RANK, D)),
        out_shape=jax.ShapeDtypeStruct((RANK, D), f32),
        compiler_params=params(),
        name="right_factor",
    )(basis, error, *pack_args(mine), *pack_args(theirs))


def pack_args(packs):
    pixels, first, second = packs
    return (pixels, first, first, first, first, second, second, second)


def low_pairs(basis, factor):
    basis3 = split3(basis)
    factor3 = split3(factor)
    high, middle = basis3[:RANK], basis3[RANK : 2 * RANK]
    return (
        jnp.concatenate([high, high, middle, jnp.zeros_like(high)], 0),
        jnp.concatenate([factor3[: 2 * RANK], factor3[:RANK], jnp.zeros_like(factor3[:RANK])], 0),
    )


def residue_kernel(basis_ref, factor_ref, error_ref, *refs):
    out_ref = refs[-1]
    basis, factor = low_pairs(basis_ref[...], -factor_ref[...])

    def run(left, first, second):
        for side, right in ((0, first), (1, second)):
            rows = pl.ds(side * HALF_ROWS, HALF_ROWS)
            low = basis[:, side * HALF_ROWS : (side + 1) * HALF_ROWS]
            lefts = jnp.concatenate([left[0][:, rows], left[1][:, rows], low], 0)
            rights = jnp.concatenate([right[0][...], right[1][...], factor], 0)
            out_ref[rows] = (tn(lefts, rights) + error_ref[rows].astype(f32)).astype(bf16)

    by_segment(refs[:-1], run)


def residue(basis, factor, error, mine, theirs):
    return pl.pallas_call(
        residue_kernel,
        grid=(ENC_BLOCKS,),
        in_specs=[
            pl.BlockSpec((RANK, ROWS), lambda j: (0, j)),
            whole((RANK, D)),
            pl.BlockSpec((ROWS, D), lambda j: (j, 0)),
        ]
        + pack_specs() * 2,
        out_specs=pl.BlockSpec((ROWS, D), lambda j: (j, 0)),
        out_shape=jax.ShapeDtypeStruct((ENC_ROWS, D), bf16),
        compiler_params=params(),
        name="residue",
    )(basis, factor, error, *pack_args(mine), *pack_args(theirs))


DEC_BLOCK = 1152


def dec_right_kernel(basis_ref, comb_ref, out_ref):
    @pl.when(pl.program_id(0) == 0)
    def _():
        out_ref[...] = jnp.zeros_like(out_ref)

    basis = split3(basis_ref[...])
    comb = comb_ref[...]
    high = comb.astype(bf16)
    rest = (comb - high.astype(f32)).astype(bf16)
    out_ref[...] += fold3(nn(basis, high) + nn(basis, rest))


def dec_right_factor(basis, comb):
    return pl.pallas_call(
        dec_right_kernel,
        grid=(DEC_ROWS // DEC_BLOCK,),
        in_specs=[
            pl.BlockSpec((RANK, DEC_BLOCK), lambda j: (0, j)),
            pl.BlockSpec((DEC_BLOCK, DD), lambda j: (j, 0)),
        ],
        out_specs=whole((RANK, DD)),
        out_shape=jax.ShapeDtypeStruct((RANK, DD), f32),
        compiler_params=params(),
        name="dec_right_factor",
    )(basis, comb)


def dec_residue_kernel(basis_ref, factor_ref, comb_ref, out_ref):
    out_ref[...] = (
        comb_ref[...] + tn(*low_pairs(basis_ref[...], -factor_ref[...]))
    ).astype(bf16)


def dec_residue(basis, factor, comb):
    return pl.pallas_call(
        dec_residue_kernel,
        grid=(DEC_ROWS // DEC_BLOCK,),
        in_specs=[
            pl.BlockSpec((RANK, DEC_BLOCK), lambda j: (0, j)),
            whole((RANK, DD)),
            pl.BlockSpec((DEC_BLOCK, DD), lambda j: (j, 0)),
        ],
        out_specs=pl.BlockSpec((DEC_BLOCK, DD), lambda j: (j, 0)),
        out_shape=jax.ShapeDtypeStruct((DEC_ROWS, DD), bf16),
        compiler_params=params(),
        name="dec_residue",
    )(basis, factor, comb)


def dec_left_kernel(start_ref, grad_ref, out_ref):
    start = split3(start_ref[0])
    grad = grad_ref[0]
    high = grad.astype(bf16)
    rest = (grad - high.astype(f32)).astype(bf16)
    out_ref[0] = fold3((nt(high, start) + nt(rest, start)).T)


def dec_left_factor(starts, grads):
    return pl.pallas_call(
        dec_left_kernel,
        grid=(2, DEC_ROWS // DEC_BLOCK),
        in_specs=[
            pl.BlockSpec((1, RANK, DD), lambda g, j: (g, 0, 0)),
            pl.BlockSpec((1, DEC_BLOCK, DD), lambda g, j: (g, j, 0)),
        ],
        out_specs=pl.BlockSpec((1, RANK, DEC_BLOCK), lambda g, j: (g, 0, j)),
        out_shape=jax.ShapeDtypeStruct((2, RANK, DEC_ROWS), f32),
        compiler_params=params(),
        name="dec_left_factor",
    )(starts, grads)


MESH_ID = pl.DeviceIdType.MESH


def greet(workers, me, partner):
    barrier = pltpu.get_barrier_semaphore()
    for distance in range(1, workers):
        pl.semaphore_signal(
            barrier, 1, device_id={"dp": lax.rem(me + distance, workers)}, device_id_type=MESH_ID
        )
    if partner is not None:
        pl.semaphore_signal(barrier, 1, device_id={"tensor": partner}, device_id_type=MESH_ID)
    pl.semaphore_wait(barrier, workers - 1 + (partner is not None))


def sum_workers(workers, me, lanes, local, slots, sums, sems):
    def share(index):
        return pl.ds(pl.multiple_of(index * lanes, 128), lanes)

    def to_all(turn, source, target):
        copies = []
        for distance in range(1, workers):
            peer = lax.rem(me + distance, workers)
            copy = pltpu.make_async_remote_copy(
                src_ref=source(peer),
                dst_ref=target(distance),
                send_sem=sems.at[2 * turn, distance],
                recv_sem=sems.at[2 * turn + 1, distance],
                device_id={"dp": peer},
                device_id_type=MESH_ID,
            )
            copy.start()
            copies.append(copy)
        return copies

    copies = to_all(0, lambda peer: local.at[:, share(peer)], lambda distance: slots.at[distance])
    total = local[:, share(me)]
    for distance, copy in enumerate(copies, 1):
        copy.wait_recv()
        total = total + slots[distance]
    sums[:, share(me)] = total
    more = to_all(1, lambda peer: sums.at[:, share(me)], lambda distance: sums.at[:, share(me)])
    for copy in copies:
        copy.wait_send()
    for copy in more:
        copy.wait()


def basis_kernel(
    workers, lanes, enc_width, first_ref, second_ref, dec_ref, error_ref, dec_error_ref,
    enc_out, dec_out,
    send, came, local, slots, sums, sems, pair_sems,
):
    me = lax.axis_index("dp")
    half = lax.axis_index("tensor")
    first = first_ref.shape[2]
    second = second_ref.shape[2]
    width = enc_width + dec_ref.shape[2]
    spans = ((first_ref, 0, first), (second_ref, first, second), (dec_ref, enc_width, width - enc_width))
    for ref, at, size in spans:
        send[:, at : at + size] = ref[1]
    if width < workers * lanes:
        tail = jnp.zeros((RANK, workers * lanes - width), f32)
        send[:, width:] = tail
    greet(workers, me, 1 - half)
    copy = pltpu.make_async_remote_copy(
        src_ref=send,
        dst_ref=came,
        send_sem=pair_sems.at[0],
        recv_sem=pair_sems.at[1],
        device_id={"tensor": 1 - half},
        device_id_type=MESH_ID,
    )
    copy.start()
    for ref, at, size in spans[:2]:
        local[:, at : at + size] = ref[0] + error_ref[:, at : at + size]
    local[:, enc_width:width] = dec_ref[0] + dec_error_ref[...]
    if width < workers * lanes:
        local[:, width:] = tail
    copy.wait()
    local[...] += came[...]
    sum_workers(workers, me, lanes, local, slots, sums, sems)
    place = lax.broadcasted_iota(jnp.int32, (RANK, 1), 0)
    for at, out in ((0, enc_out), (enc_width, dec_out)):
        left = sums[:, at : at + out.shape[1]]
        gram = lax.dot_general(
            left, left, (((1,), (1,)), ((), ())), precision=highest_precision,
            preferred_element_type=f32,
        )
        for index in range(RANK):
            scale = lax.rsqrt(gram[index : index + 1, index : index + 1])
            column = gram[:, index : index + 1] * scale
            below = jnp.where(place > index, column, 0.0)
            pivot = left[index : index + 1] * scale
            left = jnp.where(place == index, pivot, left - below * pivot)
            gram = gram - below * (gram[index : index + 1] * scale)
        out[...] = left


def lanes_for(width, workers):
    return pl.cdiv(width, 128 * workers) * 128


def summed_basis(workers, first, second, dec, error_part, dec_error_part):
    enc_width = first.shape[2] + second.shape[2]
    width = enc_width + dec.shape[2]
    lanes = lanes_for(width, workers)
    wide = pltpu.VMEM((RANK, workers * lanes), f32)
    return pl.pallas_call(
        lambda *refs: basis_kernel(workers, lanes, enc_width, *refs),
        in_specs=[vmem_spec()] * 5,
        out_specs=[vmem_spec()] * 2,
        out_shape=[
            jax.ShapeDtypeStruct((RANK, enc_width), f32),
            jax.ShapeDtypeStruct((RANK, width - enc_width), f32),
        ],
        scratch_shapes=[
            wide,
            wide,
            wide,
            pltpu.VMEM((workers, RANK, lanes), f32),
            wide,
            pltpu.SemaphoreType.DMA((4, workers)),
            pltpu.SemaphoreType.DMA((2,)),
        ],
        compiler_params=pltpu.CompilerParams(
            collective_id=1, has_side_effects=True, vmem_limit_bytes=BIG_VMEM
        ),
        name="summed_basis",
    )(first, second, dec, error_part, dec_error_part)


def sum_kernel(workers, lanes, *refs):
    count = (len(refs) - 4) // 2
    parts, outs = refs[:count], refs[count : 2 * count]
    local, slots, sums, sems = refs[2 * count :]
    me = lax.axis_index("dp")
    at = 0
    for part in parts:
        local[:, at : at + part.shape[1]] = part[...]
        at += part.shape[1]
    if at < workers * lanes:
        local[:, at:] = jnp.zeros((RANK, workers * lanes - at), f32)
    greet(workers, me, None)
    sum_workers(workers, me, lanes, local, slots, sums, sems)
    at = 0
    for out in outs:
        out[...] = sums[:, at : at + out.shape[1]] * (1.0 / workers)
        at += out.shape[1]


def mean_over_workers(workers, parts):
    lanes = lanes_for(sum(part.shape[1] for part in parts), workers)
    wide = pltpu.VMEM((RANK, workers * lanes), f32)
    return pl.pallas_call(
        lambda *refs: sum_kernel(workers, lanes, *refs),
        in_specs=[vmem_spec()] * len(parts),
        out_specs=[vmem_spec()] * len(parts),
        out_shape=[jax.ShapeDtypeStruct(part.shape, f32) for part in parts],
        scratch_shapes=[
            wide,
            pltpu.VMEM((workers, RANK, lanes), f32),
            wide,
            pltpu.SemaphoreType.DMA((4, workers)),
        ],
        compiler_params=pltpu.CompilerParams(
            collective_id=2, has_side_effects=True, vmem_limit_bytes=BIG_VMEM
        ),
        name="mean_over_workers",
    )(*parts)


def cut(block, widths):
    pieces = []
    start = 0
    for width in widths:
        pieces.append(block[start : start + width])
        start = start + width
    return pieces


def swap(value):
    return lax.ppermute(value, "tensor", [(0, 1), (1, 0)])


def per_device(
    tubes,
    tube_order,
    clip_mask,
    enc_weights,
    dec_weights,
    vec_split,
    vec_shared,
    enc_moment,
    dec_moment,
    split_moment,
    shared_moment,
    enc_error,
    dec_error,
    factors,
):
    workers = lax.axis_size("dp")
    half = lax.axis_index("tensor")
    worker_index = lax.axis_index("dp")
    dec_own = lax.all_gather(dec_weights[0].astype(bf16), "dp", axis=0, tiled=True)
    enc_own = lax.all_gather(enc_weights[0].astype(bf16), "dp", axis=0, tiled=True)
    dec_other = swap(dec_own)
    enc_other = swap(enc_own)
    counted_all = clip_mask.astype(f32)
    loss_weight = MASKED * lax.psum(jnp.sum(counted_all), "dp")

    mine = lambda both: lax.dynamic_index_in_dim(both, half, 0, keepdims=False)
    theirs = lambda both: lax.dynamic_index_in_dim(both, 1 - half, 0, keepdims=False)
    order = mine(tube_order)
    counted = mine(counted_all)
    picked = pick(tube_order, tubes)
    picked_mine = mine(picked)
    picked_theirs = theirs(picked)
    pixels = jnp.concatenate([picked_mine, swap(picked_theirs)], 1)

    split_own = vec_split[0]
    split_other = swap(split_own)
    split_widths = [HALF, HALF, HALF_FF] * 2 + [DD // 2, DD // 2, DFF // 2, PIX // 2]
    split_parts = [
        jnp.concatenate(pair)[None]
        for pair in zip(cut(split_own, split_widths), cut(split_other, split_widths))
    ]
    shared = cut(vec_shared, [D] * 15 + [DD] * 9)
    dec_widths = [D // 2, DD // 2, DFF // 2, 3 * DD // 2, DFF // 2, PIX // 2]
    own_parts = cut(dec_own, dec_widths)
    other_parts = cut(dec_other, dec_widths)
    proj = jnp.where(
        half == 0,
        jnp.concatenate([own_parts[0], other_parts[0]], 0),
        jnp.concatenate([other_parts[0], own_parts[0]], 0),
    )
    d_out, d_down, d_up, head_rows = (
        jnp.concatenate([own_parts[index], other_parts[index]], 0) for index in (1, 2, 4, 5)
    )
    kinds = lambda block: block.reshape(3, DD // 2, DD)
    d_qkv = jnp.concatenate([kinds(own_parts[3]), kinds(other_parts[3])], 1).reshape(3 * DD, DD)

    pos_enc = sinusoid_at(order[:VIS], D)
    pos_dec = sinusoid_at(order, DD)
    start_own = factors[0]
    start_other = swap(start_own)
    enc_starts = jnp.stack([start_own[:, :D], start_other[:, :D]])
    dec_starts = jnp.stack([start_own[:, D:], start_other[:, D:]])
    enc_error_part = error_factor(start_own[:, :D], enc_error[0, 0])
    dec_error_part = error_factor(start_own[:, D:], dec_error[0, 0])

    embed = jnp.concatenate([enc_own[:D], enc_other[:D]], 0)
    pixels_vis = pixels[:VIS]
    stream = nn(pixels_vis, embed) + shared[0] + pos_enc
    kept = []
    enc_vecs = []
    for layer in range(2):
        base = 1 + 6 * layer
        vecs = jnp.stack(shared[base : base + 6] + shared[13:15])
        bq, bv, bu = split_parts[3 * layer : 3 * layer + 3]
        bqkv = jnp.concatenate([bq, jnp.zeros_like(bq), bv], 1)
        result = encoder_layer(
            D + layer * LAYER_ROWS, stream, vecs, bqkv, bu, enc_own, enc_other,
            f"encoder_{layer}", proj if layer == 1 else None,
        )
        kept.append((stream, result))
        enc_vecs.append(vecs)
        stream = result[0]
    enc_normed, latent = result[8:]

    bq, bv, bu, bh = split_parts[6:]
    qkv_vecs = jnp.stack([shared[index] for index in (15, 16, 17, 15, 16, 17, 15, 16)])
    dec_start, h, qkv = decoder_qkv(
        pos_dec, latent, qkv_vecs, d_qkv, jnp.concatenate([bq, jnp.zeros_like(bq), bv], 1)
    )
    mixed, logs = attend(qkv)
    scal = jnp.broadcast_to(
        jnp.stack([counted, 2.0 * workers / (PIX * loss_weight) * counted] + [counted] * 6)[:, None],
        (8, 128),
    )
    dec_vecs = jnp.stack([shared[index] for index in (18, 19, 20, 21, 22, 23, 22, 23)])
    grad_mixed, grad_middle, dec_grads, g_vec, g_bu, g_bh, loss_lanes = decoder_tokens(
        mixed, dec_start, pixels, scal, dec_vecs, bu, bh, d_out, d_down, d_up, head_rows
    )
    dq, dk, dv = attend_back(qkv, mixed, grad_mixed, logs)
    latent_low, dec_grads, g_vec1 = decoder_qkv_back(
        half.astype(jnp.int32)[None], dq, dk, dv, h, dec_start, grad_middle, qkv_vecs, d_qkv,
        enc_normed, dec_grads,
    )
    dec_left = dec_left_factor(dec_starts, dec_grads)
    dec_comb = dec_grads[0] + swap(dec_grads[1]) + dec_error[0, 0].astype(f32)

    grad = latent_low
    packs = [None, None]
    came = [None, None]
    enc_lefts = [None, None]
    enc_vec_grads = [None, None]
    for layer in (1, 0):
        source, result = kept[layer]
        grad, packs[layer], sent, enc_lefts[layer], *enc_vec_grads[layer] = encoder_layer_back(
            D + layer * LAYER_ROWS, grad, source, enc_vecs[layer], result, enc_starts,
            enc_own, enc_other, pixels_vis, f"encoder_back_{layer}",
            (result[0], proj) if layer == 1 else (),
        )
        came[layer] = swap(sent)
    mine_packs = (picked_mine, packs[0], packs[1])
    their_packs = (picked_theirs, came[0], came[1])

    enc_basis, dec_basis = summed_basis(
        workers, enc_lefts[0], enc_lefts[1], dec_left, enc_error_part, dec_error_part
    )

    def split_half(index):
        pieces = []
        for layer in range(2):
            _, g_hidden, g_qv = enc_vec_grads[layer]
            pieces += [
                cut(g_qv[0], [HALF] * 2)[index],
                cut(g_qv[1], [HALF] * 2)[index],
                cut(g_hidden[0], [HALF_FF] * 2)[index],
            ]
        pieces += [
            cut(g_vec1[0], [DD // 2] * 2)[index],
            cut(g_vec1[1], [DD // 2] * 2)[index],
            cut(g_bu[0], [DFF // 2] * 2)[index],
            cut(g_bh[0], [PIX // 2] * 2)[index],
        ]
        return jnp.concatenate(pieces)

    g_vec_enc = [grads[0] for grads in enc_vec_grads]
    shared_grad = jnp.concatenate(
        [g_vec_enc[0][6], g_vec_enc[0][:6].reshape(-1), g_vec_enc[1].reshape(-1)]
        + [g_vec1[4], g_vec1[2], g_vec1[3], g_vec[:6].reshape(-1)]
    )
    loss_part = jnp.sum(loss_lanes) / PIX
    split_len = split_own.shape[0]
    length = split_len + shared_grad.shape[0] + 1
    vec_lanes = pl.cdiv(length, RANK * 128) * 128
    fill = jnp.zeros((RANK * vec_lanes - length,), f32)
    sent = jnp.concatenate([split_half(1), shared_grad, loss_part[None], fill])
    local = jnp.concatenate([split_half(0), shared_grad, loss_part[None], fill])
    vec_local = (local + swap(sent)).reshape(RANK, vec_lanes)

    enc_rows = enc_basis.shape[1] // workers
    dec_rows = dec_basis.shape[1] // workers
    enc_owned = lax.dynamic_slice_in_dim(enc_basis, worker_index * enc_rows, enc_rows, 1)
    dec_owned = lax.dynamic_slice_in_dim(dec_basis, worker_index * dec_rows, dec_rows, 1)
    enc_right, dec_right, vec_mean = mean_over_workers(
        workers,
        (
            right_factor(enc_basis, enc_error[0, 0], mine_packs, their_packs),
            dec_right_factor(dec_basis, dec_comb),
            vec_local,
        ),
    )
    vec_mean = vec_mean.reshape(-1)
    enc_error_new = residue(enc_basis, enc_right, enc_error[0, 0], mine_packs, their_packs)
    dec_error_new = dec_residue(dec_basis, dec_right, dec_comb)
    enc_mom = momentum_keep * enc_moment[0] + jnp.einsum(
        "rx,rc->xc", enc_owned, enc_right, precision=highest_precision
    )
    dec_mom = momentum_keep * dec_moment[0] + jnp.einsum(
        "rx,rc->xc", dec_owned, dec_right, precision=highest_precision
    )
    split_mom = momentum_keep * split_moment[0] + vec_mean[:split_len]
    shared_mom = momentum_keep * shared_moment + vec_mean[split_len : length - 1]
    return (
        vec_mean[length - 1] * workers,
        loss_weight,
        (enc_weights[0] - step_rate * enc_mom)[None],
        enc_mom[None],
        enc_error_new[None, None],
        (dec_weights[0] - step_rate * dec_mom)[None],
        dec_mom[None],
        dec_error_new[None, None],
        jnp.concatenate([enc_right, dec_right], 1)[None],
        (vec_split[0] - step_rate * split_mom)[None],
        split_mom[None],
        vec_shared - step_rate * shared_mom,
        shared_mom,
    )


def solution(mesh):
    placed = (
        P("dp", None, "tensor"),
        P("dp", None),
        P("dp"),
        P("tensor", "dp", None),
        P("tensor", "dp", None),
        P("tensor", None),
        P(),
        P("tensor", "dp", None),
        P("tensor", "dp", None),
        P("tensor", None),
        P(),
        P("dp", "tensor", None, None),
        P("dp", "tensor", None, None),
        P("tensor", None, None),
    )
    return jax.shard_map(
        per_device,
        mesh=mesh,
        in_specs=placed,
        out_specs=(
            P(),
            P(),
            P("tensor", "dp", None),
            P("tensor", "dp", None),
            P("dp", "tensor", None, None),
            P("tensor", "dp", None),
            P("tensor", "dp", None),
            P("dp", "tensor", None, None),
            P("tensor", None, None),
            P("tensor", None),
            P("tensor", None),
            P(),
            P(),
        ),
        check_vma=False,
    )
```

```python
import math

import jax
import jax.numpy as jnp
from jax import lax
from jax.experimental import pallas as pl
from jax.experimental.pallas import tpu as pltpu
from jax.sharding import PartitionSpec as P

D = 768
HEAD_DIM = 64
FF = 3072
DD = 384
DFF = 1536
PIX = 1536
TUBES = 1568
VIS = 160
MASKED = 1408
RANK = 8

f32 = jnp.float32
bf16 = jnp.bfloat16
highest_precision = lax.Precision.HIGHEST
norm_eps = 1e-06
momentum_keep = 0.9
step_rate = 1000.0
LOG2E = 1.4426950408889634
SCORE = HEAD_DIM ** (-0.5)
BIG_VMEM = 56 << 20


def nn(left, right):
    return lax.dot_general(left, right, (((1,), (0,)), ((), ())), preferred_element_type=f32)


def nt(left, right):
    return lax.dot_general(left, right, (((1,), (1,)), ((), ())), preferred_element_type=f32)


def tn(left, right):
    return lax.dot_general(left, right, (((0,), (0,)), ((), ())), preferred_element_type=f32)


def col_sum(value):
    return jnp.sum(value, 0, keepdims=True)


def norm_parts(stream):
    center = stream - jnp.mean(stream, -1, keepdims=True)
    rate = lax.rsqrt(jnp.mean(center * center, -1, keepdims=True) + norm_eps)
    return center * rate, rate


def norm_back(grad, gain, unit, rate):
    grad_unit = grad * gain
    return rate * (
        grad_unit
        - jnp.mean(grad_unit, -1, keepdims=True)
        - unit * jnp.mean(grad_unit * unit, -1, keepdims=True)
    )


def gelu_pair(before):
    cdf_tail = jnp.exp(-0.5 * before * before)
    size = jnp.abs(before) * (2.0 ** -0.5)
    t = 1.0 / (1.0 + 0.3275911 * size)
    poly = t * (
        0.254829592 + t * (-0.284496736 + t * (1.421413741 + t * (-1.453152027 + t * 1.061405429)))
    )
    tail = 0.5 * poly * cdf_tail
    cdf = jnp.where(before < 0, tail, 1.0 - tail)
    return before * cdf, cdf + before * cdf_tail * (1.0 / math.sqrt(2.0 * math.pi))


def split3(value):
    high = value.astype(bf16)
    rest = value - high.astype(f32)
    middle = rest.astype(bf16)
    low = (rest - middle.astype(f32)).astype(bf16)
    return jnp.concatenate([high, middle, low], 0)


def fold3(value):
    rows = value.shape[0] // 3
    return value[:rows] + value[rows : 2 * rows] + value[2 * rows :]


def sinusoid_at(place, width):
    column = jnp.arange(width)
    rate = jnp.exp(-(2 * (column // 2)).astype(f32) * (math.log(10000.0) / width))
    angle = place.astype(f32)[:, None] * rate[None, :]
    return jnp.where(column % 2 == 0, jnp.sin(angle), jnp.cos(angle))


def sinusoid_table(width):
    column = jnp.arange(width)
    rate = jnp.exp(-(2 * (column // 2)).astype(f32) * (math.log(10000.0) / width))[None, :]
    first = (32 * jnp.arange(TUBES // 32)).astype(f32)[:, None] * rate
    second = jnp.arange(32).astype(f32)[:, None] * rate
    even = column % 2 == 0
    ahead = jnp.where(even, jnp.sin(first), jnp.cos(first))[:, None]
    turned = jnp.where(even, jnp.cos(first), -jnp.sin(first))[:, None]
    table = ahead * jnp.cos(second)[None] + turned * jnp.sin(second)[None]
    return table.reshape(TUBES, width)


def params(**more):
    return pltpu.CompilerParams(vmem_limit_bytes=BIG_VMEM, **more)


def whole(shape):
    return pl.BlockSpec(shape, lambda *_: (0,) * len(shape))


def any_spec():
    return pl.BlockSpec(memory_space=pl.ANY)


def vmem_spec():
    return pl.BlockSpec(memory_space=pltpu.VMEM)


def pick_kernel(half_ref, order_ref, tubes_ref, out_ref):
    column = lax.broadcasted_iota(jnp.int32, (1, TUBES), 1)
    hot = jnp.where(order_ref[0] == column, 1.0, 0.0).astype(bf16)
    out_ref[0] = nn(hot, tubes_ref[0]).astype(bf16)


def pick_visible(half, order, tubes):
    clips, _, width = tubes.shape
    which = lambda c, half_ref: jnp.where(c == 0, half_ref[0], 1 - half_ref[0])
    return pl.pallas_call(
        pick_kernel,
        grid_spec=pltpu.PrefetchScalarGridSpec(
            num_scalar_prefetch=1,
            grid=(clips,),
            in_specs=[
                pl.BlockSpec((1, VIS, 1), lambda c, half_ref: (which(c, half_ref), 0, 0)),
                pl.BlockSpec((1, TUBES, width), lambda c, half_ref: (which(c, half_ref), 0, 0)),
            ],
            out_specs=pl.BlockSpec((1, VIS, width), lambda c, half_ref: (c, 0, 0)),
        ),
        out_shape=jax.ShapeDtypeStruct((clips, VIS, width), bf16),
        compiler_params=params(),
        name="pick_visible",
    )(half, order[:, :VIS, None], tubes)


QKV_ROWS = 392


def place_matrix(order, rows):
    place = lax.broadcasted_iota(jnp.int32, (rows, 1), 0) + pl.program_id(0) * rows
    return jnp.where(order == place, 1.0, 0.0)


def qkv_kernel(order_ref, pos_ref, latent_ref, vec_ref, w_ref, bias_ref, x_ref, h_ref, qkv_ref, hidden_ref):
    token, gain, shift = (vec_ref[index : index + 1] for index in range(3))
    places = place_matrix(order_ref[...], QKV_ROWS)
    hidden = 1.0 - jnp.sum(places, 1, keepdims=True)
    hidden_ref[...] = hidden
    latent = split3(latent_ref[...])
    places = places.astype(bf16)
    shown = sum(nn(places, latent[VIS * part : VIS * (part + 1)]) for part in (2, 1, 0))
    x = pos_ref[...] + (shown + hidden * token)
    x_ref[...] = x
    unit, _ = norm_parts(x)
    h = (unit * gain + shift).astype(bf16)
    h_ref[...] = h
    qkv_ref[...] = (nt(h, w_ref[...]) + bias_ref[...]).astype(bf16)


def decoder_qkv(order, pos, latent, vecs, weights, bias):
    rows = lambda width: pl.BlockSpec((QKV_ROWS, width), lambda i: (i, 0))
    return pl.pallas_call(
        qkv_kernel,
        grid=(TUBES // QKV_ROWS,),
        in_specs=[
            whole((1, VIS)),
            rows(DD),
            whole((VIS, DD)),
            whole(vecs.shape),
            whole((3 * DD, DD)),
            whole((1, 3 * DD)),
        ],
        out_specs=[rows(DD), rows(DD), rows(3 * DD), rows(1)],
        out_shape=[
            jax.ShapeDtypeStruct((TUBES, DD), f32),
            jax.ShapeDtypeStruct((TUBES, DD), bf16),
            jax.ShapeDtypeStruct((TUBES, 3 * DD), bf16),
            jax.ShapeDtypeStruct((TUBES, 1), f32),
        ],
        compiler_params=params(),
        name="decoder_qkv",
    )(order, pos, latent, vecs, weights, bias)


FWD_ROWS = 392
BWD_ROWS = 256
PAIRS = DD // 128


def half_lane(index):
    return lax.broadcasted_iota(jnp.int32, (1, 128), 1) // HEAD_DIM == index


def attend_kernel(q_ref, k_ref, v_ref, o_ref, lse_ref):
    q = q_ref[...]
    k = k_ref[...]
    v_one = jnp.concatenate([v_ref[...], jnp.ones((TUBES, 128), bf16)], 1)
    mixed, logs = [], []
    for head in range(2):
        scores = nt(jnp.where(half_lane(head), q, jnp.zeros_like(q)), k)
        top = jnp.max(scores, 1, keepdims=True)
        expo = jnp.exp2((scores - top) * (SCORE * LOG2E)).astype(bf16)
        both = nn(expo, v_one)
        total = both[:, 128:]
        mixed.append(both[:, :128] / total)
        logs.append(top * (SCORE * LOG2E) + jnp.log2(total))
    o_ref[...] = jnp.where(half_lane(0), mixed[0], mixed[1])
    lse_ref[0] = jnp.where(half_lane(0), logs[0], logs[1])


def attend(qkv):
    return pl.pallas_call(
        attend_kernel,
        grid=(PAIRS, TUBES // FWD_ROWS),
        in_specs=[
            pl.BlockSpec((FWD_ROWS, 128), lambda p, i: (i, p)),
            pl.BlockSpec((TUBES, 128), lambda p, i: (0, PAIRS + p)),
            pl.BlockSpec((TUBES, 128), lambda p, i: (0, 2 * PAIRS + p)),
        ],
        out_specs=[
            pl.BlockSpec((FWD_ROWS, 128), lambda p, i: (i, p)),
            pl.BlockSpec((1, FWD_ROWS, 128), lambda p, i: (p, i, 0)),
        ],
        out_shape=[
            jax.ShapeDtypeStruct((TUBES, DD), f32),
            jax.ShapeDtypeStruct((PAIRS, TUBES, 128), f32),
        ],
        compiler_params=params(),
        name="attend",
    )(qkv, qkv, qkv)


def attend_back_kernel(
    q_ref, k_ref, v_ref, o_ref, do_ref, lse_ref, dq_ref, dk_ref, dv_ref, k_turned, dk_sum, dv_sum
):
    step = pl.program_id(1)

    @pl.when(step == 0)
    def _():
        k_turned[...] = k_ref[...].T
        dk_sum[...] = jnp.zeros_like(dk_sum)
        dv_sum[...] = jnp.zeros_like(dv_sum)

    valid = lax.broadcasted_iota(jnp.int32, (BWD_ROWS, 1), 0) + step * BWD_ROWS < TUBES
    zero = jnp.zeros((), bf16)
    q = jnp.where(valid, q_ref[...], zero)
    grad = jnp.where(valid, do_ref[...], zero)
    dots = jnp.where(valid, o_ref[...], 0.0) * grad.astype(f32)
    logs = jnp.where(valid, lse_ref[0], 0.0).T
    select = (
        lax.broadcasted_iota(jnp.int32, (8, 128), 1) // HEAD_DIM
        == lax.broadcasted_iota(jnp.int32, (8, 128), 0)
    ).astype(f32)
    row_total = lax.dot_general(
        select, dots, (((1,), (1,)), ((), ())), precision=highest_precision,
        preferred_element_type=f32,
    )
    k = k_ref[...]
    v = v_ref[...]
    turned = []
    for head in range(2):
        mask = half_lane(head)
        q_head = jnp.where(mask, q, zero)
        grad_head = jnp.where(mask, grad, zero)
        low = head * HEAD_DIM
        probs = jnp.exp2(nt(k, q_head) * (SCORE * LOG2E) - logs[low : low + 1])
        grad_scores = (probs * (nt(v, grad_head) - row_total[head : head + 1])).astype(bf16)
        dv_sum[...] += nn(probs.astype(bf16), grad_head)
        dk_sum[...] += nn(grad_scores, q_head)
        turned.append(nn(k_turned[low : low + HEAD_DIM], grad_scores))
    dq_ref[...] = (jnp.concatenate(turned, 0).T * SCORE).astype(bf16)

    @pl.when(step == pl.num_programs(1) - 1)
    def _():
        dk_ref[...] = (dk_sum[...] * SCORE).astype(bf16)
        dv_ref[...] = dv_sum[...].astype(bf16)


def attend_back(qkv, mixed, grad_mixed, logs):
    some = pl.BlockSpec((BWD_ROWS, 128), lambda p, i: (i, p))
    full = pl.BlockSpec((TUBES, 128), lambda p, i: (0, p))
    return pl.pallas_call(
        attend_back_kernel,
        grid=(PAIRS, pl.cdiv(TUBES, BWD_ROWS)),
        in_specs=[
            some,
            pl.BlockSpec((TUBES, 128), lambda p, i: (0, PAIRS + p)),
            pl.BlockSpec((TUBES, 128), lambda p, i: (0, 2 * PAIRS + p)),
            some,
            some,
            pl.BlockSpec((1, BWD_ROWS, 128), lambda p, i: (p, i, 0)),
        ],
        out_specs=[some, full, full],
        out_shape=[jax.ShapeDtypeStruct((TUBES, DD), bf16)] * 3,
        scratch_shapes=[
            pltpu.VMEM((128, TUBES), bf16),
            pltpu.VMEM((TUBES, 128), f32),
            pltpu.VMEM((TUBES, 128), f32),
        ],
        compiler_params=params(),
        name="attend_back",
    )(qkv, qkv, qkv, mixed, grad_mixed, logs)


TOKEN_ROWS = 224
CHUNK = 384
DEC_O = D // 2
DEC_D = DEC_O + DD // 2
DEC_Q = DEC_D + DFF // 2
DEC_U = DEC_Q + 3 * DD // 2
DEC_H = DEC_U + DFF // 2
DEC_ROWS = DEC_H + PIX // 2
CHUNKS = DFF // CHUNK


def token_kernel(
    _, a_ref, x_ref, pix_ref, pix_other_ref, hidden_ref, scal_ref, vec_ref, bu_ref, bh_ref,
    wo_ref, wd_ref, wu_ref, wh_ref,
    da_ref, dx1_ref,
    own_ref, other_ref, gvec_ref, gbu_ref, gbh_ref, loss_ref,
    slope,
):
    step = pl.program_id(0)
    sums = (own_ref, other_ref, gvec_ref, gbu_ref, gbh_ref, loss_ref)
    grads = (own_ref, other_ref)

    @pl.when(step == 0)
    def _():
        for ref in sums:
            ref[...] = jnp.zeros_like(ref)

    bo, g2, b2, bd, gf, sf = (vec_ref[index : index + 1] for index in range(3, 9))
    a = a_ref[...].astype(bf16)
    x1 = x_ref[...] + (nn(a, wo_ref[...]) + bo)
    unit2, rate2 = norm_parts(x1)
    h2 = (unit2 * g2 + b2).astype(bf16)
    out = x1 + bd
    active = []
    for chunk in range(CHUNKS):
        part = pl.ds(chunk * CHUNK, CHUNK)
        value, slope_part = gelu_pair(nt(h2, wu_ref[part]) + bu_ref[:, part])
        slope[:, part] = slope_part
        active.append(value.astype(bf16))
        out = out + nn(active[-1], wd_ref[part])
    unit_f, rate_f = norm_parts(out)
    final = (unit_f * gf + sf).astype(bf16)
    pixels = [
        ref[:, pl.ds(side * CHUNK, CHUNK)].astype(f32)
        for ref in (pix_ref.at[0], pix_other_ref)
        for side in range(2)
    ]
    center = sum(jnp.sum(part, 1, keepdims=True) for part in pixels) * (1.0 / PIX)
    square = sum(jnp.sum(part * part, 1, keepdims=True) for part in pixels) * (1.0 / PIX)
    spread = lax.rsqrt(square - center * center + norm_eps)
    counted = hidden_ref[...] * scal_ref[0:1, 0:1]
    rate = hidden_ref[...] * scal_ref[1:2, 0:1]
    grad_final = jnp.zeros((TOKEN_ROWS, DD), f32)
    for chunk in range(CHUNKS):
        part = pl.ds(chunk * CHUNK, CHUNK)
        target = (pixels[chunk] - center) * spread
        miss = nt(final, wh_ref[part]) + bh_ref[:, part] - target
        loss_ref[:, part] += col_sum(counted * miss * miss)
        grad_guess = (rate * miss).astype(bf16)
        gbh_ref[:, part] += col_sum(grad_guess.astype(f32))
        grads[chunk // 2][pl.ds(DEC_H + (chunk % 2) * CHUNK, CHUNK)] += tn(grad_guess, final)
        grad_final = grad_final + nn(grad_guess, wh_ref[part])
    grad_out = norm_back(grad_final, gf, unit_f, rate_f)
    out_low = grad_out.astype(bf16)
    grad_h2 = jnp.zeros((TOKEN_ROWS, DD), f32)
    for chunk in range(CHUNKS):
        part = pl.ds(chunk * CHUNK, CHUNK)
        grads[chunk // 2][pl.ds(DEC_D + (chunk % 2) * CHUNK, CHUNK)] += tn(active[chunk], out_low)
        grad_before = (slope[:, part] * nt(out_low, wd_ref[part])).astype(bf16)
        gbu_ref[:, part] += col_sum(grad_before.astype(f32))
        grads[chunk // 2][pl.ds(DEC_U + (chunk % 2) * CHUNK, CHUNK)] += tn(grad_before, h2)
        grad_h2 = grad_h2 + nn(grad_before, wu_ref[part])
    grad_x1 = grad_out + norm_back(grad_h2, g2, unit2, rate2)
    x1_low = grad_x1.astype(bf16)
    g_out = tn(a, x1_low)
    for group in range(2):
        grads[group][pl.ds(DEC_O, DD // 2)] += g_out[group * DD // 2 : (group + 1) * DD // 2]
    da_ref[...] = nt(x1_low, wo_ref[...]).astype(bf16)
    dx1_ref[...] = grad_x1
    gvec_ref[0:1] += col_sum(x1_low.astype(f32))
    gvec_ref[1:2] += col_sum(grad_h2 * unit2)
    gvec_ref[2:3] += col_sum(grad_h2)
    gvec_ref[3:4] += col_sum(out_low.astype(f32))
    gvec_ref[4:5] += col_sum(grad_final * unit_f)
    gvec_ref[5:6] += col_sum(grad_final)


def decoder_tokens(half, mixed, x, tubes, pixels, hidden, scal, vecs, bu, bh, wo, wd, wu, wh):
    rows = lambda width: pl.BlockSpec((TOKEN_ROWS, width), lambda i, _: (i, 0))
    sums = [(DEC_ROWS, DD), (DEC_ROWS, DD), (8, DD), (1, DFF), (1, PIX), (1, PIX)]
    return pl.pallas_call(
        token_kernel,
        grid_spec=pltpu.PrefetchScalarGridSpec(
            num_scalar_prefetch=1,
            grid=(TUBES // TOKEN_ROWS,),
            in_specs=[
                rows(DD),
                rows(DD),
                pl.BlockSpec((1, TOKEN_ROWS, PIX // 2), lambda i, half_ref: (half_ref[0], i, 0)),
                rows(PIX // 2),
                rows(1),
                whole((8, 128)),
                whole(vecs.shape),
                whole((1, DFF)),
                whole((1, PIX)),
                whole((DD, DD)),
                whole((DFF, DD)),
                whole((DFF, DD)),
                whole((PIX, DD)),
            ],
            out_specs=[rows(DD), rows(DD)] + [whole(shape) for shape in sums],
            scratch_shapes=[pltpu.VMEM((TOKEN_ROWS, DFF), f32)],
        ),
        out_shape=[
            jax.ShapeDtypeStruct((TUBES, DD), bf16),
            jax.ShapeDtypeStruct((TUBES, DD), f32),
        ]
        + [jax.ShapeDtypeStruct(shape, f32) for shape in sums],
        compiler_params=params(),
        name="decoder_tokens",
    )(half, mixed, x, tubes, pixels, hidden, scal, vecs, bu, bh, wo, wd, wu, wh)


def qkv_back_kernel(
    half_ref, order_ref, dq_ref, dk_ref, dv_ref, h_ref, x_ref, dx1_ref, vec_ref, w_ref, normed_ref,
    _own, _other,
    latent_ref, own_ref, other_ref, gvec_ref,
    g_qkv, g_proj, latent_sum, sems,
):
    step = pl.program_id(0)

    @pl.when(step == 0)
    def _():
        g_qkv[...] = jnp.zeros_like(g_qkv)
        gvec_ref[...] = jnp.zeros_like(gvec_ref)
        latent_sum[...] = jnp.zeros_like(latent_sum)

    h = h_ref[...]
    grads = (dq_ref[...], dk_ref[...], dv_ref[...])
    grad_h = jnp.zeros((QKV_ROWS, DD), f32)
    for index, grad in enumerate(grads):
        g_both = tn(grad, h)
        for group in range(2):
            rows = pl.ds(index * DD // 2, DD // 2)
            g_qkv[group, rows] += g_both[group * DD // 2 : (group + 1) * DD // 2]
        grad_h = grad_h + nn(grad, w_ref[pl.ds(index * DD, DD)])
    unit, rate = norm_parts(x_ref[...])
    grad_x = dx1_ref[...] + norm_back(grad_h, vec_ref[1:2], unit, rate)
    places = place_matrix(order_ref[...], QKV_ROWS)
    hidden = 1.0 - jnp.sum(places, 1, keepdims=True)
    latent_sum[...] += tn(places.astype(bf16), grad_x.astype(bf16))
    gvec_ref[0:1] += col_sum(grads[0].astype(f32))
    gvec_ref[1:2] += col_sum(grads[2].astype(f32))
    gvec_ref[2:3] += col_sum(grad_h * unit)
    gvec_ref[3:4] += col_sum(grad_h)
    gvec_ref[4:5] += col_sum(hidden * grad_x)

    @pl.when(step == pl.num_programs(0) - 1)
    def _():
        latent = latent_sum[...].astype(bf16)
        latent_ref[...] = latent
        both = tn(normed_ref[...], latent)
        g_proj[0] = both[: D // 2]
        g_proj[1] = both[D // 2 :]
        half = half_ref[0]
        kinds = pl.ds(DEC_Q, 3 * DD // 2)
        copies = [
            pltpu.make_async_copy(g_qkv.at[0], own_ref.at[kinds], sems.at[0]),
            pltpu.make_async_copy(g_qkv.at[1], other_ref.at[kinds], sems.at[1]),
            pltpu.make_async_copy(g_proj.at[half], own_ref.at[pl.ds(0, D // 2)], sems.at[2]),
            pltpu.make_async_copy(g_proj.at[1 - half], other_ref.at[pl.ds(0, D // 2)], sems.at[3]),
        ]
        for copy in copies:
            copy.start()
        for copy in copies:
            copy.wait()


def decoder_qkv_back(half, order, dq, dk, dv, h, x, dx1, vecs, weights, normed, own, other):
    rows = lambda width: pl.BlockSpec((QKV_ROWS, width), lambda i: (i, 0))
    return pl.pallas_call(
        qkv_back_kernel,
        grid=(TUBES // QKV_ROWS,),
        in_specs=[pl.BlockSpec(memory_space=pltpu.SMEM), whole((1, VIS))]
        + [rows(DD)] * 6
        + [whole(vecs.shape), whole((3 * DD, DD)), whole((VIS, D)), any_spec(), any_spec()],
        out_specs=[whole((VIS, DD)), any_spec(), any_spec(), whole((8, DD))],
        out_shape=[
            jax.ShapeDtypeStruct((VIS, DD), bf16),
            jax.ShapeDtypeStruct((DEC_ROWS, DD), f32),
            jax.ShapeDtypeStruct((DEC_ROWS, DD), f32),
            jax.ShapeDtypeStruct((8, DD), f32),
        ],
        scratch_shapes=[
            pltpu.VMEM((2, 3 * DD // 2, DD), f32),
            pltpu.VMEM((2, D // 2, DD), f32),
            pltpu.VMEM((VIS, DD), f32),
            pltpu.SemaphoreType.DMA((4,)),
        ],
        input_output_aliases={11: 1, 12: 2},
        compiler_params=params(),
        name="decoder_qkv_back",
    )(half, order, dq, dk, dv, h, x, dx1, vecs, weights, normed, own, other)


HALF = D // 2
HALF_FF = FF // 2
LAYER_ROWS = 4 * HALF + 2 * HALF_FF
AT_O, AT_D, AT_Q, AT_U = 0, HALF, HALF + HALF_FF, HALF + HALF_FF + 3 * HALF
STAGES = ((AT_Q, 3 * HALF), (AT_O, HALF), (AT_U, HALF_FF), (AT_D, HALF_FF))


def pieces_of(start, size, per):
    pieces = []
    at = start
    while at < start + size:
        many = min(start + size, (at // per + 1) * per) - at
        pieces.append((at // per, at % per, many, at - start))
        at += many
    return pieces


def stage_copies(sources, start, per, held, sems, stages):
    copies = []
    count = 0
    for at, size in stages:
        stage = []
        for shard, row, many, before in pieces_of(start + at, size, per):
            for group in range(2):
                stage.append(
                    pltpu.make_async_copy(
                        sources[group].at[shard, pl.ds(row, many)],
                        held.at[group, pl.ds(at + before, many)],
                        sems.at[count],
                    )
                )
                count += 1
        copies.append(stage)
    return copies


MOST_COPIES = 48


def encoder_kernel(layer, per, *refs):
    if layer == 0:
        pix_ref, pix_other_ref, pos_ref, *refs = refs
    else:
        x_ref, proj_ref, *refs = refs
    vec_ref, split_ref, own_ref, other_ref, *refs = refs
    if layer == 0:
        x_out_ref, *refs = refs
    else:
        normed_ref, latent_ref, *refs = refs
    out_ref, h_ref, qkv_ref, a_ref, x1_ref, h2_ref, u_ref, slope_ref, held, sems = refs
    base = 1 + 6 * layer
    biases = layer * (2 * HALF + HALF_FF)
    if layer == 0:
        copies = stage_copies(
            (own_ref, other_ref), 0, per, held.at[:, pl.ds(LAYER_ROWS, D)], sems, ((0, D),)
        )
        used = sum(len(stage) for stage in copies)
        copies = copies + stage_copies(
            (own_ref, other_ref), D, per, held, sems.at[pl.ds(used, MOST_COPIES - used)], STAGES
        )
        copies = copies[1:] + copies[:1]
        order = (4, 0, 1, 2, 3)
    else:
        copies = stage_copies((own_ref, other_ref), D + LAYER_ROWS, per, held, sems, STAGES)
        order = (0, 1, 2, 3)
    for stage in order:
        for copy in copies[stage]:
            copy.start()

    def wait(stage):
        for copy in copies[stage]:
            copy.wait()

    g1, b1, bo, g2, b2, bd = (vec_ref[base + index : base + index + 1] for index in range(6))
    if layer == 0:
        wait(4)
        x = pos_ref[...] + vec_ref[0:1]
        for group, pixels in enumerate((pix_ref, pix_other_ref)):
            x = x + nn(pixels[...], held[group, pl.ds(LAYER_ROWS, D)])
        x_out_ref[...] = x
    else:
        x = x_ref[...]
    unit, _ = norm_parts(x)
    h = (unit * g1 + b1).astype(bf16)
    h_ref[...] = h
    wait(0)
    for kind in range(3):
        for group in range(2):
            part = pl.ds((2 * kind + group) * HALF, HALF)
            rows = pl.ds(AT_Q + kind * HALF, HALF)
            value = nt(h, held[group, rows])
            if kind != 1:
                at = biases + kind // 2 * HALF
                value = value + split_ref[group : group + 1, at : at + HALF]
            qkv_ref[:, part] = value.astype(bf16)
    for pair in range(D // 128):
        q, k, v = (qkv_ref[:, pl.ds(kind * D + pair * 128, 128)] for kind in range(3))
        v_one = jnp.concatenate([v, jnp.ones((VIS, 128), bf16)], 1)
        mixed = []
        for head in range(2):
            scores = nt(jnp.where(half_lane(head), q, jnp.zeros_like(q)), k)
            top = jnp.max(scores, 1, keepdims=True)
            expo = jnp.exp2((scores - top) * (SCORE * LOG2E)).astype(bf16)
            both = nn(expo, v_one)
            mixed.append(both[:, :128] / both[:, 128:])
        a_ref[:, pl.ds(pair * 128, 128)] = jnp.where(half_lane(0), mixed[0], mixed[1]).astype(bf16)
    wait(1)
    x1 = x + bo
    for group in range(2):
        x1 = x1 + nn(a_ref[:, pl.ds(group * HALF, HALF)], held[group, pl.ds(AT_O, HALF)])
    x1_ref[...] = x1
    unit2, _ = norm_parts(x1)
    h2 = (unit2 * g2 + b2).astype(bf16)
    h2_ref[...] = h2
    wait(2)
    wait(3)
    out = x1 + bd
    for group in range(2):
        for chunk in range(HALF_FF // CHUNK):
            part = pl.ds(group * HALF_FF + chunk * CHUNK, CHUNK)
            before = nt(h2, held[group, pl.ds(AT_U + chunk * CHUNK, CHUNK)])
            at = biases + 2 * HALF + chunk * CHUNK
            value, slope = gelu_pair(before + split_ref[group : group + 1, at : at + CHUNK])
            slope_ref[:, part] = slope
            active = value.astype(bf16)
            u_ref[:, part] = active
            out = out + nn(active, held[group, pl.ds(AT_D + chunk * CHUNK, CHUNK)])
    out_ref[...] = out
    if layer == 1:
        unit3, _ = norm_parts(out)
        normed = (unit3 * vec_ref[13:14] + vec_ref[14:15]).astype(bf16)
        normed_ref[...] = normed
        latent_ref[...] = nn(normed, proj_ref[...])


def encoder_layer(layer, per, first, vecs, split2, own, other):
    shapes = [
        ((VIS, D), f32),
        ((VIS, D), bf16),
        ((VIS, 3 * D), bf16),
        ((VIS, D), bf16),
        ((VIS, D), f32),
        ((VIS, D), bf16),
        ((VIS, FF), bf16),
        ((VIS, FF), f32),
    ]
    before = [((VIS, D), f32)] if layer == 0 else [((VIS, D), bf16), ((VIS, DD), f32)]
    shapes = before + shapes
    return pl.pallas_call(
        lambda *refs: encoder_kernel(layer, per, *refs),
        in_specs=[vmem_spec()] * (len(first) + 2) + [any_spec()] * 2,
        out_specs=[vmem_spec()] * len(shapes),
        out_shape=[jax.ShapeDtypeStruct(shape, kind) for shape, kind in shapes],
        scratch_shapes=[
            pltpu.VMEM((2, LAYER_ROWS + (D if layer == 0 else 0), D), bf16),
            pltpu.SemaphoreType.DMA((MOST_COPIES,)),
        ],
        compiler_params=params(),
        name=f"encoder_{layer}",
    )(*first, vecs, split2, own, other)


RIGHT_AT = LAYER_ROWS


def encoder_back_kernel(layer, per, *refs):
    last = layer == 1
    start = D + layer * LAYER_ROWS
    base = 1 + 6 * layer
    (
        grad_ref, x_ref, vec_ref, h_ref, qkv_ref, a_ref, x1_ref, h2_ref, u_ref, slope_ref,
        start_ref, own_ref, other_ref, pix_ref, pix_other_ref,
    ) = refs[:15]
    pixels = (pix_ref, pix_other_ref)
    refs = refs[15:]
    if last:
        out_ref, proj_ref, *refs = refs
    dx_ref, mine_ref, other_pack_ref, left_ref, gvec_ref, gbu_ref, gbq_ref = refs[:7]
    held, sems, da, dqkv = refs[7:]
    packs = (mine_ref, other_pack_ref)
    copies = stage_copies((own_ref, other_ref), start, per, held, sems, STAGES)
    for stage in (3, 2, 1, 0):
        for copy in copies[stage]:
            copy.start()

    def wait(stage):
        for copy in copies[stage]:
            copy.wait()

    g1, b1, bo, g2, b2, bd = (vec_ref[base + index : base + index + 1] for index in range(6))
    gvec_ref[6:8] = jnp.zeros((2, D), f32)
    if last:
        unit3, rate3 = norm_parts(out_ref[...])
        grad_normed = nt(grad_ref[...], proj_ref[...])
        grad_out = norm_back(grad_normed, vec_ref[13:14], unit3, rate3)
        gvec_ref[6:7] = col_sum(grad_normed * unit3)
        gvec_ref[7:8] = col_sum(grad_normed)
    else:
        grad_out = grad_ref[...]
    out_low = grad_out.astype(bf16)
    unit2, rate2 = norm_parts(x1_ref[...])
    grad_h2 = jnp.zeros((VIS, D), f32)
    wait(3)
    wait(2)
    for group in range(2):
        for chunk in range(HALF_FF // CHUNK):
            part = pl.ds(group * HALF_FF + chunk * CHUNK, CHUNK)
            grad_active = nt(out_low, held[group, pl.ds(AT_D + chunk * CHUNK, CHUNK)])
            grad_before = (slope_ref[:, part] * grad_active).astype(bf16)
            packs[group][:, pl.ds(AT_U + chunk * CHUNK, CHUNK)] = grad_before
            packs[group][:, pl.ds(AT_D + chunk * CHUNK, CHUNK)] = u_ref[:, part]
            gbu_ref[:, part] = col_sum(grad_before.astype(f32))
            grad_h2 = grad_h2 + nn(grad_before, held[group, pl.ds(AT_U + chunk * CHUNK, CHUNK)])
    grad_x1 = grad_out + norm_back(grad_h2, g2, unit2, rate2)
    x1_low = grad_x1.astype(bf16)
    wait(1)
    for group in range(2):
        part = pl.ds(group * HALF, HALF)
        da[:, part] = nt(x1_low, held[group, pl.ds(AT_O, HALF)]).astype(bf16)
        packs[group][:, pl.ds(AT_O, HALF)] = a_ref[:, part]
    zero = jnp.zeros((), bf16)
    for pair in range(D // 128):
        lanes = pl.ds(pair * 128, 128)
        q, k, v = (qkv_ref[:, pl.ds(kind * D + pair * 128, 128)] for kind in range(3))
        grad = da[:, lanes]
        dq = dk = dv = jnp.zeros((VIS, 128), f32)
        for head in range(2):
            mask = half_lane(head)
            q_head = jnp.where(mask, q, zero)
            grad_head = jnp.where(mask, grad, zero)
            scores = nt(q_head, k) * SCORE
            expo = jnp.exp(scores - jnp.max(scores, 1, keepdims=True))
            probs = expo / jnp.sum(expo, 1, keepdims=True)
            grad_probs = nt(grad_head, v)
            row_total = jnp.sum(probs * grad_probs, 1, keepdims=True)
            grad_scores = (probs * (grad_probs - row_total)).astype(bf16)
            dv = dv + tn(probs.astype(bf16), grad_head)
            dk = dk + tn(grad_scores, q_head)
            dq = dq + nn(grad_scores, jnp.where(mask, k, zero))
        dqkv[:, lanes] = (dq * SCORE).astype(bf16)
        dqkv[:, pl.ds(D + pair * 128, 128)] = (dk * SCORE).astype(bf16)
        dqkv[:, pl.ds(2 * D + pair * 128, 128)] = dv.astype(bf16)
    wait(0)
    grad_h = jnp.zeros((VIS, D), f32)
    for kind in range(3):
        for group in range(2):
            grad = dqkv[:, pl.ds((2 * kind + group) * HALF, HALF)]
            rows = pl.ds(AT_Q + kind * HALF, HALF)
            packs[group][:, rows] = grad
            grad_h = grad_h + nn(grad, held[group, rows])
    unit, rate = norm_parts(x_ref[...])
    grad_x = grad_x1 + norm_back(grad_h, g1, unit, rate)
    dx_ref[...] = grad_x
    gbq_ref[0:1] = col_sum(dqkv[:, pl.ds(0, D)].astype(f32))
    gbq_ref[1:2] = col_sum(dqkv[:, pl.ds(2 * D, D)].astype(f32))
    gvec_ref[0:1] = col_sum(grad_h * unit)
    gvec_ref[1:2] = col_sum(grad_h)
    gvec_ref[2:3] = col_sum(x1_low.astype(f32))
    gvec_ref[3:4] = col_sum(grad_h2 * unit2)
    gvec_ref[4:5] = col_sum(grad_h2)
    gvec_ref[5:6] = col_sum(out_low.astype(f32))
    rights = [x1_low, out_low, h_ref[...], h2_ref[...]]
    spans = [(AT_O, HALF, 0), (AT_D, HALF_FF, 0), (AT_Q, 3 * HALF, 0), (AT_U, HALF_FF, 0)]
    if not last:
        embed_low = grad_x.astype(bf16)
        rights.append(embed_low)
        gvec_ref[6:7] = col_sum(embed_low.astype(f32))
    starts = jnp.concatenate([split3(start_ref[0]), split3(start_ref[1])], 0)
    before = 0 if last else D
    for index, right in enumerate(rights):
        for pack in packs:
            pack[:, pl.ds(RIGHT_AT + index * D, D)] = right
        inner = nt(starts, right)
        for group in range(2):
            parts = split3(fold3(inner[3 * RANK * group : 3 * RANK * (group + 1)]))
            if index == 4:
                value = fold3(nn(parts, pixels[group][...]))
                left_ref[group, :, pl.ds(0, D)] = value
            else:
                at, size, _ = spans[index]
                value = fold3(nn(parts, packs[group][:, pl.ds(at, size)]))
                left_ref[group, :, pl.ds(before + at, size)] = value


def encoder_layer_back(layer, per, grad, source, vecs, kept, starts, own, other, pixels, last=()):
    width = RIGHT_AT + (5 - layer) * D
    shapes = [
        ((VIS, D), f32),
        ((VIS, width), bf16),
        ((VIS, width), bf16),
        ((2, RANK, LAYER_ROWS + (1 - layer) * D), f32),
        ((8, D), f32),
        ((1, FF), f32),
        ((2, D), f32),
    ]
    _, h, qkv, a, x1, h2, u, slope = kept
    return pl.pallas_call(
        lambda *refs: encoder_back_kernel(layer, per, *refs),
        in_specs=[vmem_spec()] * 11 + [any_spec()] * 2 + [vmem_spec()] * (2 + len(last)),
        out_specs=[vmem_spec()] * len(shapes),
        out_shape=[jax.ShapeDtypeStruct(shape, kind) for shape, kind in shapes],
        scratch_shapes=[
            pltpu.VMEM((2, LAYER_ROWS, D), bf16),
            pltpu.SemaphoreType.DMA((MOST_COPIES,)),
            pltpu.VMEM((VIS, D), bf16),
            pltpu.VMEM((VIS, 3 * D), bf16),
        ],
        compiler_params=params(),
        name=f"encoder_back_{layer}",
    )(grad, source, vecs, h, qkv, a, x1, h2, u, slope, starts, own, other, *pixels, *last)


ROWS = 768
HALF_ROWS = ROWS // 2
ENC_ROWS = D + 2 * LAYER_ROWS
ENC_BLOCKS = ENC_ROWS // ROWS
PER_LAYER = LAYER_ROWS // ROWS


def kinds_of(inner):
    first = jnp.where(inner < 1, 0, jnp.where(inner < 3, 1, jnp.where(inner < 4, 2, 3)))
    first = jnp.where(inner == 2, 1, first)
    second = jnp.where(inner < 2, 1, jnp.where(inner < 4, 2, 3))
    return jnp.where(inner == 3, 2, first), second


def pack_specs():
    pixel = pl.BlockSpec((VIS, D), lambda j: (0, 0))
    specs = []
    for layer in range(2):
        inner = lambda j, layer=layer: jnp.clip(j - 1 - layer * PER_LAYER, 0, PER_LAYER - 1)
        at = RIGHT_AT // D
        specs.append(pl.BlockSpec((VIS, ROWS), lambda j, inner=inner: (0, inner(j))))
        for side in range(2):
            specs.append(
                pl.BlockSpec(
                    (VIS, D), lambda j, inner=inner, side=side: (0, at + kinds_of(inner(j))[side])
                )
            )
    embed = pl.BlockSpec((VIS, D), lambda j: (0, RIGHT_AT // D + 4))
    return [pixel, embed] + specs


def by_segment(refs, run):
    step = pl.program_id(0)
    count = len(refs) // 2
    mine, theirs = refs[:count], refs[count:]

    @pl.when(step == 0)
    def _():
        run((mine[0], theirs[0]), (mine[1], theirs[1]), (mine[1], theirs[1]))

    for layer in range(2):
        low = 1 + layer * PER_LAYER

        @pl.when(jnp.logical_and(step >= low, step < low + PER_LAYER))
        def _(at=2 + 3 * layer):
            run(*((mine[at + index], theirs[at + index]) for index in range(3)))


def error_factor_kernel(start_ref, error_ref, out_ref):
    turned = nt(error_ref[...], split3(start_ref[...]))
    out_ref[...] = fold3(turned.T)


def error_factor(start, error):
    rows, width = error.shape
    return pl.pallas_call(
        error_factor_kernel,
        grid=(rows // HALF_ROWS,),
        in_specs=[whole((RANK, width)), pl.BlockSpec((HALF_ROWS, width), lambda j: (j, 0))],
        out_specs=pl.BlockSpec((RANK, HALF_ROWS), lambda j: (0, j)),
        out_shape=jax.ShapeDtypeStruct((RANK, rows), f32),
        compiler_params=params(),
        name="error_factor",
    )(start, error)


def right_factor_kernel(basis_ref, error_ref, *refs):
    out_ref = refs[-1]

    @pl.when(pl.program_id(0) == 0)
    def _():
        out_ref[...] = jnp.zeros_like(out_ref)

    basis = split3(basis_ref[...])
    out_ref[...] += fold3(nn(basis, error_ref[...]))

    def run(left, first, second):
        total = jnp.zeros((3 * RANK, D), f32)
        for clip in range(2):
            for side, right in ((0, first), (1, second)):
                lanes = pl.ds(side * HALF_ROWS, HALF_ROWS)
                inner = fold3(nt(basis[:, side * HALF_ROWS : (side + 1) * HALF_ROWS],
                                 left[clip][:, lanes]))
                total = total + nn(split3(inner), right[clip][...])
        out_ref[...] += fold3(total)

    by_segment(refs[:-1], run)


def right_factor(basis, error, mine, theirs):
    return pl.pallas_call(
        right_factor_kernel,
        grid=(ENC_BLOCKS,),
        in_specs=[
            pl.BlockSpec((RANK, ROWS), lambda j: (0, j)),
            pl.BlockSpec((ROWS, D), lambda j: (j, 0)),
        ]
        + pack_specs() * 2,
        out_specs=whole((RANK, D)),
        out_shape=jax.ShapeDtypeStruct((RANK, D), f32),
        compiler_params=params(),
        name="right_factor",
    )(basis, error, *pack_args(mine), *pack_args(theirs))


def pack_args(packs):
    pixels, first, second = packs
    return (pixels, first, first, first, first, second, second, second)


def low_pairs(basis, factor):
    basis3 = split3(basis)
    factor3 = split3(factor)
    high, middle = basis3[:RANK], basis3[RANK : 2 * RANK]
    return (
        jnp.concatenate([high, high, middle, jnp.zeros_like(high)], 0),
        jnp.concatenate([factor3[: 2 * RANK], factor3[:RANK], jnp.zeros_like(factor3[:RANK])], 0),
    )


def residue_kernel(basis_ref, factor_ref, error_ref, *refs):
    out_ref = refs[-1]
    basis, factor = low_pairs(basis_ref[...], -factor_ref[...])

    def run(left, first, second):
        for side, right in ((0, first), (1, second)):
            rows = pl.ds(side * HALF_ROWS, HALF_ROWS)
            low = basis[:, side * HALF_ROWS : (side + 1) * HALF_ROWS]
            lefts = jnp.concatenate([left[0][:, rows], left[1][:, rows], low], 0)
            rights = jnp.concatenate([right[0][...], right[1][...], factor], 0)
            out_ref[rows] = (tn(lefts, rights) + error_ref[rows].astype(f32)).astype(bf16)

    by_segment(refs[:-1], run)


def residue(basis, factor, error, mine, theirs):
    return pl.pallas_call(
        residue_kernel,
        grid=(ENC_BLOCKS,),
        in_specs=[
            pl.BlockSpec((RANK, ROWS), lambda j: (0, j)),
            whole((RANK, D)),
            pl.BlockSpec((ROWS, D), lambda j: (j, 0)),
        ]
        + pack_specs() * 2,
        out_specs=pl.BlockSpec((ROWS, D), lambda j: (j, 0)),
        out_shape=jax.ShapeDtypeStruct((ENC_ROWS, D), bf16),
        compiler_params=params(),
        name="residue",
    )(basis, factor, error, *pack_args(mine), *pack_args(theirs))


DEC_BLOCK = 1152


def dec_right_kernel(basis_ref, own_ref, came_ref, error_ref, out_ref, comb_ref):
    @pl.when(pl.program_id(0) == 0)
    def _():
        out_ref[...] = jnp.zeros_like(out_ref)

    basis = split3(basis_ref[...])
    comb = own_ref[...] + came_ref[...] + error_ref[...].astype(f32)
    comb_ref[...] = comb
    high = comb.astype(bf16)
    rest = (comb - high.astype(f32)).astype(bf16)
    out_ref[...] += fold3(nn(basis, high) + nn(basis, rest))


def dec_right_factor(basis, own, came, error):
    rows = pl.BlockSpec((DEC_BLOCK, DD), lambda j: (j, 0))
    return pl.pallas_call(
        dec_right_kernel,
        grid=(DEC_ROWS // DEC_BLOCK,),
        in_specs=[pl.BlockSpec((RANK, DEC_BLOCK), lambda j: (0, j)), rows, rows, rows],
        out_specs=[whole((RANK, DD)), rows],
        out_shape=[
            jax.ShapeDtypeStruct((RANK, DD), f32),
            jax.ShapeDtypeStruct((DEC_ROWS, DD), f32),
        ],
        compiler_params=params(),
        name="dec_right_factor",
    )(basis, own, came, error)


def dec_residue_kernel(basis_ref, factor_ref, comb_ref, out_ref):
    out_ref[...] = (
        comb_ref[...] + tn(*low_pairs(basis_ref[...], -factor_ref[...]))
    ).astype(bf16)


def dec_residue(basis, factor, comb):
    return pl.pallas_call(
        dec_residue_kernel,
        grid=(DEC_ROWS // DEC_BLOCK,),
        in_specs=[
            pl.BlockSpec((RANK, DEC_BLOCK), lambda j: (0, j)),
            whole((RANK, DD)),
            pl.BlockSpec((DEC_BLOCK, DD), lambda j: (j, 0)),
        ],
        out_specs=pl.BlockSpec((DEC_BLOCK, DD), lambda j: (j, 0)),
        out_shape=jax.ShapeDtypeStruct((DEC_ROWS, DD), bf16),
        compiler_params=params(),
        name="dec_residue",
    )(basis, factor, comb)


def dec_left_kernel(start_ref, own_ref, other_ref, out_ref):
    for group, ref in enumerate((own_ref, other_ref)):
        start = split3(start_ref[group])
        grad = ref[...]
        high = grad.astype(bf16)
        rest = (grad - high.astype(f32)).astype(bf16)
        out_ref[group] = fold3((nt(high, start) + nt(rest, start)).T)


def dec_left_factor(starts, own, other):
    rows = pl.BlockSpec((DEC_BLOCK, DD), lambda j: (j, 0))
    return pl.pallas_call(
        dec_left_kernel,
        grid=(DEC_ROWS // DEC_BLOCK,),
        in_specs=[whole((2, RANK, DD)), rows, rows],
        out_specs=pl.BlockSpec((2, RANK, DEC_BLOCK), lambda j: (0, 0, j)),
        out_shape=jax.ShapeDtypeStruct((2, RANK, DEC_ROWS), f32),
        compiler_params=params(),
        name="dec_left_factor",
    )(starts, own, other)


MESH_ID = pl.DeviceIdType.MESH


def greet(workers, me, partner):
    barrier = pltpu.get_barrier_semaphore()
    for distance in range(1, workers):
        pl.semaphore_signal(
            barrier, 1, device_id={"dp": lax.rem(me + distance, workers)}, device_id_type=MESH_ID
        )
    if partner is not None:
        pl.semaphore_signal(barrier, 1, device_id={"tensor": partner}, device_id_type=MESH_ID)
    pl.semaphore_wait(barrier, workers - 1 + (partner is not None))


def sum_workers(workers, me, lanes, local, slots, sums, sems):
    def share(index):
        return pl.ds(pl.multiple_of(index * lanes, 128), lanes)

    def to_all(turn, source, target):
        copies = []
        for distance in range(1, workers):
            peer = lax.rem(me + distance, workers)
            copy = pltpu.make_async_remote_copy(
                src_ref=source(peer),
                dst_ref=target(distance),
                send_sem=sems.at[2 * turn, distance],
                recv_sem=sems.at[2 * turn + 1, distance],
                device_id={"dp": peer},
                device_id_type=MESH_ID,
            )
            copy.start()
            copies.append(copy)
        return copies

    copies = to_all(0, lambda peer: local.at[:, share(peer)], lambda distance: slots.at[distance])
    total = local[:, share(me)]
    for distance, copy in enumerate(copies, 1):
        copy.wait_recv()
        total = total + slots[distance]
    sums[:, share(me)] = total
    more = to_all(1, lambda peer: sums.at[:, share(me)], lambda distance: sums.at[:, share(me)])
    for copy in copies:
        copy.wait_send()
    for copy in more:
        copy.wait()


def basis_kernel(
    workers, lanes, enc_width, first_ref, second_ref, dec_ref, error_ref, dec_error_ref,
    enc_out, dec_out,
    send, came, local, slots, sums, sems, pair_sems,
):
    me = lax.axis_index("dp")
    half = lax.axis_index("tensor")
    first = first_ref.shape[2]
    second = second_ref.shape[2]
    width = enc_width + dec_ref.shape[2]
    spans = ((first_ref, 0, first), (second_ref, first, second), (dec_ref, enc_width, width - enc_width))
    for ref, at, size in spans:
        send[:, at : at + size] = ref[1]
    if width < workers * lanes:
        tail = jnp.zeros((RANK, workers * lanes - width), f32)
        send[:, width:] = tail
    greet(workers, me, 1 - half)
    copy = pltpu.make_async_remote_copy(
        src_ref=send,
        dst_ref=came,
        send_sem=pair_sems.at[0],
        recv_sem=pair_sems.at[1],
        device_id={"tensor": 1 - half},
        device_id_type=MESH_ID,
    )
    copy.start()
    for ref, at, size in spans[:2]:
        local[:, at : at + size] = ref[0] + error_ref[:, at : at + size]
    local[:, enc_width:width] = dec_ref[0] + dec_error_ref[...]
    if width < workers * lanes:
        local[:, width:] = tail
    copy.wait()
    local[...] += came[...]
    sum_workers(workers, me, lanes, local, slots, sums, sems)
    place = lax.broadcasted_iota(jnp.int32, (RANK, 1), 0)
    for at, out in ((0, enc_out), (enc_width, dec_out)):
        left = sums[:, at : at + out.shape[1]]
        gram = lax.dot_general(
            left, left, (((1,), (1,)), ((), ())), precision=highest_precision,
            preferred_element_type=f32,
        )
        for index in range(RANK):
            scale = lax.rsqrt(gram[index : index + 1, index : index + 1])
            column = gram[:, index : index + 1] * scale
            below = jnp.where(place > index, column, 0.0)
            pivot = left[index : index + 1] * scale
            left = jnp.where(place == index, pivot, left - below * pivot)
            gram = gram - below * (gram[index : index + 1] * scale)
        out[...] = left


def lanes_for(width, workers):
    return pl.cdiv(width, 128 * workers) * 128


def summed_basis(workers, first, second, dec, error_part, dec_error_part):
    enc_width = first.shape[2] + second.shape[2]
    width = enc_width + dec.shape[2]
    lanes = lanes_for(width, workers)
    wide = pltpu.VMEM((RANK, workers * lanes), f32)
    return pl.pallas_call(
        lambda *refs: basis_kernel(workers, lanes, enc_width, *refs),
        in_specs=[vmem_spec()] * 5,
        out_specs=[vmem_spec()] * 2,
        out_shape=[
            jax.ShapeDtypeStruct((RANK, enc_width), f32),
            jax.ShapeDtypeStruct((RANK, width - enc_width), f32),
        ],
        scratch_shapes=[
            wide,
            wide,
            wide,
            pltpu.VMEM((workers, RANK, lanes), f32),
            wide,
            pltpu.SemaphoreType.DMA((4, workers)),
            pltpu.SemaphoreType.DMA((2,)),
        ],
        compiler_params=pltpu.CompilerParams(
            collective_id=1, has_side_effects=True, vmem_limit_bytes=BIG_VMEM
        ),
        name="summed_basis",
    )(first, second, dec, error_part, dec_error_part)


def sum_kernel(workers, lanes, *refs):
    count = (len(refs) - 4) // 2
    parts, outs = refs[:count], refs[count : 2 * count]
    local, slots, sums, sems = refs[2 * count :]
    me = lax.axis_index("dp")
    at = 0
    for part in parts:
        local[:, at : at + part.shape[1]] = part[...]
        at += part.shape[1]
    if at < workers * lanes:
        local[:, at:] = jnp.zeros((RANK, workers * lanes - at), f32)
    greet(workers, me, None)
    sum_workers(workers, me, lanes, local, slots, sums, sems)
    at = 0
    for out in outs:
        out[...] = sums[:, at : at + out.shape[1]] * (1.0 / workers)
        at += out.shape[1]


def mean_over_workers(workers, parts):
    lanes = lanes_for(sum(part.shape[1] for part in parts), workers)
    wide = pltpu.VMEM((RANK, workers * lanes), f32)
    return pl.pallas_call(
        lambda *refs: sum_kernel(workers, lanes, *refs),
        in_specs=[vmem_spec()] * len(parts),
        out_specs=[vmem_spec()] * len(parts),
        out_shape=[jax.ShapeDtypeStruct(part.shape, f32) for part in parts],
        scratch_shapes=[
            wide,
            pltpu.VMEM((workers, RANK, lanes), f32),
            wide,
            pltpu.SemaphoreType.DMA((4, workers)),
        ],
        compiler_params=pltpu.CompilerParams(
            collective_id=2, has_side_effects=True, vmem_limit_bytes=BIG_VMEM
        ),
        name="mean_over_workers",
    )(*parts)


PLANE = 4
PART_Z_X_Y, PART_Z_Y_X, PART_X_Y_Z = range(3)
WAY_X, WAY_Y, WAY_UP, WAY_DOWN = range(4)
ERROR_ROWS = 1248


def gather_kernel(
    parts, planes, shard_ref, tubes_ref, error_ref, dec_error_ref, start_ref,
    own_ref, other_ref, pixels_ref, part_ref, dec_part_ref,
    held, dec_held, send_sems, recv_sems, pair_sems, sems,
):
    me = lax.axis_index("dp")
    half = lax.axis_index("tensor")
    z = me // PLANE
    column = lax.rem(me, PLANE)
    column_x = column + 1 - 2 * lax.rem(column, 2)
    column_y = lax.rem(column + 2, PLANE)
    column_xy = lax.rem(column_x + 2, PLANE)
    up = z < planes - 1
    down = z > 0
    peers = (
        z * PLANE + column_x,
        z * PLANE + column_y,
        jnp.minimum(me + PLANE, PLANE * planes - 1),
        jnp.maximum(me - PLANE, 0),
    )
    rows = [pl.ds(at, size) for at, size in parts]

    def copy(way, part, slot, mine=False):
        return pltpu.make_async_remote_copy(
            src_ref=shard_ref.at[rows[part]] if mine else own_ref.at[slot, rows[part]],
            dst_ref=own_ref.at[slot, rows[part]],
            send_sem=send_sems.at[way, part, slot],
            recv_sem=recv_sems.at[part, slot],
            device_id={"dp": peers[way]},
            device_id_type=MESH_ID,
        )

    def send(way, part, slot, mine=False):
        copy(way, part, slot, mine).start()

    def recv(part, slot):
        copy(WAY_X, part, slot).wait_recv()

    def pair(part, plane):
        block = pl.ds(plane * PLANE, PLANE)
        return pltpu.make_async_remote_copy(
            src_ref=own_ref.at[block, rows[part]],
            dst_ref=other_ref.at[block, rows[part]],
            send_sem=pair_sems.at[0, part, plane],
            recv_sem=pair_sems.at[1, part, plane],
            device_id={"tensor": 1 - half},
            device_id_type=MESH_ID,
        )

    def load(index):
        return pltpu.make_async_copy(
            error_ref.at[pl.ds(index * ERROR_ROWS, ERROR_ROWS)], held.at[index % 2], sems.at[index % 2]
        )

    load(0).start()
    load(1).start()
    dec_load = pltpu.make_async_copy(dec_error_ref, dec_held, sems.at[2])
    dec_load.start()

    barrier = pltpu.get_barrier_semaphore()
    for way in (WAY_X, WAY_Y):
        pl.semaphore_signal(barrier, 1, device_id={"dp": peers[way]}, device_id_type=MESH_ID)
    pl.semaphore_signal(barrier, 1, device_id={"tensor": 1 - half}, device_id_type=MESH_ID)
    for ok, way in ((up, WAY_UP), (down, WAY_DOWN)):

        @pl.when(ok)
        def _(way=way):
            pl.semaphore_signal(barrier, 1, device_id={"dp": peers[way]}, device_id_type=MESH_ID)

    pl.semaphore_wait(barrier, 3 + up.astype(jnp.int32) + down.astype(jnp.int32))

    def both_z(part, slot, mine=False):
        @pl.when(up)
        def _():
            send(WAY_UP, part, slot, mine)

        @pl.when(down)
        def _():
            send(WAY_DOWN, part, slot, mine)

    def sides(distance):
        return [
            ((z + side * distance >= 0) & (z + side * distance < planes), z + side * distance, on, way)
            for side, on, way in ((-1, up, WAY_UP), (1, down, WAY_DOWN))
        ]

    def along(distance):
        for there, plane, on, way in sides(distance):

            @pl.when(there)
            def _(slot=plane * PLANE + column, on=on, way=way):
                for part in (PART_Z_X_Y, PART_Z_Y_X):
                    recv(part, slot)

                    @pl.when(on)
                    def _():
                        send(way, part, slot)

                    send(WAY_X if part == PART_Z_X_Y else WAY_Y, part, slot)
                send(WAY_Y, PART_Z_X_Y, slot)
                send(WAY_X, PART_Z_Y_X, slot)

    def cross(distance):
        for there, plane, _, _ in sides(distance):

            @pl.when(there)
            def _(base=plane * PLANE):
                recv(PART_Z_X_Y, base + column_x)
                send(WAY_Y, PART_Z_X_Y, base + column_x)
                recv(PART_Z_Y_X, base + column_y)
                send(WAY_X, PART_Z_Y_X, base + column_y)

    def finish(distance):
        for there, plane, _, _ in sides(distance)[: 2 if distance else 1]:

            @pl.when(there)
            def _(plane=plane, base=plane * PLANE):
                recv(PART_Z_X_Y, base + column_y)
                recv(PART_Z_X_Y, base + column_xy)
                pair(PART_Z_X_Y, plane).start()
                recv(PART_Z_Y_X, base + column_x)
                recv(PART_Z_Y_X, base + column_xy)
                pair(PART_Z_Y_X, plane).start()

    def whole_plane(distance):
        for there, plane, on, way in sides(distance):

            @pl.when(there)
            def _(plane=plane, on=on, way=way):
                for index in range(PLANE):
                    slot = plane * PLANE + index
                    recv(PART_X_Y_Z, slot)

                    @pl.when(on)
                    def _(slot=slot):
                        send(way, PART_X_Y_Z, slot)

                pair(PART_X_Y_Z, plane).start()

    start3 = split3(start_ref[:, :D])
    chunks = error_ref.shape[0] // ERROR_ROWS

    def work(index):
        load(index).wait()
        lanes = pl.ds(index * ERROR_ROWS, ERROR_ROWS)
        part_ref[:, lanes] = fold3(nt(start3, held[index % 2]))
        if index + 2 < chunks:
            load(index + 2).start()

    send(WAY_X, PART_X_Y_Z, me, True)
    send(WAY_Y, PART_X_Y_Z, me, True)
    both_z(PART_Z_X_Y, me, True)
    both_z(PART_Z_Y_X, me, True)
    send(WAY_X, PART_Z_X_Y, me, True)
    send(WAY_Y, PART_Z_Y_X, me, True)
    send(WAY_X, PART_Z_Y_X, me, True)
    send(WAY_Y, PART_Z_X_Y, me, True)
    keep = pltpu.make_async_copy(shard_ref, own_ref.at[me], sems.at[3])
    keep.start()
    swap_pixels = pltpu.make_async_remote_copy(
        src_ref=tubes_ref.at[1 - half],
        dst_ref=pixels_ref,
        send_sem=sems.at[4],
        recv_sem=sems.at[5],
        device_id={"tensor": 1 - half},
        device_id_type=MESH_ID,
    )
    swap_pixels.start()
    work(0)
    near = z * PLANE
    recv(PART_X_Y_Z, near + column_x)
    send(WAY_Y, PART_X_Y_Z, near + column_x)
    recv(PART_Z_X_Y, near + column_x)
    send(WAY_Y, PART_Z_X_Y, near + column_x)
    recv(PART_Z_Y_X, near + column_y)
    send(WAY_X, PART_Z_Y_X, near + column_y)
    keep.wait()
    work(1)
    along(1)
    recv(PART_X_Y_Z, near + column_y)
    recv(PART_X_Y_Z, near + column_xy)
    for index in range(PLANE):
        both_z(PART_X_Y_Z, near + index)
    pair(PART_X_Y_Z, z).start()
    work(2)
    cross(1)
    finish(0)
    work(3)
    along(2)
    work(4)
    whole_plane(1)
    cross(2)
    work(5)
    finish(1)
    along(3)
    work(6)
    whole_plane(2)
    cross(3)
    work(7)
    finish(2)
    dec_load.wait()
    dec_part_ref[...] = fold3(nt(split3(start_ref[:, D:]), dec_held[...]))
    whole_plane(3)
    finish(3)
    swap_pixels.wait()
    for plane in range(planes):
        for part in range(3):
            pair(part, plane).wait()
        for index in range(PLANE):
            slot = plane * PLANE + index

            @pl.when(column == index)
            def _():
                for part in (PART_Z_X_Y, PART_Z_Y_X):
                    copy(WAY_X, part, slot).wait_send()
                    copy(WAY_Y, part, slot).wait_send()

            @pl.when(column_x == index)
            def _():
                copy(WAY_Y, PART_Z_X_Y, slot).wait_send()

            @pl.when(column_y == index)
            def _():
                copy(WAY_X, PART_Z_Y_X, slot).wait_send()

            for part in range(3):
                sent = True if part == PART_X_Y_Z else column == index

                @pl.when(up & (plane <= z) & sent)
                def _():
                    copy(WAY_UP, part, slot).wait_send()

                @pl.when(down & (plane >= z) & sent)
                def _():
                    copy(WAY_DOWN, part, slot).wait_send()

    copy(WAY_X, PART_X_Y_Z, me).wait_send()
    copy(WAY_Y, PART_X_Y_Z, me).wait_send()
    copy(WAY_Y, PART_X_Y_Z, near + column_x).wait_send()


def gather_weights(planes, shard, tubes, error, dec_error, start):
    workers = planes * PLANE
    size = shard.shape[0]
    long = (size * 2 // 5 + 15) // 16 * 16
    parts = ((0, long), (long, long), (2 * long, size - 2 * long))
    shards = jax.ShapeDtypeStruct((workers,) + shard.shape, shard.dtype)
    return pl.pallas_call(
        lambda *refs: gather_kernel(parts, planes, *refs),
        in_specs=[any_spec()] * 4 + [vmem_spec()],
        out_specs=[any_spec()] * 3 + [vmem_spec()] * 2,
        out_shape=[
            shards,
            shards,
            jax.ShapeDtypeStruct(tubes.shape[1:], tubes.dtype),
            jax.ShapeDtypeStruct((RANK, error.shape[0]), f32),
            jax.ShapeDtypeStruct((RANK, dec_error.shape[0]), f32),
        ],
        scratch_shapes=[
            pltpu.VMEM((2, ERROR_ROWS, D), bf16),
            pltpu.VMEM(dec_error.shape, bf16),
            pltpu.SemaphoreType.DMA((4, 3, workers)),
            pltpu.SemaphoreType.DMA((3, workers)),
            pltpu.SemaphoreType.DMA((2, 3, planes)),
            pltpu.SemaphoreType.DMA((6,)),
        ],
        compiler_params=pltpu.CompilerParams(
            collective_id=3, has_side_effects=True, vmem_limit_bytes=BIG_VMEM
        ),
        name="gather_weights",
    )(shard, tubes, error, dec_error, start)


def cut(block, widths):
    pieces = []
    start = 0
    for width in widths:
        pieces.append(block[start : start + width])
        start = start + width
    return pieces


def swap(value):
    return lax.ppermute(value, "tensor", [(0, 1), (1, 0)])


def per_device(
    tubes,
    tube_order,
    clip_mask,
    enc_weights,
    dec_weights,
    vec_split,
    vec_shared,
    enc_moment,
    dec_moment,
    split_moment,
    shared_moment,
    enc_error,
    dec_error,
    factors,
):
    workers = lax.axis_size("dp")
    half = lax.axis_index("tensor")
    worker_index = lax.axis_index("dp")
    mine = lambda both: lax.dynamic_index_in_dim(both, half, 0, keepdims=False)
    which = half.astype(jnp.int32)[None]
    counted_all = clip_mask.astype(f32)
    counted = mine(counted_all)
    enc_per = enc_weights.shape[1]
    dec_per = dec_weights.shape[1] * DD // D
    spare = -(enc_per + dec_per + 1) % 16 + 1
    shard = jnp.concatenate(
        [
            enc_weights[0].astype(bf16),
            dec_weights[0].astype(bf16).reshape(dec_per, D),
            jnp.broadcast_to(jnp.sum(counted_all).astype(bf16), (spare, D)),
        ],
        0,
    )
    start_own = factors[0]
    picked = pick_visible(which, tube_order, tubes)
    pix_vis = picked[0]
    pix_vis_other = swap(picked[1])
    if workers == 4 * PLANE:
        per = enc_per
        own, other, pixels, enc_error_part, dec_error_part = gather_weights(
            workers // PLANE, shard, tubes, enc_error[0, 0], dec_error[0, 0], start_own
        )
        enc_own, enc_other = own, other
    else:
        own = lax.all_gather(shard, "dp", axis=0)
        other = swap(own)
        pixels = swap(lax.dynamic_index_in_dim(tubes, 1 - half, 0, keepdims=False))
        per = enc_per * workers
        enc_own, enc_other = (shards[:, :enc_per].reshape(1, per, D) for shards in (own, other))
        enc_error_part = error_factor(start_own[:, :D], enc_error[0, 0])
        dec_error_part = error_factor(start_own[:, D:], dec_error[0, 0])
    dec_own, dec_other = (
        shards[:, enc_per : enc_per + dec_per].reshape(DEC_ROWS, DD) for shards in (own, other)
    )
    loss_weight = MASKED * jnp.sum(own[:, enc_per + dec_per, 0].astype(f32))

    split_own = vec_split[0]
    split2 = jnp.stack([split_own, swap(split_own)])
    dec_at = 2 * (2 * HALF + HALF_FF)
    bq, bv, bu, bh = (
        split2[:, at : at + size].reshape(1, 2 * size)
        for at, size in (
            (dec_at, DD // 2),
            (dec_at + DD // 2, DD // 2),
            (dec_at + DD, DFF // 2),
            (dec_at + DD + DFF // 2, PIX // 2),
        )
    )
    wide = vec_shared[: 15 * D].reshape(15, D)
    narrow = vec_shared[15 * D :].reshape(9, DD)
    dec_widths = [D // 2, DD // 2, DFF // 2, 3 * DD // 2, DFF // 2, PIX // 2]
    own_parts = cut(dec_own, dec_widths)
    other_parts = cut(dec_other, dec_widths)
    proj = jnp.where(
        half == 0,
        jnp.concatenate([own_parts[0], other_parts[0]], 0),
        jnp.concatenate([other_parts[0], own_parts[0]], 0),
    )
    d_out, d_down, d_up, head_rows = (
        jnp.concatenate([own_parts[index], other_parts[index]], 0) for index in (1, 2, 4, 5)
    )
    kinds = lambda block: block.reshape(3, DD // 2, DD)
    d_qkv = jnp.concatenate([kinds(own_parts[3]), kinds(other_parts[3])], 1).reshape(3 * DD, DD)

    visible = mine(tube_order)[:VIS]
    pos_enc = sinusoid_at(visible, D)
    pos_dec = sinusoid_table(DD)
    start_other = swap(start_own)
    enc_starts = jnp.stack([start_own[:, :D], start_other[:, :D]])
    dec_starts = jnp.stack([start_own[:, D:], start_other[:, D:]])

    stream0, *kept0 = encoder_layer(
        0, per, (pix_vis, pix_vis_other, pos_enc), wide, split2, enc_own, enc_other
    )
    stream1 = kept0[0]
    enc_normed, latent, *kept1 = encoder_layer(
        1, per, (stream1, proj), wide, split2, enc_own, enc_other
    )
    kept = [(stream0, kept0), (stream1, kept1)]

    dec_start, h, qkv, hidden = decoder_qkv(
        visible[None], pos_dec, latent, narrow, d_qkv,
        jnp.concatenate([bq, jnp.zeros_like(bq), bv], 1),
    )
    mixed, logs = attend(qkv)
    scal = jnp.broadcast_to(
        jnp.stack([counted, 2.0 * workers / (PIX * loss_weight) * counted] + [counted] * 6)[:, None],
        (8, 128),
    )
    grad_mixed, grad_middle, dec_grads, dec_sent, g_vec, g_bu, g_bh, loss_lanes = decoder_tokens(
        which, mixed, dec_start, tubes, pixels, hidden, scal, narrow, bu, bh, d_out, d_down, d_up,
        head_rows,
    )
    dq, dk, dv = attend_back(qkv, mixed, grad_mixed, logs)
    latent_low, dec_grads, dec_sent, g_vec1 = decoder_qkv_back(
        which, visible[None], dq, dk, dv, h, dec_start, grad_middle, narrow, d_qkv, enc_normed,
        dec_grads, dec_sent,
    )
    dec_left = dec_left_factor(dec_starts, dec_grads, dec_sent)
    dec_came = swap(dec_sent)

    grad = latent_low
    packs = [None, None]
    came = [None, None]
    enc_lefts = [None, None]
    enc_vec_grads = [None, None]
    for layer in (1, 0):
        source, result = kept[layer]
        grad, packs[layer], sent, enc_lefts[layer], *enc_vec_grads[layer] = encoder_layer_back(
            layer, per, grad, source, wide, result, enc_starts, enc_own, enc_other,
            (pix_vis, pix_vis_other), (result[0], proj) if layer == 1 else (),
        )
        came[layer] = swap(sent)
    mine_packs = (pix_vis, packs[0], packs[1])
    their_packs = (picked[1], came[0], came[1])

    enc_basis, dec_basis = summed_basis(
        workers, enc_lefts[0], enc_lefts[1], dec_left, enc_error_part, dec_error_part
    )

    def split_half(index):
        pieces = []
        for layer in range(2):
            _, g_hidden, g_qv = enc_vec_grads[layer]
            pieces += [
                cut(g_qv[0], [HALF] * 2)[index],
                cut(g_qv[1], [HALF] * 2)[index],
                cut(g_hidden[0], [HALF_FF] * 2)[index],
            ]
        pieces += [
            cut(g_vec1[0], [DD // 2] * 2)[index],
            cut(g_vec1[1], [DD // 2] * 2)[index],
            cut(g_bu[0], [DFF // 2] * 2)[index],
            cut(g_bh[0], [PIX // 2] * 2)[index],
        ]
        return jnp.concatenate(pieces)

    g_vec_enc = [grads[0] for grads in enc_vec_grads]
    shared_grad = jnp.concatenate(
        [g_vec_enc[0][6], g_vec_enc[0][:6].reshape(-1), g_vec_enc[1].reshape(-1)]
        + [g_vec1[4], g_vec1[2], g_vec1[3], g_vec[:6].reshape(-1)]
    )
    loss_part = jnp.sum(loss_lanes) / PIX
    split_len = split_own.shape[0]
    length = split_len + shared_grad.shape[0] + 1
    vec_lanes = pl.cdiv(length, RANK * 128) * 128
    fill = jnp.zeros((RANK * vec_lanes - length,), f32)
    sent = jnp.concatenate([split_half(1), shared_grad, loss_part[None], fill])
    local = jnp.concatenate([split_half(0), shared_grad, loss_part[None], fill])
    vec_local = (local + swap(sent)).reshape(RANK, vec_lanes)

    enc_rows = enc_basis.shape[1] // workers
    dec_rows = dec_basis.shape[1] // workers
    enc_owned = lax.dynamic_slice_in_dim(enc_basis, worker_index * enc_rows, enc_rows, 1)
    dec_owned = lax.dynamic_slice_in_dim(dec_basis, worker_index * dec_rows, dec_rows, 1)
    dec_right_part, dec_comb = dec_right_factor(dec_basis, dec_grads, dec_came, dec_error[0, 0])
    enc_right, dec_right, vec_mean = mean_over_workers(
        workers,
        (
            right_factor(enc_basis, enc_error[0, 0], mine_packs, their_packs),
            dec_right_part,
            vec_local,
        ),
    )
    vec_mean = vec_mean.reshape(-1)
    enc_error_new = residue(enc_basis, enc_right, enc_error[0, 0], mine_packs, their_packs)
    dec_error_new = dec_residue(dec_basis, dec_right, dec_comb)
    enc_mom = momentum_keep * enc_moment[0] + jnp.einsum(
        "rx,rc->xc", enc_owned, enc_right, precision=highest_precision
    )
    dec_mom = momentum_keep * dec_moment[0] + jnp.einsum(
        "rx,rc->xc", dec_owned, dec_right, precision=highest_precision
    )
    split_mom = momentum_keep * split_moment[0] + vec_mean[:split_len]
    shared_mom = momentum_keep * shared_moment + vec_mean[split_len : length - 1]
    return (
        vec_mean[length - 1] * workers,
        loss_weight,
        (enc_weights[0] - step_rate * enc_mom)[None],
        enc_mom[None],
        enc_error_new[None, None],
        (dec_weights[0] - step_rate * dec_mom)[None],
        dec_mom[None],
        dec_error_new[None, None],
        jnp.concatenate([enc_right, dec_right], 1)[None],
        (vec_split[0] - step_rate * split_mom)[None],
        split_mom[None],
        vec_shared - step_rate * shared_mom,
        shared_mom,
    )


def solution(mesh):
    placed = (
        P("dp", None, "tensor"),
        P("dp", None),
        P("dp"),
        P("tensor", "dp", None),
        P("tensor", "dp", None),
        P("tensor", None),
        P(),
        P("tensor", "dp", None),
        P("tensor", "dp", None),
        P("tensor", None),
        P(),
        P("dp", "tensor", None, None),
        P("dp", "tensor", None, None),
        P("tensor", None, None),
    )
    return jax.shard_map(
        per_device,
        mesh=mesh,
        in_specs=placed,
        out_specs=(
            P(),
            P(),
            P("tensor", "dp", None),
            P("tensor", "dp", None),
            P("dp", "tensor", None, None),
            P("tensor", "dp", None),
            P("tensor", "dp", None),
            P("dp", "tensor", None, None),
            P("tensor", None, None),
            P("tensor", None),
            P("tensor", None),
            P(),
            P(),
        ),
        check_vma=False,
    )
```

```python
import math

import jax
import jax.numpy as jnp
from jax import lax
from jax.experimental import pallas as pl
from jax.experimental.pallas import tpu as pltpu
from jax.sharding import PartitionSpec as P

D = 768
HEAD_DIM = 64
FF = 3072
DD = 384
DFF = 1536
PIX = 1536
TUBES = 1568
VIS = 160
MASKED = 1408
RANK = 8

f32 = jnp.float32
bf16 = jnp.bfloat16
highest_precision = lax.Precision.HIGHEST
norm_eps = 1e-06
momentum_keep = 0.9
step_rate = 1000.0
LOG2E = 1.4426950408889634
SCORE = HEAD_DIM ** (-0.5)
BIG_VMEM = 56 << 20


def nn(left, right):
    return lax.dot_general(left, right, (((1,), (0,)), ((), ())), preferred_element_type=f32)


def nt(left, right):
    return lax.dot_general(left, right, (((1,), (1,)), ((), ())), preferred_element_type=f32)


def tn(left, right):
    return lax.dot_general(left, right, (((0,), (0,)), ((), ())), preferred_element_type=f32)


def col_sum(value):
    return jnp.sum(value, 0, keepdims=True)


def norm_parts(stream):
    center = stream - jnp.mean(stream, -1, keepdims=True)
    rate = lax.rsqrt(jnp.mean(center * center, -1, keepdims=True) + norm_eps)
    return center * rate, rate


def norm_back(grad, gain, unit, rate):
    grad_unit = grad * gain
    return rate * (
        grad_unit
        - jnp.mean(grad_unit, -1, keepdims=True)
        - unit * jnp.mean(grad_unit * unit, -1, keepdims=True)
    )


def gelu_pair(before):
    cdf_tail = jnp.exp(-0.5 * before * before)
    size = jnp.abs(before) * (2.0 ** -0.5)
    t = 1.0 / (1.0 + 0.3275911 * size)
    poly = t * (
        0.254829592 + t * (-0.284496736 + t * (1.421413741 + t * (-1.453152027 + t * 1.061405429)))
    )
    tail = 0.5 * poly * cdf_tail
    cdf = jnp.where(before < 0, tail, 1.0 - tail)
    return before * cdf, cdf + before * cdf_tail * (1.0 / math.sqrt(2.0 * math.pi))


def split3(value):
    high = value.astype(bf16)
    rest = value - high.astype(f32)
    middle = rest.astype(bf16)
    low = (rest - middle.astype(f32)).astype(bf16)
    return jnp.concatenate([high, middle, low], 0)


def fold3(value):
    rows = value.shape[0] // 3
    return value[:rows] + value[rows : 2 * rows] + value[2 * rows :]


def rates(width):
    column = lax.broadcasted_iota(jnp.int32, (1, width), 1)
    low_bit = lax.rem(column, 2)
    rate = jnp.exp((column - low_bit).astype(f32) * (-math.log(10000.0) / width))
    return rate, low_bit == 0


def sinusoid_of(place, width):
    rate, even = rates(width)
    angle = place * rate
    return jnp.where(even, jnp.sin(angle), jnp.cos(angle))


def params(**more):
    return pltpu.CompilerParams(vmem_limit_bytes=BIG_VMEM, **more)


def whole(shape):
    return pl.BlockSpec(shape, lambda *_: (0,) * len(shape))


def any_spec():
    return pl.BlockSpec(memory_space=pl.ANY)


def vmem_spec():
    return pl.BlockSpec(memory_space=pltpu.VMEM)


def pick_kernel(half_ref, order_ref, tubes_ref, out_ref):
    column = lax.broadcasted_iota(jnp.int32, (1, TUBES), 1)
    hot = jnp.where(order_ref[0] == column, 1.0, 0.0).astype(bf16)
    out_ref[0] = nn(hot, tubes_ref[0]).astype(bf16)


def pick_visible(half, order, tubes):
    clips, _, width = tubes.shape
    which = lambda c, half_ref: jnp.where(c == 0, half_ref[0], 1 - half_ref[0])
    return pl.pallas_call(
        pick_kernel,
        grid_spec=pltpu.PrefetchScalarGridSpec(
            num_scalar_prefetch=1,
            grid=(clips,),
            in_specs=[
                pl.BlockSpec((1, VIS, 1), lambda c, half_ref: (which(c, half_ref), 0, 0)),
                pl.BlockSpec((1, TUBES, width), lambda c, half_ref: (which(c, half_ref), 0, 0)),
            ],
            out_specs=pl.BlockSpec((1, VIS, width), lambda c, half_ref: (c, 0, 0)),
        ),
        out_shape=jax.ShapeDtypeStruct((clips, VIS, width), bf16),
        compiler_params=params(),
        name="pick_visible",
    )(half, order[:, :VIS, None], tubes)


QKV_ROWS = 392


def place_matrix(order, rows):
    place = lax.broadcasted_iota(jnp.int32, (rows, 1), 0) + pl.program_id(0) * rows
    return jnp.where(order == place, 1.0, 0.0)


def qkv_kernel(order_ref, pos_ref, latent_ref, vec_ref, w_ref, bias_ref, x_ref, h_ref, qkv_ref, hidden_ref):
    token, gain, shift = (vec_ref[index : index + 1] for index in range(3))
    places = place_matrix(order_ref[...], QKV_ROWS)
    hidden = 1.0 - jnp.sum(places, 1, keepdims=True)
    hidden_ref[...] = hidden
    latent = split3(latent_ref[...])
    places = places.astype(bf16)
    shown = sum(nn(places, latent[VIS * part : VIS * (part + 1)]) for part in (2, 1, 0))
    x = pos_ref[...] + (shown + hidden * token)
    x_ref[...] = x
    unit, _ = norm_parts(x)
    h = (unit * gain + shift).astype(bf16)
    h_ref[...] = h
    qkv_ref[...] = (nt(h, w_ref[...]) + bias_ref[...]).astype(bf16)


def decoder_qkv(order, pos, latent, vecs, weights, bias):
    rows = lambda width: pl.BlockSpec((QKV_ROWS, width), lambda i: (i, 0))
    return pl.pallas_call(
        qkv_kernel,
        grid=(TUBES // QKV_ROWS,),
        in_specs=[
            whole((1, VIS)),
            rows(DD),
            whole((VIS, DD)),
            whole(vecs.shape),
            whole((3 * DD, DD)),
            whole((1, 3 * DD)),
        ],
        out_specs=[rows(DD), rows(DD), rows(3 * DD), rows(1)],
        out_shape=[
            jax.ShapeDtypeStruct((TUBES, DD), f32),
            jax.ShapeDtypeStruct((TUBES, DD), bf16),
            jax.ShapeDtypeStruct((TUBES, 3 * DD), bf16),
            jax.ShapeDtypeStruct((TUBES, 1), f32),
        ],
        compiler_params=params(),
        name="decoder_qkv",
    )(order, pos, latent, vecs, weights, bias)


PAIRS = DD // 128


def half_lane(index):
    return lax.broadcasted_iota(jnp.int32, (1, 128), 1) // HEAD_DIM == index


def attend_kernel(q_ref, k_ref, v_ref, o_ref, lse_ref):
    q = q_ref[...]
    k = k_ref[...]
    v_one = jnp.concatenate([v_ref[...], jnp.ones((TUBES, 128), bf16)], 1)
    mixed, logs = [], []
    for head in range(2):
        scores = nt(jnp.where(half_lane(head), q, jnp.zeros_like(q)), k)
        top = jnp.max(scores, 1, keepdims=True)
        expo = jnp.exp2((scores - top) * (SCORE * LOG2E)).astype(bf16)
        both = nn(expo, v_one)
        total = both[:, 128:]
        mixed.append(both[:, :128] / total)
        logs.append(top * (SCORE * LOG2E) + jnp.log2(total))
    o_ref[...] = jnp.where(half_lane(0), mixed[0], mixed[1])
    lse_ref[0] = jnp.where(half_lane(0), logs[0], logs[1])


def attend(qkv):
    return pl.pallas_call(
        attend_kernel,
        grid=(PAIRS, TUBES // TUBES),
        in_specs=[
            pl.BlockSpec((TUBES, 128), lambda p, i: (i, p)),
            pl.BlockSpec((TUBES, 128), lambda p, i: (0, PAIRS + p)),
            pl.BlockSpec((TUBES, 128), lambda p, i: (0, 2 * PAIRS + p)),
        ],
        out_specs=[
            pl.BlockSpec((TUBES, 128), lambda p, i: (i, p)),
            pl.BlockSpec((1, TUBES, 128), lambda p, i: (p, i, 0)),
        ],
        out_shape=[
            jax.ShapeDtypeStruct((TUBES, DD), f32),
            jax.ShapeDtypeStruct((PAIRS, TUBES, 128), f32),
        ],
        compiler_params=params(),
        name="attend",
    )(qkv, qkv, qkv)


def attend_back_kernel(q_ref, k_ref, v_ref, o_ref, do_ref, lse_ref, dq_ref, dk_ref, dv_ref):
    q, k, v, grad = q_ref[...], k_ref[...], v_ref[...], do_ref[...]
    k_turned = k.T
    dots = o_ref[...] * grad.astype(f32)
    logs = lse_ref[0].T
    select = (
        lax.broadcasted_iota(jnp.int32, (8, 128), 1) // HEAD_DIM
        == lax.broadcasted_iota(jnp.int32, (8, 128), 0)
    ).astype(f32)
    row_total = lax.dot_general(
        select, dots, (((1,), (1,)), ((), ())), precision=highest_precision,
        preferred_element_type=f32,
    )
    zero = jnp.zeros((), bf16)
    dk = dv = jnp.zeros((TUBES, 128), f32)
    turned = []
    for head in range(2):
        mask = half_lane(head)
        q_head = jnp.where(mask, q, zero)
        grad_head = jnp.where(mask, grad, zero)
        low = head * HEAD_DIM
        probs = jnp.exp2(nt(k, q_head) * (SCORE * LOG2E) - logs[low : low + 1])
        grad_scores = (probs * (nt(v, grad_head) - row_total[head : head + 1])).astype(bf16)
        dv = dv + nn(probs.astype(bf16), grad_head)
        dk = dk + nn(grad_scores, q_head)
        turned.append(nn(k_turned[low : low + HEAD_DIM], grad_scores))
    dq_ref[...] = (jnp.concatenate(turned, 0).T * SCORE).astype(bf16)
    dk_ref[...] = (dk * SCORE).astype(bf16)
    dv_ref[...] = dv.astype(bf16)


def attend_back(qkv, mixed, grad_mixed, logs):
    pair = lambda kind: pl.BlockSpec((TUBES, 128), lambda p: (0, kind * PAIRS + p))
    return pl.pallas_call(
        attend_back_kernel,
        grid=(PAIRS,),
        in_specs=[
            pair(0),
            pair(1),
            pair(2),
            pair(0),
            pair(0),
            pl.BlockSpec((1, TUBES, 128), lambda p: (p, 0, 0)),
        ],
        out_specs=[pair(0)] * 3,
        out_shape=[jax.ShapeDtypeStruct((TUBES, DD), bf16)] * 3,
        compiler_params=params(),
        name="attend_back",
    )(qkv, qkv, qkv, mixed, grad_mixed, logs)


TOKEN_ROWS = 784
CHUNK = 384
DEC_O = D // 2
DEC_D = DEC_O + DD // 2
DEC_Q = DEC_D + DFF // 2
DEC_U = DEC_Q + 3 * DD // 2
DEC_H = DEC_U + DFF // 2
DEC_ROWS = DEC_H + PIX // 2
CHUNKS = DFF // CHUNK


def token_kernel(
    _, a_ref, x_ref, pix_ref, pix_other_ref, hidden_ref, scal_ref, vec_ref, bu_ref, bh_ref,
    wo_ref, wd_ref, wu_ref, wh_ref,
    da_ref, dx1_ref,
    own_ref, other_ref, gvec_ref, gbu_ref, gbh_ref, loss_ref,
    slope,
):
    step = pl.program_id(0)
    sums = (own_ref, other_ref, gvec_ref, gbu_ref, gbh_ref, loss_ref)
    grads = (own_ref, other_ref)

    @pl.when(step == 0)
    def _():
        for ref in sums:
            ref[...] = jnp.zeros_like(ref)

    bo, g2, b2, bd, gf, sf = (vec_ref[index : index + 1] for index in range(3, 9))
    a = a_ref[...].astype(bf16)
    x1 = x_ref[...] + (nn(a, wo_ref[...]) + bo)
    unit2, rate2 = norm_parts(x1)
    h2 = (unit2 * g2 + b2).astype(bf16)
    out = x1 + bd
    active = []
    for chunk in range(CHUNKS):
        part = pl.ds(chunk * CHUNK, CHUNK)
        value, slope_part = gelu_pair(nt(h2, wu_ref[part]) + bu_ref[:, part])
        slope[:, part] = slope_part
        active.append(value.astype(bf16))
        out = out + nn(active[-1], wd_ref[part])
    unit_f, rate_f = norm_parts(out)
    final = (unit_f * gf + sf).astype(bf16)
    pixels = [
        ref[:, pl.ds(side * CHUNK, CHUNK)].astype(f32)
        for ref in (pix_ref.at[0], pix_other_ref)
        for side in range(2)
    ]
    center = sum(jnp.sum(part, 1, keepdims=True) for part in pixels) * (1.0 / PIX)
    square = sum(jnp.sum(part * part, 1, keepdims=True) for part in pixels) * (1.0 / PIX)
    spread = lax.rsqrt(square - center * center + norm_eps)
    counted = hidden_ref[...] * scal_ref[0:1, 0:1]
    rate = hidden_ref[...] * scal_ref[1:2, 0:1]
    grad_final = jnp.zeros((TOKEN_ROWS, DD), f32)
    for chunk in range(CHUNKS):
        part = pl.ds(chunk * CHUNK, CHUNK)
        target = (pixels[chunk] - center) * spread
        miss = nt(final, wh_ref[part]) + bh_ref[:, part] - target
        loss_ref[:, part] += col_sum(counted * miss * miss)
        grad_guess = (rate * miss).astype(bf16)
        gbh_ref[:, part] += col_sum(grad_guess.astype(f32))
        grads[chunk // 2][pl.ds(DEC_H + (chunk % 2) * CHUNK, CHUNK)] += tn(grad_guess, final)
        grad_final = grad_final + nn(grad_guess, wh_ref[part])
    grad_out = norm_back(grad_final, gf, unit_f, rate_f)
    out_low = grad_out.astype(bf16)
    grad_h2 = jnp.zeros((TOKEN_ROWS, DD), f32)
    for chunk in range(CHUNKS):
        part = pl.ds(chunk * CHUNK, CHUNK)
        grads[chunk // 2][pl.ds(DEC_D + (chunk % 2) * CHUNK, CHUNK)] += tn(active[chunk], out_low)
        grad_before = (slope[:, part] * nt(out_low, wd_ref[part])).astype(bf16)
        gbu_ref[:, part] += col_sum(grad_before.astype(f32))
        grads[chunk // 2][pl.ds(DEC_U + (chunk % 2) * CHUNK, CHUNK)] += tn(grad_before, h2)
        grad_h2 = grad_h2 + nn(grad_before, wu_ref[part])
    grad_x1 = grad_out + norm_back(grad_h2, g2, unit2, rate2)
    x1_low = grad_x1.astype(bf16)
    g_out = tn(a, x1_low)
    for group in range(2):
        grads[group][pl.ds(DEC_O, DD // 2)] += g_out[group * DD // 2 : (group + 1) * DD // 2]
    da_ref[...] = nt(x1_low, wo_ref[...]).astype(bf16)
    dx1_ref[...] = grad_x1
    gvec_ref[0:1] += col_sum(x1_low.astype(f32))
    gvec_ref[1:2] += col_sum(grad_h2 * unit2)
    gvec_ref[2:3] += col_sum(grad_h2)
    gvec_ref[3:4] += col_sum(out_low.astype(f32))
    gvec_ref[4:5] += col_sum(grad_final * unit_f)
    gvec_ref[5:6] += col_sum(grad_final)


def decoder_tokens(half, mixed, x, tubes, pixels, hidden, scal, vecs, bu, bh, wo, wd, wu, wh):
    rows = lambda width: pl.BlockSpec((TOKEN_ROWS, width), lambda i, _: (i, 0))
    sums = [(DEC_ROWS, DD), (DEC_ROWS, DD), (8, DD), (1, DFF), (1, PIX), (1, PIX)]
    return pl.pallas_call(
        token_kernel,
        grid_spec=pltpu.PrefetchScalarGridSpec(
            num_scalar_prefetch=1,
            grid=(TUBES // TOKEN_ROWS,),
            in_specs=[
                rows(DD),
                rows(DD),
                pl.BlockSpec((1, TOKEN_ROWS, PIX // 2), lambda i, half_ref: (half_ref[0], i, 0)),
                rows(PIX // 2),
                rows(1),
                whole((8, 128)),
                whole(vecs.shape),
                whole((1, DFF)),
                whole((1, PIX)),
                whole((DD, DD)),
                whole((DFF, DD)),
                whole((DFF, DD)),
                whole((PIX, DD)),
            ],
            out_specs=[rows(DD), rows(DD)] + [whole(shape) for shape in sums],
            scratch_shapes=[pltpu.VMEM((TOKEN_ROWS, DFF), f32)],
        ),
        out_shape=[
            jax.ShapeDtypeStruct((TUBES, DD), bf16),
            jax.ShapeDtypeStruct((TUBES, DD), f32),
        ]
        + [jax.ShapeDtypeStruct(shape, f32) for shape in sums],
        compiler_params=params(),
        name="decoder_tokens",
    )(half, mixed, x, tubes, pixels, hidden, scal, vecs, bu, bh, wo, wd, wu, wh)


def qkv_back_kernel(
    half_ref, order_ref, dq_ref, dk_ref, dv_ref, h_ref, x_ref, dx1_ref, vec_ref, w_ref, normed_ref,
    _own, _other,
    latent_ref, own_ref, other_ref, gvec_ref,
    g_qkv, g_proj, latent_sum, sems,
):
    step = pl.program_id(0)

    @pl.when(step == 0)
    def _():
        g_qkv[...] = jnp.zeros_like(g_qkv)
        gvec_ref[...] = jnp.zeros_like(gvec_ref)
        latent_sum[...] = jnp.zeros_like(latent_sum)

    h = h_ref[...]
    grads = (dq_ref[...], dk_ref[...], dv_ref[...])
    grad_h = jnp.zeros((QKV_ROWS, DD), f32)
    for index, grad in enumerate(grads):
        g_both = tn(grad, h)
        for group in range(2):
            rows = pl.ds(index * DD // 2, DD // 2)
            g_qkv[group, rows] += g_both[group * DD // 2 : (group + 1) * DD // 2]
        grad_h = grad_h + nn(grad, w_ref[pl.ds(index * DD, DD)])
    unit, rate = norm_parts(x_ref[...])
    grad_x = dx1_ref[...] + norm_back(grad_h, vec_ref[1:2], unit, rate)
    places = place_matrix(order_ref[...], QKV_ROWS)
    hidden = 1.0 - jnp.sum(places, 1, keepdims=True)
    latent_sum[...] += tn(places.astype(bf16), grad_x.astype(bf16))
    gvec_ref[0:1] += col_sum(grads[0].astype(f32))
    gvec_ref[1:2] += col_sum(grads[2].astype(f32))
    gvec_ref[2:3] += col_sum(grad_h * unit)
    gvec_ref[3:4] += col_sum(grad_h)
    gvec_ref[4:5] += col_sum(hidden * grad_x)

    @pl.when(step == pl.num_programs(0) - 1)
    def _():
        latent = latent_sum[...].astype(bf16)
        latent_ref[...] = latent
        both = tn(normed_ref[...], latent)
        g_proj[0] = both[: D // 2]
        g_proj[1] = both[D // 2 :]
        half = half_ref[0]
        kinds = pl.ds(DEC_Q, 3 * DD // 2)
        copies = [
            pltpu.make_async_copy(g_qkv.at[0], own_ref.at[kinds], sems.at[0]),
            pltpu.make_async_copy(g_qkv.at[1], other_ref.at[kinds], sems.at[1]),
            pltpu.make_async_copy(g_proj.at[half], own_ref.at[pl.ds(0, D // 2)], sems.at[2]),
            pltpu.make_async_copy(g_proj.at[1 - half], other_ref.at[pl.ds(0, D // 2)], sems.at[3]),
        ]
        for copy in copies:
            copy.start()
        for copy in copies:
            copy.wait()


def decoder_qkv_back(half, order, dq, dk, dv, h, x, dx1, vecs, weights, normed, own, other):
    rows = lambda width: pl.BlockSpec((QKV_ROWS, width), lambda i: (i, 0))
    return pl.pallas_call(
        qkv_back_kernel,
        grid=(TUBES // QKV_ROWS,),
        in_specs=[pl.BlockSpec(memory_space=pltpu.SMEM), whole((1, VIS))]
        + [rows(DD)] * 6
        + [whole(vecs.shape), whole((3 * DD, DD)), whole((VIS, D)), any_spec(), any_spec()],
        out_specs=[whole((VIS, DD)), any_spec(), any_spec(), whole((8, DD))],
        out_shape=[
            jax.ShapeDtypeStruct((VIS, DD), bf16),
            jax.ShapeDtypeStruct((DEC_ROWS, DD), f32),
            jax.ShapeDtypeStruct((DEC_ROWS, DD), f32),
            jax.ShapeDtypeStruct((8, DD), f32),
        ],
        scratch_shapes=[
            pltpu.VMEM((2, 3 * DD // 2, DD), f32),
            pltpu.VMEM((2, D // 2, DD), f32),
            pltpu.VMEM((VIS, DD), f32),
            pltpu.SemaphoreType.DMA((4,)),
        ],
        input_output_aliases={11: 1, 12: 2},
        compiler_params=params(),
        name="decoder_qkv_back",
    )(half, order, dq, dk, dv, h, x, dx1, vecs, weights, normed, own, other)


HALF = D // 2
HALF_FF = FF // 2
LAYER_ROWS = 4 * HALF + 2 * HALF_FF
AT_O, AT_D, AT_Q, AT_U = 0, HALF, HALF + HALF_FF, HALF + HALF_FF + 3 * HALF
STAGES = ((AT_Q, 3 * HALF), (AT_O, HALF), (AT_U, HALF_FF), (AT_D, HALF_FF))


def pieces_of(start, size, per):
    pieces = []
    at = start
    while at < start + size:
        many = min(start + size, (at // per + 1) * per) - at
        pieces.append((at // per, at % per, many, at - start))
        at += many
    return pieces


def stage_copies(sources, start, per, held, sems, stages):
    copies = []
    count = 0
    for at, size in stages:
        stage = []
        for shard, row, many, before in pieces_of(start + at, size, per):
            for group in range(2):
                stage.append(
                    pltpu.make_async_copy(
                        sources[group].at[shard, pl.ds(row, many)],
                        held.at[group, pl.ds(at + before, many)],
                        sems.at[count],
                    )
                )
                count += 1
        copies.append(stage)
    return copies


MOST_COPIES = 48


def encoder_kernel(layer, per, *refs):
    if layer == 0:
        pix_ref, pix_other_ref, pos_ref, *refs = refs
    else:
        x_ref, proj_ref, *refs = refs
    vec_ref, split_own_ref, split_other_ref, own_ref, other_ref, *refs = refs
    splits = (split_own_ref, split_other_ref)
    if layer == 0:
        x_out_ref, *refs = refs
    else:
        normed_ref, latent_ref, *refs = refs
    out_ref, h_ref, qkv_ref, a_ref, x1_ref, h2_ref, u_ref, slope_ref, held, sems = refs
    base = 1 + 6 * layer
    biases = layer * (2 * HALF + HALF_FF)
    if layer == 0:
        copies = stage_copies(
            (own_ref, other_ref), 0, per, held.at[:, pl.ds(LAYER_ROWS, D)], sems, ((0, D),)
        )
        used = sum(len(stage) for stage in copies)
        copies = copies + stage_copies(
            (own_ref, other_ref), D, per, held, sems.at[pl.ds(used, MOST_COPIES - used)], STAGES
        )
        copies = copies[1:] + copies[:1]
        order = (4, 0, 1, 2, 3)
    else:
        copies = stage_copies((own_ref, other_ref), D + LAYER_ROWS, per, held, sems, STAGES)
        order = (0, 1, 2, 3)
    for stage in order:
        for copy in copies[stage]:
            copy.start()

    def wait(stage):
        for copy in copies[stage]:
            copy.wait()

    g1, b1, bo, g2, b2, bd = (vec_ref[base + index : base + index + 1] for index in range(6))
    if layer == 0:
        wait(4)
        x = pos_ref[...] + vec_ref[0:1]
        for group, pixels in enumerate((pix_ref, pix_other_ref)):
            x = x + nn(pixels[...], held[group, pl.ds(LAYER_ROWS, D)])
        x_out_ref[...] = x
    else:
        x = x_ref[...]
    unit, _ = norm_parts(x)
    h = (unit * g1 + b1).astype(bf16)
    h_ref[...] = h
    wait(0)
    for kind in range(3):
        for group in range(2):
            part = pl.ds((2 * kind + group) * HALF, HALF)
            rows = pl.ds(AT_Q + kind * HALF, HALF)
            value = nt(h, held[group, rows])
            if kind != 1:
                at = biases + kind // 2 * HALF
                value = value + splits[group][:, at : at + HALF]
            qkv_ref[:, part] = value.astype(bf16)
    for pair in range(D // 128):
        q, k, v = (qkv_ref[:, pl.ds(kind * D + pair * 128, 128)] for kind in range(3))
        v_one = jnp.concatenate([v, jnp.ones((VIS, 128), bf16)], 1)
        mixed = []
        for head in range(2):
            scores = nt(jnp.where(half_lane(head), q, jnp.zeros_like(q)), k)
            top = jnp.max(scores, 1, keepdims=True)
            expo = jnp.exp2((scores - top) * (SCORE * LOG2E)).astype(bf16)
            both = nn(expo, v_one)
            mixed.append(both[:, :128] / both[:, 128:])
        a_ref[:, pl.ds(pair * 128, 128)] = jnp.where(half_lane(0), mixed[0], mixed[1]).astype(bf16)
    wait(1)
    x1 = x + bo
    for group in range(2):
        x1 = x1 + nn(a_ref[:, pl.ds(group * HALF, HALF)], held[group, pl.ds(AT_O, HALF)])
    x1_ref[...] = x1
    unit2, _ = norm_parts(x1)
    h2 = (unit2 * g2 + b2).astype(bf16)
    h2_ref[...] = h2
    wait(2)
    wait(3)
    out = x1 + bd
    for group in range(2):
        for chunk in range(HALF_FF // CHUNK):
            part = pl.ds(group * HALF_FF + chunk * CHUNK, CHUNK)
            before = nt(h2, held[group, pl.ds(AT_U + chunk * CHUNK, CHUNK)])
            at = biases + 2 * HALF + chunk * CHUNK
            value, slope = gelu_pair(before + splits[group][:, at : at + CHUNK])
            slope_ref[:, part] = slope
            active = value.astype(bf16)
            u_ref[:, part] = active
            out = out + nn(active, held[group, pl.ds(AT_D + chunk * CHUNK, CHUNK)])
    out_ref[...] = out
    if layer == 1:
        unit3, _ = norm_parts(out)
        normed = (unit3 * vec_ref[13:14] + vec_ref[14:15]).astype(bf16)
        normed_ref[...] = normed
        latent_ref[...] = nn(normed, proj_ref[...])


def encoder_layer(layer, per, first, vecs, splits, own, other):
    shapes = [
        ((VIS, D), f32),
        ((VIS, D), bf16),
        ((VIS, 3 * D), bf16),
        ((VIS, D), bf16),
        ((VIS, D), f32),
        ((VIS, D), bf16),
        ((VIS, FF), bf16),
        ((VIS, FF), f32),
    ]
    before = [((VIS, D), f32)] if layer == 0 else [((VIS, D), bf16), ((VIS, DD), f32)]
    shapes = before + shapes
    return pl.pallas_call(
        lambda *refs: encoder_kernel(layer, per, *refs),
        in_specs=[vmem_spec()] * (len(first) + 3) + [any_spec()] * 2,
        out_specs=[vmem_spec()] * len(shapes),
        out_shape=[jax.ShapeDtypeStruct(shape, kind) for shape, kind in shapes],
        scratch_shapes=[
            pltpu.VMEM((2, LAYER_ROWS + (D if layer == 0 else 0), D), bf16),
            pltpu.SemaphoreType.DMA((MOST_COPIES,)),
        ],
        compiler_params=params(),
        name=f"encoder_{layer}",
    )(*first, vecs, *splits, own, other)


RIGHT_AT = LAYER_ROWS


def encoder_back_kernel(layer, per, *refs):
    last = layer == 1
    start = D + layer * LAYER_ROWS
    base = 1 + 6 * layer
    (
        grad_ref, x_ref, vec_ref, h_ref, qkv_ref, a_ref, x1_ref, h2_ref, u_ref, slope_ref,
        start_ref, start_other_ref, own_ref, other_ref, pix_ref, pix_other_ref,
    ) = refs[:16]
    pixels = (pix_ref, pix_other_ref)
    refs = refs[16:]
    if last:
        out_ref, proj_ref, *refs = refs
    dx_ref, mine_ref, other_pack_ref, left_ref, gvec_ref, gbu_ref, gbq_ref = refs[:7]
    held, sems, da, dqkv = refs[7:]
    packs = (mine_ref, other_pack_ref)
    copies = stage_copies((own_ref, other_ref), start, per, held, sems, STAGES)
    for stage in (3, 2, 1, 0):
        for copy in copies[stage]:
            copy.start()

    def wait(stage):
        for copy in copies[stage]:
            copy.wait()

    g1, b1, bo, g2, b2, bd = (vec_ref[base + index : base + index + 1] for index in range(6))
    gvec_ref[6:8] = jnp.zeros((2, D), f32)
    if last:
        unit3, rate3 = norm_parts(out_ref[...])
        grad_normed = nt(grad_ref[...], proj_ref[...])
        grad_out = norm_back(grad_normed, vec_ref[13:14], unit3, rate3)
        gvec_ref[6:7] = col_sum(grad_normed * unit3)
        gvec_ref[7:8] = col_sum(grad_normed)
    else:
        grad_out = grad_ref[...]
    out_low = grad_out.astype(bf16)
    unit2, rate2 = norm_parts(x1_ref[...])
    grad_h2 = jnp.zeros((VIS, D), f32)
    wait(3)
    wait(2)
    for group in range(2):
        for chunk in range(HALF_FF // CHUNK):
            part = pl.ds(group * HALF_FF + chunk * CHUNK, CHUNK)
            grad_active = nt(out_low, held[group, pl.ds(AT_D + chunk * CHUNK, CHUNK)])
            grad_before = (slope_ref[:, part] * grad_active).astype(bf16)
            packs[group][:, pl.ds(AT_U + chunk * CHUNK, CHUNK)] = grad_before
            packs[group][:, pl.ds(AT_D + chunk * CHUNK, CHUNK)] = u_ref[:, part]
            gbu_ref[:, part] = col_sum(grad_before.astype(f32))
            grad_h2 = grad_h2 + nn(grad_before, held[group, pl.ds(AT_U + chunk * CHUNK, CHUNK)])
    grad_x1 = grad_out + norm_back(grad_h2, g2, unit2, rate2)
    x1_low = grad_x1.astype(bf16)
    wait(1)
    for group in range(2):
        part = pl.ds(group * HALF, HALF)
        da[:, part] = nt(x1_low, held[group, pl.ds(AT_O, HALF)]).astype(bf16)
        packs[group][:, pl.ds(AT_O, HALF)] = a_ref[:, part]
    zero = jnp.zeros((), bf16)
    for pair in range(D // 128):
        lanes = pl.ds(pair * 128, 128)
        q, k, v = (qkv_ref[:, pl.ds(kind * D + pair * 128, 128)] for kind in range(3))
        grad = da[:, lanes]
        dq = dk = dv = jnp.zeros((VIS, 128), f32)
        for head in range(2):
            mask = half_lane(head)
            q_head = jnp.where(mask, q, zero)
            grad_head = jnp.where(mask, grad, zero)
            scores = nt(q_head, k) * SCORE
            expo = jnp.exp(scores - jnp.max(scores, 1, keepdims=True))
            probs = expo / jnp.sum(expo, 1, keepdims=True)
            grad_probs = nt(grad_head, v)
            row_total = jnp.sum(probs * grad_probs, 1, keepdims=True)
            grad_scores = (probs * (grad_probs - row_total)).astype(bf16)
            dv = dv + tn(probs.astype(bf16), grad_head)
            dk = dk + tn(grad_scores, q_head)
            dq = dq + nn(grad_scores, jnp.where(mask, k, zero))
        dqkv[:, lanes] = (dq * SCORE).astype(bf16)
        dqkv[:, pl.ds(D + pair * 128, 128)] = (dk * SCORE).astype(bf16)
        dqkv[:, pl.ds(2 * D + pair * 128, 128)] = dv.astype(bf16)
    wait(0)
    grad_h = jnp.zeros((VIS, D), f32)
    for kind in range(3):
        for group in range(2):
            grad = dqkv[:, pl.ds((2 * kind + group) * HALF, HALF)]
            rows = pl.ds(AT_Q + kind * HALF, HALF)
            packs[group][:, rows] = grad
            grad_h = grad_h + nn(grad, held[group, rows])
    unit, rate = norm_parts(x_ref[...])
    grad_x = grad_x1 + norm_back(grad_h, g1, unit, rate)
    dx_ref[...] = grad_x
    gbq_ref[0:1] = col_sum(dqkv[:, pl.ds(0, D)].astype(f32))
    gbq_ref[1:2] = col_sum(dqkv[:, pl.ds(2 * D, D)].astype(f32))
    gvec_ref[0:1] = col_sum(grad_h * unit)
    gvec_ref[1:2] = col_sum(grad_h)
    gvec_ref[2:3] = col_sum(x1_low.astype(f32))
    gvec_ref[3:4] = col_sum(grad_h2 * unit2)
    gvec_ref[4:5] = col_sum(grad_h2)
    gvec_ref[5:6] = col_sum(out_low.astype(f32))
    rights = [x1_low, out_low, h_ref[...], h2_ref[...]]
    spans = [(AT_O, HALF, 0), (AT_D, HALF_FF, 0), (AT_Q, 3 * HALF, 0), (AT_U, HALF_FF, 0)]
    if not last:
        embed_low = grad_x.astype(bf16)
        rights.append(embed_low)
        gvec_ref[6:7] = col_sum(embed_low.astype(f32))
    starts = jnp.concatenate([split3(ref[:, :D]) for ref in (start_ref, start_other_ref)], 0)
    before = 0 if last else D
    for index, right in enumerate(rights):
        for pack in packs:
            pack[:, pl.ds(RIGHT_AT + index * D, D)] = right
        inner = nt(starts, right)
        for group in range(2):
            parts = split3(fold3(inner[3 * RANK * group : 3 * RANK * (group + 1)]))
            if index == 4:
                value = fold3(nn(parts, pixels[group][...]))
                left_ref[group, :, pl.ds(0, D)] = value
            else:
                at, size, _ = spans[index]
                value = fold3(nn(parts, packs[group][:, pl.ds(at, size)]))
                left_ref[group, :, pl.ds(before + at, size)] = value


def encoder_layer_back(layer, per, grad, source, vecs, kept, starts, own, other, pixels, last=()):
    width = RIGHT_AT + (5 - layer) * D
    shapes = [
        ((VIS, D), f32),
        ((VIS, width), bf16),
        ((VIS, width), bf16),
        ((2, RANK, LAYER_ROWS + (1 - layer) * D), f32),
        ((8, D), f32),
        ((1, FF), f32),
        ((2, D), f32),
    ]
    _, h, qkv, a, x1, h2, u, slope = kept
    return pl.pallas_call(
        lambda *refs: encoder_back_kernel(layer, per, *refs),
        in_specs=[vmem_spec()] * 12 + [any_spec()] * 2 + [vmem_spec()] * (2 + len(last)),
        out_specs=[vmem_spec()] * len(shapes),
        out_shape=[jax.ShapeDtypeStruct(shape, kind) for shape, kind in shapes],
        scratch_shapes=[
            pltpu.VMEM((2, LAYER_ROWS, D), bf16),
            pltpu.SemaphoreType.DMA((MOST_COPIES,)),
            pltpu.VMEM((VIS, D), bf16),
            pltpu.VMEM((VIS, 3 * D), bf16),
        ],
        compiler_params=params(),
        name=f"encoder_back_{layer}",
    )(grad, source, vecs, h, qkv, a, x1, h2, u, slope, *starts, own, other, *pixels, *last)


ROWS = 768
HALF_ROWS = ROWS // 2
ENC_ROWS = D + 2 * LAYER_ROWS
ENC_BLOCKS = ENC_ROWS // ROWS
PER_LAYER = LAYER_ROWS // ROWS


def kinds_of(inner):
    first = jnp.where(inner < 1, 0, jnp.where(inner < 3, 1, jnp.where(inner < 4, 2, 3)))
    first = jnp.where(inner == 2, 1, first)
    second = jnp.where(inner < 2, 1, jnp.where(inner < 4, 2, 3))
    return jnp.where(inner == 3, 2, first), second


def pack_specs():
    pixel = pl.BlockSpec((VIS, D), lambda j: (0, 0))
    specs = []
    for layer in range(2):
        inner = lambda j, layer=layer: jnp.clip(j - 1 - layer * PER_LAYER, 0, PER_LAYER - 1)
        at = RIGHT_AT // D
        specs.append(pl.BlockSpec((VIS, ROWS), lambda j, inner=inner: (0, inner(j))))
        for side in range(2):
            specs.append(
                pl.BlockSpec(
                    (VIS, D), lambda j, inner=inner, side=side: (0, at + kinds_of(inner(j))[side])
                )
            )
    embed = pl.BlockSpec((VIS, D), lambda j: (0, RIGHT_AT // D + 4))
    return [pixel, embed] + specs


def by_segment(refs, run):
    step = pl.program_id(0)
    count = len(refs) // 2
    mine, theirs = refs[:count], refs[count:]

    @pl.when(step == 0)
    def _():
        run((mine[0], theirs[0]), (mine[1], theirs[1]), (mine[1], theirs[1]))

    for layer in range(2):
        low = 1 + layer * PER_LAYER

        @pl.when(jnp.logical_and(step >= low, step < low + PER_LAYER))
        def _(at=2 + 3 * layer):
            run(*((mine[at + index], theirs[at + index]) for index in range(3)))


def error_factor_kernel(start_ref, error_ref, out_ref):
    turned = nt(error_ref[...], split3(start_ref[...]))
    out_ref[...] = fold3(turned.T)


def error_factor(start, error):
    rows, width = error.shape
    return pl.pallas_call(
        error_factor_kernel,
        grid=(rows // HALF_ROWS,),
        in_specs=[whole((RANK, width)), pl.BlockSpec((HALF_ROWS, width), lambda j: (j, 0))],
        out_specs=pl.BlockSpec((RANK, HALF_ROWS), lambda j: (0, j)),
        out_shape=jax.ShapeDtypeStruct((RANK, rows), f32),
        compiler_params=params(),
        name="error_factor",
    )(start, error)


def right_factor_kernel(basis_ref, error_ref, *refs):
    out_ref = refs[-1]

    @pl.when(pl.program_id(0) == 0)
    def _():
        out_ref[...] = jnp.zeros_like(out_ref)

    basis = split3(basis_ref[...])
    out_ref[...] += fold3(nn(basis, error_ref[...]))

    def run(left, first, second):
        total = jnp.zeros((3 * RANK, D), f32)
        for clip in range(2):
            for side, right in ((0, first), (1, second)):
                lanes = pl.ds(side * HALF_ROWS, HALF_ROWS)
                inner = fold3(nt(basis[:, side * HALF_ROWS : (side + 1) * HALF_ROWS],
                                 left[clip][:, lanes]))
                total = total + nn(split3(inner), right[clip][...])
        out_ref[...] += fold3(total)

    by_segment(refs[:-1], run)


def right_factor(basis, error, mine, theirs):
    return pl.pallas_call(
        right_factor_kernel,
        grid=(ENC_BLOCKS,),
        in_specs=[
            pl.BlockSpec((RANK, ROWS), lambda j: (0, j)),
            pl.BlockSpec((ROWS, D), lambda j: (j, 0)),
        ]
        + pack_specs() * 2,
        out_specs=whole((RANK, D)),
        out_shape=jax.ShapeDtypeStruct((RANK, D), f32),
        compiler_params=params(),
        name="right_factor",
    )(basis, error, *pack_args(mine), *pack_args(theirs))


def pack_args(packs):
    pixels, first, second = packs
    return (pixels, first, first, first, first, second, second, second)


def low_pairs(basis, factor):
    basis3 = split3(basis)
    factor3 = split3(factor)
    high, middle = basis3[:RANK], basis3[RANK : 2 * RANK]
    return (
        jnp.concatenate([high, high, middle, jnp.zeros_like(high)], 0),
        jnp.concatenate([factor3[: 2 * RANK], factor3[:RANK], jnp.zeros_like(factor3[:RANK])], 0),
    )


def residue_kernel(basis_ref, factor_ref, error_ref, *refs):
    out_ref = refs[-1]
    basis, factor = low_pairs(basis_ref[...], -factor_ref[...])

    def run(left, first, second):
        for side, right in ((0, first), (1, second)):
            rows = pl.ds(side * HALF_ROWS, HALF_ROWS)
            low = basis[:, side * HALF_ROWS : (side + 1) * HALF_ROWS]
            lefts = jnp.concatenate([left[0][:, rows], left[1][:, rows], low], 0)
            rights = jnp.concatenate([right[0][...], right[1][...], factor], 0)
            out_ref[rows] = (tn(lefts, rights) + error_ref[rows].astype(f32)).astype(bf16)

    by_segment(refs[:-1], run)


def residue(basis, factor, error, mine, theirs):
    return pl.pallas_call(
        residue_kernel,
        grid=(ENC_BLOCKS,),
        in_specs=[
            pl.BlockSpec((RANK, ROWS), lambda j: (0, j)),
            whole((RANK, D)),
            pl.BlockSpec((ROWS, D), lambda j: (j, 0)),
        ]
        + pack_specs() * 2,
        out_specs=pl.BlockSpec((ROWS, D), lambda j: (j, 0)),
        out_shape=jax.ShapeDtypeStruct((ENC_ROWS, D), bf16),
        compiler_params=params(),
        name="residue",
    )(basis, factor, error, *pack_args(mine), *pack_args(theirs))


DEC_BLOCK = 1152


def dec_right_kernel(basis_ref, own_ref, came_ref, error_ref, out_ref, comb_ref):
    @pl.when(pl.program_id(0) == 0)
    def _():
        out_ref[...] = jnp.zeros_like(out_ref)

    basis = split3(basis_ref[...])
    comb = own_ref[...] + came_ref[...] + error_ref[...].astype(f32)
    comb_ref[...] = comb
    high = comb.astype(bf16)
    rest = (comb - high.astype(f32)).astype(bf16)
    out_ref[...] += fold3(nn(basis, high) + nn(basis, rest))


def dec_right_factor(basis, own, came, error):
    rows = pl.BlockSpec((DEC_BLOCK, DD), lambda j: (j, 0))
    return pl.pallas_call(
        dec_right_kernel,
        grid=(DEC_ROWS // DEC_BLOCK,),
        in_specs=[pl.BlockSpec((RANK, DEC_BLOCK), lambda j: (0, j)), rows, rows, rows],
        out_specs=[whole((RANK, DD)), rows],
        out_shape=[
            jax.ShapeDtypeStruct((RANK, DD), f32),
            jax.ShapeDtypeStruct((DEC_ROWS, DD), f32),
        ],
        compiler_params=params(),
        name="dec_right_factor",
    )(basis, own, came, error)


def dec_residue_kernel(basis_ref, factor_ref, comb_ref, out_ref):
    out_ref[...] = (
        comb_ref[...] + tn(*low_pairs(basis_ref[...], -factor_ref[...]))
    ).astype(bf16)


def dec_residue(basis, factor, comb):
    return pl.pallas_call(
        dec_residue_kernel,
        grid=(DEC_ROWS // DEC_BLOCK,),
        in_specs=[
            pl.BlockSpec((RANK, DEC_BLOCK), lambda j: (0, j)),
            whole((RANK, DD)),
            pl.BlockSpec((DEC_BLOCK, DD), lambda j: (j, 0)),
        ],
        out_specs=pl.BlockSpec((DEC_BLOCK, DD), lambda j: (j, 0)),
        out_shape=jax.ShapeDtypeStruct((DEC_ROWS, DD), bf16),
        compiler_params=params(),
        name="dec_residue",
    )(basis, factor, comb)


def dec_left_kernel(start_ref, start_other_ref, own_ref, other_ref, out_ref):
    for group, (begin_ref, ref) in enumerate(((start_ref, own_ref), (start_other_ref, other_ref))):
        start = split3(begin_ref[:, D:])
        grad = ref[...]
        high = grad.astype(bf16)
        rest = (grad - high.astype(f32)).astype(bf16)
        out_ref[group] = fold3((nt(high, start) + nt(rest, start)).T)


def dec_left_factor(starts, own, other):
    rows = pl.BlockSpec((DEC_BLOCK, DD), lambda j: (j, 0))
    return pl.pallas_call(
        dec_left_kernel,
        grid=(DEC_ROWS // DEC_BLOCK,),
        in_specs=[whole((RANK, D + DD))] * 2 + [rows, rows],
        out_specs=pl.BlockSpec((2, RANK, DEC_BLOCK), lambda j: (0, 0, j)),
        out_shape=jax.ShapeDtypeStruct((2, RANK, DEC_ROWS), f32),
        compiler_params=params(),
        name="dec_left_factor",
    )(*starts, own, other)


MESH_ID = pl.DeviceIdType.MESH


def greet(workers, me, partner):
    barrier = pltpu.get_barrier_semaphore()
    for distance in range(1, workers):
        pl.semaphore_signal(
            barrier, 1, device_id={"dp": lax.rem(me + distance, workers)}, device_id_type=MESH_ID
        )
    if partner is not None:
        pl.semaphore_signal(barrier, 1, device_id={"tensor": partner}, device_id_type=MESH_ID)
    pl.semaphore_wait(barrier, workers - 1 + (partner is not None))


def sum_workers(workers, me, lanes, local, slots, sums, sems):
    def share(index):
        return pl.ds(pl.multiple_of(index * lanes, 128), lanes)

    def to_all(turn, source, target):
        copies = []
        for distance in range(1, workers):
            peer = lax.rem(me + distance, workers)
            copy = pltpu.make_async_remote_copy(
                src_ref=source(peer),
                dst_ref=target(distance),
                send_sem=sems.at[2 * turn, distance],
                recv_sem=sems.at[2 * turn + 1, distance],
                device_id={"dp": peer},
                device_id_type=MESH_ID,
            )
            copy.start()
            copies.append(copy)
        return copies

    copies = to_all(0, lambda peer: local.at[:, share(peer)], lambda distance: slots.at[distance])
    total = local[:, share(me)]
    for distance, copy in enumerate(copies, 1):
        copy.wait_recv()
        total = total + slots[distance]
    sums[:, share(me)] = total
    more = to_all(1, lambda peer: sums.at[:, share(me)], lambda distance: sums.at[:, share(me)])
    for copy in copies:
        copy.wait_send()
    for copy in more:
        copy.wait()


def basis_kernel(
    workers, lanes, enc_width, first_ref, second_ref, dec_ref, error_ref, dec_error_ref,
    enc_out, dec_out,
    send, came, local, slots, sums, sems, pair_sems,
):
    me = lax.axis_index("dp")
    half = lax.axis_index("tensor")
    first = first_ref.shape[2]
    second = second_ref.shape[2]
    width = enc_width + dec_ref.shape[2]
    spans = ((first_ref, 0, first), (second_ref, first, second), (dec_ref, enc_width, width - enc_width))
    for ref, at, size in spans:
        send[:, at : at + size] = ref[1]
    if width < workers * lanes:
        tail = jnp.zeros((RANK, workers * lanes - width), f32)
        send[:, width:] = tail
    greet(workers, me, 1 - half)
    copy = pltpu.make_async_remote_copy(
        src_ref=send,
        dst_ref=came,
        send_sem=pair_sems.at[0],
        recv_sem=pair_sems.at[1],
        device_id={"tensor": 1 - half},
        device_id_type=MESH_ID,
    )
    copy.start()
    for ref, at, size in spans[:2]:
        local[:, at : at + size] = ref[0] + error_ref[:, at : at + size]
    local[:, enc_width:width] = dec_ref[0] + dec_error_ref[...]
    if width < workers * lanes:
        local[:, width:] = tail
    copy.wait()
    local[...] += came[...]
    sum_workers(workers, me, lanes, local, slots, sums, sems)
    place = lax.broadcasted_iota(jnp.int32, (RANK, 1), 0)
    for at, out in ((0, enc_out), (enc_width, dec_out)):
        left = sums[:, at : at + out.shape[1]]
        gram = lax.dot_general(
            left, left, (((1,), (1,)), ((), ())), precision=highest_precision,
            preferred_element_type=f32,
        )
        for index in range(RANK):
            scale = lax.rsqrt(gram[index : index + 1, index : index + 1])
            column = gram[:, index : index + 1] * scale
            below = jnp.where(place > index, column, 0.0)
            pivot = left[index : index + 1] * scale
            left = jnp.where(place == index, pivot, left - below * pivot)
            gram = gram - below * (gram[index : index + 1] * scale)
        out[...] = left


def lanes_for(width, workers):
    return pl.cdiv(width, 128 * workers) * 128


def summed_basis(workers, first, second, dec, error_part, dec_error_part):
    enc_width = first.shape[2] + second.shape[2]
    width = enc_width + dec.shape[2]
    lanes = lanes_for(width, workers)
    wide = pltpu.VMEM((RANK, workers * lanes), f32)
    return pl.pallas_call(
        lambda *refs: basis_kernel(workers, lanes, enc_width, *refs),
        in_specs=[vmem_spec()] * 5,
        out_specs=[vmem_spec()] * 2,
        out_shape=[
            jax.ShapeDtypeStruct((RANK, enc_width), f32),
            jax.ShapeDtypeStruct((RANK, width - enc_width), f32),
        ],
        scratch_shapes=[
            wide,
            wide,
            wide,
            pltpu.VMEM((workers, RANK, lanes), f32),
            wide,
            pltpu.SemaphoreType.DMA((4, workers)),
            pltpu.SemaphoreType.DMA((2,)),
        ],
        compiler_params=pltpu.CompilerParams(
            collective_id=1, has_side_effects=True, vmem_limit_bytes=BIG_VMEM
        ),
        name="summed_basis",
    )(first, second, dec, error_part, dec_error_part)


def sum_kernel(workers, lanes, *refs):
    count = (len(refs) - 4) // 2
    parts, outs = refs[:count], refs[count : 2 * count]
    local, slots, sums, sems = refs[2 * count :]
    me = lax.axis_index("dp")
    at = 0
    for part in parts:
        local[:, at : at + part.shape[1]] = part[...]
        at += part.shape[1]
    if at < workers * lanes:
        local[:, at:] = jnp.zeros((RANK, workers * lanes - at), f32)
    greet(workers, me, None)
    sum_workers(workers, me, lanes, local, slots, sums, sems)
    at = 0
    for out in outs:
        out[...] = sums[:, at : at + out.shape[1]] * (1.0 / workers)
        at += out.shape[1]


def mean_over_workers(workers, parts):
    lanes = lanes_for(sum(part.shape[1] for part in parts), workers)
    wide = pltpu.VMEM((RANK, workers * lanes), f32)
    return pl.pallas_call(
        lambda *refs: sum_kernel(workers, lanes, *refs),
        in_specs=[vmem_spec()] * len(parts),
        out_specs=[vmem_spec()] * len(parts),
        out_shape=[jax.ShapeDtypeStruct(part.shape, f32) for part in parts],
        scratch_shapes=[
            wide,
            pltpu.VMEM((workers, RANK, lanes), f32),
            wide,
            pltpu.SemaphoreType.DMA((4, workers)),
        ],
        compiler_params=pltpu.CompilerParams(
            collective_id=2, has_side_effects=True, vmem_limit_bytes=BIG_VMEM
        ),
        name="mean_over_workers",
    )(*parts)


PLANE = 4
PART_Z_X_Y, PART_Z_Y_X, PART_X_Y_Z, PART_DEC = range(4)
Z_X_Y_PARTS = (PART_DEC, PART_Z_X_Y)
WAY_X, WAY_Y, WAY_UP, WAY_DOWN = range(4)
ERROR_ROWS = 1248


def gather_kernel(
    parts, planes, shard_ref, dec_shard_ref, tubes_ref, error_ref, dec_error_ref, start_ref, order_ref,
    counted_ref,
    own_ref, other_ref, pixels_ref, part_ref, dec_part_ref, picked_ref, pix_other_ref,
    pos_enc_ref, pos_dec_ref, scal_ref, proj_ref, wqkv_ref, wo_ref, wd_ref, wu_ref, wh_ref,
    held, dec_held, dec_own, dec_other, joined, pix_held,
    send_sems, recv_sems, pair_sems, sems,
):
    me = lax.axis_index("dp")
    half = lax.axis_index("tensor")
    z = me // PLANE
    column = lax.rem(me, PLANE)
    column_x = column + 1 - 2 * lax.rem(column, 2)
    column_y = lax.rem(column + 2, PLANE)
    column_xy = lax.rem(column_x + 2, PLANE)
    up = z < planes - 1
    down = z > 0
    peers = (
        z * PLANE + column_x,
        z * PLANE + column_y,
        jnp.minimum(me + PLANE, PLANE * planes - 1),
        jnp.maximum(me - PLANE, 0),
    )
    rows = [pl.ds(at, size) for at, size in parts]

    def place(part, slot):
        return dec_own.at[slot] if part == PART_DEC else own_ref.at[slot, rows[part]]

    def copy(way, part, slot, mine=False):
        source = place(part, slot)
        if mine:
            source = dec_shard_ref if part == PART_DEC else shard_ref.at[rows[part]]
        return pltpu.make_async_remote_copy(
            src_ref=source,
            dst_ref=place(part, slot),
            send_sem=send_sems.at[way, part, slot],
            recv_sem=recv_sems.at[part, slot],
            device_id={"dp": peers[way]},
            device_id_type=MESH_ID,
        )

    def send(way, part, slot, mine=False):
        copy(way, part, slot, mine).start()

    def recv(part, slot):
        copy(WAY_X, part, slot).wait_recv()

    def pair(part, plane):
        block = pl.ds(plane * PLANE, PLANE)
        if part == PART_DEC:
            source, target = dec_own.at[block], dec_other.at[block]
        else:
            source, target = own_ref.at[block, rows[part]], other_ref.at[block, rows[part]]
        return pltpu.make_async_remote_copy(
            src_ref=source,
            dst_ref=target,
            send_sem=pair_sems.at[0, part, plane],
            recv_sem=pair_sems.at[1, part, plane],
            device_id={"tensor": 1 - half},
            device_id_type=MESH_ID,
        )

    def load(index):
        return pltpu.make_async_copy(
            error_ref.at[pl.ds(index * ERROR_ROWS, ERROR_ROWS)], held.at[index % 2], sems.at[index % 2]
        )

    load(0).start()
    load(1).start()
    dec_load = pltpu.make_async_copy(dec_error_ref, dec_held, sems.at[2])
    dec_load.start()

    barrier = pltpu.get_barrier_semaphore()
    for way in (WAY_X, WAY_Y):
        pl.semaphore_signal(barrier, 1, device_id={"dp": peers[way]}, device_id_type=MESH_ID)
    pl.semaphore_signal(barrier, 1, device_id={"tensor": 1 - half}, device_id_type=MESH_ID)
    for ok, way in ((up, WAY_UP), (down, WAY_DOWN)):

        @pl.when(ok)
        def _(way=way):
            pl.semaphore_signal(barrier, 1, device_id={"dp": peers[way]}, device_id_type=MESH_ID)

    pl.semaphore_wait(barrier, 3 + up.astype(jnp.int32) + down.astype(jnp.int32))

    def both_z(part, slot, mine=False):
        @pl.when(up)
        def _():
            send(WAY_UP, part, slot, mine)

        @pl.when(down)
        def _():
            send(WAY_DOWN, part, slot, mine)

    def sides(distance):
        return [
            ((z + side * distance >= 0) & (z + side * distance < planes), z + side * distance, on, way)
            for side, on, way in ((-1, up, WAY_UP), (1, down, WAY_DOWN))
        ]

    def along(distance):
        for there, plane, on, way in sides(distance):

            @pl.when(there)
            def _(slot=plane * PLANE + column, on=on, way=way):
                for part in Z_X_Y_PARTS + (PART_Z_Y_X,):
                    recv(part, slot)

                    @pl.when(on)
                    def _():
                        send(way, part, slot)

                    send(WAY_Y if part == PART_Z_Y_X else WAY_X, part, slot)
                for part in Z_X_Y_PARTS:
                    send(WAY_Y, part, slot)
                send(WAY_X, PART_Z_Y_X, slot)

    def cross(distance):
        for there, plane, _, _ in sides(distance):

            @pl.when(there)
            def _(base=plane * PLANE):
                for part in Z_X_Y_PARTS:
                    recv(part, base + column_x)
                    send(WAY_Y, part, base + column_x)
                recv(PART_Z_Y_X, base + column_y)
                send(WAY_X, PART_Z_Y_X, base + column_y)

    def finish(distance):
        for there, plane, _, _ in sides(distance)[: 2 if distance else 1]:

            @pl.when(there)
            def _(plane=plane, base=plane * PLANE):
                for part in Z_X_Y_PARTS:
                    recv(part, base + column_y)
                    recv(part, base + column_xy)
                    pair(part, plane).start()
                recv(PART_Z_Y_X, base + column_x)
                recv(PART_Z_Y_X, base + column_xy)
                pair(PART_Z_Y_X, plane).start()

    def whole_plane(distance):
        for there, plane, on, way in sides(distance):

            @pl.when(there)
            def _(plane=plane, on=on, way=way):
                for index in range(PLANE):
                    slot = plane * PLANE + index
                    recv(PART_X_Y_Z, slot)

                    @pl.when(on)
                    def _(slot=slot):
                        send(way, PART_X_Y_Z, slot)

                pair(PART_X_Y_Z, plane).start()

    workers = planes * PLANE
    start3 = split3(start_ref[:, :D])
    chunks = error_ref.shape[0] // ERROR_ROWS

    def work(index):
        load(index).wait()
        lanes = pl.ds(index * ERROR_ROWS, ERROR_ROWS)
        part_ref[:, lanes] = fold3(nt(start3, held[index % 2]))
        if index + 2 < chunks:
            load(index + 2).start()

    send(WAY_X, PART_X_Y_Z, me, True)
    send(WAY_Y, PART_X_Y_Z, me, True)
    for part in (PART_DEC, PART_Z_X_Y, PART_Z_Y_X):
        both_z(part, me, True)
    for part in Z_X_Y_PARTS:
        send(WAY_X, part, me, True)
    send(WAY_Y, PART_Z_Y_X, me, True)
    send(WAY_X, PART_Z_Y_X, me, True)
    for part in Z_X_Y_PARTS:
        send(WAY_Y, part, me, True)
    keeps = [
        pltpu.make_async_copy(shard_ref, own_ref.at[me], sems.at[3]),
        pltpu.make_async_copy(dec_shard_ref, dec_own.at[me], sems.at[6]),
    ]
    for keep in keeps:
        keep.start()
    swap_pixels = pltpu.make_async_remote_copy(
        src_ref=tubes_ref.at[1 - half],
        dst_ref=pixels_ref,
        send_sem=sems.at[4],
        recv_sem=sems.at[5],
        device_id={"tensor": 1 - half},
        device_id_type=MESH_ID,
    )
    swap_pixels.start()
    loads = [
        pltpu.make_async_copy(tubes_ref.at[index], pix_held.at[clip], sems.at[7 + clip])
        for clip, index in ((0, half), (1, 1 - half))
    ]
    for get in loads:
        get.start()
    work(0)
    near = z * PLANE
    recv(PART_X_Y_Z, near + column_x)
    send(WAY_Y, PART_X_Y_Z, near + column_x)
    for part in Z_X_Y_PARTS:
        recv(part, near + column_x)
        send(WAY_Y, part, near + column_x)
    recv(PART_Z_Y_X, near + column_y)
    send(WAY_X, PART_Z_Y_X, near + column_y)
    for keep in keeps:
        keep.wait()
    place_index = lax.broadcasted_iota(jnp.int32, (1, TUBES), 1)
    for clip, index in ((0, half), (1, 1 - half)):
        loads[clip].wait()
        hot = jnp.where(order_ref[index] == place_index, 1.0, 0.0).astype(bf16)
        picked_ref[clip] = nn(hot, pix_held[clip]).astype(bf16)
    swap_picked = pltpu.make_async_remote_copy(
        src_ref=picked_ref.at[1],
        dst_ref=pix_other_ref,
        send_sem=sems.at[9],
        recv_sem=sems.at[10],
        device_id={"tensor": 1 - half},
        device_id_type=MESH_ID,
    )
    swap_picked.start()
    work(1)
    along(1)
    recv(PART_X_Y_Z, near + column_y)
    recv(PART_X_Y_Z, near + column_xy)
    for index in range(PLANE):
        both_z(PART_X_Y_Z, near + index)
    pair(PART_X_Y_Z, z).start()
    work(2)
    cross(1)
    finish(0)
    pos_enc_ref[...] = sinusoid_of(order_ref[half].astype(f32), D)
    work(3)
    along(2)
    first_place = lax.broadcasted_iota(jnp.int32, (TUBES // 32, 1), 0).astype(f32) * 32.0
    second_place = lax.broadcasted_iota(jnp.int32, (32, 1), 0).astype(f32)
    rate, even = rates(DD)
    first = first_place * rate
    second = second_place * rate
    ahead = jnp.where(even, jnp.sin(first), jnp.cos(first))
    turned = jnp.where(even, jnp.cos(first), -jnp.sin(first))
    cos2, sin2 = jnp.cos(second), jnp.sin(second)
    for index in range(TUBES // 32):
        pos_dec_ref[pl.ds(32 * index, 32)] = (
            ahead[index : index + 1] * cos2 + turned[index : index + 1] * sin2
        )
    work(4)
    whole_plane(1)
    cross(2)
    work(5)
    finish(1)
    along(3)
    work(6)
    whole_plane(2)
    cross(3)
    work(7)
    finish(2)
    dec_load.wait()
    dec_part_ref[...] = fold3(nt(split3(start_ref[:, D:]), dec_held[...]))
    whole_plane(3)
    finish(3)
    for plane in range(planes):
        pair(PART_DEC, plane).wait()
    total = jnp.zeros((1, 128), f32)
    per = joined.shape[1] // workers
    for index in range(workers):
        for group, ref in enumerate((dec_own, dec_other)):
            block = ref[index].astype(f32)
            joined[group, pl.ds(index * per, per)] = block[:per]
            if group == 0:
                total = total + block[per : per + 1, :128]
    for group in range(2):

        def matrix(at, size):
            return joined[group, pl.ds(at, size)].astype(bf16)

        wo_ref[pl.ds(group * DD // 2, DD // 2)] = matrix(DEC_O, DD // 2)
        for kind in range(3):
            wqkv_ref[pl.ds((2 * kind + group) * DD // 2, DD // 2)] = matrix(
                DEC_Q + kind * DD // 2, DD // 2
            )
        for ref, at in ((wd_ref, DEC_D), (wu_ref, DEC_U), (wh_ref, DEC_H)):
            ref[pl.ds(group * DFF // 2, DFF // 2)] = matrix(at, DFF // 2)
        proj_ref[half if group == 0 else 1 - half] = matrix(0, D // 2)
    counted = counted_ref[half]
    scal_ref[0:1] = jnp.zeros((1, 128), f32) + counted
    scal_ref[1:2] = counted * (2.0 * workers / PIX) / (MASKED * total)
    scal_ref[2:3] = MASKED * total
    scal_ref[3:8] = jnp.zeros((5, 128), f32)
    swap_pixels.wait()
    swap_picked.wait()
    for plane in range(planes):
        for part in range(3):
            pair(part, plane).wait()
        for index in range(PLANE):
            slot = plane * PLANE + index

            @pl.when(column == index)
            def _():
                for part in (PART_DEC, PART_Z_X_Y, PART_Z_Y_X):
                    copy(WAY_X, part, slot).wait_send()
                    copy(WAY_Y, part, slot).wait_send()

            @pl.when(column_x == index)
            def _():
                for part in Z_X_Y_PARTS:
                    copy(WAY_Y, part, slot).wait_send()

            @pl.when(column_y == index)
            def _():
                copy(WAY_X, PART_Z_Y_X, slot).wait_send()

            for part in range(4):
                sent = True if part == PART_X_Y_Z else column == index

                @pl.when(up & (plane <= z) & sent)
                def _():
                    copy(WAY_UP, part, slot).wait_send()

                @pl.when(down & (plane >= z) & sent)
                def _():
                    copy(WAY_DOWN, part, slot).wait_send()

    copy(WAY_X, PART_X_Y_Z, me).wait_send()
    copy(WAY_Y, PART_X_Y_Z, me).wait_send()
    copy(WAY_Y, PART_X_Y_Z, near + column_x).wait_send()


def gather_weights(planes, shard, dec_shard, tubes, error, dec_error, start, order, counted):
    workers = planes * PLANE
    size = shard.shape[0]
    same = dec_shard.shape[0] * DD // D
    long = (size + same) * 2 // 5 // 16 * 16 + 16
    parts = ((0, long - same), (long - same, long), (2 * long - same, size - 2 * long + same))
    shards = jax.ShapeDtypeStruct((workers,) + shard.shape, shard.dtype)
    low = lambda *shape: jax.ShapeDtypeStruct(shape, bf16)
    wide = lambda *shape: jax.ShapeDtypeStruct(shape, f32)
    dec_shards = pltpu.VMEM((workers,) + dec_shard.shape, bf16)
    return pl.pallas_call(
        lambda *refs: gather_kernel(parts, planes, *refs),
        in_specs=[any_spec()] * 5
        + [vmem_spec()] * 2
        + [pl.BlockSpec(memory_space=pltpu.SMEM)],
        out_specs=[any_spec()] * 3 + [vmem_spec()] * 13,
        out_shape=[
            shards,
            shards,
            jax.ShapeDtypeStruct(tubes.shape[1:], tubes.dtype),
            wide(RANK, error.shape[0]),
            wide(RANK, dec_error.shape[0]),
            low(2, VIS, D),
            low(VIS, D),
            wide(VIS, D),
            wide(TUBES, DD),
            wide(8, 128),
            low(2, D // 2, DD),
            low(3 * DD, DD),
            low(DD, DD),
            low(DFF, DD),
            low(DFF, DD),
            low(PIX, DD),
        ],
        scratch_shapes=[
            pltpu.VMEM((2, ERROR_ROWS, D), bf16),
            pltpu.VMEM(dec_error.shape, bf16),
            dec_shards,
            dec_shards,
            pltpu.VMEM((2, DEC_ROWS, DD), f32),
            pltpu.VMEM((2, TUBES, D), bf16),
            pltpu.SemaphoreType.DMA((4, 4, workers)),
            pltpu.SemaphoreType.DMA((4, workers)),
            pltpu.SemaphoreType.DMA((2, 4, planes)),
            pltpu.SemaphoreType.DMA((11,)),
        ],
        compiler_params=pltpu.CompilerParams(
            collective_id=3, has_side_effects=True, vmem_limit_bytes=BIG_VMEM
        ),
        name="gather_weights",
    )(shard, dec_shard, tubes, error, dec_error, start, order, counted)


def cut(block, widths):
    pieces = []
    start = 0
    for width in widths:
        pieces.append(block[start : start + width])
        start = start + width
    return pieces


def swap(value):
    return lax.ppermute(value, "tensor", [(0, 1), (1, 0)])


def per_device(
    tubes,
    tube_order,
    clip_mask,
    enc_weights,
    dec_weights,
    vec_split,
    vec_shared,
    enc_moment,
    dec_moment,
    split_moment,
    shared_moment,
    enc_error,
    dec_error,
    factors,
):
    workers = lax.axis_size("dp")
    half = lax.axis_index("tensor")
    worker_index = lax.axis_index("dp")
    mine = lambda both: lax.dynamic_index_in_dim(both, half, 0, keepdims=False)
    which = half.astype(jnp.int32)[None]
    counted_all = clip_mask.astype(f32)
    counted = mine(counted_all)
    enc_per = enc_weights.shape[1]
    dec_per = dec_weights.shape[1]
    spare = -(dec_per + 1) % 16 + 1
    shard = enc_weights[0].astype(bf16)
    dec_shard = jnp.concatenate(
        [
            dec_weights[0].astype(bf16),
            jnp.broadcast_to(jnp.sum(counted_all).astype(bf16), (spare, DD)),
        ],
        0,
    )
    start_own = factors[0]
    start_other = swap(start_own)
    starts = (start_own, start_other)
    splits = (vec_split, swap(vec_split))
    dec_at = 2 * (2 * HALF + HALF_FF)
    bq, bv, bu, bh = (
        jnp.concatenate([split[:, at : at + size] for split in splits], 1)
        for at, size in (
            (dec_at, DD // 2),
            (dec_at + DD // 2, DD // 2),
            (dec_at + DD, DFF // 2),
            (dec_at + DD + DFF // 2, PIX // 2),
        )
    )
    bqkv = jnp.concatenate([bq, jnp.zeros_like(bq), bv], 1)
    wide = vec_shared[: 15 * D].reshape(15, D)
    narrow = vec_shared[15 * D :].reshape(9, DD)
    visible = mine(tube_order)[None, :VIS]
    if workers == 4 * PLANE:
        per = enc_per
        (
            enc_own, enc_other, pixels, enc_error_part, dec_error_part, picked, pix_vis_other,
            pos_enc, pos_dec, scal, proj, d_qkv, d_out, d_down, d_up, head_rows,
        ) = gather_weights(
            workers // PLANE, shard, dec_shard, tubes, enc_error[0, 0], dec_error[0, 0], start_own,
            tube_order[:, :VIS, None], counted_all,
        )
        proj = proj.reshape(D, DD)
        loss_weight = scal[2, 0]
    else:
        picked = pick_visible(which, tube_order, tubes)
        pix_vis_other = swap(picked[1])
        own = lax.all_gather(shard, "dp", axis=0)
        dec_all = lax.all_gather(dec_shard, "dp", axis=0)
        pixels = swap(lax.dynamic_index_in_dim(tubes, 1 - half, 0, keepdims=False))
        per = enc_per * workers
        enc_own = own.reshape(1, per, D)
        enc_other = swap(enc_own)
        enc_error_part = error_factor(start_own[:, :D], enc_error[0, 0])
        dec_error_part = error_factor(start_own[:, D:], dec_error[0, 0])
        dec_own = dec_all[:, :dec_per].reshape(DEC_ROWS, DD)
        dec_other = swap(dec_own)
        loss_weight = MASKED * jnp.sum(dec_all[:, dec_per, 0].astype(f32))
        dec_widths = [D // 2, DD // 2, DFF // 2, 3 * DD // 2, DFF // 2, PIX // 2]
        own_parts = cut(dec_own, dec_widths)
        other_parts = cut(dec_other, dec_widths)
        proj = jnp.where(
            half == 0,
            jnp.concatenate([own_parts[0], other_parts[0]], 0),
            jnp.concatenate([other_parts[0], own_parts[0]], 0),
        )
        d_out, d_down, d_up, head_rows = (
            jnp.concatenate([own_parts[index], other_parts[index]], 0) for index in (1, 2, 4, 5)
        )
        kinds = lambda block: block.reshape(3, DD // 2, DD)
        d_qkv = jnp.concatenate([kinds(own_parts[3]), kinds(other_parts[3])], 1)
        d_qkv = d_qkv.reshape(3 * DD, DD)
        pos_enc = sinusoid_of(visible.reshape(VIS, 1).astype(f32), D)
        pos_dec = sinusoid_of(jnp.arange(TUBES).astype(f32)[:, None], DD)
        scal = jnp.broadcast_to(
            jnp.stack([counted, 2.0 * workers / (PIX * loss_weight) * counted] + [counted] * 6)[
                :, None
            ],
            (8, 128),
        )
    pix_vis = picked[0]

    stream0, *kept0 = encoder_layer(
        0, per, (pix_vis, pix_vis_other, pos_enc), wide, splits, enc_own, enc_other
    )
    stream1 = kept0[0]
    enc_normed, latent, *kept1 = encoder_layer(
        1, per, (stream1, proj), wide, splits, enc_own, enc_other
    )
    kept = [(stream0, kept0), (stream1, kept1)]

    dec_start, h, qkv, hidden = decoder_qkv(
        visible, pos_dec, latent, narrow, d_qkv, bqkv
    )
    mixed, logs = attend(qkv)
    grad_mixed, grad_middle, dec_grads, dec_sent, g_vec, g_bu, g_bh, loss_lanes = decoder_tokens(
        which, mixed, dec_start, tubes, pixels, hidden, scal, narrow, bu, bh, d_out, d_down, d_up,
        head_rows,
    )
    dq, dk, dv = attend_back(qkv, mixed, grad_mixed, logs)
    latent_low, dec_grads, dec_sent, g_vec1 = decoder_qkv_back(
        which, visible, dq, dk, dv, h, dec_start, grad_middle, narrow, d_qkv, enc_normed,
        dec_grads, dec_sent,
    )
    dec_left = dec_left_factor(starts, dec_grads, dec_sent)
    dec_came = swap(dec_sent)

    grad = latent_low
    packs = [None, None]
    came = [None, None]
    enc_lefts = [None, None]
    enc_vec_grads = [None, None]
    for layer in (1, 0):
        source, result = kept[layer]
        grad, packs[layer], sent, enc_lefts[layer], *enc_vec_grads[layer] = encoder_layer_back(
            layer, per, grad, source, wide, result, starts, enc_own, enc_other,
            (pix_vis, pix_vis_other), (result[0], proj) if layer == 1 else (),
        )
        came[layer] = swap(sent)
    mine_packs = (pix_vis, packs[0], packs[1])
    their_packs = (picked[1], came[0], came[1])

    enc_basis, dec_basis = summed_basis(
        workers, enc_lefts[0], enc_lefts[1], dec_left, enc_error_part, dec_error_part
    )

    def split_half(index):
        pieces = []
        for layer in range(2):
            _, g_hidden, g_qv = enc_vec_grads[layer]
            pieces += [
                cut(g_qv[0], [HALF] * 2)[index],
                cut(g_qv[1], [HALF] * 2)[index],
                cut(g_hidden[0], [HALF_FF] * 2)[index],
            ]
        pieces += [
            cut(g_vec1[0], [DD // 2] * 2)[index],
            cut(g_vec1[1], [DD // 2] * 2)[index],
            cut(g_bu[0], [DFF // 2] * 2)[index],
            cut(g_bh[0], [PIX // 2] * 2)[index],
        ]
        return jnp.concatenate(pieces)

    g_vec_enc = [grads[0] for grads in enc_vec_grads]
    shared_grad = jnp.concatenate(
        [g_vec_enc[0][6], g_vec_enc[0][:6].reshape(-1), g_vec_enc[1].reshape(-1)]
        + [g_vec1[4], g_vec1[2], g_vec1[3], g_vec[:6].reshape(-1)]
    )
    loss_part = jnp.sum(loss_lanes) / PIX
    split_len = vec_split.shape[1]
    length = split_len + shared_grad.shape[0] + 1
    vec_lanes = pl.cdiv(length, RANK * 128) * 128
    fill = jnp.zeros((RANK * vec_lanes - length,), f32)
    sent = jnp.concatenate([split_half(1), shared_grad, loss_part[None], fill])
    local = jnp.concatenate([split_half(0), shared_grad, loss_part[None], fill])
    vec_local = (local + swap(sent)).reshape(RANK, vec_lanes)

    enc_rows = enc_basis.shape[1] // workers
    dec_rows = dec_basis.shape[1] // workers
    enc_owned = lax.dynamic_slice_in_dim(enc_basis, worker_index * enc_rows, enc_rows, 1)
    dec_owned = lax.dynamic_slice_in_dim(dec_basis, worker_index * dec_rows, dec_rows, 1)
    dec_right_part, dec_comb = dec_right_factor(dec_basis, dec_grads, dec_came, dec_error[0, 0])
    enc_right, dec_right, vec_mean = mean_over_workers(
        workers,
        (
            right_factor(enc_basis, enc_error[0, 0], mine_packs, their_packs),
            dec_right_part,
            vec_local,
        ),
    )
    vec_mean = vec_mean.reshape(-1)
    enc_error_new = residue(enc_basis, enc_right, enc_error[0, 0], mine_packs, their_packs)
    dec_error_new = dec_residue(dec_basis, dec_right, dec_comb)
    enc_mom = momentum_keep * enc_moment[0] + jnp.einsum(
        "rx,rc->xc", enc_owned, enc_right, precision=highest_precision
    )
    dec_mom = momentum_keep * dec_moment[0] + jnp.einsum(
        "rx,rc->xc", dec_owned, dec_right, precision=highest_precision
    )
    split_mom = momentum_keep * split_moment[0] + vec_mean[:split_len]
    shared_mom = momentum_keep * shared_moment + vec_mean[split_len : length - 1]
    return (
        vec_mean[length - 1] * workers,
        loss_weight,
        (enc_weights[0] - step_rate * enc_mom)[None],
        enc_mom[None],
        enc_error_new[None, None],
        (dec_weights[0] - step_rate * dec_mom)[None],
        dec_mom[None],
        dec_error_new[None, None],
        jnp.concatenate([enc_right, dec_right], 1)[None],
        (vec_split[0] - step_rate * split_mom)[None],
        split_mom[None],
        vec_shared - step_rate * shared_mom,
        shared_mom,
    )


def solution(mesh):
    placed = (
        P("dp", None, "tensor"),
        P("dp", None),
        P("dp"),
        P("tensor", "dp", None),
        P("tensor", "dp", None),
        P("tensor", None),
        P(),
        P("tensor", "dp", None),
        P("tensor", "dp", None),
        P("tensor", None),
        P(),
        P("dp", "tensor", None, None),
        P("dp", "tensor", None, None),
        P("tensor", None, None),
    )
    return jax.shard_map(
        per_device,
        mesh=mesh,
        in_specs=placed,
        out_specs=(
            P(),
            P(),
            P("tensor", "dp", None),
            P("tensor", "dp", None),
            P("dp", "tensor", None, None),
            P("tensor", "dp", None),
            P("tensor", "dp", None),
            P("dp", "tensor", None, None),
            P("tensor", None, None),
            P("tensor", None),
            P("tensor", None),
            P(),
            P(),
        ),
        check_vma=False,
    )
```

```python
import math

import jax
import jax.numpy as jnp
from jax import lax
from jax.experimental import pallas as pl
from jax.experimental.pallas import tpu as pltpu
from jax.sharding import PartitionSpec as P

D = 768
HEAD_DIM = 64
FF = 3072
DD = 384
DFF = 1536
PIX = 1536
TUBES = 1568
VIS = 160
MASKED = 1408
RANK = 8

f32 = jnp.float32
bf16 = jnp.bfloat16
highest_precision = lax.Precision.HIGHEST
norm_eps = 1e-06
momentum_keep = 0.9
step_rate = 1000.0
LOG2E = 1.4426950408889634
SCORE = HEAD_DIM ** (-0.5)
BIG_VMEM = 56 << 20


def nn(left, right):
    return lax.dot_general(left, right, (((1,), (0,)), ((), ())), preferred_element_type=f32)


def nt(left, right):
    return lax.dot_general(left, right, (((1,), (1,)), ((), ())), preferred_element_type=f32)


def tn(left, right):
    return lax.dot_general(left, right, (((0,), (0,)), ((), ())), preferred_element_type=f32)


def ahead(count, product):
    value = product(0)
    for index in range(count):
        later = product(index + 1) if index + 1 < count else None
        yield index, value
        value = later


def col_sum(value):
    return jnp.sum(value, 0, keepdims=True)


def norm_parts(stream):
    center = stream - jnp.mean(stream, -1, keepdims=True)
    rate = lax.rsqrt(jnp.mean(center * center, -1, keepdims=True) + norm_eps)
    return center * rate, rate


def norm_back(grad, gain, unit, rate):
    grad_unit = grad * gain
    return rate * (
        grad_unit
        - jnp.mean(grad_unit, -1, keepdims=True)
        - unit * jnp.mean(grad_unit * unit, -1, keepdims=True)
    )


def gelu_pair(before):
    cdf_tail = jnp.exp(-0.5 * before * before)
    size = jnp.abs(before) * (2.0 ** -0.5)
    t = 1.0 / (1.0 + 0.3275911 * size)
    poly = t * (
        0.254829592 + t * (-0.284496736 + t * (1.421413741 + t * (-1.453152027 + t * 1.061405429)))
    )
    tail = 0.5 * poly * cdf_tail
    cdf = jnp.where(before < 0, tail, 1.0 - tail)
    return before * cdf, cdf + before * cdf_tail * (1.0 / math.sqrt(2.0 * math.pi))


def split3(value):
    high = value.astype(bf16)
    rest = value - high.astype(f32)
    middle = rest.astype(bf16)
    low = (rest - middle.astype(f32)).astype(bf16)
    return jnp.concatenate([high, middle, low], 0)


def fold3(value):
    rows = value.shape[0] // 3
    return value[:rows] + value[rows : 2 * rows] + value[2 * rows :]


def rates(width):
    column = lax.broadcasted_iota(jnp.int32, (1, width), 1)
    low_bit = lax.rem(column, 2)
    rate = jnp.exp((column - low_bit).astype(f32) * (-math.log(10000.0) / width))
    return rate, low_bit == 0


def sinusoid_of(place, width):
    rate, even = rates(width)
    angle = place * rate
    return jnp.where(even, jnp.sin(angle), jnp.cos(angle))


def params(**more):
    return pltpu.CompilerParams(vmem_limit_bytes=BIG_VMEM, **more)


def whole(shape):
    return pl.BlockSpec(shape, lambda *_: (0,) * len(shape))


def any_spec():
    return pl.BlockSpec(memory_space=pl.ANY)


def vmem_spec():
    return pl.BlockSpec(memory_space=pltpu.VMEM)


def pick_kernel(half_ref, order_ref, tubes_ref, out_ref):
    column = lax.broadcasted_iota(jnp.int32, (1, TUBES), 1)
    hot = jnp.where(order_ref[0] == column, 1.0, 0.0).astype(bf16)
    out_ref[0] = nn(hot, tubes_ref[0]).astype(bf16)


def pick_visible(half, order, tubes):
    clips, _, width = tubes.shape
    which = lambda c, half_ref: jnp.where(c == 0, half_ref[0], 1 - half_ref[0])
    return pl.pallas_call(
        pick_kernel,
        grid_spec=pltpu.PrefetchScalarGridSpec(
            num_scalar_prefetch=1,
            grid=(clips,),
            in_specs=[
                pl.BlockSpec((1, VIS, 1), lambda c, half_ref: (which(c, half_ref), 0, 0)),
                pl.BlockSpec((1, TUBES, width), lambda c, half_ref: (which(c, half_ref), 0, 0)),
            ],
            out_specs=pl.BlockSpec((1, VIS, width), lambda c, half_ref: (c, 0, 0)),
        ),
        out_shape=jax.ShapeDtypeStruct((clips, VIS, width), bf16),
        compiler_params=params(),
        name="pick_visible",
    )(half, order[:, :VIS, None], tubes)


QKV_ROWS = 392


def place_matrix(order, rows):
    place = lax.broadcasted_iota(jnp.int32, (rows, 1), 0) + pl.program_id(0) * rows
    return jnp.where(order == place, 1.0, 0.0)


def qkv_kernel(order_ref, pos_ref, latent_ref, vec_ref, w_ref, bias_ref, x_ref, h_ref, qkv_ref, hidden_ref):
    token, gain, shift = (vec_ref[index : index + 1] for index in range(3))
    places = place_matrix(order_ref[...], QKV_ROWS)
    hidden = 1.0 - jnp.sum(places, 1, keepdims=True)
    hidden_ref[...] = hidden
    latent = split3(latent_ref[...])
    places = places.astype(bf16)
    shown = sum(nn(places, latent[VIS * part : VIS * (part + 1)]) for part in (2, 1, 0))
    x = pos_ref[...] + (shown + hidden * token)
    x_ref[...] = x
    unit, _ = norm_parts(x)
    h = (unit * gain + shift).astype(bf16)
    h_ref[...] = h
    qkv_ref[...] = (nt(h, w_ref[...]) + bias_ref[...]).astype(bf16)


def decoder_qkv(order, pos, latent, vecs, weights, bias):
    rows = lambda width: pl.BlockSpec((QKV_ROWS, width), lambda i: (i, 0))
    return pl.pallas_call(
        qkv_kernel,
        grid=(TUBES // QKV_ROWS,),
        in_specs=[
            whole((1, VIS)),
            rows(DD),
            whole((VIS, DD)),
            whole(vecs.shape),
            whole((3 * DD, DD)),
            whole((1, 3 * DD)),
        ],
        out_specs=[rows(DD), rows(DD), rows(3 * DD), rows(1)],
        out_shape=[
            jax.ShapeDtypeStruct((TUBES, DD), f32),
            jax.ShapeDtypeStruct((TUBES, DD), bf16),
            jax.ShapeDtypeStruct((TUBES, 3 * DD), bf16),
            jax.ShapeDtypeStruct((TUBES, 1), f32),
        ],
        compiler_params=params(),
        name="decoder_qkv",
    )(order, pos, latent, vecs, weights, bias)


PAIRS = DD // 128


def half_lane(index):
    return lax.broadcasted_iota(jnp.int32, (1, 128), 1) // HEAD_DIM == index


ATTEND_ROWS = 784


def attend_kernel(q_ref, k_ref, v_ref, o_ref, lse_ref):
    k = k_ref[...]
    v_one = jnp.concatenate([v_ref[...], jnp.ones((TUBES, 128), bf16)], 1)
    turns = [(at, head) for at in range(0, TUBES, ATTEND_ROWS) for head in range(2)]

    def scores_of(turn):
        at, head = turn
        q = q_ref[pl.ds(at, ATTEND_ROWS)]
        return nt(jnp.where(half_lane(head), q, jnp.zeros_like(q)), k)

    mixed, logs = [], []
    scores = scores_of(turns[0])
    for index, (at, head) in enumerate(turns):
        later = scores_of(turns[index + 1]) if index + 1 < len(turns) else None
        top = jnp.max(scores, 1, keepdims=True)
        expo = jnp.exp2((scores - top) * (SCORE * LOG2E)).astype(bf16)
        both = nn(expo, v_one)
        total = both[:, 128:]
        mixed.append(both[:, :128] / total)
        logs.append(top * (SCORE * LOG2E) + jnp.log2(total))
        if head == 1:
            rows = pl.ds(at, ATTEND_ROWS)
            o_ref[rows] = jnp.where(half_lane(0), mixed[-2], mixed[-1])
            lse_ref[0, rows] = jnp.where(half_lane(0), logs[-2], logs[-1])
        scores = later


def attend(qkv):
    pair = lambda kind: pl.BlockSpec((TUBES, 128), lambda p: (0, kind * PAIRS + p))
    return pl.pallas_call(
        attend_kernel,
        grid=(PAIRS,),
        in_specs=[pair(0), pair(1), pair(2)],
        out_specs=[pair(0), pl.BlockSpec((1, TUBES, 128), lambda p: (p, 0, 0))],
        out_shape=[
            jax.ShapeDtypeStruct((TUBES, DD), f32),
            jax.ShapeDtypeStruct((PAIRS, TUBES, 128), f32),
        ],
        compiler_params=params(),
        name="attend",
    )(qkv, qkv, qkv)


def attend_back_kernel(q_ref, k_ref, v_ref, o_ref, do_ref, lse_ref, dq_ref, dk_ref, dv_ref):
    q, k, v, grad = q_ref[...], k_ref[...], v_ref[...], do_ref[...]
    k_turned = k.T
    dots = o_ref[...] * grad.astype(f32)
    logs = lse_ref[0].T
    select = (
        lax.broadcasted_iota(jnp.int32, (8, 128), 1) // HEAD_DIM
        == lax.broadcasted_iota(jnp.int32, (8, 128), 0)
    ).astype(f32)
    row_total = lax.dot_general(
        select, dots, (((1,), (1,)), ((), ())), precision=highest_precision,
        preferred_element_type=f32,
    )
    zero = jnp.zeros((), bf16)
    dk = dv = jnp.zeros((TUBES, 128), f32)
    turned = []
    for head in range(2):
        mask = half_lane(head)
        q_head = jnp.where(mask, q, zero)
        grad_head = jnp.where(mask, grad, zero)
        low = head * HEAD_DIM
        probs = jnp.exp2(nt(k, q_head) * (SCORE * LOG2E) - logs[low : low + 1])
        grad_scores = (probs * (nt(v, grad_head) - row_total[head : head + 1])).astype(bf16)
        dv = dv + nn(probs.astype(bf16), grad_head)
        dk = dk + nn(grad_scores, q_head)
        turned.append(nn(k_turned[low : low + HEAD_DIM], grad_scores))
    dq_ref[...] = (jnp.concatenate(turned, 0).T * SCORE).astype(bf16)
    dk_ref[...] = (dk * SCORE).astype(bf16)
    dv_ref[...] = dv.astype(bf16)


def attend_back(qkv, mixed, grad_mixed, logs):
    pair = lambda kind: pl.BlockSpec((TUBES, 128), lambda p: (0, kind * PAIRS + p))
    return pl.pallas_call(
        attend_back_kernel,
        grid=(PAIRS,),
        in_specs=[
            pair(0),
            pair(1),
            pair(2),
            pair(0),
            pair(0),
            pl.BlockSpec((1, TUBES, 128), lambda p: (p, 0, 0)),
        ],
        out_specs=[pair(0)] * 3,
        out_shape=[jax.ShapeDtypeStruct((TUBES, DD), bf16)] * 3,
        compiler_params=params(),
        name="attend_back",
    )(qkv, qkv, qkv, mixed, grad_mixed, logs)


TOKEN_ROWS = 784
CHUNK = 384
DEC_O = D // 2
DEC_D = DEC_O + DD // 2
DEC_Q = DEC_D + DFF // 2
DEC_U = DEC_Q + 3 * DD // 2
DEC_H = DEC_U + DFF // 2
DEC_ROWS = DEC_H + PIX // 2
CHUNKS = DFF // CHUNK


def token_kernel(
    _, a_ref, x_ref, pix_ref, pix_other_ref, hidden_ref, scal_ref, vec_ref, bu_ref, bh_ref,
    wo_ref, wd_ref, wu_ref, wh_ref,
    da_ref, dx1_ref,
    own_ref, other_ref, gvec_ref, gbu_ref, gbh_ref, loss_ref,
    slope,
):
    step = pl.program_id(0)
    sums = (own_ref, other_ref, gvec_ref, gbu_ref, gbh_ref, loss_ref)
    grads = (own_ref, other_ref)

    @pl.when(step == 0)
    def _():
        for ref in sums:
            ref[...] = jnp.zeros_like(ref)

    bo, g2, b2, bd, gf, sf = (vec_ref[index : index + 1] for index in range(3, 9))
    a = a_ref[...].astype(bf16)
    x1 = x_ref[...] + (nn(a, wo_ref[...]) + bo)
    unit2, rate2 = norm_parts(x1)
    h2 = (unit2 * g2 + b2).astype(bf16)
    out = x1 + bd
    active = []
    part_of = lambda chunk: pl.ds(chunk * CHUNK, CHUNK)
    for chunk, before in ahead(CHUNKS, lambda chunk: nt(h2, wu_ref[part_of(chunk)])):
        part = part_of(chunk)
        value, slope_part = gelu_pair(before + bu_ref[:, part])
        slope[:, part] = slope_part
        active.append(value.astype(bf16))
        out = out + nn(active[-1], wd_ref[part])
    unit_f, rate_f = norm_parts(out)
    final = (unit_f * gf + sf).astype(bf16)
    pixels = [
        ref[:, pl.ds(side * CHUNK, CHUNK)].astype(f32)
        for ref in (pix_ref.at[0], pix_other_ref)
        for side in range(2)
    ]
    center = sum(jnp.sum(part, 1, keepdims=True) for part in pixels) * (1.0 / PIX)
    square = sum(jnp.sum(part * part, 1, keepdims=True) for part in pixels) * (1.0 / PIX)
    spread = lax.rsqrt(square - center * center + norm_eps)
    counted = hidden_ref[...] * scal_ref[0:1, 0:1]
    rate = hidden_ref[...] * scal_ref[1:2, 0:1]
    grad_final = jnp.zeros((TOKEN_ROWS, DD), f32)
    for chunk, guess in ahead(CHUNKS, lambda chunk: nt(final, wh_ref[part_of(chunk)])):
        part = part_of(chunk)
        target = (pixels[chunk] - center) * spread
        miss = guess + bh_ref[:, part] - target
        loss_ref[:, part] += col_sum(counted * miss * miss)
        grad_guess = (rate * miss).astype(bf16)
        gbh_ref[:, part] += col_sum(grad_guess.astype(f32))
        grads[chunk // 2][pl.ds(DEC_H + (chunk % 2) * CHUNK, CHUNK)] += tn(grad_guess, final)
        grad_final = grad_final + nn(grad_guess, wh_ref[part])
    grad_out = norm_back(grad_final, gf, unit_f, rate_f)
    out_low = grad_out.astype(bf16)
    grad_h2 = jnp.zeros((TOKEN_ROWS, DD), f32)
    for chunk, grad_active in ahead(CHUNKS, lambda chunk: nt(out_low, wd_ref[part_of(chunk)])):
        part = part_of(chunk)
        grads[chunk // 2][pl.ds(DEC_D + (chunk % 2) * CHUNK, CHUNK)] += tn(active[chunk], out_low)
        grad_before = (slope[:, part] * grad_active).astype(bf16)
        gbu_ref[:, part] += col_sum(grad_before.astype(f32))
        grads[chunk // 2][pl.ds(DEC_U + (chunk % 2) * CHUNK, CHUNK)] += tn(grad_before, h2)
        grad_h2 = grad_h2 + nn(grad_before, wu_ref[part])
    grad_x1 = grad_out + norm_back(grad_h2, g2, unit2, rate2)
    x1_low = grad_x1.astype(bf16)
    g_out = tn(a, x1_low)
    for group in range(2):
        grads[group][pl.ds(DEC_O, DD // 2)] += g_out[group * DD // 2 : (group + 1) * DD // 2]
    da_ref[...] = nt(x1_low, wo_ref[...]).astype(bf16)
    dx1_ref[...] = grad_x1
    gvec_ref[0:1] += col_sum(x1_low.astype(f32))
    gvec_ref[1:2] += col_sum(grad_h2 * unit2)
    gvec_ref[2:3] += col_sum(grad_h2)
    gvec_ref[3:4] += col_sum(out_low.astype(f32))
    gvec_ref[4:5] += col_sum(grad_final * unit_f)
    gvec_ref[5:6] += col_sum(grad_final)


def decoder_tokens(half, mixed, x, tubes, pixels, hidden, scal, vecs, bu, bh, wo, wd, wu, wh):
    rows = lambda width: pl.BlockSpec((TOKEN_ROWS, width), lambda i, _: (i, 0))
    sums = [(DEC_ROWS, DD), (DEC_ROWS, DD), (8, DD), (1, DFF), (1, PIX), (1, PIX)]
    return pl.pallas_call(
        token_kernel,
        grid_spec=pltpu.PrefetchScalarGridSpec(
            num_scalar_prefetch=1,
            grid=(TUBES // TOKEN_ROWS,),
            in_specs=[
                rows(DD),
                rows(DD),
                pl.BlockSpec((1, TOKEN_ROWS, PIX // 2), lambda i, half_ref: (half_ref[0], i, 0)),
                rows(PIX // 2),
                rows(1),
                whole((8, 128)),
                whole(vecs.shape),
                whole((1, DFF)),
                whole((1, PIX)),
                whole((DD, DD)),
                whole((DFF, DD)),
                whole((DFF, DD)),
                whole((PIX, DD)),
            ],
            out_specs=[rows(DD), rows(DD)] + [whole(shape) for shape in sums],
            scratch_shapes=[pltpu.VMEM((TOKEN_ROWS, DFF), f32)],
        ),
        out_shape=[
            jax.ShapeDtypeStruct((TUBES, DD), bf16),
            jax.ShapeDtypeStruct((TUBES, DD), f32),
        ]
        + [jax.ShapeDtypeStruct(shape, f32) for shape in sums],
        compiler_params=params(),
        name="decoder_tokens",
    )(half, mixed, x, tubes, pixels, hidden, scal, vecs, bu, bh, wo, wd, wu, wh)


def qkv_back_kernel(
    half_ref, order_ref, dq_ref, dk_ref, dv_ref, h_ref, x_ref, dx1_ref, vec_ref, w_ref, normed_ref,
    _own, _other,
    latent_ref, own_ref, other_ref, gvec_ref,
    g_qkv, g_proj, latent_sum, sems,
):
    step = pl.program_id(0)

    @pl.when(step == 0)
    def _():
        g_qkv[...] = jnp.zeros_like(g_qkv)
        gvec_ref[...] = jnp.zeros_like(gvec_ref)
        latent_sum[...] = jnp.zeros_like(latent_sum)

    h = h_ref[...]
    grads = (dq_ref[...], dk_ref[...], dv_ref[...])
    grad_h = jnp.zeros((QKV_ROWS, DD), f32)
    for index, grad in enumerate(grads):
        g_both = tn(grad, h)
        for group in range(2):
            rows = pl.ds(index * DD // 2, DD // 2)
            g_qkv[group, rows] += g_both[group * DD // 2 : (group + 1) * DD // 2]
        grad_h = grad_h + nn(grad, w_ref[pl.ds(index * DD, DD)])
    unit, rate = norm_parts(x_ref[...])
    grad_x = dx1_ref[...] + norm_back(grad_h, vec_ref[1:2], unit, rate)
    places = place_matrix(order_ref[...], QKV_ROWS)
    hidden = 1.0 - jnp.sum(places, 1, keepdims=True)
    latent_sum[...] += tn(places.astype(bf16), grad_x.astype(bf16))
    gvec_ref[0:1] += col_sum(grads[0].astype(f32))
    gvec_ref[1:2] += col_sum(grads[2].astype(f32))
    gvec_ref[2:3] += col_sum(grad_h * unit)
    gvec_ref[3:4] += col_sum(grad_h)
    gvec_ref[4:5] += col_sum(hidden * grad_x)

    @pl.when(step == pl.num_programs(0) - 1)
    def _():
        latent = latent_sum[...].astype(bf16)
        latent_ref[...] = latent
        both = tn(normed_ref[...], latent)
        g_proj[0] = both[: D // 2]
        g_proj[1] = both[D // 2 :]
        half = half_ref[0]
        kinds = pl.ds(DEC_Q, 3 * DD // 2)
        copies = [
            pltpu.make_async_copy(g_qkv.at[0], own_ref.at[kinds], sems.at[0]),
            pltpu.make_async_copy(g_qkv.at[1], other_ref.at[kinds], sems.at[1]),
            pltpu.make_async_copy(g_proj.at[half], own_ref.at[pl.ds(0, D // 2)], sems.at[2]),
            pltpu.make_async_copy(g_proj.at[1 - half], other_ref.at[pl.ds(0, D // 2)], sems.at[3]),
        ]
        for copy in copies:
            copy.start()
        for copy in copies:
            copy.wait()


def decoder_qkv_back(half, order, dq, dk, dv, h, x, dx1, vecs, weights, normed, own, other):
    rows = lambda width: pl.BlockSpec((QKV_ROWS, width), lambda i: (i, 0))
    return pl.pallas_call(
        qkv_back_kernel,
        grid=(TUBES // QKV_ROWS,),
        in_specs=[pl.BlockSpec(memory_space=pltpu.SMEM), whole((1, VIS))]
        + [rows(DD)] * 6
        + [whole(vecs.shape), whole((3 * DD, DD)), whole((VIS, D)), any_spec(), any_spec()],
        out_specs=[whole((VIS, DD)), any_spec(), any_spec(), whole((8, DD))],
        out_shape=[
            jax.ShapeDtypeStruct((VIS, DD), bf16),
            jax.ShapeDtypeStruct((DEC_ROWS, DD), f32),
            jax.ShapeDtypeStruct((DEC_ROWS, DD), f32),
            jax.ShapeDtypeStruct((8, DD), f32),
        ],
        scratch_shapes=[
            pltpu.VMEM((2, 3 * DD // 2, DD), f32),
            pltpu.VMEM((2, D // 2, DD), f32),
            pltpu.VMEM((VIS, DD), f32),
            pltpu.SemaphoreType.DMA((4,)),
        ],
        input_output_aliases={11: 1, 12: 2},
        compiler_params=params(),
        name="decoder_qkv_back",
    )(half, order, dq, dk, dv, h, x, dx1, vecs, weights, normed, own, other)


HALF = D // 2
HALF_FF = FF // 2
LAYER_ROWS = 4 * HALF + 2 * HALF_FF
AT_O, AT_D, AT_Q, AT_U = 0, HALF, HALF + HALF_FF, HALF + HALF_FF + 3 * HALF
STAGES = ((AT_Q, 3 * HALF), (AT_O, HALF), (AT_U, HALF_FF), (AT_D, HALF_FF))


def pieces_of(start, size, per):
    pieces = []
    at = start
    while at < start + size:
        many = min(start + size, (at // per + 1) * per) - at
        pieces.append((at // per, at % per, many, at - start))
        at += many
    return pieces


def stage_copies(sources, start, per, held, sems, stages):
    copies = []
    count = 0
    for at, size in stages:
        stage = []
        for shard, row, many, before in pieces_of(start + at, size, per):
            for group in range(2):
                stage.append(
                    pltpu.make_async_copy(
                        sources[group].at[shard, pl.ds(row, many)],
                        held.at[group, pl.ds(at + before, many)],
                        sems.at[count],
                    )
                )
                count += 1
        copies.append(stage)
    return copies


MOST_COPIES = 48


def encoder_kernel(layer, per, *refs):
    if layer == 0:
        pix_ref, pix_other_ref, pos_ref, *refs = refs
    else:
        x_ref, proj_ref, *refs = refs
    vec_ref, split_own_ref, split_other_ref, own_ref, other_ref, *refs = refs
    splits = (split_own_ref, split_other_ref)
    if layer == 0:
        x_out_ref, *refs = refs
    else:
        normed_ref, latent_ref, *refs = refs
    out_ref, h_ref, qkv_ref, a_ref, x1_ref, h2_ref, u_ref, slope_ref, held, sems = refs
    base = 1 + 6 * layer
    biases = layer * (2 * HALF + HALF_FF)
    if layer == 0:
        copies = stage_copies(
            (own_ref, other_ref), 0, per, held.at[:, pl.ds(LAYER_ROWS, D)], sems, ((0, D),)
        )
        used = sum(len(stage) for stage in copies)
        copies = copies + stage_copies(
            (own_ref, other_ref), D, per, held, sems.at[pl.ds(used, MOST_COPIES - used)], STAGES
        )
        copies = copies[1:] + copies[:1]
        order = (4, 0, 1, 2, 3)
    else:
        copies = stage_copies((own_ref, other_ref), D + LAYER_ROWS, per, held, sems, STAGES)
        order = (0, 1, 2, 3)
    for stage in order:
        for copy in copies[stage]:
            copy.start()

    def wait(stage):
        for copy in copies[stage]:
            copy.wait()

    g1, b1, bo, g2, b2, bd = (vec_ref[base + index : base + index + 1] for index in range(6))
    if layer == 0:
        wait(4)
        x = pos_ref[...] + vec_ref[0:1]
        for group, pixels in enumerate((pix_ref, pix_other_ref)):
            x = x + nn(pixels[...], held[group, pl.ds(LAYER_ROWS, D)])
        x_out_ref[...] = x
    else:
        x = x_ref[...]
    unit, _ = norm_parts(x)
    h = (unit * g1 + b1).astype(bf16)
    h_ref[...] = h
    wait(0)
    for kind in range(3):
        for group in range(2):
            part = pl.ds((2 * kind + group) * HALF, HALF)
            rows = pl.ds(AT_Q + kind * HALF, HALF)
            value = nt(h, held[group, rows])
            if kind != 1:
                at = biases + kind // 2 * HALF
                value = value + splits[group][:, at : at + HALF]
            qkv_ref[:, part] = value.astype(bf16)
    for pair in range(D // 128):
        q, k, v = (qkv_ref[:, pl.ds(kind * D + pair * 128, 128)] for kind in range(3))
        v_one = jnp.concatenate([v, jnp.ones((VIS, 128), bf16)], 1)
        mixed = []
        for head in range(2):
            scores = nt(jnp.where(half_lane(head), q, jnp.zeros_like(q)), k)
            top = jnp.max(scores, 1, keepdims=True)
            expo = jnp.exp2((scores - top) * (SCORE * LOG2E)).astype(bf16)
            both = nn(expo, v_one)
            mixed.append(both[:, :128] / both[:, 128:])
        a_ref[:, pl.ds(pair * 128, 128)] = jnp.where(half_lane(0), mixed[0], mixed[1]).astype(bf16)
    wait(1)
    x1 = x + bo
    for group in range(2):
        x1 = x1 + nn(a_ref[:, pl.ds(group * HALF, HALF)], held[group, pl.ds(AT_O, HALF)])
    x1_ref[...] = x1
    unit2, _ = norm_parts(x1)
    h2 = (unit2 * g2 + b2).astype(bf16)
    h2_ref[...] = h2
    wait(2)
    wait(3)
    out = x1 + bd
    for group in range(2):
        rows_of = lambda chunk: pl.ds(AT_U + chunk * CHUNK, CHUNK)
        for chunk, before in ahead(HALF_FF // CHUNK, lambda chunk: nt(h2, held[group, rows_of(chunk)])):
            part = pl.ds(group * HALF_FF + chunk * CHUNK, CHUNK)
            at = biases + 2 * HALF + chunk * CHUNK
            value, slope = gelu_pair(before + splits[group][:, at : at + CHUNK])
            slope_ref[:, part] = slope
            active = value.astype(bf16)
            u_ref[:, part] = active
            out = out + nn(active, held[group, pl.ds(AT_D + chunk * CHUNK, CHUNK)])
    out_ref[...] = out
    if layer == 1:
        unit3, _ = norm_parts(out)
        normed = (unit3 * vec_ref[13:14] + vec_ref[14:15]).astype(bf16)
        normed_ref[...] = normed
        latent_ref[...] = nn(normed, proj_ref[...])


def encoder_layer(layer, per, first, vecs, splits, own, other):
    shapes = [
        ((VIS, D), f32),
        ((VIS, D), bf16),
        ((VIS, 3 * D), bf16),
        ((VIS, D), bf16),
        ((VIS, D), f32),
        ((VIS, D), bf16),
        ((VIS, FF), bf16),
        ((VIS, FF), f32),
    ]
    before = [((VIS, D), f32)] if layer == 0 else [((VIS, D), bf16), ((VIS, DD), f32)]
    shapes = before + shapes
    return pl.pallas_call(
        lambda *refs: encoder_kernel(layer, per, *refs),
        in_specs=[vmem_spec()] * (len(first) + 3) + [any_spec()] * 2,
        out_specs=[vmem_spec()] * len(shapes),
        out_shape=[jax.ShapeDtypeStruct(shape, kind) for shape, kind in shapes],
        scratch_shapes=[
            pltpu.VMEM((2, LAYER_ROWS + (D if layer == 0 else 0), D), bf16),
            pltpu.SemaphoreType.DMA((MOST_COPIES,)),
        ],
        compiler_params=params(),
        name=f"encoder_{layer}",
    )(*first, vecs, *splits, own, other)


RIGHT_AT = LAYER_ROWS


def encoder_back_kernel(layer, per, *refs):
    last = layer == 1
    start = D + layer * LAYER_ROWS
    base = 1 + 6 * layer
    (
        grad_ref, x_ref, vec_ref, h_ref, qkv_ref, a_ref, x1_ref, h2_ref, u_ref, slope_ref,
        start_ref, start_other_ref, own_ref, other_ref, pix_ref, pix_other_ref,
    ) = refs[:16]
    pixels = (pix_ref, pix_other_ref)
    refs = refs[16:]
    if last:
        out_ref, proj_ref, *refs = refs
    dx_ref, mine_ref, other_pack_ref, left_ref, gvec_ref, gbu_ref, gbq_ref = refs[:7]
    held, sems, da, dqkv = refs[7:]
    packs = (mine_ref, other_pack_ref)
    copies = stage_copies((own_ref, other_ref), start, per, held, sems, STAGES)
    for stage in (3, 2, 1, 0):
        for copy in copies[stage]:
            copy.start()

    def wait(stage):
        for copy in copies[stage]:
            copy.wait()

    g1, b1, bo, g2, b2, bd = (vec_ref[base + index : base + index + 1] for index in range(6))
    gvec_ref[6:8] = jnp.zeros((2, D), f32)
    if last:
        unit3, rate3 = norm_parts(out_ref[...])
        grad_normed = nt(grad_ref[...], proj_ref[...])
        grad_out = norm_back(grad_normed, vec_ref[13:14], unit3, rate3)
        gvec_ref[6:7] = col_sum(grad_normed * unit3)
        gvec_ref[7:8] = col_sum(grad_normed)
    else:
        grad_out = grad_ref[...]
    out_low = grad_out.astype(bf16)
    unit2, rate2 = norm_parts(x1_ref[...])
    grad_h2 = jnp.zeros((VIS, D), f32)
    wait(3)
    wait(2)
    for group in range(2):
        for chunk in range(HALF_FF // CHUNK):
            part = pl.ds(group * HALF_FF + chunk * CHUNK, CHUNK)
            grad_active = nt(out_low, held[group, pl.ds(AT_D + chunk * CHUNK, CHUNK)])
            grad_before = (slope_ref[:, part] * grad_active).astype(bf16)
            packs[group][:, pl.ds(AT_U + chunk * CHUNK, CHUNK)] = grad_before
            packs[group][:, pl.ds(AT_D + chunk * CHUNK, CHUNK)] = u_ref[:, part]
            gbu_ref[:, part] = col_sum(grad_before.astype(f32))
            grad_h2 = grad_h2 + nn(grad_before, held[group, pl.ds(AT_U + chunk * CHUNK, CHUNK)])
    grad_x1 = grad_out + norm_back(grad_h2, g2, unit2, rate2)
    x1_low = grad_x1.astype(bf16)
    wait(1)
    for group in range(2):
        part = pl.ds(group * HALF, HALF)
        da[:, part] = nt(x1_low, held[group, pl.ds(AT_O, HALF)]).astype(bf16)
        packs[group][:, pl.ds(AT_O, HALF)] = a_ref[:, part]
    zero = jnp.zeros((), bf16)
    for pair in range(D // 128):
        lanes = pl.ds(pair * 128, 128)
        q, k, v = (qkv_ref[:, pl.ds(kind * D + pair * 128, 128)] for kind in range(3))
        grad = da[:, lanes]
        dq = dk = dv = jnp.zeros((VIS, 128), f32)
        for head in range(2):
            mask = half_lane(head)
            q_head = jnp.where(mask, q, zero)
            grad_head = jnp.where(mask, grad, zero)
            scores = nt(q_head, k) * SCORE
            expo = jnp.exp(scores - jnp.max(scores, 1, keepdims=True))
            probs = expo / jnp.sum(expo, 1, keepdims=True)
            grad_probs = nt(grad_head, v)
            row_total = jnp.sum(probs * grad_probs, 1, keepdims=True)
            grad_scores = (probs * (grad_probs - row_total)).astype(bf16)
            dv = dv + tn(probs.astype(bf16), grad_head)
            dk = dk + tn(grad_scores, q_head)
            dq = dq + nn(grad_scores, jnp.where(mask, k, zero))
        dqkv[:, lanes] = (dq * SCORE).astype(bf16)
        dqkv[:, pl.ds(D + pair * 128, 128)] = (dk * SCORE).astype(bf16)
        dqkv[:, pl.ds(2 * D + pair * 128, 128)] = dv.astype(bf16)
    wait(0)
    grad_h = jnp.zeros((VIS, D), f32)
    for kind in range(3):
        for group in range(2):
            grad = dqkv[:, pl.ds((2 * kind + group) * HALF, HALF)]
            rows = pl.ds(AT_Q + kind * HALF, HALF)
            packs[group][:, rows] = grad
            grad_h = grad_h + nn(grad, held[group, rows])
    unit, rate = norm_parts(x_ref[...])
    grad_x = grad_x1 + norm_back(grad_h, g1, unit, rate)
    dx_ref[...] = grad_x
    gbq_ref[0:1] = col_sum(dqkv[:, pl.ds(0, D)].astype(f32))
    gbq_ref[1:2] = col_sum(dqkv[:, pl.ds(2 * D, D)].astype(f32))
    gvec_ref[0:1] = col_sum(grad_h * unit)
    gvec_ref[1:2] = col_sum(grad_h)
    gvec_ref[2:3] = col_sum(x1_low.astype(f32))
    gvec_ref[3:4] = col_sum(grad_h2 * unit2)
    gvec_ref[4:5] = col_sum(grad_h2)
    gvec_ref[5:6] = col_sum(out_low.astype(f32))
    rights = [x1_low, out_low, h_ref[...], h2_ref[...]]
    spans = [(AT_O, HALF, 0), (AT_D, HALF_FF, 0), (AT_Q, 3 * HALF, 0), (AT_U, HALF_FF, 0)]
    if not last:
        embed_low = grad_x.astype(bf16)
        rights.append(embed_low)
        gvec_ref[6:7] = col_sum(embed_low.astype(f32))
    starts = jnp.concatenate([split3(ref[:, :D]) for ref in (start_ref, start_other_ref)], 0)
    before = 0 if last else D
    for index, right in enumerate(rights):
        for pack in packs:
            pack[:, pl.ds(RIGHT_AT + index * D, D)] = right
        inner = nt(starts, right)
        for group in range(2):
            parts = split3(fold3(inner[3 * RANK * group : 3 * RANK * (group + 1)]))
            if index == 4:
                value = fold3(nn(parts, pixels[group][...]))
                left_ref[group, :, pl.ds(0, D)] = value
            else:
                at, size, _ = spans[index]
                value = fold3(nn(parts, packs[group][:, pl.ds(at, size)]))
                left_ref[group, :, pl.ds(before + at, size)] = value


def encoder_layer_back(layer, per, grad, source, vecs, kept, starts, own, other, pixels, last=()):
    width = RIGHT_AT + (5 - layer) * D
    shapes = [
        ((VIS, D), f32),
        ((VIS, width), bf16),
        ((VIS, width), bf16),
        ((2, RANK, LAYER_ROWS + (1 - layer) * D), f32),
        ((8, D), f32),
        ((1, FF), f32),
        ((2, D), f32),
    ]
    _, h, qkv, a, x1, h2, u, slope = kept
    return pl.pallas_call(
        lambda *refs: encoder_back_kernel(layer, per, *refs),
        in_specs=[vmem_spec()] * 12 + [any_spec()] * 2 + [vmem_spec()] * (2 + len(last)),
        out_specs=[vmem_spec()] * len(shapes),
        out_shape=[jax.ShapeDtypeStruct(shape, kind) for shape, kind in shapes],
        scratch_shapes=[
            pltpu.VMEM((2, LAYER_ROWS, D), bf16),
            pltpu.SemaphoreType.DMA((MOST_COPIES,)),
            pltpu.VMEM((VIS, D), bf16),
            pltpu.VMEM((VIS, 3 * D), bf16),
        ],
        compiler_params=params(),
        name=f"encoder_back_{layer}",
    )(grad, source, vecs, h, qkv, a, x1, h2, u, slope, *starts, own, other, *pixels, *last)


HALF_ROWS = 384
ENC_ROWS = D + 2 * LAYER_ROWS


def error_factor_kernel(start_ref, error_ref, out_ref):
    turned = nt(error_ref[...], split3(start_ref[...]))
    out_ref[...] = fold3(turned.T)


def error_factor(start, error):
    rows, width = error.shape
    return pl.pallas_call(
        error_factor_kernel,
        grid=(rows // HALF_ROWS,),
        in_specs=[whole((RANK, width)), pl.BlockSpec((HALF_ROWS, width), lambda j: (j, 0))],
        out_specs=pl.BlockSpec((RANK, HALF_ROWS), lambda j: (0, j)),
        out_shape=jax.ShapeDtypeStruct((RANK, rows), f32),
        compiler_params=params(),
        name="error_factor",
    )(start, error)


def low_left(basis3):
    high, middle = basis3[:RANK], basis3[RANK : 2 * RANK]
    return jnp.concatenate([high, high, middle, jnp.zeros_like(high)], 0)


def low_right(factor3):
    high = factor3[:RANK]
    return jnp.concatenate([factor3[: 2 * RANK], high, jnp.zeros_like(high)], 0)


DEC_BLOCK = 1152


def dec_left_kernel(start_ref, start_other_ref, own_ref, other_ref, out_ref):
    for group, (begin_ref, ref) in enumerate(((start_ref, own_ref), (start_other_ref, other_ref))):
        start = split3(begin_ref[:, D:])
        grad = ref[...]
        high = grad.astype(bf16)
        rest = (grad - high.astype(f32)).astype(bf16)
        out_ref[group] = fold3(nt(start, high) + nt(start, rest))


def dec_left_factor(starts, own, other):
    rows = pl.BlockSpec((DEC_BLOCK, DD), lambda j: (j, 0))
    return pl.pallas_call(
        dec_left_kernel,
        grid=(DEC_ROWS // DEC_BLOCK,),
        in_specs=[whole((RANK, D + DD))] * 2 + [rows, rows],
        out_specs=pl.BlockSpec((2, RANK, DEC_BLOCK), lambda j: (0, 0, j)),
        out_shape=jax.ShapeDtypeStruct((2, RANK, DEC_ROWS), f32),
        compiler_params=params(),
        name="dec_left_factor",
    )(*starts, own, other)


MESH_ID = pl.DeviceIdType.MESH


def greet(workers, me, partner):
    barrier = pltpu.get_barrier_semaphore()
    for distance in range(1, workers):
        pl.semaphore_signal(
            barrier, 1, device_id={"dp": lax.rem(me + distance, workers)}, device_id_type=MESH_ID
        )
    if partner is not None:
        pl.semaphore_signal(barrier, 1, device_id={"tensor": partner}, device_id_type=MESH_ID)
    pl.semaphore_wait(barrier, workers - 1 + (partner is not None))


def sum_workers(workers, me, lanes, local, slots, sums, sems, work=lambda turn: None):
    def share(index):
        return pl.ds(pl.multiple_of(index * lanes, 128), lanes)

    def to_all(turn, source, target):
        copies = []
        for distance in range(1, workers):
            peer = lax.rem(me + distance, workers)
            copy = pltpu.make_async_remote_copy(
                src_ref=source(peer),
                dst_ref=target(distance),
                send_sem=sems.at[2 * turn, distance],
                recv_sem=sems.at[2 * turn + 1, distance],
                device_id={"dp": peer},
                device_id_type=MESH_ID,
            )
            copy.start()
            copies.append(copy)
        return copies

    copies = to_all(0, lambda peer: local.at[:, share(peer)], lambda distance: slots.at[distance])
    work(0)
    total = local[:, share(me)]
    for distance, copy in enumerate(copies, 1):
        copy.wait_recv()
        total = total + slots[distance]
    sums[:, share(me)] = total
    more = to_all(1, lambda peer: sums.at[:, share(me)], lambda distance: sums.at[:, share(me)])
    work(1)
    for copy in copies:
        copy.wait_send()
    for copy in more:
        copy.wait()


def orthonormal(left):
    place = lax.broadcasted_iota(jnp.int32, (RANK, 1), 0)
    gram = lax.dot_general(
        left, left, (((1,), (1,)), ((), ())), precision=highest_precision,
        preferred_element_type=f32,
    )
    for index in range(RANK):
        scale = lax.rsqrt(gram[index : index + 1, index : index + 1])
        column = gram[:, index : index + 1] * scale
        below = jnp.where(place > index, column, 0.0)
        pivot = left[index : index + 1] * scale
        left = jnp.where(place == index, pivot, left - below * pivot)
        gram = gram - below * (gram[index : index + 1] * scale)
    return left


def lanes_for(width, workers):
    return pl.cdiv(width, 128 * workers) * 128


RANGES = [(0, D)] + [
    (D + layer * LAYER_ROWS + at, size)
    for layer in range(2)
    for at, size in ((AT_O, HALF), (AT_D, HALF_FF), (AT_Q, 3 * HALF), (AT_U, HALF_FF))
]
LOW = 4 * RANK
LOADS = 2 * (3 + len(RANGES)) + 4 + 3
ERROR_PARTS = 4


def compress_kernel(
    workers, lanes, vec_lanes,
    first_ref, second_ref, dec_ref, error_part_ref, dec_error_part_ref, vec_ref,
    error_ref, pix_ref, pack0_ref, pack1_ref, pix_came_ref, pack0_came_ref, pack1_came_ref,
    dec_own_ref, dec_came_ref, dec_error_ref,
    enc_basis, dec_basis, enc_factor, dec_factor, vec_out, turned_out, rights_out, comb_out,
    send, came, local, slots, sums, local2, slots2, sums2, parts, dec_parts,
    held, lefts, turned, rights, comb, dec_came, dec_held,
    sems, sems2, pair_sems, load_sems, out_sems,
):
    me = lax.axis_index("dp")
    half = lax.axis_index("tensor")
    first = first_ref.shape[2]
    width = ENC_ROWS + DEC_ROWS
    clips = ((pix_ref, pack0_ref, pack1_ref), (pix_came_ref, pack0_came_ref, pack1_came_ref))

    left_loads, right_loads, error_loads, dec_loads = [], [], [], []

    def load(group, source, target):
        count = sum(len(loads) for loads in (left_loads, right_loads, error_loads, dec_loads))
        copy = pltpu.make_async_copy(source, target, load_sems.at[count])
        copy.start()
        group.append(copy)

    for clip, (pixels, pack0, pack1) in enumerate(clips):
        load(left_loads, pixels, lefts.at[clip, :, pl.ds(0, D)])
        for layer, pack in enumerate((pack0, pack1)):
            target = lefts.at[clip, :, pl.ds(D + layer * LAYER_ROWS, LAYER_ROWS)]
            load(left_loads, pack.at[:, pl.ds(0, LAYER_ROWS)], target)
    size = ENC_ROWS // ERROR_PARTS
    for index in range(ERROR_PARTS):
        block = pl.ds(index * size, size)
        load(error_loads, error_ref.at[block], held.at[block])
    for clip, (_, pack0, pack1) in enumerate(clips):
        rows = pl.ds(clip * VIS, VIS)
        load(right_loads, pack0.at[:, pl.ds(RIGHT_AT + 4 * D, D)], rights.at[0, rows])
        for layer, pack in enumerate((pack0, pack1)):
            for kind in range(4):
                target = rights.at[1 + 4 * layer + kind, rows]
                load(right_loads, pack.at[:, pl.ds(RIGHT_AT + kind * D, D)], target)
    load(dec_loads, dec_own_ref, comb)
    load(dec_loads, dec_came_ref, dec_came)
    load(dec_loads, dec_error_ref, dec_held)

    spans = ((first_ref, 0, first), (second_ref, first, ENC_ROWS - first), (dec_ref, ENC_ROWS, DEC_ROWS))
    for ref, at, size in spans:
        send[:, at : at + size] = ref[1]
    if width < workers * lanes:
        tail = jnp.zeros((RANK, workers * lanes - width), f32)
        send[:, width:] = tail
    greet(workers, me, 1 - half)
    pair = pltpu.make_async_remote_copy(
        src_ref=send,
        dst_ref=came,
        send_sem=pair_sems.at[0],
        recv_sem=pair_sems.at[1],
        device_id={"tensor": 1 - half},
        device_id_type=MESH_ID,
    )
    pair.start()
    for ref, at, size in spans[:2]:
        local[:, at : at + size] = ref[0] + error_part_ref[:, at : at + size]
    local[:, ENC_ROWS:width] = dec_ref[0] + dec_error_part_ref[...]
    if width < workers * lanes:
        local[:, width:] = tail
    pair.wait()
    local[...] += came[...]

    blocks = ENC_ROWS // HALF_ROWS
    dec_blocks = DEC_ROWS // HALF_ROWS

    def rows_of(index):
        return pl.ds(pl.multiple_of(index * HALF_ROWS, HALF_ROWS), HALF_ROWS)

    def turn(index, _):
        rows = rows_of(index)
        both = jnp.concatenate([lefts[0, :, rows], lefts[1, :, rows]], 0)
        turned[rows, 0 : 2 * VIS] = both.T
        return 0

    def combine(index, _):
        rows = rows_of(index)
        comb[rows] = comb[rows] + dec_came[rows] + dec_held[rows].astype(f32)
        return 0

    def meanwhile(phase):
        if phase == 0:
            for copy in left_loads:
                copy.wait()
            lax.fori_loop(0, blocks // 2, turn, 0)
        else:
            lax.fori_loop(blocks // 2, blocks, turn, 0)
            for copy in dec_loads:
                copy.wait()
            lax.fori_loop(0, dec_blocks, combine, 0)

    sum_workers(workers, me, lanes, local, slots, sums, sems, meanwhile)
    enc = orthonormal(sums[:, :ENC_ROWS])
    enc_basis[...] = enc
    parts[...] = split3(enc)
    dec = orthonormal(sums[:, ENC_ROWS:width])
    dec_basis[...] = dec
    dec_parts[...] = split3(dec)

    for copy in error_loads + right_loads:
        copy.wait()
    wide_rows = 2 * HALF_ROWS

    def add_error(index, total):
        rows = pl.ds(pl.multiple_of(index * wide_rows, wide_rows), wide_rows)
        return total + nn(parts[:, rows], held[rows])

    total = lax.fori_loop(0, ENC_ROWS // wide_rows, add_error, jnp.zeros((3 * RANK, D), f32))
    for index, (at, size) in enumerate(RANGES):
        rows = pl.ds(at, size)
        inner = fold3(nn(parts[:, rows], turned[rows, 0 : 2 * VIS]))
        total = total + nn(split3(inner), rights[index, 0 : 2 * VIS])
    local2[:, :D] = fold3(total)

    def add_dec(index, total):
        rows = rows_of(index)
        block = comb[rows]
        high = block.astype(bf16)
        rest = (block - high.astype(f32)).astype(bf16)
        return total + nn(dec_parts[:, rows], high) + nn(dec_parts[:, rows], rest)

    local2[:, D : D + DD] = fold3(
        lax.fori_loop(0, dec_blocks, add_dec, jnp.zeros((3 * RANK, DD), f32))
    )
    end = D + DD + vec_ref.shape[1]
    local2[:, D + DD : end] = vec_ref[...]
    if end < workers * vec_lanes:
        local2[:, end:] = jnp.zeros((RANK, workers * vec_lanes - end), f32)

    def turn_basis(index, _):
        rows = rows_of(index)
        turned[rows, 2 * VIS : 2 * VIS + LOW] = low_left(parts[:, rows]).T
        return 0

    comb_store = pltpu.make_async_copy(comb, comb_out, out_sems.at[0])
    turned_store = pltpu.make_async_copy(turned, turned_out, out_sems.at[1])
    right_store = pltpu.make_async_copy(
        rights.at[:, pl.ds(0, 2 * VIS)], rights_out.at[:, pl.ds(0, 2 * VIS)], out_sems.at[2]
    )
    low_store = pltpu.make_async_copy(
        rights.at[:, pl.ds(2 * VIS, LOW)], rights_out.at[:, pl.ds(2 * VIS, LOW)], out_sems.at[3]
    )

    def meanwhile2(phase):
        if phase == 0:
            comb_store.start()
            right_store.start()
            lax.fori_loop(0, blocks, turn_basis, 0)
            turned_store.start()

    sum_workers(workers, me, vec_lanes, local2, slots2, sums2, sems2, meanwhile2)
    factor = sums2[:, :D] * (1.0 / workers)
    enc_factor[...] = factor
    low = low_right(split3(-factor))
    for index in range(len(RANGES)):
        rights[index, 2 * VIS :] = low
    dec_mean = sums2[:, D : D + DD] * (1.0 / workers)
    dec_factor[...] = dec_mean
    low_store.start()
    vec_out[...] = sums2[:, D + DD : end] * (1.0 / workers)
    for copy in (comb_store, turned_store, right_store, low_store):
        copy.wait()


def compress(
    workers, first, second, dec, error_part, dec_error_part, vec, error, mine, came, dec_own, dec_came,
    dec_error,
):
    lanes = lanes_for(ENC_ROWS + DEC_ROWS, workers)
    vec_lanes = lanes_for(D + DD + vec.shape[1], workers)
    wide = pltpu.VMEM((RANK, workers * lanes), f32)
    wide2 = pltpu.VMEM((RANK, workers * vec_lanes), f32)
    return pl.pallas_call(
        lambda *refs: compress_kernel(workers, lanes, vec_lanes, *refs),
        in_specs=[vmem_spec()] * 6 + [any_spec()] * 10,
        out_specs=[vmem_spec()] * 5 + [any_spec()] * 3,
        out_shape=[
            jax.ShapeDtypeStruct((RANK, ENC_ROWS), f32),
            jax.ShapeDtypeStruct((RANK, DEC_ROWS), f32),
            jax.ShapeDtypeStruct((RANK, D), f32),
            jax.ShapeDtypeStruct((RANK, DD), f32),
            jax.ShapeDtypeStruct(vec.shape, f32),
            jax.ShapeDtypeStruct((ENC_ROWS, 2 * VIS + LOW), bf16),
            jax.ShapeDtypeStruct((len(RANGES), 2 * VIS + LOW, D), bf16),
            jax.ShapeDtypeStruct((DEC_ROWS, DD), f32),
        ],
        scratch_shapes=[
            wide,
            wide,
            wide,
            pltpu.VMEM((workers, RANK, lanes), f32),
            wide,
            wide2,
            pltpu.VMEM((workers, RANK, vec_lanes), f32),
            wide2,
            pltpu.VMEM((3 * RANK, ENC_ROWS), bf16),
            pltpu.VMEM((3 * RANK, DEC_ROWS), bf16),
            pltpu.VMEM((ENC_ROWS, D), bf16),
            pltpu.VMEM((2, VIS, ENC_ROWS), bf16),
            pltpu.VMEM((ENC_ROWS, 2 * VIS + LOW), bf16),
            pltpu.VMEM((len(RANGES), 2 * VIS + LOW, D), bf16),
            pltpu.VMEM((DEC_ROWS, DD), f32),
            pltpu.VMEM((DEC_ROWS, DD), f32),
            pltpu.VMEM((DEC_ROWS, DD), bf16),
            pltpu.SemaphoreType.DMA((4, workers)),
            pltpu.SemaphoreType.DMA((4, workers)),
            pltpu.SemaphoreType.DMA((2,)),
            pltpu.SemaphoreType.DMA((LOADS,)),
            pltpu.SemaphoreType.DMA((4,)),
        ],
        compiler_params=pltpu.CompilerParams(
            collective_id=1, has_side_effects=True, vmem_limit_bytes=60 << 20
        ),
        name="compress",
    )(
        first, second, dec, error_part, dec_error_part, vec, error, *mine, *came, dec_own, dec_came,
        dec_error,
    )


def new_errors_kernel(
    turned_ref, rights_ref, error_ref, comb_ref, basis_ref, factor_ref, out_ref, dec_out_ref,
    turned, rights, held, comb, dec_held, in_sems, out_sems,
):
    blocks = ENC_ROWS // HALF_ROWS
    dec_blocks = DEC_ROWS // HALF_ROWS

    def rows_of(index):
        start = index * HALF_ROWS
        if not isinstance(index, int):
            start = pl.multiple_of(start, HALF_ROWS)
        return pl.ds(start, HALF_ROWS)

    def loads(index):
        rows = rows_of(index)
        return (
            pltpu.make_async_copy(error_ref.at[rows], held.at[rows], in_sems.at[0, index]),
            pltpu.make_async_copy(turned_ref.at[rows], turned.at[rows], in_sems.at[1, index]),
        )

    def right_load(kind):
        return pltpu.make_async_copy(rights_ref.at[kind], rights.at[kind], in_sems.at[2, kind])

    def store(index):
        rows = rows_of(index)
        return pltpu.make_async_copy(held.at[rows], out_ref.at[rows], out_sems.at[index])

    comb_load = pltpu.make_async_copy(comb_ref, comb, in_sems.at[2, len(RANGES)])
    comb_load.start()
    for kind, (at, size) in enumerate(RANGES):
        right_load(kind).start()
        for index in range(at // HALF_ROWS, (at + size) // HALF_ROWS):
            for copy in loads(index):
                copy.start()
    comb_load.wait()
    dec_right = low_right(split3(-factor_ref[...]))

    def dec_residue(index, _):
        rows = rows_of(index)
        left = low_left(split3(basis_ref[:, rows]))
        dec_held[rows] = (comb[rows] + tn(left, dec_right)).astype(bf16)
        return 0

    lax.fori_loop(0, dec_blocks, dec_residue, 0)
    dec_store = pltpu.make_async_copy(dec_held, dec_out_ref, out_sems.at[blocks])
    dec_store.start()
    for kind, (at, size) in enumerate(RANGES):
        right_load(kind).wait()

        def residue(index, _, kind=kind):
            for copy in loads(index):
                copy.wait()
            rows = rows_of(index)
            value = nn(turned[rows], rights[kind]) + held[rows].astype(f32)
            held[rows] = value.astype(bf16)
            store(index).start()
            return 0

        lax.fori_loop(at // HALF_ROWS, (at + size) // HALF_ROWS, residue, 0)
    for index in range(blocks):
        store(index).wait()
    dec_store.wait()


def new_errors(turned, rights, error, dec_basis, dec_factor, comb):
    blocks = ENC_ROWS // HALF_ROWS
    return pl.pallas_call(
        new_errors_kernel,
        in_specs=[any_spec()] * 4 + [vmem_spec()] * 2,
        out_specs=[any_spec()] * 2,
        out_shape=[
            jax.ShapeDtypeStruct((ENC_ROWS, D), bf16),
            jax.ShapeDtypeStruct((DEC_ROWS, DD), bf16),
        ],
        scratch_shapes=[
            pltpu.VMEM(turned.shape, bf16),
            pltpu.VMEM(rights.shape, bf16),
            pltpu.VMEM(error.shape, bf16),
            pltpu.VMEM(comb.shape, f32),
            pltpu.VMEM(comb.shape, bf16),
            pltpu.SemaphoreType.DMA((3, blocks)),
            pltpu.SemaphoreType.DMA((blocks + 1,)),
        ],
        compiler_params=params(),
        name="new_errors",
    )(turned, rights, error, comb, dec_basis, dec_factor)


PLANE = 4
PART_Z_X_Y, PART_Z_Y_X, PART_X_Y_Z, PART_DEC = range(4)
Z_X_Y_PARTS = (PART_DEC, PART_Z_X_Y)
WAY_X, WAY_Y, WAY_UP, WAY_DOWN = range(4)
ERROR_ROWS = 1248


def gather_kernel(
    parts, planes, shard_ref, dec_shard_ref, tubes_ref, error_ref, dec_error_ref, start_ref, order_ref,
    counted_ref,
    own_ref, other_ref, pixels_ref, part_ref, dec_part_ref, picked_ref, pix_other_ref,
    pos_enc_ref, pos_dec_ref, scal_ref, proj_ref, wqkv_ref, wo_ref, wd_ref, wu_ref, wh_ref,
    held, dec_held, dec_own, dec_other, joined, pix_held,
    send_sems, recv_sems, pair_sems, sems,
):
    me = lax.axis_index("dp")
    half = lax.axis_index("tensor")
    z = me // PLANE
    column = lax.rem(me, PLANE)
    column_x = column + 1 - 2 * lax.rem(column, 2)
    column_y = lax.rem(column + 2, PLANE)
    column_xy = lax.rem(column_x + 2, PLANE)
    up = z < planes - 1
    down = z > 0
    peers = (
        z * PLANE + column_x,
        z * PLANE + column_y,
        jnp.minimum(me + PLANE, PLANE * planes - 1),
        jnp.maximum(me - PLANE, 0),
    )
    rows = [pl.ds(at, size) for at, size in parts]

    def place(part, slot):
        return dec_own.at[slot] if part == PART_DEC else own_ref.at[slot, rows[part]]

    def copy(way, part, slot, mine=False):
        source = place(part, slot)
        if mine:
            source = dec_shard_ref if part == PART_DEC else shard_ref.at[rows[part]]
        return pltpu.make_async_remote_copy(
            src_ref=source,
            dst_ref=place(part, slot),
            send_sem=send_sems.at[way, part, slot],
            recv_sem=recv_sems.at[part, slot],
            device_id={"dp": peers[way]},
            device_id_type=MESH_ID,
        )

    def send(way, part, slot, mine=False):
        copy(way, part, slot, mine).start()

    def recv(part, slot):
        copy(WAY_X, part, slot).wait_recv()

    def pair(part, plane):
        block = pl.ds(plane * PLANE, PLANE)
        if part == PART_DEC:
            source, target = dec_own.at[block], dec_other.at[block]
        else:
            source, target = own_ref.at[block, rows[part]], other_ref.at[block, rows[part]]
        return pltpu.make_async_remote_copy(
            src_ref=source,
            dst_ref=target,
            send_sem=pair_sems.at[0, part, plane],
            recv_sem=pair_sems.at[1, part, plane],
            device_id={"tensor": 1 - half},
            device_id_type=MESH_ID,
        )

    def load(index):
        return pltpu.make_async_copy(
            error_ref.at[pl.ds(index * ERROR_ROWS, ERROR_ROWS)], held.at[index % 2], sems.at[index % 2]
        )

    load(0).start()
    load(1).start()
    dec_load = pltpu.make_async_copy(dec_error_ref, dec_held, sems.at[2])
    dec_load.start()

    barrier = pltpu.get_barrier_semaphore()
    for way in (WAY_X, WAY_Y):
        pl.semaphore_signal(barrier, 1, device_id={"dp": peers[way]}, device_id_type=MESH_ID)
    pl.semaphore_signal(barrier, 1, device_id={"tensor": 1 - half}, device_id_type=MESH_ID)
    for ok, way in ((up, WAY_UP), (down, WAY_DOWN)):

        @pl.when(ok)
        def _(way=way):
            pl.semaphore_signal(barrier, 1, device_id={"dp": peers[way]}, device_id_type=MESH_ID)

    pl.semaphore_wait(barrier, 3 + up.astype(jnp.int32) + down.astype(jnp.int32))

    def both_z(part, slot, mine=False):
        @pl.when(up)
        def _():
            send(WAY_UP, part, slot, mine)

        @pl.when(down)
        def _():
            send(WAY_DOWN, part, slot, mine)

    def sides(distance):
        return [
            ((z + side * distance >= 0) & (z + side * distance < planes), z + side * distance, on, way)
            for side, on, way in ((-1, up, WAY_UP), (1, down, WAY_DOWN))
        ]

    def along(distance):
        for there, plane, on, way in sides(distance):

            @pl.when(there)
            def _(slot=plane * PLANE + column, on=on, way=way):
                for part in Z_X_Y_PARTS + (PART_Z_Y_X,):
                    recv(part, slot)

                    @pl.when(on)
                    def _():
                        send(way, part, slot)

                    send(WAY_Y if part == PART_Z_Y_X else WAY_X, part, slot)
                for part in Z_X_Y_PARTS:
                    send(WAY_Y, part, slot)
                send(WAY_X, PART_Z_Y_X, slot)

    def cross(distance):
        for there, plane, _, _ in sides(distance):

            @pl.when(there)
            def _(base=plane * PLANE):
                for part in Z_X_Y_PARTS:
                    recv(part, base + column_x)
                    send(WAY_Y, part, base + column_x)
                recv(PART_Z_Y_X, base + column_y)
                send(WAY_X, PART_Z_Y_X, base + column_y)

    def finish(distance):
        for there, plane, _, _ in sides(distance)[: 2 if distance else 1]:

            @pl.when(there)
            def _(plane=plane, base=plane * PLANE):
                for part in Z_X_Y_PARTS:
                    recv(part, base + column_y)
                    recv(part, base + column_xy)
                    pair(part, plane).start()
                recv(PART_Z_Y_X, base + column_x)
                recv(PART_Z_Y_X, base + column_xy)
                pair(PART_Z_Y_X, plane).start()

    def whole_plane(distance):
        for there, plane, on, way in sides(distance):

            @pl.when(there)
            def _(plane=plane, on=on, way=way):
                for index in range(PLANE):
                    slot = plane * PLANE + index
                    recv(PART_X_Y_Z, slot)

                    @pl.when(on)
                    def _(slot=slot):
                        send(way, PART_X_Y_Z, slot)

                pair(PART_X_Y_Z, plane).start()

    workers = planes * PLANE
    start3 = split3(start_ref[:, :D])
    chunks = error_ref.shape[0] // ERROR_ROWS

    def work(index):
        load(index).wait()
        lanes = pl.ds(index * ERROR_ROWS, ERROR_ROWS)
        part_ref[:, lanes] = fold3(nt(start3, held[index % 2]))
        if index + 2 < chunks:
            load(index + 2).start()

    send(WAY_X, PART_X_Y_Z, me, True)
    send(WAY_Y, PART_X_Y_Z, me, True)
    for part in (PART_DEC, PART_Z_X_Y, PART_Z_Y_X):
        both_z(part, me, True)
    for part in Z_X_Y_PARTS:
        send(WAY_X, part, me, True)
    send(WAY_Y, PART_Z_Y_X, me, True)
    send(WAY_X, PART_Z_Y_X, me, True)
    for part in Z_X_Y_PARTS:
        send(WAY_Y, part, me, True)
    keeps = [
        pltpu.make_async_copy(shard_ref, own_ref.at[me], sems.at[3]),
        pltpu.make_async_copy(dec_shard_ref, dec_own.at[me], sems.at[6]),
    ]
    for keep in keeps:
        keep.start()
    swap_pixels = pltpu.make_async_remote_copy(
        src_ref=tubes_ref.at[1 - half],
        dst_ref=pixels_ref,
        send_sem=sems.at[4],
        recv_sem=sems.at[5],
        device_id={"tensor": 1 - half},
        device_id_type=MESH_ID,
    )
    swap_pixels.start()
    loads = [
        pltpu.make_async_copy(tubes_ref.at[index], pix_held.at[clip], sems.at[7 + clip])
        for clip, index in ((0, half), (1, 1 - half))
    ]
    for get in loads:
        get.start()
    work(0)
    near = z * PLANE
    recv(PART_X_Y_Z, near + column_x)
    send(WAY_Y, PART_X_Y_Z, near + column_x)
    for part in Z_X_Y_PARTS:
        recv(part, near + column_x)
        send(WAY_Y, part, near + column_x)
    recv(PART_Z_Y_X, near + column_y)
    send(WAY_X, PART_Z_Y_X, near + column_y)
    for keep in keeps:
        keep.wait()
    place_index = lax.broadcasted_iota(jnp.int32, (1, TUBES), 1)
    for clip, index in ((0, half), (1, 1 - half)):
        loads[clip].wait()
        hot = jnp.where(order_ref[index] == place_index, 1.0, 0.0).astype(bf16)
        picked_ref[clip] = nn(hot, pix_held[clip]).astype(bf16)
    swap_picked = pltpu.make_async_remote_copy(
        src_ref=picked_ref.at[1],
        dst_ref=pix_other_ref,
        send_sem=sems.at[9],
        recv_sem=sems.at[10],
        device_id={"tensor": 1 - half},
        device_id_type=MESH_ID,
    )
    swap_picked.start()
    work(1)
    along(1)
    recv(PART_X_Y_Z, near + column_y)
    recv(PART_X_Y_Z, near + column_xy)
    for index in range(PLANE):
        both_z(PART_X_Y_Z, near + index)
    pair(PART_X_Y_Z, z).start()
    work(2)
    cross(1)
    finish(0)
    pos_enc_ref[...] = sinusoid_of(order_ref[half].astype(f32), D)
    work(3)
    along(2)
    first_place = lax.broadcasted_iota(jnp.int32, (TUBES // 32, 1), 0).astype(f32) * 32.0
    second_place = lax.broadcasted_iota(jnp.int32, (32, 1), 0).astype(f32)
    rate, even = rates(DD)
    first = first_place * rate
    second = second_place * rate
    ahead = jnp.where(even, jnp.sin(first), jnp.cos(first))
    turned = jnp.where(even, jnp.cos(first), -jnp.sin(first))
    cos2, sin2 = jnp.cos(second), jnp.sin(second)
    for index in range(TUBES // 32):
        pos_dec_ref[pl.ds(32 * index, 32)] = (
            ahead[index : index + 1] * cos2 + turned[index : index + 1] * sin2
        )
    work(4)
    whole_plane(1)
    cross(2)
    work(5)
    finish(1)
    along(3)
    work(6)
    whole_plane(2)
    cross(3)
    work(7)
    finish(2)
    dec_load.wait()
    dec_part_ref[...] = fold3(nt(split3(start_ref[:, D:]), dec_held[...]))
    whole_plane(3)
    finish(3)
    for plane in range(planes):
        pair(PART_DEC, plane).wait()
    total = jnp.zeros((1, 128), f32)
    per = joined.shape[1] // workers
    for index in range(workers):
        for group, ref in enumerate((dec_own, dec_other)):
            block = ref[index].astype(f32)
            joined[group, pl.ds(index * per, per)] = block[:per]
            if group == 0:
                total = total + block[per : per + 1, :128]
    for group in range(2):

        def matrix(at, size):
            return joined[group, pl.ds(at, size)].astype(bf16)

        wo_ref[pl.ds(group * DD // 2, DD // 2)] = matrix(DEC_O, DD // 2)
        for kind in range(3):
            wqkv_ref[pl.ds((2 * kind + group) * DD // 2, DD // 2)] = matrix(
                DEC_Q + kind * DD // 2, DD // 2
            )
        for ref, at in ((wd_ref, DEC_D), (wu_ref, DEC_U), (wh_ref, DEC_H)):
            ref[pl.ds(group * DFF // 2, DFF // 2)] = matrix(at, DFF // 2)
        proj_ref[half if group == 0 else 1 - half] = matrix(0, D // 2)
    counted = counted_ref[half]
    scal_ref[0:1] = jnp.zeros((1, 128), f32) + counted
    scal_ref[1:2] = counted * (2.0 * workers / PIX) / (MASKED * total)
    scal_ref[2:3] = MASKED * total
    scal_ref[3:8] = jnp.zeros((5, 128), f32)
    swap_pixels.wait()
    swap_picked.wait()
    for plane in range(planes):
        for part in range(3):
            pair(part, plane).wait()
        for index in range(PLANE):
            slot = plane * PLANE + index

            @pl.when(column == index)
            def _():
                for part in (PART_DEC, PART_Z_X_Y, PART_Z_Y_X):
                    copy(WAY_X, part, slot).wait_send()
                    copy(WAY_Y, part, slot).wait_send()

            @pl.when(column_x == index)
            def _():
                for part in Z_X_Y_PARTS:
                    copy(WAY_Y, part, slot).wait_send()

            @pl.when(column_y == index)
            def _():
                copy(WAY_X, PART_Z_Y_X, slot).wait_send()

            for part in range(4):
                sent = True if part == PART_X_Y_Z else column == index

                @pl.when(up & (plane <= z) & sent)
                def _():
                    copy(WAY_UP, part, slot).wait_send()

                @pl.when(down & (plane >= z) & sent)
                def _():
                    copy(WAY_DOWN, part, slot).wait_send()

    copy(WAY_X, PART_X_Y_Z, me).wait_send()
    copy(WAY_Y, PART_X_Y_Z, me).wait_send()
    copy(WAY_Y, PART_X_Y_Z, near + column_x).wait_send()


def gather_weights(planes, shard, dec_shard, tubes, error, dec_error, start, order, counted):
    workers = planes * PLANE
    size = shard.shape[0]
    same = dec_shard.shape[0] * DD // D
    long = (size + same) * 2 // 5 // 16 * 16 + 16
    parts = ((0, long - same), (long - same, long), (2 * long - same, size - 2 * long + same))
    shards = jax.ShapeDtypeStruct((workers,) + shard.shape, shard.dtype)
    low = lambda *shape: jax.ShapeDtypeStruct(shape, bf16)
    wide = lambda *shape: jax.ShapeDtypeStruct(shape, f32)
    dec_shards = pltpu.VMEM((workers,) + dec_shard.shape, bf16)
    return pl.pallas_call(
        lambda *refs: gather_kernel(parts, planes, *refs),
        in_specs=[any_spec()] * 5
        + [vmem_spec()] * 2
        + [pl.BlockSpec(memory_space=pltpu.SMEM)],
        out_specs=[any_spec()] * 3 + [vmem_spec()] * 13,
        out_shape=[
            shards,
            shards,
            jax.ShapeDtypeStruct(tubes.shape[1:], tubes.dtype),
            wide(RANK, error.shape[0]),
            wide(RANK, dec_error.shape[0]),
            low(2, VIS, D),
            low(VIS, D),
            wide(VIS, D),
            wide(TUBES, DD),
            wide(8, 128),
            low(2, D // 2, DD),
            low(3 * DD, DD),
            low(DD, DD),
            low(DFF, DD),
            low(DFF, DD),
            low(PIX, DD),
        ],
        scratch_shapes=[
            pltpu.VMEM((2, ERROR_ROWS, D), bf16),
            pltpu.VMEM(dec_error.shape, bf16),
            dec_shards,
            dec_shards,
            pltpu.VMEM((2, DEC_ROWS, DD), f32),
            pltpu.VMEM((2, TUBES, D), bf16),
            pltpu.SemaphoreType.DMA((4, 4, workers)),
            pltpu.SemaphoreType.DMA((4, workers)),
            pltpu.SemaphoreType.DMA((2, 4, planes)),
            pltpu.SemaphoreType.DMA((11,)),
        ],
        compiler_params=pltpu.CompilerParams(
            collective_id=3, has_side_effects=True, vmem_limit_bytes=BIG_VMEM
        ),
        name="gather_weights",
    )(shard, dec_shard, tubes, error, dec_error, start, order, counted)


def cut(block, widths):
    pieces = []
    start = 0
    for width in widths:
        pieces.append(block[start : start + width])
        start = start + width
    return pieces


def swap(value):
    return lax.ppermute(value, "tensor", [(0, 1), (1, 0)])


def per_device(
    tubes,
    tube_order,
    clip_mask,
    enc_weights,
    dec_weights,
    vec_split,
    vec_shared,
    enc_moment,
    dec_moment,
    split_moment,
    shared_moment,
    enc_error,
    dec_error,
    factors,
):
    workers = lax.axis_size("dp")
    half = lax.axis_index("tensor")
    worker_index = lax.axis_index("dp")
    mine = lambda both: lax.dynamic_index_in_dim(both, half, 0, keepdims=False)
    which = half.astype(jnp.int32)[None]
    counted_all = clip_mask.astype(f32)
    counted = mine(counted_all)
    enc_per = enc_weights.shape[1]
    dec_per = dec_weights.shape[1]
    spare = -(dec_per + 1) % 16 + 1
    shard = enc_weights[0].astype(bf16)
    dec_shard = jnp.concatenate(
        [
            dec_weights[0].astype(bf16),
            jnp.broadcast_to(jnp.sum(counted_all).astype(bf16), (spare, DD)),
        ],
        0,
    )
    start_own = factors[0]
    start_other = swap(start_own)
    starts = (start_own, start_other)
    splits = (vec_split, swap(vec_split))
    dec_at = 2 * (2 * HALF + HALF_FF)
    bq, bv, bu, bh = (
        jnp.concatenate([split[:, at : at + size] for split in splits], 1)
        for at, size in (
            (dec_at, DD // 2),
            (dec_at + DD // 2, DD // 2),
            (dec_at + DD, DFF // 2),
            (dec_at + DD + DFF // 2, PIX // 2),
        )
    )
    bqkv = jnp.concatenate([bq, jnp.zeros_like(bq), bv], 1)
    wide = vec_shared[: 15 * D].reshape(15, D)
    narrow = vec_shared[15 * D :].reshape(9, DD)
    visible = mine(tube_order)[None, :VIS]
    if workers == 4 * PLANE:
        per = enc_per
        (
            enc_own, enc_other, pixels, enc_error_part, dec_error_part, picked, pix_vis_other,
            pos_enc, pos_dec, scal, proj, d_qkv, d_out, d_down, d_up, head_rows,
        ) = gather_weights(
            workers // PLANE, shard, dec_shard, tubes, enc_error[0, 0], dec_error[0, 0], start_own,
            tube_order[:, :VIS, None], counted_all,
        )
        proj = proj.reshape(D, DD)
        loss_weight = scal[2, 0]
    else:
        picked = pick_visible(which, tube_order, tubes)
        pix_vis_other = swap(picked[1])
        own = lax.all_gather(shard, "dp", axis=0)
        dec_all = lax.all_gather(dec_shard, "dp", axis=0)
        pixels = swap(lax.dynamic_index_in_dim(tubes, 1 - half, 0, keepdims=False))
        per = enc_per * workers
        enc_own = own.reshape(1, per, D)
        enc_other = swap(enc_own)
        enc_error_part = error_factor(start_own[:, :D], enc_error[0, 0])
        dec_error_part = error_factor(start_own[:, D:], dec_error[0, 0])
        dec_own = dec_all[:, :dec_per].reshape(DEC_ROWS, DD)
        dec_other = swap(dec_own)
        loss_weight = MASKED * jnp.sum(dec_all[:, dec_per, 0].astype(f32))
        dec_widths = [D // 2, DD // 2, DFF // 2, 3 * DD // 2, DFF // 2, PIX // 2]
        own_parts = cut(dec_own, dec_widths)
        other_parts = cut(dec_other, dec_widths)
        proj = jnp.where(
            half == 0,
            jnp.concatenate([own_parts[0], other_parts[0]], 0),
            jnp.concatenate([other_parts[0], own_parts[0]], 0),
        )
        d_out, d_down, d_up, head_rows = (
            jnp.concatenate([own_parts[index], other_parts[index]], 0) for index in (1, 2, 4, 5)
        )
        kinds = lambda block: block.reshape(3, DD // 2, DD)
        d_qkv = jnp.concatenate([kinds(own_parts[3]), kinds(other_parts[3])], 1)
        d_qkv = d_qkv.reshape(3 * DD, DD)
        pos_enc = sinusoid_of(visible.reshape(VIS, 1).astype(f32), D)
        pos_dec = sinusoid_of(jnp.arange(TUBES).astype(f32)[:, None], DD)
        scal = jnp.broadcast_to(
            jnp.stack([counted, 2.0 * workers / (PIX * loss_weight) * counted] + [counted] * 6)[
                :, None
            ],
            (8, 128),
        )
    pix_vis = picked[0]

    stream0, *kept0 = encoder_layer(
        0, per, (pix_vis, pix_vis_other, pos_enc), wide, splits, enc_own, enc_other
    )
    stream1 = kept0[0]
    enc_normed, latent, *kept1 = encoder_layer(
        1, per, (stream1, proj), wide, splits, enc_own, enc_other
    )
    kept = [(stream0, kept0), (stream1, kept1)]

    dec_start, h, qkv, hidden = decoder_qkv(
        visible, pos_dec, latent, narrow, d_qkv, bqkv
    )
    mixed, logs = attend(qkv)
    grad_mixed, grad_middle, dec_grads, dec_sent, g_vec, g_bu, g_bh, loss_lanes = decoder_tokens(
        which, mixed, dec_start, tubes, pixels, hidden, scal, narrow, bu, bh, d_out, d_down, d_up,
        head_rows,
    )
    dq, dk, dv = attend_back(qkv, mixed, grad_mixed, logs)
    latent_low, dec_grads, dec_sent, g_vec1 = decoder_qkv_back(
        which, visible, dq, dk, dv, h, dec_start, grad_middle, narrow, d_qkv, enc_normed,
        dec_grads, dec_sent,
    )
    dec_left = dec_left_factor(starts, dec_grads, dec_sent)
    dec_came = swap(dec_sent)

    grad = latent_low
    packs = [None, None]
    came = [None, None]
    enc_lefts = [None, None]
    enc_vec_grads = [None, None]
    for layer in (1, 0):
        source, result = kept[layer]
        grad, packs[layer], sent, enc_lefts[layer], *enc_vec_grads[layer] = encoder_layer_back(
            layer, per, grad, source, wide, result, starts, enc_own, enc_other,
            (pix_vis, pix_vis_other), (result[0], proj) if layer == 1 else (),
        )
        came[layer] = swap(sent)
    mine_packs = (pix_vis, packs[0], packs[1])
    their_packs = (picked[1], came[0], came[1])

    def split_half(index):
        pieces = []
        for layer in range(2):
            _, g_hidden, g_qv = enc_vec_grads[layer]
            pieces += [
                cut(g_qv[0], [HALF] * 2)[index],
                cut(g_qv[1], [HALF] * 2)[index],
                cut(g_hidden[0], [HALF_FF] * 2)[index],
            ]
        pieces += [
            cut(g_vec1[0], [DD // 2] * 2)[index],
            cut(g_vec1[1], [DD // 2] * 2)[index],
            cut(g_bu[0], [DFF // 2] * 2)[index],
            cut(g_bh[0], [PIX // 2] * 2)[index],
        ]
        return jnp.concatenate(pieces)

    g_vec_enc = [grads[0] for grads in enc_vec_grads]
    shared_grad = jnp.concatenate(
        [g_vec_enc[0][6], g_vec_enc[0][:6].reshape(-1), g_vec_enc[1].reshape(-1)]
        + [g_vec1[4], g_vec1[2], g_vec1[3], g_vec[:6].reshape(-1)]
    )
    loss_part = jnp.sum(loss_lanes) / PIX
    split_len = vec_split.shape[1]
    length = split_len + shared_grad.shape[0] + 1
    vec_lanes = pl.cdiv(length, RANK * 128) * 128
    fill = jnp.zeros((RANK * vec_lanes - length,), f32)
    sent = jnp.concatenate([split_half(1), shared_grad, loss_part[None], fill])
    local = jnp.concatenate([split_half(0), shared_grad, loss_part[None], fill])
    vec_local = (local + swap(sent)).reshape(RANK, vec_lanes)

    enc_basis, dec_basis, enc_right, dec_right, vec_mean, turned, rights, dec_comb = compress(
        workers, enc_lefts[0], enc_lefts[1], dec_left, enc_error_part, dec_error_part, vec_local,
        enc_error[0, 0], mine_packs, their_packs, dec_grads, dec_came, dec_error[0, 0],
    )
    enc_error_new, dec_error_new = new_errors(
        turned, rights, enc_error[0, 0], dec_basis, dec_right, dec_comb
    )
    vec_mean = vec_mean.reshape(-1)
    enc_rows = enc_basis.shape[1] // workers
    dec_rows = dec_basis.shape[1] // workers
    enc_owned = lax.dynamic_slice_in_dim(enc_basis, worker_index * enc_rows, enc_rows, 1)
    dec_owned = lax.dynamic_slice_in_dim(dec_basis, worker_index * dec_rows, dec_rows, 1)
    enc_mom = momentum_keep * enc_moment[0] + jnp.einsum(
        "rx,rc->xc", enc_owned, enc_right, precision=highest_precision
    )
    dec_mom = momentum_keep * dec_moment[0] + jnp.einsum(
        "rx,rc->xc", dec_owned, dec_right, precision=highest_precision
    )
    split_mom = momentum_keep * split_moment[0] + vec_mean[:split_len]
    shared_mom = momentum_keep * shared_moment + vec_mean[split_len : length - 1]
    return (
        vec_mean[length - 1] * workers,
        loss_weight,
        (enc_weights[0] - step_rate * enc_mom)[None],
        enc_mom[None],
        enc_error_new[None, None],
        (dec_weights[0] - step_rate * dec_mom)[None],
        dec_mom[None],
        dec_error_new[None, None],
        jnp.concatenate([enc_right, dec_right], 1)[None],
        (vec_split[0] - step_rate * split_mom)[None],
        split_mom[None],
        vec_shared - step_rate * shared_mom,
        shared_mom,
    )


def solution(mesh):
    placed = (
        P("dp", None, "tensor"),
        P("dp", None),
        P("dp"),
        P("tensor", "dp", None),
        P("tensor", "dp", None),
        P("tensor", None),
        P(),
        P("tensor", "dp", None),
        P("tensor", "dp", None),
        P("tensor", None),
        P(),
        P("dp", "tensor", None, None),
        P("dp", "tensor", None, None),
        P("tensor", None, None),
    )
    return jax.shard_map(
        per_device,
        mesh=mesh,
        in_specs=placed,
        out_specs=(
            P(),
            P(),
            P("tensor", "dp", None),
            P("tensor", "dp", None),
            P("dp", "tensor", None, None),
            P("tensor", "dp", None),
            P("tensor", "dp", None),
            P("dp", "tensor", None, None),
            P("tensor", None, None),
            P("tensor", None),
            P("tensor", None),
            P(),
            P(),
        ),
        check_vma=False,
    )
```

```python
import math

import jax
import jax.numpy as jnp
from jax import lax
from jax.experimental import pallas as pl
from jax.experimental.pallas import tpu as pltpu
from jax.sharding import PartitionSpec as P

D = 768
HEAD_DIM = 64
FF = 3072
DD = 384
DFF = 1536
PIX = 1536
TUBES = 1568
VIS = 160
MASKED = 1408
RANK = 8

f32 = jnp.float32
bf16 = jnp.bfloat16
highest_precision = lax.Precision.HIGHEST
norm_eps = 1e-06
momentum_keep = 0.9
step_rate = 1000.0
LOG2E = 1.4426950408889634
SCORE = HEAD_DIM ** (-0.5)
BIG_VMEM = 56 << 20


def nn(left, right):
    return lax.dot_general(left, right, (((1,), (0,)), ((), ())), preferred_element_type=f32)


def nt(left, right):
    return lax.dot_general(left, right, (((1,), (1,)), ((), ())), preferred_element_type=f32)


def tn(left, right):
    return lax.dot_general(left, right, (((0,), (0,)), ((), ())), preferred_element_type=f32)


def ahead(count, product):
    value = product(0)
    for index in range(count):
        later = product(index + 1) if index + 1 < count else None
        yield index, value
        value = later


def col_sum(value):
    return jnp.sum(value, 0, keepdims=True)


def norm_parts(stream):
    center = stream - jnp.mean(stream, -1, keepdims=True)
    rate = lax.rsqrt(jnp.mean(center * center, -1, keepdims=True) + norm_eps)
    return center * rate, rate


def norm_back(grad, gain, unit, rate):
    grad_unit = grad * gain
    return rate * (
        grad_unit
        - jnp.mean(grad_unit, -1, keepdims=True)
        - unit * jnp.mean(grad_unit * unit, -1, keepdims=True)
    )


def gelu_pair(before):
    cdf_tail = jnp.exp(-0.5 * before * before)
    size = jnp.abs(before) * (2.0 ** -0.5)
    t = 1.0 / (1.0 + 0.3275911 * size)
    poly = t * (
        0.254829592 + t * (-0.284496736 + t * (1.421413741 + t * (-1.453152027 + t * 1.061405429)))
    )
    tail = 0.5 * poly * cdf_tail
    cdf = jnp.where(before < 0, tail, 1.0 - tail)
    return before * cdf, cdf + before * cdf_tail * (1.0 / math.sqrt(2.0 * math.pi))


def split3(value):
    high = value.astype(bf16)
    rest = value - high.astype(f32)
    middle = rest.astype(bf16)
    low = (rest - middle.astype(f32)).astype(bf16)
    return jnp.concatenate([high, middle, low], 0)


def fold3(value):
    rows = value.shape[0] // 3
    return value[:rows] + value[rows : 2 * rows] + value[2 * rows :]


def rates(width):
    column = lax.broadcasted_iota(jnp.int32, (1, width), 1)
    low_bit = lax.rem(column, 2)
    rate = jnp.exp((column - low_bit).astype(f32) * (-math.log(10000.0) / width))
    return rate, low_bit == 0


def sinusoid_of(place, width):
    rate, even = rates(width)
    angle = place * rate
    return jnp.where(even, jnp.sin(angle), jnp.cos(angle))


def params(**more):
    return pltpu.CompilerParams(vmem_limit_bytes=BIG_VMEM, **more)


def whole(shape):
    return pl.BlockSpec(shape, lambda *_: (0,) * len(shape))


def any_spec():
    return pl.BlockSpec(memory_space=pl.ANY)


def vmem_spec():
    return pl.BlockSpec(memory_space=pltpu.VMEM)


def pick_kernel(half_ref, order_ref, tubes_ref, out_ref):
    column = lax.broadcasted_iota(jnp.int32, (1, TUBES), 1)
    hot = jnp.where(order_ref[0] == column, 1.0, 0.0).astype(bf16)
    out_ref[0] = nn(hot, tubes_ref[0]).astype(bf16)


def pick_visible(half, order, tubes):
    clips, _, width = tubes.shape
    which = lambda c, half_ref: jnp.where(c == 0, half_ref[0], 1 - half_ref[0])
    return pl.pallas_call(
        pick_kernel,
        grid_spec=pltpu.PrefetchScalarGridSpec(
            num_scalar_prefetch=1,
            grid=(clips,),
            in_specs=[
                pl.BlockSpec((1, VIS, 1), lambda c, half_ref: (which(c, half_ref), 0, 0)),
                pl.BlockSpec((1, TUBES, width), lambda c, half_ref: (which(c, half_ref), 0, 0)),
            ],
            out_specs=pl.BlockSpec((1, VIS, width), lambda c, half_ref: (c, 0, 0)),
        ),
        out_shape=jax.ShapeDtypeStruct((clips, VIS, width), bf16),
        compiler_params=params(),
        name="pick_visible",
    )(half, order[:, :VIS, None], tubes)


QKV_ROWS = 392


def place_matrix(order, rows):
    place = lax.broadcasted_iota(jnp.int32, (rows, 1), 0) + pl.program_id(0) * rows
    return jnp.where(order == place, 1.0, 0.0)


def qkv_kernel(order_ref, pos_ref, latent_ref, vec_ref, w_ref, bias_ref, x_ref, h_ref, qkv_ref, hidden_ref):
    token, gain, shift = (vec_ref[index : index + 1] for index in range(3))
    places = place_matrix(order_ref[...], QKV_ROWS)
    hidden = 1.0 - jnp.sum(places, 1, keepdims=True)
    hidden_ref[...] = hidden
    latent = split3(latent_ref[...])
    places = places.astype(bf16)
    shown = sum(nn(places, latent[VIS * part : VIS * (part + 1)]) for part in (2, 1, 0))
    x = pos_ref[...] + (shown + hidden * token)
    x_ref[...] = x
    unit, _ = norm_parts(x)
    h = (unit * gain + shift).astype(bf16)
    h_ref[...] = h
    qkv_ref[...] = (nt(h, w_ref[...]) + bias_ref[...]).astype(bf16)


def decoder_qkv(order, pos, latent, vecs, weights, bias):
    rows = lambda width: pl.BlockSpec((QKV_ROWS, width), lambda i: (i, 0))
    return pl.pallas_call(
        qkv_kernel,
        grid=(TUBES // QKV_ROWS,),
        in_specs=[
            whole((1, VIS)),
            rows(DD),
            whole((VIS, DD)),
            whole(vecs.shape),
            whole((3 * DD, DD)),
            whole((1, 3 * DD)),
        ],
        out_specs=[rows(DD), rows(DD), rows(3 * DD), rows(1)],
        out_shape=[
            jax.ShapeDtypeStruct((TUBES, DD), f32),
            jax.ShapeDtypeStruct((TUBES, DD), bf16),
            jax.ShapeDtypeStruct((TUBES, 3 * DD), bf16),
            jax.ShapeDtypeStruct((TUBES, 1), f32),
        ],
        compiler_params=params(),
        name="decoder_qkv",
    )(order, pos, latent, vecs, weights, bias)


PAIRS = DD // 128


def half_lane(index):
    return lax.broadcasted_iota(jnp.int32, (1, 128), 1) // HEAD_DIM == index


ATTEND_ROWS = 784


def attend_kernel(q_ref, k_ref, v_ref, o_ref, lse_ref):
    k = k_ref[...]
    v_one = jnp.concatenate([v_ref[...], jnp.ones((TUBES, 128), bf16)], 1)
    turns = [(at, head) for at in range(0, TUBES, ATTEND_ROWS) for head in range(2)]

    def scores_of(turn):
        at, head = turn
        q = q_ref[pl.ds(at, ATTEND_ROWS)]
        return nt(jnp.where(half_lane(head), q, jnp.zeros_like(q)), k)

    mixed, logs = [], []
    scores = scores_of(turns[0])
    for index, (at, head) in enumerate(turns):
        later = scores_of(turns[index + 1]) if index + 1 < len(turns) else None
        top = jnp.max(scores, 1, keepdims=True)
        expo = jnp.exp2((scores - top) * (SCORE * LOG2E)).astype(bf16)
        both = nn(expo, v_one)
        total = both[:, 128:]
        mixed.append(both[:, :128] / total)
        logs.append(top * (SCORE * LOG2E) + jnp.log2(total))
        if head == 1:
            rows = pl.ds(at, ATTEND_ROWS)
            o_ref[rows] = jnp.where(half_lane(0), mixed[-2], mixed[-1])
            lse_ref[0, rows] = jnp.where(half_lane(0), logs[-2], logs[-1])
        scores = later


def attend(qkv):
    pair = lambda kind: pl.BlockSpec((TUBES, 128), lambda p: (0, kind * PAIRS + p))
    return pl.pallas_call(
        attend_kernel,
        grid=(PAIRS,),
        in_specs=[pair(0), pair(1), pair(2)],
        out_specs=[pair(0), pl.BlockSpec((1, TUBES, 128), lambda p: (p, 0, 0))],
        out_shape=[
            jax.ShapeDtypeStruct((TUBES, DD), f32),
            jax.ShapeDtypeStruct((PAIRS, TUBES, 128), f32),
        ],
        compiler_params=params(),
        name="attend",
    )(qkv, qkv, qkv)


def attend_back_kernel(q_ref, k_ref, v_ref, o_ref, do_ref, lse_ref, dq_ref, dk_ref, dv_ref):
    q, k, v, grad = q_ref[...], k_ref[...], v_ref[...], do_ref[...]
    k_turned = k.T
    dots = o_ref[...] * grad.astype(f32)
    logs = lse_ref[0].T
    select = (
        lax.broadcasted_iota(jnp.int32, (8, 128), 1) // HEAD_DIM
        == lax.broadcasted_iota(jnp.int32, (8, 128), 0)
    ).astype(f32)
    row_total = lax.dot_general(
        select, dots, (((1,), (1,)), ((), ())), precision=highest_precision,
        preferred_element_type=f32,
    )
    zero = jnp.zeros((), bf16)
    dk = dv = jnp.zeros((TUBES, 128), f32)
    turned = []
    for head in range(2):
        mask = half_lane(head)
        q_head = jnp.where(mask, q, zero)
        grad_head = jnp.where(mask, grad, zero)
        low = head * HEAD_DIM
        probs = jnp.exp2(nt(k, q_head) * (SCORE * LOG2E) - logs[low : low + 1])
        grad_scores = (probs * (nt(v, grad_head) - row_total[head : head + 1])).astype(bf16)
        dv = dv + nn(probs.astype(bf16), grad_head)
        dk = dk + nn(grad_scores, q_head)
        turned.append(nn(k_turned[low : low + HEAD_DIM], grad_scores))
    dq_ref[...] = (jnp.concatenate(turned, 0).T * SCORE).astype(bf16)
    dk_ref[...] = (dk * SCORE).astype(bf16)
    dv_ref[...] = dv.astype(bf16)


def attend_back(qkv, mixed, grad_mixed, logs):
    pair = lambda kind: pl.BlockSpec((TUBES, 128), lambda p: (0, kind * PAIRS + p))
    return pl.pallas_call(
        attend_back_kernel,
        grid=(PAIRS,),
        in_specs=[
            pair(0),
            pair(1),
            pair(2),
            pair(0),
            pair(0),
            pl.BlockSpec((1, TUBES, 128), lambda p: (p, 0, 0)),
        ],
        out_specs=[pair(0)] * 3,
        out_shape=[jax.ShapeDtypeStruct((TUBES, DD), bf16)] * 3,
        compiler_params=params(),
        name="attend_back",
    )(qkv, qkv, qkv, mixed, grad_mixed, logs)


TOKEN_ROWS = 784
CHUNK = 384
DEC_O = D // 2
DEC_D = DEC_O + DD // 2
DEC_Q = DEC_D + DFF // 2
DEC_U = DEC_Q + 3 * DD // 2
DEC_H = DEC_U + DFF // 2
DEC_ROWS = DEC_H + PIX // 2
CHUNKS = DFF // CHUNK


def token_kernel(
    _, a_ref, x_ref, pix_ref, pix_other_ref, hidden_ref, scal_ref, vec_ref, bu_ref, bh_ref,
    wo_ref, wd_ref, wu_ref, wh_ref,
    da_ref, dx1_ref,
    own_ref, other_ref, gvec_ref, gbu_ref, gbh_ref, loss_ref,
    slope,
):
    step = pl.program_id(0)
    sums = (own_ref, other_ref, gvec_ref, gbu_ref, gbh_ref, loss_ref)
    grads = (own_ref, other_ref)

    @pl.when(step == 0)
    def _():
        for ref in sums:
            ref[...] = jnp.zeros_like(ref)

    bo, g2, b2, bd, gf, sf = (vec_ref[index : index + 1] for index in range(3, 9))
    a = a_ref[...].astype(bf16)
    x1 = x_ref[...] + (nn(a, wo_ref[...]) + bo)
    unit2, rate2 = norm_parts(x1)
    h2 = (unit2 * g2 + b2).astype(bf16)
    out = x1 + bd
    active = []
    part_of = lambda chunk: pl.ds(chunk * CHUNK, CHUNK)
    for chunk, before in ahead(CHUNKS, lambda chunk: nt(h2, wu_ref[part_of(chunk)])):
        part = part_of(chunk)
        value, slope_part = gelu_pair(before + bu_ref[:, part])
        slope[:, part] = slope_part
        active.append(value.astype(bf16))
        out = out + nn(active[-1], wd_ref[part])
    unit_f, rate_f = norm_parts(out)
    final = (unit_f * gf + sf).astype(bf16)
    pixels = [
        ref[:, pl.ds(side * CHUNK, CHUNK)].astype(f32)
        for ref in (pix_ref.at[0], pix_other_ref)
        for side in range(2)
    ]
    center = sum(jnp.sum(part, 1, keepdims=True) for part in pixels) * (1.0 / PIX)
    square = sum(jnp.sum(part * part, 1, keepdims=True) for part in pixels) * (1.0 / PIX)
    spread = lax.rsqrt(square - center * center + norm_eps)
    counted = hidden_ref[...] * scal_ref[0:1, 0:1]
    rate = hidden_ref[...] * scal_ref[1:2, 0:1]
    grad_final = jnp.zeros((TOKEN_ROWS, DD), f32)
    for chunk, guess in ahead(CHUNKS, lambda chunk: nt(final, wh_ref[part_of(chunk)])):
        part = part_of(chunk)
        target = (pixels[chunk] - center) * spread
        miss = guess + bh_ref[:, part] - target
        loss_ref[:, part] += col_sum(counted * miss * miss)
        grad_guess = (rate * miss).astype(bf16)
        gbh_ref[:, part] += col_sum(grad_guess.astype(f32))
        grads[chunk // 2][pl.ds(DEC_H + (chunk % 2) * CHUNK, CHUNK)] += tn(grad_guess, final)
        grad_final = grad_final + nn(grad_guess, wh_ref[part])
    grad_out = norm_back(grad_final, gf, unit_f, rate_f)
    out_low = grad_out.astype(bf16)
    grad_h2 = jnp.zeros((TOKEN_ROWS, DD), f32)
    for chunk, grad_active in ahead(CHUNKS, lambda chunk: nt(out_low, wd_ref[part_of(chunk)])):
        part = part_of(chunk)
        grads[chunk // 2][pl.ds(DEC_D + (chunk % 2) * CHUNK, CHUNK)] += tn(active[chunk], out_low)
        grad_before = (slope[:, part] * grad_active).astype(bf16)
        gbu_ref[:, part] += col_sum(grad_before.astype(f32))
        grads[chunk // 2][pl.ds(DEC_U + (chunk % 2) * CHUNK, CHUNK)] += tn(grad_before, h2)
        grad_h2 = grad_h2 + nn(grad_before, wu_ref[part])
    grad_x1 = grad_out + norm_back(grad_h2, g2, unit2, rate2)
    x1_low = grad_x1.astype(bf16)
    g_out = tn(a, x1_low)
    for group in range(2):
        grads[group][pl.ds(DEC_O, DD // 2)] += g_out[group * DD // 2 : (group + 1) * DD // 2]
    da_ref[...] = nt(x1_low, wo_ref[...]).astype(bf16)
    dx1_ref[...] = grad_x1
    gvec_ref[0:1] += col_sum(x1_low.astype(f32))
    gvec_ref[1:2] += col_sum(grad_h2 * unit2)
    gvec_ref[2:3] += col_sum(grad_h2)
    gvec_ref[3:4] += col_sum(out_low.astype(f32))
    gvec_ref[4:5] += col_sum(grad_final * unit_f)
    gvec_ref[5:6] += col_sum(grad_final)


def decoder_tokens(half, mixed, x, tubes, pixels, hidden, scal, vecs, bu, bh, wo, wd, wu, wh):
    rows = lambda width: pl.BlockSpec((TOKEN_ROWS, width), lambda i, _: (i, 0))
    sums = [(DEC_ROWS, DD), (DEC_ROWS, DD), (8, DD), (1, DFF), (1, PIX), (1, PIX)]
    return pl.pallas_call(
        token_kernel,
        grid_spec=pltpu.PrefetchScalarGridSpec(
            num_scalar_prefetch=1,
            grid=(TUBES // TOKEN_ROWS,),
            in_specs=[
                rows(DD),
                rows(DD),
                pl.BlockSpec((1, TOKEN_ROWS, PIX // 2), lambda i, half_ref: (half_ref[0], i, 0)),
                rows(PIX // 2),
                rows(1),
                whole((8, 128)),
                whole(vecs.shape),
                whole((1, DFF)),
                whole((1, PIX)),
                whole((DD, DD)),
                whole((DFF, DD)),
                whole((DFF, DD)),
                whole((PIX, DD)),
            ],
            out_specs=[rows(DD), rows(DD)] + [whole(shape) for shape in sums],
            scratch_shapes=[pltpu.VMEM((TOKEN_ROWS, DFF), f32)],
        ),
        out_shape=[
            jax.ShapeDtypeStruct((TUBES, DD), bf16),
            jax.ShapeDtypeStruct((TUBES, DD), f32),
        ]
        + [jax.ShapeDtypeStruct(shape, f32) for shape in sums],
        compiler_params=params(),
        name="decoder_tokens",
    )(half, mixed, x, tubes, pixels, hidden, scal, vecs, bu, bh, wo, wd, wu, wh)


def qkv_back_kernel(
    half_ref, order_ref, dq_ref, dk_ref, dv_ref, h_ref, x_ref, dx1_ref, vec_ref, w_ref, normed_ref,
    _own, _other,
    latent_ref, own_ref, other_ref, gvec_ref,
    g_qkv, g_proj, latent_sum, sems,
):
    step = pl.program_id(0)

    @pl.when(step == 0)
    def _():
        g_qkv[...] = jnp.zeros_like(g_qkv)
        gvec_ref[...] = jnp.zeros_like(gvec_ref)
        latent_sum[...] = jnp.zeros_like(latent_sum)

    h = h_ref[...]
    grads = (dq_ref[...], dk_ref[...], dv_ref[...])
    grad_h = jnp.zeros((QKV_ROWS, DD), f32)
    for index, grad in enumerate(grads):
        g_both = tn(grad, h)
        for group in range(2):
            rows = pl.ds(index * DD // 2, DD // 2)
            g_qkv[group, rows] += g_both[group * DD // 2 : (group + 1) * DD // 2]
        grad_h = grad_h + nn(grad, w_ref[pl.ds(index * DD, DD)])
    unit, rate = norm_parts(x_ref[...])
    grad_x = dx1_ref[...] + norm_back(grad_h, vec_ref[1:2], unit, rate)
    places = place_matrix(order_ref[...], QKV_ROWS)
    hidden = 1.0 - jnp.sum(places, 1, keepdims=True)
    latent_sum[...] += tn(places.astype(bf16), grad_x.astype(bf16))
    gvec_ref[0:1] += col_sum(grads[0].astype(f32))
    gvec_ref[1:2] += col_sum(grads[2].astype(f32))
    gvec_ref[2:3] += col_sum(grad_h * unit)
    gvec_ref[3:4] += col_sum(grad_h)
    gvec_ref[4:5] += col_sum(hidden * grad_x)

    @pl.when(step == pl.num_programs(0) - 1)
    def _():
        latent = latent_sum[...].astype(bf16)
        latent_ref[...] = latent
        both = tn(normed_ref[...], latent)
        g_proj[0] = both[: D // 2]
        g_proj[1] = both[D // 2 :]
        half = half_ref[0]
        kinds = pl.ds(DEC_Q, 3 * DD // 2)
        copies = [
            pltpu.make_async_copy(g_qkv.at[0], own_ref.at[kinds], sems.at[0]),
            pltpu.make_async_copy(g_qkv.at[1], other_ref.at[kinds], sems.at[1]),
            pltpu.make_async_copy(g_proj.at[half], own_ref.at[pl.ds(0, D // 2)], sems.at[2]),
            pltpu.make_async_copy(g_proj.at[1 - half], other_ref.at[pl.ds(0, D // 2)], sems.at[3]),
        ]
        for copy in copies:
            copy.start()
        for copy in copies:
            copy.wait()


def decoder_qkv_back(half, order, dq, dk, dv, h, x, dx1, vecs, weights, normed, own, other):
    rows = lambda width: pl.BlockSpec((QKV_ROWS, width), lambda i: (i, 0))
    return pl.pallas_call(
        qkv_back_kernel,
        grid=(TUBES // QKV_ROWS,),
        in_specs=[pl.BlockSpec(memory_space=pltpu.SMEM), whole((1, VIS))]
        + [rows(DD)] * 6
        + [whole(vecs.shape), whole((3 * DD, DD)), whole((VIS, D)), any_spec(), any_spec()],
        out_specs=[whole((VIS, DD)), any_spec(), any_spec(), whole((8, DD))],
        out_shape=[
            jax.ShapeDtypeStruct((VIS, DD), bf16),
            jax.ShapeDtypeStruct((DEC_ROWS, DD), f32),
            jax.ShapeDtypeStruct((DEC_ROWS, DD), f32),
            jax.ShapeDtypeStruct((8, DD), f32),
        ],
        scratch_shapes=[
            pltpu.VMEM((2, 3 * DD // 2, DD), f32),
            pltpu.VMEM((2, D // 2, DD), f32),
            pltpu.VMEM((VIS, DD), f32),
            pltpu.SemaphoreType.DMA((4,)),
        ],
        input_output_aliases={11: 1, 12: 2},
        compiler_params=params(),
        name="decoder_qkv_back",
    )(half, order, dq, dk, dv, h, x, dx1, vecs, weights, normed, own, other)


HALF = D // 2
HALF_FF = FF // 2
LAYER_ROWS = 4 * HALF + 2 * HALF_FF
ENC_ROWS = D + 2 * LAYER_ROWS
AT_O, AT_D, AT_Q, AT_U = 0, HALF, HALF + HALF_FF, HALF + HALF_FF + 3 * HALF
STAGES = ((AT_Q, 3 * HALF), (AT_O, HALF), (AT_U, HALF_FF), (AT_D, HALF_FF))


def pieces_of(start, size, per):
    pieces = []
    at = start
    while at < start + size:
        many = min(start + size, (at // per + 1) * per) - at
        pieces.append((at // per, at % per, many, at - start))
        at += many
    return pieces


def stage_copies(sources, per, held, sems, stages):
    copies = []
    count = 0
    first = min(at for at, _ in stages)
    for at, size in stages:
        stage = []
        for shard, row, many, before in pieces_of(at, size, per):
            for group in range(2):
                stage.append(
                    pltpu.make_async_copy(
                        sources[group].at[shard, pl.ds(row, many)],
                        held.at[group, pl.ds(at - first + before, many)],
                        sems.at[count],
                    )
                )
                count += 1
        copies.append(stage)
    return copies


MOST_COPIES = 96


def layer_stages(layer):
    start = D + layer * LAYER_ROWS
    return [(start + at, size) for at, size in STAGES]


def encoder_kernel(per, *refs):
    pix_ref, pix_other_ref, pos_ref, proj_ref, vec_ref, split_own_ref, split_other_ref = refs[:7]
    splits = (split_own_ref, split_other_ref)
    own_ref, other_ref, normed_ref, latent_ref, out_ref = refs[7:12]
    kept = (refs[12:20], refs[20:28])
    held, sems = refs[28:]
    copies = stage_copies(
        (own_ref, other_ref), per, held, sems, [(0, D)] + layer_stages(0) + layer_stages(1)
    )
    for stage in copies:
        for copy in stage:
            copy.start()

    def wait(stage):
        for copy in copies[stage]:
            copy.wait()

    wait(0)
    x = pos_ref[...] + vec_ref[0:1]
    for group, pixels in enumerate((pix_ref, pix_other_ref)):
        x = x + nn(pixels[...], held[group, pl.ds(0, D)])
    for layer in range(2):
        stages = [1 + 4 * layer + index for index in range(4)]
        x = encoder_layer(layer, x, vec_ref, splits, held, lambda index: wait(stages[index]), kept[layer])
    out_ref[...] = x
    unit3, _ = norm_parts(x)
    normed = (unit3 * vec_ref[13:14] + vec_ref[14:15]).astype(bf16)
    normed_ref[...] = normed
    latent_ref[...] = nn(normed, proj_ref[...])


def encoder_layer(layer, x, vec_ref, splits, held, wait, kept):
    x_ref, h_ref, qkv_ref, a_ref, x1_ref, h2_ref, u_ref, slope_ref = kept
    base = 1 + 6 * layer
    biases = layer * (2 * HALF + HALF_FF)
    start = D + layer * LAYER_ROWS
    g1, b1, bo, g2, b2, bd = (vec_ref[base + index : base + index + 1] for index in range(6))
    x_ref[...] = x
    unit, _ = norm_parts(x)
    h = (unit * g1 + b1).astype(bf16)
    h_ref[...] = h
    wait(0)
    for kind in range(3):
        for group in range(2):
            part = pl.ds((2 * kind + group) * HALF, HALF)
            value = nt(h, held[group, pl.ds(start + AT_Q + kind * HALF, HALF)])
            if kind != 1:
                at = biases + kind // 2 * HALF
                value = value + splits[group][:, at : at + HALF]
            qkv_ref[:, part] = value.astype(bf16)
    for pair in range(D // 128):
        q, k, v = (qkv_ref[:, pl.ds(kind * D + pair * 128, 128)] for kind in range(3))
        v_one = jnp.concatenate([v, jnp.ones((VIS, 128), bf16)], 1)
        mixed = []
        for head in range(2):
            scores = nt(jnp.where(half_lane(head), q, jnp.zeros_like(q)), k)
            top = jnp.max(scores, 1, keepdims=True)
            expo = jnp.exp2((scores - top) * (SCORE * LOG2E)).astype(bf16)
            both = nn(expo, v_one)
            mixed.append(both[:, :128] / both[:, 128:])
        a_ref[:, pl.ds(pair * 128, 128)] = jnp.where(half_lane(0), mixed[0], mixed[1]).astype(bf16)
    wait(1)
    x1 = x + bo
    for group in range(2):
        x1 = x1 + nn(a_ref[:, pl.ds(group * HALF, HALF)], held[group, pl.ds(start + AT_O, HALF)])
    x1_ref[...] = x1
    unit2, _ = norm_parts(x1)
    h2 = (unit2 * g2 + b2).astype(bf16)
    h2_ref[...] = h2
    wait(2)
    wait(3)
    out = x1 + bd
    for group in range(2):
        rows_of = lambda chunk: pl.ds(start + AT_U + chunk * CHUNK, CHUNK)
        for chunk, before in ahead(HALF_FF // CHUNK, lambda chunk: nt(h2, held[group, rows_of(chunk)])):
            part = pl.ds(group * HALF_FF + chunk * CHUNK, CHUNK)
            at = biases + 2 * HALF + chunk * CHUNK
            value, slope = gelu_pair(before + splits[group][:, at : at + CHUNK])
            slope_ref[:, part] = slope
            active = value.astype(bf16)
            u_ref[:, part] = active
            out = out + nn(active, held[group, pl.ds(start + AT_D + chunk * CHUNK, CHUNK)])
    return out


def encoder(per, pixels, pos, proj, vecs, splits, own, other):
    shapes = [((VIS, D), bf16), ((VIS, DD), f32), ((VIS, D), f32)] + 2 * [
        ((VIS, D), f32),
        ((VIS, D), bf16),
        ((VIS, 3 * D), bf16),
        ((VIS, D), bf16),
        ((VIS, D), f32),
        ((VIS, D), bf16),
        ((VIS, FF), bf16),
        ((VIS, FF), f32),
    ]
    result = pl.pallas_call(
        lambda *refs: encoder_kernel(per, *refs),
        in_specs=[vmem_spec()] * 7 + [any_spec()] * 2,
        out_specs=[vmem_spec()] * len(shapes),
        out_shape=[jax.ShapeDtypeStruct(shape, kind) for shape, kind in shapes],
        scratch_shapes=[
            pltpu.VMEM((2, ENC_ROWS, D), bf16),
            pltpu.SemaphoreType.DMA((MOST_COPIES,)),
        ],
        compiler_params=params(),
        name="encoder",
    )(*pixels, pos, proj, vecs, *splits, own, other)
    return result[:3], (result[3:11], result[11:])


RIGHT_AT = LAYER_ROWS


def encoder_back_kernel(per, *refs):
    (
        latent_ref, out_ref, proj_ref, vec_ref, pix_ref, pix_other_ref, start_ref, start_other_ref
    ) = refs[:8]
    kept = (refs[8:16], refs[16:24])
    own_ref, other_ref = refs[24:26]
    results = (refs[26:32], refs[32:38])
    held, sems, da, dqkv = refs[38:]
    order = (3, 2, 1, 0)
    stages = [layer_stages(layer)[index] for layer in (1, 0) for index in order]
    copies = stage_copies((own_ref, other_ref), per, held, sems, stages)
    for stage in copies:
        for copy in stage:
            copy.start()

    def wait(turn, index):
        for copy in copies[4 * turn + order.index(index)]:
            copy.wait()

    starts = jnp.concatenate([split3(ref[:, :D]) for ref in (start_ref, start_other_ref)], 0)
    grad = None
    for turn, layer in enumerate((1, 0)):
        grad = encoder_layer_back(
            layer, grad, latent_ref, out_ref, proj_ref, vec_ref, starts, (pix_ref, pix_other_ref),
            kept[layer], held, lambda index: wait(turn, index), da, dqkv, results[layer],
        )


def encoder_layer_back(
    layer, grad, latent_ref, out_ref, proj_ref, vec_ref, starts, pixels, kept, held, wait, da, dqkv, results
):
    last = layer == 1
    base = 1 + 6 * layer
    start = layer * LAYER_ROWS
    x_ref, h_ref, qkv_ref, a_ref, x1_ref, h2_ref, u_ref, slope_ref = kept
    mine_ref, other_pack_ref, left_ref, gvec_ref, gbu_ref, gbq_ref = results
    packs = (mine_ref, other_pack_ref)
    g1, b1, bo, g2, b2, bd = (vec_ref[base + index : base + index + 1] for index in range(6))
    gvec_ref[6:8] = jnp.zeros((2, D), f32)
    if last:
        unit3, rate3 = norm_parts(out_ref[...])
        grad_normed = nt(latent_ref[...], proj_ref[...])
        grad_out = norm_back(grad_normed, vec_ref[13:14], unit3, rate3)
        gvec_ref[6:7] = col_sum(grad_normed * unit3)
        gvec_ref[7:8] = col_sum(grad_normed)
    else:
        grad_out = grad
    out_low = grad_out.astype(bf16)
    unit2, rate2 = norm_parts(x1_ref[...])
    grad_h2 = jnp.zeros((VIS, D), f32)
    wait(3)
    wait(2)
    for group in range(2):
        for chunk in range(HALF_FF // CHUNK):
            part = pl.ds(group * HALF_FF + chunk * CHUNK, CHUNK)
            grad_active = nt(out_low, held[group, pl.ds(start + AT_D + chunk * CHUNK, CHUNK)])
            grad_before = (slope_ref[:, part] * grad_active).astype(bf16)
            packs[group][:, pl.ds(AT_U + chunk * CHUNK, CHUNK)] = grad_before
            packs[group][:, pl.ds(AT_D + chunk * CHUNK, CHUNK)] = u_ref[:, part]
            gbu_ref[:, part] = col_sum(grad_before.astype(f32))
            grad_h2 = grad_h2 + nn(grad_before, held[group, pl.ds(start + AT_U + chunk * CHUNK, CHUNK)])
    grad_x1 = grad_out + norm_back(grad_h2, g2, unit2, rate2)
    x1_low = grad_x1.astype(bf16)
    wait(1)
    for group in range(2):
        part = pl.ds(group * HALF, HALF)
        da[:, part] = nt(x1_low, held[group, pl.ds(start + AT_O, HALF)]).astype(bf16)
        packs[group][:, pl.ds(AT_O, HALF)] = a_ref[:, part]
    zero = jnp.zeros((), bf16)
    for pair in range(D // 128):
        lanes = pl.ds(pair * 128, 128)
        q, k, v = (qkv_ref[:, pl.ds(kind * D + pair * 128, 128)] for kind in range(3))
        grad = da[:, lanes]
        dq = dk = dv = jnp.zeros((VIS, 128), f32)
        for head in range(2):
            mask = half_lane(head)
            q_head = jnp.where(mask, q, zero)
            grad_head = jnp.where(mask, grad, zero)
            scores = nt(q_head, k) * SCORE
            expo = jnp.exp(scores - jnp.max(scores, 1, keepdims=True))
            probs = expo / jnp.sum(expo, 1, keepdims=True)
            grad_probs = nt(grad_head, v)
            row_total = jnp.sum(probs * grad_probs, 1, keepdims=True)
            grad_scores = (probs * (grad_probs - row_total)).astype(bf16)
            dv = dv + tn(probs.astype(bf16), grad_head)
            dk = dk + tn(grad_scores, q_head)
            dq = dq + nn(grad_scores, jnp.where(mask, k, zero))
        dqkv[:, lanes] = (dq * SCORE).astype(bf16)
        dqkv[:, pl.ds(D + pair * 128, 128)] = (dk * SCORE).astype(bf16)
        dqkv[:, pl.ds(2 * D + pair * 128, 128)] = dv.astype(bf16)
    wait(0)
    grad_h = jnp.zeros((VIS, D), f32)
    for kind in range(3):
        for group in range(2):
            grad = dqkv[:, pl.ds((2 * kind + group) * HALF, HALF)]
            rows = pl.ds(AT_Q + kind * HALF, HALF)
            packs[group][:, rows] = grad
            grad_h = grad_h + nn(
                grad, held[group, pl.ds(start + AT_Q + kind * HALF, HALF)]
            )
    unit, rate = norm_parts(x_ref[...])
    grad_x = grad_x1 + norm_back(grad_h, g1, unit, rate)
    gbq_ref[0:1] = col_sum(dqkv[:, pl.ds(0, D)].astype(f32))
    gbq_ref[1:2] = col_sum(dqkv[:, pl.ds(2 * D, D)].astype(f32))
    gvec_ref[0:1] = col_sum(grad_h * unit)
    gvec_ref[1:2] = col_sum(grad_h)
    gvec_ref[2:3] = col_sum(x1_low.astype(f32))
    gvec_ref[3:4] = col_sum(grad_h2 * unit2)
    gvec_ref[4:5] = col_sum(grad_h2)
    gvec_ref[5:6] = col_sum(out_low.astype(f32))
    rights = [x1_low, out_low, h_ref[...], h2_ref[...]]
    spans = [(AT_O, HALF, 0), (AT_D, HALF_FF, 0), (AT_Q, 3 * HALF, 0), (AT_U, HALF_FF, 0)]
    if not last:
        embed_low = grad_x.astype(bf16)
        rights.append(embed_low)
        gvec_ref[6:7] = col_sum(embed_low.astype(f32))
    before = 0 if last else D
    for index, right in enumerate(rights):
        for pack in packs:
            pack[:, pl.ds(RIGHT_AT + index * D, D)] = right
        inner = nt(starts, right)
        for group in range(2):
            parts = split3(fold3(inner[3 * RANK * group : 3 * RANK * (group + 1)]))
            if index == 4:
                value = fold3(nn(parts, pixels[group][...]))
                left_ref[group, :, pl.ds(0, D)] = value
            else:
                at, size, _ = spans[index]
                value = fold3(nn(parts, packs[group][:, pl.ds(at, size)]))
                left_ref[group, :, pl.ds(before + at, size)] = value
    return grad_x


def encoder_back(per, latent, out, proj, vecs, pixels, starts, kept, own, other):
    shapes = []
    for layer in range(2):
        width = RIGHT_AT + (5 - layer) * D
        shapes += [
            ((VIS, width), bf16),
            ((VIS, width), bf16),
            ((2, RANK, LAYER_ROWS + (1 - layer) * D), f32),
            ((8, D), f32),
            ((1, FF), f32),
            ((2, D), f32),
        ]
    result = pl.pallas_call(
        lambda *refs: encoder_back_kernel(per, *refs),
        in_specs=[vmem_spec()] * 24 + [any_spec()] * 2,
        out_specs=[vmem_spec()] * len(shapes),
        out_shape=[jax.ShapeDtypeStruct(shape, kind) for shape, kind in shapes],
        scratch_shapes=[
            pltpu.VMEM((2, 2 * LAYER_ROWS, D), bf16),
            pltpu.SemaphoreType.DMA((MOST_COPIES,)),
            pltpu.VMEM((VIS, D), bf16),
            pltpu.VMEM((VIS, 3 * D), bf16),
        ],
        compiler_params=pltpu.CompilerParams(vmem_limit_bytes=60 << 20),
        name="encoder_back",
    )(latent, out, proj, vecs, *pixels, *starts, *kept[0], *kept[1], own, other)
    return result[:6], result[6:]


HALF_ROWS = 384


def error_factor_kernel(start_ref, error_ref, out_ref):
    turned = nt(error_ref[...], split3(start_ref[...]))
    out_ref[...] = fold3(turned.T)


def error_factor(start, error):
    rows, width = error.shape
    return pl.pallas_call(
        error_factor_kernel,
        grid=(rows // HALF_ROWS,),
        in_specs=[whole((RANK, width)), pl.BlockSpec((HALF_ROWS, width), lambda j: (j, 0))],
        out_specs=pl.BlockSpec((RANK, HALF_ROWS), lambda j: (0, j)),
        out_shape=jax.ShapeDtypeStruct((RANK, rows), f32),
        compiler_params=params(),
        name="error_factor",
    )(start, error)


def low_left(basis3):
    high, middle = basis3[:RANK], basis3[RANK : 2 * RANK]
    return jnp.concatenate([high, high, middle, jnp.zeros_like(high)], 0)


def low_right(factor3):
    high = factor3[:RANK]
    return jnp.concatenate([factor3[: 2 * RANK], high, jnp.zeros_like(high)], 0)


DEC_BLOCK = 1152


def dec_left_kernel(start_ref, start_other_ref, own_ref, other_ref, out_ref):
    for group, (begin_ref, ref) in enumerate(((start_ref, own_ref), (start_other_ref, other_ref))):
        start = split3(begin_ref[:, D:])
        grad = ref[...]
        high = grad.astype(bf16)
        rest = (grad - high.astype(f32)).astype(bf16)
        out_ref[group] = fold3(nt(start, high) + nt(start, rest))


def dec_left_factor(starts, own, other):
    rows = pl.BlockSpec((DEC_BLOCK, DD), lambda j: (j, 0))
    return pl.pallas_call(
        dec_left_kernel,
        grid=(DEC_ROWS // DEC_BLOCK,),
        in_specs=[whole((RANK, D + DD))] * 2 + [rows, rows],
        out_specs=pl.BlockSpec((2, RANK, DEC_BLOCK), lambda j: (0, 0, j)),
        out_shape=jax.ShapeDtypeStruct((2, RANK, DEC_ROWS), f32),
        compiler_params=params(),
        name="dec_left_factor",
    )(*starts, own, other)


MESH_ID = pl.DeviceIdType.MESH
PLANE = 4


def levels_of(workers):
    return (PLANE, workers // PLANE) if workers == 4 * PLANE else (workers,)


def peers_of(workers, me, level):
    counts = levels_of(workers)
    if len(counts) == 1:
        return [lax.rem(me + distance, workers) for distance in range(1, workers)]
    plane, column = me // PLANE, lax.rem(me, PLANE)
    if level == 0:
        return [plane * PLANE + lax.rem(column + d, PLANE) for d in range(1, counts[0])]
    return [lax.rem(plane + d, counts[1]) * PLANE + column for d in range(1, counts[1])]


def greet(workers, me, partner):
    barrier = pltpu.get_barrier_semaphore()
    count = 0
    for level in range(len(levels_of(workers))):
        for peer in peers_of(workers, me, level):
            pl.semaphore_signal(barrier, 1, device_id={"dp": peer}, device_id_type=MESH_ID)
            count += 1
    pl.semaphore_signal(barrier, 1, device_id={"tensor": partner}, device_id_type=MESH_ID)
    pl.semaphore_wait(barrier, count + 1)


def sum_workers(workers, me, lanes, local, slots, sums, sems, work=lambda turn: None):
    counts = levels_of(workers)
    deep = len(counts) == 2
    if deep:
        plane, column = me // PLANE, lax.rem(me, PLANE)
        own, inner = column, plane
        sizes = (lanes * counts[1], lanes)
    else:
        own, inner = me, 0
        sizes = (lanes, 0)

    def span(level, index, base=0):
        return pl.ds(pl.multiple_of(base + index * sizes[level], 128), sizes[level])

    base = own * sizes[0]
    peers = [peers_of(workers, me, level) for level in range(len(counts))]
    places = [
        [lax.rem(mine + d, count) for d in range(1, count)]
        for mine, count in zip((own, inner), counts)
    ]
    first_sem = [0, counts[0]]

    def exchange(turn, level, source, target):
        copies = []
        for index, peer in enumerate(peers[level]):
            sem = first_sem[level] + index
            copy = pltpu.make_async_remote_copy(
                src_ref=source(index),
                dst_ref=target(index),
                send_sem=sems.at[2 * turn, sem],
                recv_sem=sems.at[2 * turn + 1, sem],
                device_id={"dp": peer},
                device_id_type=MESH_ID,
            )
            copy.start()
            copies.append(copy)
        return copies

    def slot(level, index):
        at = index * sizes[0] if level == 0 else counts[0] * sizes[0] + index * sizes[1]
        return slots.at[:, pl.ds(at, sizes[level])]

    def gathered(level, copies, total):
        for index, copy in enumerate(copies):
            copy.wait_recv()
            total = total + slot(level, index)[...]
        return total

    sent = exchange(
        0, 0, lambda index: local.at[:, span(0, places[0][index])], lambda index: slot(0, index)
    )
    work(0)
    here = span(0, own)
    total = gathered(0, sent, local[:, here])
    if deep:
        local[:, here] = total
        more = exchange(
            0, 1, lambda index: local.at[:, span(1, places[1][index], base)],
            lambda index: slot(1, index),
        )
        work(1)
        share = span(1, inner, base)
        sums[:, share] = gathered(1, more, local[:, share])
        back = exchange(1, 1, lambda _: sums.at[:, share], lambda _: sums.at[:, share])
        work(2)
        for copy in more:
            copy.wait_send()
        for copy in back:
            copy.wait()
    else:
        sums[:, here] = total
        work(1)
        work(2)
    last = exchange(1, 0, lambda _: sums.at[:, here], lambda _: sums.at[:, here])
    work(3)
    for copy in sent:
        copy.wait_send()
    for copy in last:
        copy.wait()


def sum_small(workers, me, local, slots, sums, sems, work):
    width = local.shape[1]
    counts = levels_of(workers)
    if len(counts) == 1:
        work(0)
        work(1)
        sum_workers(workers, me, width // workers, local, slots, sums, sems)
        return
    places = (lax.rem(me, PLANE), me // PLANE)
    for level, count in enumerate(counts):
        base = 0 if level == 0 else counts[0]

        def slot(index):
            return slots.at[:, pl.ds(pl.multiple_of((base + index) * width, 128), width)]

        mine = slot(places[level])
        mine[...] = local[...] if level == 0 else sums[...]
        copies = []
        for index, peer in enumerate(peers_of(workers, me, level)):
            copy = pltpu.make_async_remote_copy(
                src_ref=mine,
                dst_ref=mine,
                send_sem=sems.at[2 * level, index],
                recv_sem=sems.at[2 * level + 1, index],
                device_id={"dp": peer},
                device_id_type=MESH_ID,
            )
            copy.start()
            copies.append(copy)
        work(level)
        for copy in copies:
            copy.wait()
        total = slot(0)[...]
        for index in range(1, count):
            total = total + slot(index)[...]
        sums[...] = total


def orthonormal(left):
    place = lax.broadcasted_iota(jnp.int32, (RANK, 1), 0)
    gram = lax.dot_general(
        left, left, (((1,), (1,)), ((), ())), precision=highest_precision,
        preferred_element_type=f32,
    )
    for index in range(RANK):
        scale = lax.rsqrt(gram[index : index + 1, index : index + 1])
        column = gram[:, index : index + 1] * scale
        below = jnp.where(place > index, column, 0.0)
        pivot = left[index : index + 1] * scale
        left = jnp.where(place == index, pivot, left - below * pivot)
        gram = gram - below * (gram[index : index + 1] * scale)
    return left


def lanes_for(width, workers):
    return pl.cdiv(width, 128 * workers) * 128


RANGES = [(0, D)] + [
    (D + layer * LAYER_ROWS + at, size)
    for layer in range(2)
    for at, size in ((AT_O, HALF), (AT_D, HALF_FF), (AT_Q, 3 * HALF), (AT_U, HALF_FF))
]
LOW = 4 * RANK
LOADS = 2 * (3 + len(RANGES)) + 4 + 3
ERROR_PARTS = 4


def compress_kernel(
    workers, lanes,
    first_ref, second_ref, dec_ref, error_part_ref, dec_error_part_ref,
    enc_vec0_ref, enc_bu0_ref, enc_bq0_ref, enc_vec1_ref, enc_bu1_ref, enc_bq1_ref,
    dec_vec_ref, dec_vec1_ref, dec_bu_ref, dec_bh_ref, loss_ref,
    error_ref, pix_ref, pack0_ref, pack1_ref, pix_came_ref, pack0_came_ref, pack1_came_ref,
    dec_own_ref, dec_came_ref, dec_error_ref,
    enc_basis, dec_basis, enc_factor, dec_factor, wide_out, narrow_out, split_out,
    turned_out, rights_out, comb_out,
    send, came, local, slots, sums, local2, slots2, sums2, parts, dec_parts,
    held, lefts, turned, rights, comb, dec_came, dec_held,
    sems, sems2, pair_sems, load_sems, out_sems,
):
    me = lax.axis_index("dp")
    half = lax.axis_index("tensor")
    first = first_ref.shape[2]
    factor_width = ENC_ROWS + DEC_ROWS
    width = factor_width + VEC_LANES
    clips = ((pix_ref, pack0_ref, pack1_ref), (pix_came_ref, pack0_came_ref, pack1_came_ref))

    left_loads, right_loads, error_loads, dec_loads = [], [], [], []

    def load(group, source, target):
        count = sum(len(loads) for loads in (left_loads, right_loads, error_loads, dec_loads))
        group.append(pltpu.make_async_copy(source, target, load_sems.at[count]))

    def begin(group):
        for copy in group:
            copy.start()

    for clip, (pixels, pack0, pack1) in enumerate(clips):
        load(left_loads, pixels, lefts.at[clip, :, pl.ds(0, D)])
        for layer, pack in enumerate((pack0, pack1)):
            target = lefts.at[clip, :, pl.ds(D + layer * LAYER_ROWS, LAYER_ROWS)]
            load(left_loads, pack.at[:, pl.ds(0, LAYER_ROWS)], target)
    size = ENC_ROWS // ERROR_PARTS
    for index in range(ERROR_PARTS):
        block = pl.ds(index * size, size)
        load(error_loads, error_ref.at[block], held.at[block])
    for clip, (_, pack0, pack1) in enumerate(clips):
        rows = pl.ds(clip * VIS, VIS)
        load(right_loads, pack0.at[:, pl.ds(RIGHT_AT + 4 * D, D)], rights.at[0, rows])
        for layer, pack in enumerate((pack0, pack1)):
            for kind in range(4):
                target = rights.at[1 + 4 * layer + kind, rows]
                load(right_loads, pack.at[:, pl.ds(RIGHT_AT + kind * D, D)], target)
    load(dec_loads, dec_own_ref, comb)
    load(dec_loads, dec_came_ref, dec_came)
    load(dec_loads, dec_error_ref, dec_held)

    spans = ((first_ref, 0, first), (second_ref, first, ENC_ROWS - first), (dec_ref, ENC_ROWS, DEC_ROWS))
    for ref, at, size in spans:
        send[:, at : at + size] = ref[1]
    shared_refs = (enc_vec0_ref, enc_vec1_ref, dec_vec_ref, dec_vec1_ref)
    for target in (send, local):
        at = factor_width
        for ref in shared_refs:
            target[:, at : at + ref.shape[1]] = ref[...]
            at += ref.shape[1]
    for group, target in ((1, send), (0, local)):
        pieces = []
        for bq_ref, bu_ref in ((enc_bq0_ref, enc_bu0_ref), (enc_bq1_ref, enc_bu1_ref)):
            for row in range(2):
                pieces.append(bq_ref[row : row + 1, group * HALF : (group + 1) * HALF])
            for index in range(HALF_FF // CHUNK):
                low = group * HALF_FF + index * CHUNK
                pieces.append(bu_ref[:, low : low + CHUNK])
        low = group * DD // 2
        pieces.append(
            jnp.concatenate([dec_vec1_ref[row : row + 1, low : low + DD // 2] for row in range(2)], 1)
        )
        for ref in (dec_bu_ref, dec_bh_ref):
            for index in range(2):
                low = (2 * group + index) * CHUNK
                pieces.append(ref[:, low : low + CHUNK])
        pieces.append(sum(loss_ref[:, index * CHUNK : (index + 1) * CHUNK] for index in range(CHUNKS)))
        pieces += [jnp.zeros((1, CHUNK), f32)] * (3 * RANK - len(pieces))
        for index in range(3):
            low = at + index * CHUNK
            target[:, low : low + CHUNK] = jnp.concatenate(pieces[RANK * index : RANK * (index + 1)], 0)
    if width < workers * lanes:
        tail = jnp.zeros((RANK, workers * lanes - width), f32)
        send[:, width:] = tail
    greet(workers, me, 1 - half)
    pair = pltpu.make_async_remote_copy(
        src_ref=send,
        dst_ref=came,
        send_sem=pair_sems.at[0],
        recv_sem=pair_sems.at[1],
        device_id={"tensor": 1 - half},
        device_id_type=MESH_ID,
    )
    pair.start()
    for ref, at, size in spans[:2]:
        local[:, at : at + size] = ref[0] + error_part_ref[:, at : at + size]
    local[:, ENC_ROWS:factor_width] = dec_ref[0] + dec_error_part_ref[...]
    if width < workers * lanes:
        local[:, width:] = tail
    pair.wait()
    local[...] += came[...]

    blocks = ENC_ROWS // HALF_ROWS
    dec_blocks = DEC_ROWS // HALF_ROWS

    def rows_of(index):
        return pl.ds(pl.multiple_of(index * HALF_ROWS, HALF_ROWS), HALF_ROWS)

    def turn(index, _):
        rows = rows_of(index)
        both = jnp.concatenate([lefts[0, :, rows], lefts[1, :, rows]], 0)
        turned[rows, 0 : 2 * VIS] = both.T
        return 0

    def combine(index, _):
        rows = rows_of(index)
        comb[rows] = comb[rows] + dec_came[rows] + dec_held[rows].astype(f32)
        return 0

    def meanwhile(phase):
        if phase == 0:
            begin(left_loads)
        elif phase == 1:
            begin(dec_loads)
            for copy in left_loads:
                copy.wait()
            lax.fori_loop(0, 10, turn, 0)
        elif phase == 2:
            begin(error_loads)
            lax.fori_loop(10, 18, turn, 0)
        else:
            begin(right_loads)
            lax.fori_loop(18, blocks, turn, 0)
            for copy in dec_loads:
                copy.wait()
            lax.fori_loop(0, dec_blocks, combine, 0)

    sum_workers(workers, me, lanes, local, slots, sums, sems, meanwhile)
    enc = orthonormal(sums[:, :ENC_ROWS])
    enc_basis[...] = enc
    parts[...] = split3(enc)
    dec = orthonormal(sums[:, ENC_ROWS:factor_width])
    dec_basis[...] = dec
    dec_parts[...] = split3(dec)

    for copy in error_loads + right_loads:
        copy.wait()
    stores = [
        pltpu.make_async_copy(source, target, out_sems.at[index])
        for index, (source, target) in enumerate(
            ((rights, rights_out), (comb, comb_out), (turned, turned_out))
        )
    ]
    begin(stores[:2])
    wide_rows = 2 * HALF_ROWS

    def add_error(index, total):
        rows = pl.ds(pl.multiple_of(index * wide_rows, wide_rows), wide_rows)
        return total + nn(parts[:, rows], held[rows])

    total = lax.fori_loop(0, ENC_ROWS // wide_rows, add_error, jnp.zeros((3 * RANK, D), f32))
    inners = [nn(parts[:, pl.ds(at, size)], turned[pl.ds(at, size), 0 : 2 * VIS]) for at, size in RANGES]
    inners = [split3(fold3(inner)) for inner in inners]
    for index, inner in enumerate(inners):
        total = total + nn(inner, rights[index])
    local2[:, :D] = fold3(total)

    def add_dec(index, total):
        rows = rows_of(index)
        block = comb[rows]
        high = block.astype(bf16)
        rest = (block - high.astype(f32)).astype(bf16)
        return total + nn(dec_parts[:, rows], high) + nn(dec_parts[:, rows], rest)

    local2[:, D : D + DD] = fold3(
        lax.fori_loop(0, dec_blocks, add_dec, jnp.zeros((3 * RANK, DD), f32))
    )
    if D + DD < local2.shape[1]:
        local2[:, D + DD :] = jnp.zeros((RANK, local2.shape[1] - D - DD), f32)
    mean = lambda at, size: sums[:, at : at + size] * (1.0 / workers)
    at = factor_width
    vec0, vec1 = mean(at, D), mean(at + D, D)
    dec0, dec1 = mean(at + 2 * D, DD), mean(at + 2 * D + DD, DD)
    wide_out[...] = jnp.concatenate([vec0[6:7], vec0[:6], vec1], 0)
    narrow_out[...] = jnp.concatenate([dec1[4:5], dec1[2:4], dec0[:6]], 0)
    for index in range(3):
        split_out[RANK * index : RANK * (index + 1)] = mean(at + 2 * D + 2 * DD + index * CHUNK, CHUNK)

    def turn_basis(index, _):
        rows = rows_of(index)
        turned[rows, 2 * VIS :] = low_left(parts[:, rows]).T
        return 0

    def meanwhile2(level):
        if level == 0:
            lax.fori_loop(0, blocks // 2, turn_basis, 0)
        else:
            lax.fori_loop(blocks // 2, blocks, turn_basis, 0)
            stores[2].start()

    sum_small(workers, me, local2, slots2, sums2, sems2, meanwhile2)
    for copy in stores:
        copy.wait()
    enc_factor[...] = sums2[:, :D] * (1.0 / workers)
    dec_factor[...] = sums2[:, D : D + DD] * (1.0 / workers)


VEC_LANES = 2 * D + 2 * DD + 3 * CHUNK


def compress(
    workers, first, second, dec, error_part, dec_error_part, vecs, error, mine, came, dec_own, dec_came,
    dec_error,
):
    lanes = lanes_for(ENC_ROWS + DEC_ROWS + VEC_LANES, workers)
    wide = pltpu.VMEM((RANK, workers * lanes), f32)
    small = D + DD if len(levels_of(workers)) == 2 else workers * lanes_for(D + DD, workers)
    wide2 = pltpu.VMEM((RANK, small), f32)
    return pl.pallas_call(
        lambda *refs: compress_kernel(workers, lanes, *refs),
        in_specs=[vmem_spec()] * (5 + len(vecs)) + [any_spec()] * 10,
        out_specs=[vmem_spec()] * 7 + [any_spec()] * 3,
        out_shape=[
            jax.ShapeDtypeStruct((RANK, ENC_ROWS), f32),
            jax.ShapeDtypeStruct((RANK, DEC_ROWS), f32),
            jax.ShapeDtypeStruct((RANK, D), f32),
            jax.ShapeDtypeStruct((RANK, DD), f32),
            jax.ShapeDtypeStruct((15, D), f32),
            jax.ShapeDtypeStruct((9, DD), f32),
            jax.ShapeDtypeStruct((3 * RANK, CHUNK), f32),
            jax.ShapeDtypeStruct((ENC_ROWS, 2 * VIS + LOW), bf16),
            jax.ShapeDtypeStruct((len(RANGES), 2 * VIS, D), bf16),
            jax.ShapeDtypeStruct((DEC_ROWS, DD), f32),
        ],
        scratch_shapes=[
            wide,
            wide,
            wide,
            pltpu.VMEM((RANK, (workers + 4) * lanes), f32),
            wide,
            wide2,
            pltpu.VMEM((RANK, 8 * small), f32),
            wide2,
            pltpu.VMEM((3 * RANK, ENC_ROWS), bf16),
            pltpu.VMEM((3 * RANK, DEC_ROWS), bf16),
            pltpu.VMEM((ENC_ROWS, D), bf16),
            pltpu.VMEM((2, VIS, ENC_ROWS), bf16),
            pltpu.VMEM((ENC_ROWS, 2 * VIS + LOW), bf16),
            pltpu.VMEM((len(RANGES), 2 * VIS, D), bf16),
            pltpu.VMEM((DEC_ROWS, DD), f32),
            pltpu.VMEM((DEC_ROWS, DD), f32),
            pltpu.VMEM((DEC_ROWS, DD), bf16),
            pltpu.SemaphoreType.DMA((4, workers)),
            pltpu.SemaphoreType.DMA((4, workers)),
            pltpu.SemaphoreType.DMA((2,)),
            pltpu.SemaphoreType.DMA((LOADS,)),
            pltpu.SemaphoreType.DMA((4,)),
        ],
        compiler_params=pltpu.CompilerParams(
            collective_id=1, has_side_effects=True, vmem_limit_bytes=60 << 20
        ),
        name="compress",
    )(
        first, second, dec, error_part, dec_error_part, *vecs, error, *mine, *came, dec_own, dec_came,
        dec_error,
    )


def new_errors_kernel(
    turned_ref, rights_ref, error_ref, comb_ref, enc_factor_ref, basis_ref, factor_ref,
    out_ref, dec_out_ref,
    turned, rights, held, comb, dec_held, in_sems, out_sems,
):
    blocks = ENC_ROWS // HALF_ROWS
    dec_blocks = DEC_ROWS // HALF_ROWS

    def rows_of(index):
        start = index * HALF_ROWS
        if not isinstance(index, int):
            start = pl.multiple_of(start, HALF_ROWS)
        return pl.ds(start, HALF_ROWS)

    def loads(index):
        rows = rows_of(index)
        return (
            pltpu.make_async_copy(error_ref.at[rows], held.at[rows], in_sems.at[0, index]),
            pltpu.make_async_copy(turned_ref.at[rows], turned.at[rows], in_sems.at[1, index]),
        )

    def right_load(kind):
        target = rights.at[kind, pl.ds(0, 2 * VIS)]
        return pltpu.make_async_copy(rights_ref.at[kind], target, in_sems.at[2, kind])

    def store(index):
        rows = rows_of(index)
        return pltpu.make_async_copy(held.at[rows], out_ref.at[rows], out_sems.at[index])

    comb_load = pltpu.make_async_copy(comb_ref, comb, in_sems.at[2, len(RANGES)])
    comb_load.start()
    for kind, (at, size) in enumerate(RANGES):
        right_load(kind).start()
        for index in range(at // HALF_ROWS, (at + size) // HALF_ROWS):
            for copy in loads(index):
                copy.start()
    comb_load.wait()
    dec_right = low_right(split3(-factor_ref[...]))
    enc_right = low_right(split3(-enc_factor_ref[...]))
    for kind in range(len(RANGES)):
        rights[kind, 2 * VIS :] = enc_right

    def dec_residue(index, _):
        rows = rows_of(index)
        left = low_left(split3(basis_ref[:, rows]))
        dec_held[rows] = (comb[rows] + tn(left, dec_right)).astype(bf16)
        return 0

    lax.fori_loop(0, dec_blocks, dec_residue, 0)
    dec_store = pltpu.make_async_copy(dec_held, dec_out_ref, out_sems.at[blocks])
    dec_store.start()
    for kind, (at, size) in enumerate(RANGES):
        right_load(kind).wait()

        def residue(index, _, kind=kind):
            for copy in loads(index):
                copy.wait()
            rows = rows_of(index)
            value = nn(turned[rows], rights[kind]) + held[rows].astype(f32)
            held[rows] = value.astype(bf16)
            store(index).start()
            return 0

        lax.fori_loop(at // HALF_ROWS, (at + size) // HALF_ROWS, residue, 0)
    for index in range(blocks):
        store(index).wait()
    dec_store.wait()


def new_errors(turned, rights, error, comb, bases):
    blocks = ENC_ROWS // HALF_ROWS
    return pl.pallas_call(
        new_errors_kernel,
        in_specs=[any_spec()] * 4 + [vmem_spec()] * 3,
        out_specs=[any_spec()] * 2,
        out_shape=[
            jax.ShapeDtypeStruct((ENC_ROWS, D), bf16),
            jax.ShapeDtypeStruct((DEC_ROWS, DD), bf16),
        ],
        scratch_shapes=[
            pltpu.VMEM(turned.shape, bf16),
            pltpu.VMEM((len(RANGES), 2 * VIS + LOW, D), bf16),
            pltpu.VMEM(error.shape, bf16),
            pltpu.VMEM(comb.shape, f32),
            pltpu.VMEM(comb.shape, bf16),
            pltpu.SemaphoreType.DMA((3, blocks)),
            pltpu.SemaphoreType.DMA((blocks + 1,)),
        ],
        compiler_params=params(),
        name="new_errors",
    )(turned, rights, error, comb, *bases)


PART_Z_X_Y, PART_Z_Y_X, PART_X_Y_Z, PART_DEC = range(4)
Z_X_Y_PARTS = (PART_DEC, PART_Z_X_Y)
WAY_X, WAY_Y, WAY_UP, WAY_DOWN = range(4)
ERROR_ROWS = 1248


def gather_kernel(
    parts, planes, weights_ref, dec_weights_ref, tubes_ref, error_ref, dec_error_ref, start_ref, order_ref,
    split_ref, mask_ref,
    own_ref, other_ref, pixels_ref, part_ref, dec_part_ref, picked_ref, picked_other_ref, pix_other_ref,
    start_other_ref, split_other_ref, visible_ref, bqkv_ref, bu_ref, bh_ref, pos_enc_ref, pos_dec_ref, scal_ref, proj_ref, wqkv_ref, wo_ref, wd_ref, wu_ref, wh_ref,
    held, dec_held, dec_own, dec_other, joined, pix_held, shard_ref, dec_shard_ref,
    send_sems, recv_sems, pair_sems, sems,
):
    me = lax.axis_index("dp")
    half = lax.axis_index("tensor")
    z = me // PLANE
    column = lax.rem(me, PLANE)
    column_x = column + 1 - 2 * lax.rem(column, 2)
    column_y = lax.rem(column + 2, PLANE)
    column_xy = lax.rem(column_x + 2, PLANE)
    up = z < planes - 1
    down = z > 0
    peers = (
        z * PLANE + column_x,
        z * PLANE + column_y,
        jnp.minimum(me + PLANE, PLANE * planes - 1),
        jnp.maximum(me - PLANE, 0),
    )
    rows = [pl.ds(at, size) for at, size in parts]

    def place(part, slot):
        return dec_own.at[slot] if part == PART_DEC else own_ref.at[slot, rows[part]]

    def copy(way, part, slot, mine=False):
        source = place(part, slot)
        if mine:
            source = dec_shard_ref if part == PART_DEC else shard_ref.at[rows[part]]
        return pltpu.make_async_remote_copy(
            src_ref=source,
            dst_ref=place(part, slot),
            send_sem=send_sems.at[way, part, slot],
            recv_sem=recv_sems.at[part, slot],
            device_id={"dp": peers[way]},
            device_id_type=MESH_ID,
        )

    def send(way, part, slot, mine=False):
        copy(way, part, slot, mine).start()

    def recv(part, slot):
        copy(WAY_X, part, slot).wait_recv()

    def pair(part, plane):
        block = pl.ds(plane * PLANE, PLANE)
        if part == PART_DEC:
            source, target = dec_own.at[block], dec_other.at[block]
        else:
            source, target = own_ref.at[block, rows[part]], other_ref.at[block, rows[part]]
        return pltpu.make_async_remote_copy(
            src_ref=source,
            dst_ref=target,
            send_sem=pair_sems.at[0, part, plane],
            recv_sem=pair_sems.at[1, part, plane],
            device_id={"tensor": 1 - half},
            device_id_type=MESH_ID,
        )

    def load(index):
        return pltpu.make_async_copy(
            error_ref.at[pl.ds(index * ERROR_ROWS, ERROR_ROWS)], held.at[index % 2], sems.at[index % 2]
        )

    load(0).start()
    load(1).start()
    dec_load = pltpu.make_async_copy(dec_error_ref, dec_held, sems.at[2])
    dec_load.start()

    shard_ref[...] = weights_ref[...].astype(bf16)
    spare = dec_shard_ref.shape[0] - dec_weights_ref.shape[0]
    count = jnp.zeros((spare, DD), f32) + (mask_ref[0] + mask_ref[1]).astype(f32)
    dec_shard_ref[...] = jnp.concatenate([dec_weights_ref[...], count], 0).astype(bf16)

    barrier = pltpu.get_barrier_semaphore()
    for way in (WAY_X, WAY_Y):
        pl.semaphore_signal(barrier, 1, device_id={"dp": peers[way]}, device_id_type=MESH_ID)
    pl.semaphore_signal(barrier, 1, device_id={"tensor": 1 - half}, device_id_type=MESH_ID)
    for ok, way in ((up, WAY_UP), (down, WAY_DOWN)):

        @pl.when(ok)
        def _(way=way):
            pl.semaphore_signal(barrier, 1, device_id={"dp": peers[way]}, device_id_type=MESH_ID)

    pl.semaphore_wait(barrier, 3 + up.astype(jnp.int32) + down.astype(jnp.int32))

    def both_z(part, slot, mine=False):
        @pl.when(up)
        def _():
            send(WAY_UP, part, slot, mine)

        @pl.when(down)
        def _():
            send(WAY_DOWN, part, slot, mine)

    def sides(distance):
        return [
            ((z + side * distance >= 0) & (z + side * distance < planes), z + side * distance, on, way)
            for side, on, way in ((-1, up, WAY_UP), (1, down, WAY_DOWN))
        ]

    def along(distance):
        for there, plane, on, way in sides(distance):

            @pl.when(there)
            def _(slot=plane * PLANE + column, on=on, way=way):
                for part in Z_X_Y_PARTS + (PART_Z_Y_X,):
                    recv(part, slot)

                    @pl.when(on)
                    def _():
                        send(way, part, slot)

                    send(WAY_Y if part == PART_Z_Y_X else WAY_X, part, slot)
                for part in Z_X_Y_PARTS:
                    send(WAY_Y, part, slot)
                send(WAY_X, PART_Z_Y_X, slot)

    def cross(distance):
        for there, plane, _, _ in sides(distance):

            @pl.when(there)
            def _(base=plane * PLANE):
                for part in Z_X_Y_PARTS:
                    recv(part, base + column_x)
                    send(WAY_Y, part, base + column_x)
                recv(PART_Z_Y_X, base + column_y)
                send(WAY_X, PART_Z_Y_X, base + column_y)

    def finish(distance):
        for there, plane, _, _ in sides(distance)[: 2 if distance else 1]:

            @pl.when(there)
            def _(plane=plane, base=plane * PLANE):
                for part in Z_X_Y_PARTS:
                    recv(part, base + column_y)
                    recv(part, base + column_xy)
                    pair(part, plane).start()
                recv(PART_Z_Y_X, base + column_x)
                recv(PART_Z_Y_X, base + column_xy)
                pair(PART_Z_Y_X, plane).start()

    def whole_plane(distance):
        for there, plane, on, way in sides(distance):

            @pl.when(there)
            def _(plane=plane, on=on, way=way):
                for index in range(PLANE):
                    slot = plane * PLANE + index
                    recv(PART_X_Y_Z, slot)

                    @pl.when(on)
                    def _(slot=slot):
                        send(way, PART_X_Y_Z, slot)

                pair(PART_X_Y_Z, plane).start()

    workers = planes * PLANE
    start3 = split3(start_ref[:, :D])
    chunks = error_ref.shape[0] // ERROR_ROWS

    def work(index):
        load(index).wait()
        lanes = pl.ds(index * ERROR_ROWS, ERROR_ROWS)
        part_ref[:, lanes] = fold3(nt(start3, held[index % 2]))
        if index + 2 < chunks:
            load(index + 2).start()

    send(WAY_X, PART_X_Y_Z, me, True)
    send(WAY_Y, PART_X_Y_Z, me, True)
    for part in (PART_DEC, PART_Z_X_Y, PART_Z_Y_X):
        both_z(part, me, True)
    for part in Z_X_Y_PARTS:
        send(WAY_X, part, me, True)
    send(WAY_Y, PART_Z_Y_X, me, True)
    send(WAY_X, PART_Z_Y_X, me, True)
    for part in Z_X_Y_PARTS:
        send(WAY_Y, part, me, True)
    keeps = [
        pltpu.make_async_copy(shard_ref, own_ref.at[me], sems.at[3]),
        pltpu.make_async_copy(dec_shard_ref, dec_own.at[me], sems.at[6]),
    ]
    for keep in keeps:
        keep.start()
    swap_pixels = pltpu.make_async_remote_copy(
        src_ref=tubes_ref.at[1 - half],
        dst_ref=pixels_ref,
        send_sem=sems.at[4],
        recv_sem=sems.at[5],
        device_id={"tensor": 1 - half},
        device_id_type=MESH_ID,
    )
    swap_pixels.start()
    small_swaps = [
        pltpu.make_async_remote_copy(
            src_ref=source,
            dst_ref=target,
            send_sem=sems.at[11 + 2 * index],
            recv_sem=sems.at[12 + 2 * index],
            device_id={"tensor": 1 - half},
            device_id_type=MESH_ID,
        )
        for index, (source, target) in enumerate(
            ((start_ref, start_other_ref), (split_ref, split_other_ref))
        )
    ]
    for small in small_swaps:
        small.start()
    loads = [
        pltpu.make_async_copy(tubes_ref.at[index], pix_held.at[clip], sems.at[7 + clip])
        for clip, index in ((0, half), (1, 1 - half))
    ]
    for get in loads:
        get.start()
    work(0)
    near = z * PLANE
    recv(PART_X_Y_Z, near + column_x)
    send(WAY_Y, PART_X_Y_Z, near + column_x)
    for part in Z_X_Y_PARTS:
        recv(part, near + column_x)
        send(WAY_Y, part, near + column_x)
    recv(PART_Z_Y_X, near + column_y)
    send(WAY_X, PART_Z_Y_X, near + column_y)
    for keep in keeps:
        keep.wait()
    place_index = lax.broadcasted_iota(jnp.int32, (1, TUBES), 1)
    place_index = place_index.astype(f32)
    orders = []
    for clip, (index, out) in enumerate(((half, picked_ref), (1 - half, picked_other_ref))):
        row = order_ref[pl.ds(index, 1), :VIS]
        if clip == 0:
            visible_ref[...] = row
        orders.append(jnp.broadcast_to(row.astype(f32), (8, VIS)).T[:, :1])
        loads[clip].wait()
        hot = jnp.where(orders[clip] == place_index, 1.0, 0.0).astype(bf16)
        out[...] = nn(hot, pix_held[clip]).astype(bf16)
    swap_picked = pltpu.make_async_remote_copy(
        src_ref=picked_other_ref,
        dst_ref=pix_other_ref,
        send_sem=sems.at[9],
        recv_sem=sems.at[10],
        device_id={"tensor": 1 - half},
        device_id_type=MESH_ID,
    )
    swap_picked.start()
    work(1)
    along(1)
    recv(PART_X_Y_Z, near + column_y)
    recv(PART_X_Y_Z, near + column_xy)
    for index in range(PLANE):
        both_z(PART_X_Y_Z, near + index)
    pair(PART_X_Y_Z, z).start()
    work(2)
    cross(1)
    finish(0)
    pos_enc_ref[...] = sinusoid_of(orders[0], D)
    work(3)
    along(2)
    first_place = lax.broadcasted_iota(jnp.int32, (TUBES // 32, 1), 0).astype(f32) * 32.0
    second_place = lax.broadcasted_iota(jnp.int32, (32, 1), 0).astype(f32)
    rate, even = rates(DD)
    first = first_place * rate
    second = second_place * rate
    ahead = jnp.where(even, jnp.sin(first), jnp.cos(first))
    turned = jnp.where(even, jnp.cos(first), -jnp.sin(first))
    cos2, sin2 = jnp.cos(second), jnp.sin(second)
    for index in range(TUBES // 32):
        pos_dec_ref[pl.ds(32 * index, 32)] = (
            ahead[index : index + 1] * cos2 + turned[index : index + 1] * sin2
        )
    work(4)
    whole_plane(1)
    cross(2)
    work(5)
    finish(1)
    along(3)
    work(6)
    whole_plane(2)
    cross(3)
    work(7)
    finish(2)
    dec_load.wait()
    dec_part_ref[...] = fold3(nt(split3(start_ref[:, D:]), dec_held[...]))
    whole_plane(3)
    finish(3)
    for plane in range(planes):
        pair(PART_DEC, plane).wait()
    total = jnp.zeros((1, 128), f32)
    per = joined.shape[1] // workers
    for index in range(workers):
        for group, ref in enumerate((dec_own, dec_other)):
            block = ref[index].astype(f32)
            joined[group, pl.ds(index * per, per)] = block[:per]
            if group == 0:
                total = total + block[per : per + 1, :128]
    for group in range(2):

        def matrix(at, size):
            return joined[group, pl.ds(at, size)].astype(bf16)

        wo_ref[pl.ds(group * DD // 2, DD // 2)] = matrix(DEC_O, DD // 2)
        for kind in range(3):
            wqkv_ref[pl.ds((2 * kind + group) * DD // 2, DD // 2)] = matrix(
                DEC_Q + kind * DD // 2, DD // 2
            )
        for ref, at in ((wd_ref, DEC_D), (wu_ref, DEC_U), (wh_ref, DEC_H)):
            ref[pl.ds(group * DFF // 2, DFF // 2)] = matrix(at, DFF // 2)
        proj_ref[half if group == 0 else 1 - half] = matrix(0, D // 2)
    counted = mask_ref[half].astype(f32)
    scal_ref[0:1] = jnp.zeros((1, 128), f32) + counted
    scal_ref[1:2] = counted * (2.0 * workers / PIX) / (MASKED * total)
    scal_ref[2:3] = MASKED * total
    scal_ref[3:8] = jnp.zeros((5, 128), f32)
    swap_pixels.wait()
    swap_picked.wait()
    for small in small_swaps:
        small.wait()
    dec_at = 2 * (2 * HALF + HALF_FF)
    bqkv_ref[...] = jnp.zeros_like(bqkv_ref)
    for group, ref in enumerate((split_ref, split_other_ref)):
        for kind in range(2):
            low = 2 * kind * DD + group * DD // 2
            bqkv_ref[:, low : low + DD // 2] = ref[:, dec_at + kind * DD // 2 : dec_at + (kind + 1) * DD // 2]
        for out, at in ((bu_ref, dec_at + DD), (bh_ref, dec_at + DD + DFF // 2)):
            out[:, group * DFF // 2 : (group + 1) * DFF // 2] = ref[:, at : at + DFF // 2]
    for plane in range(planes):
        for part in range(3):
            pair(part, plane).wait()
        for index in range(PLANE):
            slot = plane * PLANE + index

            @pl.when(column == index)
            def _():
                for part in (PART_DEC, PART_Z_X_Y, PART_Z_Y_X):
                    copy(WAY_X, part, slot).wait_send()
                    copy(WAY_Y, part, slot).wait_send()

            @pl.when(column_x == index)
            def _():
                for part in Z_X_Y_PARTS:
                    copy(WAY_Y, part, slot).wait_send()

            @pl.when(column_y == index)
            def _():
                copy(WAY_X, PART_Z_Y_X, slot).wait_send()

            for part in range(4):
                sent = True if part == PART_X_Y_Z else column == index

                @pl.when(up & (plane <= z) & sent)
                def _():
                    copy(WAY_UP, part, slot).wait_send()

                @pl.when(down & (plane >= z) & sent)
                def _():
                    copy(WAY_DOWN, part, slot).wait_send()

    copy(WAY_X, PART_X_Y_Z, me).wait_send()
    copy(WAY_Y, PART_X_Y_Z, me).wait_send()
    copy(WAY_Y, PART_X_Y_Z, near + column_x).wait_send()


def spare_rows(rows):
    return -(rows + 1) % 16 + 1


def gather_weights(planes, weights, dec_weights, tubes, error, dec_error, start, order, split, mask):
    workers = planes * PLANE
    size = weights.shape[0]
    dec_size = dec_weights.shape[0] + spare_rows(dec_weights.shape[0])
    same = dec_size * DD // D
    long = (size + same) * 2 // 5 // 16 * 16 + 16
    parts = ((0, long - same), (long - same, long), (2 * long - same, size - 2 * long + same))
    shards = jax.ShapeDtypeStruct((workers,) + weights.shape, bf16)
    low = lambda *shape: jax.ShapeDtypeStruct(shape, bf16)
    wide = lambda *shape: jax.ShapeDtypeStruct(shape, f32)
    dec_shards = pltpu.VMEM((workers, dec_size, DD), bf16)
    return pl.pallas_call(
        lambda *refs: gather_kernel(parts, planes, *refs),
        in_specs=[vmem_spec()] * 2
        + [any_spec()] * 3
        + [vmem_spec()] * 3
        + [pl.BlockSpec(memory_space=pltpu.SMEM)],
        out_specs=[any_spec()] * 3 + [vmem_spec()] * 20,
        out_shape=[
            shards,
            shards,
            jax.ShapeDtypeStruct(tubes.shape[1:], tubes.dtype),
            wide(RANK, error.shape[0]),
            wide(RANK, dec_error.shape[0]),
            low(VIS, D),
            low(VIS, D),
            low(VIS, D),
            wide(*start.shape),
            wide(*split.shape),
            jax.ShapeDtypeStruct((1, VIS), jnp.int32),
            wide(1, 3 * DD),
            wide(1, DFF),
            wide(1, PIX),
            wide(VIS, D),
            wide(TUBES, DD),
            wide(8, 128),
            low(2, D // 2, DD),
            low(3 * DD, DD),
            low(DD, DD),
            low(DFF, DD),
            low(DFF, DD),
            low(PIX, DD),
        ],
        scratch_shapes=[
            pltpu.VMEM((2, ERROR_ROWS, D), bf16),
            pltpu.VMEM(dec_error.shape, bf16),
            dec_shards,
            dec_shards,
            pltpu.VMEM((2, DEC_ROWS, DD), f32),
            pltpu.VMEM((2, TUBES, D), bf16),
            pltpu.VMEM(weights.shape, bf16),
            pltpu.VMEM((dec_size, DD), bf16),
            pltpu.SemaphoreType.DMA((4, 4, workers)),
            pltpu.SemaphoreType.DMA((4, workers)),
            pltpu.SemaphoreType.DMA((2, 4, planes)),
            pltpu.SemaphoreType.DMA((15,)),
        ],
        compiler_params=pltpu.CompilerParams(
            collective_id=3, has_side_effects=True, vmem_limit_bytes=BIG_VMEM
        ),
        name="gather_weights",
    )(weights, dec_weights, tubes, error, dec_error, start, order, split, mask)


def cut(block, widths):
    pieces = []
    start = 0
    for width in widths:
        pieces.append(block[start : start + width])
        start = start + width
    return pieces


def swap(value):
    return lax.ppermute(value, "tensor", [(0, 1), (1, 0)])


def per_device(
    tubes,
    tube_order,
    clip_mask,
    enc_weights,
    dec_weights,
    vec_split,
    vec_shared,
    enc_moment,
    dec_moment,
    split_moment,
    shared_moment,
    enc_error,
    dec_error,
    factors,
):
    workers = lax.axis_size("dp")
    half = lax.axis_index("tensor")
    worker_index = lax.axis_index("dp")
    mine = lambda both: lax.dynamic_index_in_dim(both, half, 0, keepdims=False)
    which = half.astype(jnp.int32)[None]
    enc_per = enc_weights.shape[1]
    start_own = factors[0]
    wide = vec_shared[: 15 * D].reshape(15, D)
    narrow = vec_shared[15 * D :].reshape(9, DD)
    if workers == 4 * PLANE:
        per = enc_per
        (
            enc_own, enc_other, pixels, enc_error_part, dec_error_part, pix_vis, picked_other,
            pix_vis_other, start_other, split_other, visible, bqkv, bu, bh, pos_enc, pos_dec, scal, proj, d_qkv, d_out, d_down, d_up, head_rows,
        ) = gather_weights(
            workers // PLANE, enc_weights[0], dec_weights[0], tubes, enc_error[0, 0], dec_error[0, 0],
            start_own,
            tube_order, vec_split, clip_mask,
        )
        proj = proj.reshape(D, DD)
        loss_weight = scal[2, 0]
    else:
        visible = mine(tube_order)[None, :VIS]
        start_other = swap(start_own)
        split_other = swap(vec_split)
        counted_all = clip_mask.astype(f32)
        counted = mine(counted_all)
        picked = pick_visible(which, tube_order, tubes)
        pix_vis, picked_other = picked
        pix_vis_other = swap(picked_other)
        own = lax.all_gather(enc_weights[0].astype(bf16), "dp", axis=0)
        dec_all = lax.all_gather(dec_weights[0].astype(bf16), "dp", axis=0)
        loss_weight = MASKED * lax.psum(jnp.sum(counted_all), "dp")
        pixels = swap(lax.dynamic_index_in_dim(tubes, 1 - half, 0, keepdims=False))
        per = enc_per * workers
        enc_own = own.reshape(1, per, D)
        enc_other = swap(enc_own)
        enc_error_part = error_factor(start_own[:, :D], enc_error[0, 0])
        dec_error_part = error_factor(start_own[:, D:], dec_error[0, 0])
        dec_own = dec_all.reshape(DEC_ROWS, DD)
        dec_other = swap(dec_own)
        dec_widths = [D // 2, DD // 2, DFF // 2, 3 * DD // 2, DFF // 2, PIX // 2]
        own_parts = cut(dec_own, dec_widths)
        other_parts = cut(dec_other, dec_widths)
        proj = jnp.where(
            half == 0,
            jnp.concatenate([own_parts[0], other_parts[0]], 0),
            jnp.concatenate([other_parts[0], own_parts[0]], 0),
        )
        d_out, d_down, d_up, head_rows = (
            jnp.concatenate([own_parts[index], other_parts[index]], 0) for index in (1, 2, 4, 5)
        )
        kinds = lambda block: block.reshape(3, DD // 2, DD)
        d_qkv = jnp.concatenate([kinds(own_parts[3]), kinds(other_parts[3])], 1)
        d_qkv = d_qkv.reshape(3 * DD, DD)
        pos_enc = sinusoid_of(visible.reshape(VIS, 1).astype(f32), D)
        pos_dec = sinusoid_of(jnp.arange(TUBES).astype(f32)[:, None], DD)
        scal = jnp.broadcast_to(
            jnp.stack([counted, 2.0 * workers / (PIX * loss_weight) * counted] + [counted] * 6)[
                :, None
            ],
            (8, 128),
        )
        dec_at = 2 * (2 * HALF + HALF_FF)
        bq, bv, bu, bh = (
            jnp.concatenate([split[:, at : at + size] for split in (vec_split, split_other)], 1)
            for at, size in (
                (dec_at, DD // 2),
                (dec_at + DD // 2, DD // 2),
                (dec_at + DD, DFF // 2),
                (dec_at + DD + DFF // 2, PIX // 2),
            )
        )
        bqkv = jnp.concatenate([bq, jnp.zeros_like(bq), bv], 1)
    starts = (start_own, start_other)
    splits = (vec_split, split_other)

    (enc_normed, latent, enc_out), kept = encoder(
        per, (pix_vis, pix_vis_other), pos_enc, proj, wide, splits, enc_own, enc_other
    )

    dec_start, h, qkv, hidden = decoder_qkv(
        visible, pos_dec, latent, narrow, d_qkv, bqkv
    )
    mixed, logs = attend(qkv)
    grad_mixed, grad_middle, dec_grads, dec_sent, g_vec, g_bu, g_bh, loss_lanes = decoder_tokens(
        which, mixed, dec_start, tubes, pixels, hidden, scal, narrow, bu, bh, d_out, d_down, d_up,
        head_rows,
    )
    dq, dk, dv = attend_back(qkv, mixed, grad_mixed, logs)
    latent_low, dec_grads, dec_sent, g_vec1 = decoder_qkv_back(
        which, visible, dq, dk, dv, h, dec_start, grad_middle, narrow, d_qkv, enc_normed,
        dec_grads, dec_sent,
    )
    dec_left = dec_left_factor(starts, dec_grads, dec_sent)
    dec_came = swap(dec_sent)

    back = encoder_back(
        per, latent_low, enc_out, proj, wide, (pix_vis, pix_vis_other), starts, kept, enc_own, enc_other
    )
    packs, sent, enc_lefts = ([layer[index] for layer in back] for index in range(3))
    enc_vec_grads = [layer[3:] for layer in back]
    came = [swap(value) for value in sent]
    mine_packs = (pix_vis, packs[0], packs[1])
    their_packs = (picked_other, came[0], came[1])

    (
        enc_basis, dec_basis, enc_right, dec_right, g_wide, g_narrow, g_split, turned, rights, dec_comb
    ) = compress(
        workers, enc_lefts[0], enc_lefts[1], dec_left, enc_error_part, dec_error_part,
        (*enc_vec_grads[0], *enc_vec_grads[1], g_vec, g_vec1, g_bu, g_bh, loss_lanes),
        enc_error[0, 0], mine_packs, their_packs, dec_grads, dec_came, dec_error[0, 0],
    )
    enc_error_new, dec_error_new = new_errors(
        turned, rights, enc_error[0, 0], dec_comb, (enc_right, dec_basis, dec_right)
    )
    enc_rows = enc_basis.shape[1] // workers
    dec_rows = dec_basis.shape[1] // workers
    enc_owned = lax.dynamic_slice_in_dim(enc_basis, worker_index * enc_rows, enc_rows, 1)
    dec_owned = lax.dynamic_slice_in_dim(dec_basis, worker_index * dec_rows, dec_rows, 1)
    enc_mom = momentum_keep * enc_moment[0] + jnp.einsum(
        "rx,rc->xc", enc_owned, enc_right, precision=highest_precision
    )
    dec_mom = momentum_keep * dec_moment[0] + jnp.einsum(
        "rx,rc->xc", dec_owned, dec_right, precision=highest_precision
    )
    pieces = vec_split.shape[1] // CHUNK
    split_mom = momentum_keep * split_moment[0] + g_split[:pieces].reshape(-1)
    shared_mom = momentum_keep * shared_moment + jnp.concatenate(
        [g_wide.reshape(-1), g_narrow.reshape(-1)]
    )
    return (
        jnp.sum(g_split[pieces]) * (workers / PIX),
        loss_weight,
        (enc_weights[0] - step_rate * enc_mom)[None],
        enc_mom[None],
        enc_error_new[None, None],
        (dec_weights[0] - step_rate * dec_mom)[None],
        dec_mom[None],
        dec_error_new[None, None],
        jnp.concatenate([enc_right, dec_right], 1)[None],
        (vec_split[0] - step_rate * split_mom)[None],
        split_mom[None],
        vec_shared - step_rate * shared_mom,
        shared_mom,
    )


def solution(mesh):
    placed = (
        P("dp", None, "tensor"),
        P("dp", None),
        P("dp"),
        P("tensor", "dp", None),
        P("tensor", "dp", None),
        P("tensor", None),
        P(),
        P("tensor", "dp", None),
        P("tensor", "dp", None),
        P("tensor", None),
        P(),
        P("dp", "tensor", None, None),
        P("dp", "tensor", None, None),
        P("tensor", None, None),
    )
    return jax.shard_map(
        per_device,
        mesh=mesh,
        in_specs=placed,
        out_specs=(
            P(),
            P(),
            P("tensor", "dp", None),
            P("tensor", "dp", None),
            P("dp", "tensor", None, None),
            P("tensor", "dp", None),
            P("tensor", "dp", None),
            P("dp", "tensor", None, None),
            P("tensor", None, None),
            P("tensor", None),
            P("tensor", None),
            P(),
            P(),
        ),
        check_vma=False,
    )
```

```python
import math

import jax
import jax.numpy as jnp
from jax import lax
from jax.experimental import pallas as pl
from jax.experimental.pallas import tpu as pltpu
from jax.sharding import PartitionSpec as P

D = 768
HEAD_DIM = 64
FF = 3072
DD = 384
DFF = 1536
PIX = 1536
TUBES = 1568
VIS = 160
MASKED = 1408
RANK = 8

f32 = jnp.float32
bf16 = jnp.bfloat16
highest_precision = lax.Precision.HIGHEST
norm_eps = 1e-06
momentum_keep = 0.9
step_rate = 1000.0
LOG2E = 1.4426950408889634
SCORE = HEAD_DIM ** (-0.5)
BIG_VMEM = 56 << 20


def nn(left, right):
    return lax.dot_general(left, right, (((1,), (0,)), ((), ())), preferred_element_type=f32)


def nt(left, right):
    return lax.dot_general(left, right, (((1,), (1,)), ((), ())), preferred_element_type=f32)


def tn(left, right):
    return lax.dot_general(left, right, (((0,), (0,)), ((), ())), preferred_element_type=f32)


def ahead(count, product):
    value = product(0)
    for index in range(count):
        later = product(index + 1) if index + 1 < count else None
        yield index, value
        value = later


def col_sum(value):
    return jnp.sum(value, 0, keepdims=True)


def norm_parts(stream):
    center = stream - jnp.mean(stream, -1, keepdims=True)
    rate = lax.rsqrt(jnp.mean(center * center, -1, keepdims=True) + norm_eps)
    return center * rate, rate


def norm_back(grad, gain, unit, rate):
    grad_unit = grad * gain
    return rate * (
        grad_unit
        - jnp.mean(grad_unit, -1, keepdims=True)
        - unit * jnp.mean(grad_unit * unit, -1, keepdims=True)
    )


def gelu_pair(before):
    cdf_tail = jnp.exp(-0.5 * before * before)
    size = jnp.abs(before) * (2.0 ** -0.5)
    t = 1.0 / (1.0 + 0.3275911 * size)
    poly = t * (
        0.254829592 + t * (-0.284496736 + t * (1.421413741 + t * (-1.453152027 + t * 1.061405429)))
    )
    tail = 0.5 * poly * cdf_tail
    cdf = jnp.where(before < 0, tail, 1.0 - tail)
    return before * cdf, cdf + before * cdf_tail * (1.0 / math.sqrt(2.0 * math.pi))


def split3(value):
    high = value.astype(bf16)
    rest = value - high.astype(f32)
    middle = rest.astype(bf16)
    low = (rest - middle.astype(f32)).astype(bf16)
    return jnp.concatenate([high, middle, low], 0)


def fold3(value):
    rows = value.shape[0] // 3
    return value[:rows] + value[rows : 2 * rows] + value[2 * rows :]


def rates(width):
    column = lax.broadcasted_iota(jnp.int32, (1, width), 1)
    low_bit = lax.rem(column, 2)
    rate = jnp.exp((column - low_bit).astype(f32) * (-math.log(10000.0) / width))
    return rate, low_bit == 0


def sinusoid_of(place, width):
    rate, even = rates(width)
    angle = place * rate
    return jnp.where(even, jnp.sin(angle), jnp.cos(angle))


def params(**more):
    return pltpu.CompilerParams(vmem_limit_bytes=BIG_VMEM, **more)


def whole(shape):
    return pl.BlockSpec(shape, lambda *_: (0,) * len(shape))


def any_spec():
    return pl.BlockSpec(memory_space=pl.ANY)


def vmem_spec():
    return pl.BlockSpec(memory_space=pltpu.VMEM)


def pick_kernel(half_ref, order_ref, tubes_ref, out_ref):
    column = lax.broadcasted_iota(jnp.int32, (1, TUBES), 1)
    hot = jnp.where(order_ref[0] == column, 1.0, 0.0).astype(bf16)
    out_ref[0] = nn(hot, tubes_ref[0]).astype(bf16)


def pick_visible(half, order, tubes):
    clips, _, width = tubes.shape
    which = lambda c, half_ref: jnp.where(c == 0, half_ref[0], 1 - half_ref[0])
    return pl.pallas_call(
        pick_kernel,
        grid_spec=pltpu.PrefetchScalarGridSpec(
            num_scalar_prefetch=1,
            grid=(clips,),
            in_specs=[
                pl.BlockSpec((1, VIS, 1), lambda c, half_ref: (which(c, half_ref), 0, 0)),
                pl.BlockSpec((1, TUBES, width), lambda c, half_ref: (which(c, half_ref), 0, 0)),
            ],
            out_specs=pl.BlockSpec((1, VIS, width), lambda c, half_ref: (c, 0, 0)),
        ),
        out_shape=jax.ShapeDtypeStruct((clips, VIS, width), bf16),
        compiler_params=params(),
        name="pick_visible",
    )(half, order[:, :VIS, None], tubes)


QKV_ROWS = 392


def place_matrix(order, rows):
    place = lax.broadcasted_iota(jnp.int32, (rows, 1), 0) + pl.program_id(0) * rows
    return jnp.where(order == place, 1.0, 0.0)


def qkv_kernel(order_ref, pos_ref, latent_ref, vec_ref, w_ref, bias_ref, x_ref, h_ref, qkv_ref, hidden_ref):
    token, gain, shift = (vec_ref[index : index + 1] for index in range(3))
    places = place_matrix(order_ref[...], QKV_ROWS)
    hidden = 1.0 - jnp.sum(places, 1, keepdims=True)
    hidden_ref[...] = hidden
    latent = split3(latent_ref[...])
    places = places.astype(bf16)
    shown = sum(nn(places, latent[VIS * part : VIS * (part + 1)]) for part in (2, 1, 0))
    x = pos_ref[...] + (shown + hidden * token)
    x_ref[...] = x
    unit, _ = norm_parts(x)
    h = (unit * gain + shift).astype(bf16)
    h_ref[...] = h
    qkv_ref[...] = (nt(h, w_ref[...]) + bias_ref[...]).astype(bf16)


def decoder_qkv(order, pos, latent, vecs, weights, bias):
    rows = lambda width: pl.BlockSpec((QKV_ROWS, width), lambda i: (i, 0))
    return pl.pallas_call(
        qkv_kernel,
        grid=(TUBES // QKV_ROWS,),
        in_specs=[
            whole((1, VIS)),
            rows(DD),
            whole((VIS, DD)),
            whole(vecs.shape),
            whole((3 * DD, DD)),
            whole((1, 3 * DD)),
        ],
        out_specs=[rows(DD), rows(DD), rows(3 * DD), rows(1)],
        out_shape=[
            jax.ShapeDtypeStruct((TUBES, DD), f32),
            jax.ShapeDtypeStruct((TUBES, DD), bf16),
            jax.ShapeDtypeStruct((TUBES, 3 * DD), bf16),
            jax.ShapeDtypeStruct((TUBES, 1), f32),
        ],
        compiler_params=params(),
        name="decoder_qkv",
    )(order, pos, latent, vecs, weights, bias)


PAIRS = DD // 128


def half_lane(index):
    return lax.broadcasted_iota(jnp.int32, (1, 128), 1) // HEAD_DIM == index


ATTEND_ROWS = 784


def attend_kernel(q_ref, k_ref, v_ref, o_ref, lse_ref):
    k = k_ref[...]
    v_one = jnp.concatenate([v_ref[...], jnp.ones((TUBES, 128), bf16)], 1)
    turns = [(at, head) for at in range(0, TUBES, ATTEND_ROWS) for head in range(2)]

    def scores_of(turn):
        at, head = turn
        q = q_ref[pl.ds(at, ATTEND_ROWS)]
        return nt(jnp.where(half_lane(head), q, jnp.zeros_like(q)), k)

    mixed, logs = [], []
    scores = scores_of(turns[0])
    for index, (at, head) in enumerate(turns):
        later = scores_of(turns[index + 1]) if index + 1 < len(turns) else None
        top = jnp.max(scores, 1, keepdims=True)
        expo = jnp.exp2((scores - top) * (SCORE * LOG2E)).astype(bf16)
        both = nn(expo, v_one)
        total = both[:, 128:]
        mixed.append(both[:, :128] / total)
        logs.append(top * (SCORE * LOG2E) + jnp.log2(total))
        if head == 1:
            rows = pl.ds(at, ATTEND_ROWS)
            o_ref[rows] = jnp.where(half_lane(0), mixed[-2], mixed[-1])
            lse_ref[0, rows] = jnp.where(half_lane(0), logs[-2], logs[-1])
        scores = later


def attend(qkv):
    pair = lambda kind: pl.BlockSpec((TUBES, 128), lambda p: (0, kind * PAIRS + p))
    return pl.pallas_call(
        attend_kernel,
        grid=(PAIRS,),
        in_specs=[pair(0), pair(1), pair(2)],
        out_specs=[pair(0), pl.BlockSpec((1, TUBES, 128), lambda p: (p, 0, 0))],
        out_shape=[
            jax.ShapeDtypeStruct((TUBES, DD), f32),
            jax.ShapeDtypeStruct((PAIRS, TUBES, 128), f32),
        ],
        compiler_params=params(),
        name="attend",
    )(qkv, qkv, qkv)


def attend_back_kernel(q_ref, k_ref, v_ref, o_ref, do_ref, lse_ref, dq_ref, dk_ref, dv_ref):
    q, k, v, grad = q_ref[...], k_ref[...], v_ref[...], do_ref[...]
    k_turned = k.T
    dots = o_ref[...] * grad.astype(f32)
    logs = lse_ref[0].T
    select = (
        lax.broadcasted_iota(jnp.int32, (8, 128), 1) // HEAD_DIM
        == lax.broadcasted_iota(jnp.int32, (8, 128), 0)
    ).astype(f32)
    row_total = lax.dot_general(
        select, dots, (((1,), (1,)), ((), ())), precision=highest_precision,
        preferred_element_type=f32,
    )
    zero = jnp.zeros((), bf16)
    dk = dv = jnp.zeros((TUBES, 128), f32)
    turned = []
    for head in range(2):
        mask = half_lane(head)
        q_head = jnp.where(mask, q, zero)
        grad_head = jnp.where(mask, grad, zero)
        low = head * HEAD_DIM
        probs = jnp.exp2(nt(k, q_head) * (SCORE * LOG2E) - logs[low : low + 1])
        grad_scores = (probs * (nt(v, grad_head) - row_total[head : head + 1])).astype(bf16)
        dv = dv + nn(probs.astype(bf16), grad_head)
        dk = dk + nn(grad_scores, q_head)
        turned.append(nn(k_turned[low : low + HEAD_DIM], grad_scores))
    dq_ref[...] = (jnp.concatenate(turned, 0).T * SCORE).astype(bf16)
    dk_ref[...] = (dk * SCORE).astype(bf16)
    dv_ref[...] = dv.astype(bf16)


def attend_back(qkv, mixed, grad_mixed, logs):
    pair = lambda kind: pl.BlockSpec((TUBES, 128), lambda p: (0, kind * PAIRS + p))
    return pl.pallas_call(
        attend_back_kernel,
        grid=(PAIRS,),
        in_specs=[
            pair(0),
            pair(1),
            pair(2),
            pair(0),
            pair(0),
            pl.BlockSpec((1, TUBES, 128), lambda p: (p, 0, 0)),
        ],
        out_specs=[pair(0)] * 3,
        out_shape=[jax.ShapeDtypeStruct((TUBES, DD), bf16)] * 3,
        compiler_params=params(),
        name="attend_back",
    )(qkv, qkv, qkv, mixed, grad_mixed, logs)


TOKEN_ROWS = 784
CHUNK = 384
WIDE = 768
DEC_O = D // 2
DEC_D = DEC_O + DD // 2
DEC_Q = DEC_D + DFF // 2
DEC_U = DEC_Q + 3 * DD // 2
DEC_H = DEC_U + DFF // 2
DEC_ROWS = DEC_H + PIX // 2
CHUNKS = DFF // CHUNK


def token_kernel(
    _, a_ref, x_ref, pix_ref, pix_other_ref, hidden_ref, scal_ref, vec_ref, bu_ref, bh_ref,
    wo_ref, wd_ref, wu_ref, wh_ref,
    da_ref, dx1_ref,
    own_ref, other_ref, gvec_ref, gbu_ref, gbh_ref, loss_ref,
    slope,
):
    step = pl.program_id(0)
    sums = (own_ref, other_ref, gvec_ref, gbu_ref, gbh_ref, loss_ref)
    grads = (own_ref, other_ref)

    @pl.when(step == 0)
    def _():
        for ref in sums:
            ref[...] = jnp.zeros_like(ref)

    bo, g2, b2, bd, gf, sf = (vec_ref[index : index + 1] for index in range(3, 9))
    a = a_ref[...].astype(bf16)
    x1 = x_ref[...] + (nn(a, wo_ref[...]) + bo)
    unit2, rate2 = norm_parts(x1)
    h2 = (unit2 * g2 + b2).astype(bf16)
    out = x1 + bd
    active = []
    part_of = lambda chunk: pl.ds(chunk * WIDE, WIDE)
    for chunk, before in ahead(2, lambda chunk: nt(h2, wu_ref[part_of(chunk)])):
        part = part_of(chunk)
        value, slope_part = gelu_pair(before + bu_ref[:, part])
        slope[:, part] = slope_part
        active.append(value.astype(bf16))
        out = out + nn(active[-1], wd_ref[part])
    unit_f, rate_f = norm_parts(out)
    final = (unit_f * gf + sf).astype(bf16)
    pixels = [ref[...].astype(f32) for ref in (pix_ref.at[0], pix_other_ref)]
    center = sum(jnp.sum(part, 1, keepdims=True) for part in pixels) * (1.0 / PIX)
    square = sum(jnp.sum(part * part, 1, keepdims=True) for part in pixels) * (1.0 / PIX)
    spread = lax.rsqrt(square - center * center + norm_eps)
    counted = hidden_ref[...] * scal_ref[0:1, 0:1]
    rate = hidden_ref[...] * scal_ref[1:2, 0:1]
    grad_final = jnp.zeros((TOKEN_ROWS, DD), f32)
    for chunk, guess in ahead(2, lambda chunk: nt(final, wh_ref[part_of(chunk)])):
        part = part_of(chunk)
        target = (pixels[chunk] - center) * spread
        miss = guess + bh_ref[:, part] - target
        loss_ref[:, part] += col_sum(counted * miss * miss)
        grad_guess = (rate * miss).astype(bf16)
        gbh_ref[:, part] += col_sum(grad_guess.astype(f32))
        grads[chunk][pl.ds(DEC_H, WIDE)] += tn(grad_guess, final)
        grad_final = grad_final + nn(grad_guess, wh_ref[part])
    grad_out = norm_back(grad_final, gf, unit_f, rate_f)
    out_low = grad_out.astype(bf16)
    grad_h2 = jnp.zeros((TOKEN_ROWS, DD), f32)
    for chunk, grad_active in ahead(2, lambda chunk: nt(out_low, wd_ref[part_of(chunk)])):
        part = part_of(chunk)
        grads[chunk][pl.ds(DEC_D, WIDE)] += tn(active[chunk], out_low)
        grad_before = (slope[:, part] * grad_active).astype(bf16)
        gbu_ref[:, part] += col_sum(grad_before.astype(f32))
        grads[chunk][pl.ds(DEC_U, WIDE)] += tn(grad_before, h2)
        grad_h2 = grad_h2 + nn(grad_before, wu_ref[part])
    grad_x1 = grad_out + norm_back(grad_h2, g2, unit2, rate2)
    x1_low = grad_x1.astype(bf16)
    g_out = tn(a, x1_low)
    for group in range(2):
        grads[group][pl.ds(DEC_O, DD // 2)] += g_out[group * DD // 2 : (group + 1) * DD // 2]
    da_ref[...] = nt(x1_low, wo_ref[...]).astype(bf16)
    dx1_ref[...] = grad_x1
    gvec_ref[0:1] += col_sum(x1_low.astype(f32))
    gvec_ref[1:2] += col_sum(grad_h2 * unit2)
    gvec_ref[2:3] += col_sum(grad_h2)
    gvec_ref[3:4] += col_sum(out_low.astype(f32))
    gvec_ref[4:5] += col_sum(grad_final * unit_f)
    gvec_ref[5:6] += col_sum(grad_final)


def decoder_tokens(half, mixed, x, tubes, pixels, hidden, scal, vecs, bu, bh, wo, wd, wu, wh):
    rows = lambda width: pl.BlockSpec((TOKEN_ROWS, width), lambda i, _: (i, 0))
    sums = [(DEC_ROWS, DD), (DEC_ROWS, DD), (8, DD), (1, DFF), (1, PIX), (1, PIX)]
    return pl.pallas_call(
        token_kernel,
        grid_spec=pltpu.PrefetchScalarGridSpec(
            num_scalar_prefetch=1,
            grid=(TUBES // TOKEN_ROWS,),
            in_specs=[
                rows(DD),
                rows(DD),
                pl.BlockSpec((1, TOKEN_ROWS, PIX // 2), lambda i, half_ref: (half_ref[0], i, 0)),
                rows(PIX // 2),
                rows(1),
                whole((8, 128)),
                whole(vecs.shape),
                whole((1, DFF)),
                whole((1, PIX)),
                whole((DD, DD)),
                whole((DFF, DD)),
                whole((DFF, DD)),
                whole((PIX, DD)),
            ],
            out_specs=[rows(DD), rows(DD)] + [whole(shape) for shape in sums],
            scratch_shapes=[pltpu.VMEM((TOKEN_ROWS, DFF), f32)],
        ),
        out_shape=[
            jax.ShapeDtypeStruct((TUBES, DD), bf16),
            jax.ShapeDtypeStruct((TUBES, DD), f32),
        ]
        + [jax.ShapeDtypeStruct(shape, f32) for shape in sums],
        compiler_params=params(),
        name="decoder_tokens",
    )(half, mixed, x, tubes, pixels, hidden, scal, vecs, bu, bh, wo, wd, wu, wh)


def qkv_back_kernel(
    half_ref, order_ref, dq_ref, dk_ref, dv_ref, h_ref, x_ref, dx1_ref, vec_ref, w_ref, normed_ref,
    _own, _other,
    latent_ref, own_ref, other_ref, gvec_ref,
    g_qkv, g_proj, latent_sum, sems,
):
    step = pl.program_id(0)

    @pl.when(step == 0)
    def _():
        g_qkv[...] = jnp.zeros_like(g_qkv)
        gvec_ref[...] = jnp.zeros_like(gvec_ref)
        latent_sum[...] = jnp.zeros_like(latent_sum)

    h = h_ref[...]
    grads = (dq_ref[...], dk_ref[...], dv_ref[...])
    grad_h = jnp.zeros((QKV_ROWS, DD), f32)
    for index, grad in enumerate(grads):
        g_both = tn(grad, h)
        for group in range(2):
            rows = pl.ds(index * DD // 2, DD // 2)
            g_qkv[group, rows] += g_both[group * DD // 2 : (group + 1) * DD // 2]
        grad_h = grad_h + nn(grad, w_ref[pl.ds(index * DD, DD)])
    unit, rate = norm_parts(x_ref[...])
    grad_x = dx1_ref[...] + norm_back(grad_h, vec_ref[1:2], unit, rate)
    places = place_matrix(order_ref[...], QKV_ROWS)
    hidden = 1.0 - jnp.sum(places, 1, keepdims=True)
    latent_sum[...] += tn(places.astype(bf16), grad_x.astype(bf16))
    gvec_ref[0:1] += col_sum(grads[0].astype(f32))
    gvec_ref[1:2] += col_sum(grads[2].astype(f32))
    gvec_ref[2:3] += col_sum(grad_h * unit)
    gvec_ref[3:4] += col_sum(grad_h)
    gvec_ref[4:5] += col_sum(hidden * grad_x)

    @pl.when(step == pl.num_programs(0) - 1)
    def _():
        latent = latent_sum[...].astype(bf16)
        latent_ref[...] = latent
        both = tn(normed_ref[...], latent)
        g_proj[0] = both[: D // 2]
        g_proj[1] = both[D // 2 :]
        half = half_ref[0]
        kinds = pl.ds(DEC_Q, 3 * DD // 2)
        copies = [
            pltpu.make_async_copy(g_qkv.at[0], own_ref.at[kinds], sems.at[0]),
            pltpu.make_async_copy(g_qkv.at[1], other_ref.at[kinds], sems.at[1]),
            pltpu.make_async_copy(g_proj.at[half], own_ref.at[pl.ds(0, D // 2)], sems.at[2]),
            pltpu.make_async_copy(g_proj.at[1 - half], other_ref.at[pl.ds(0, D // 2)], sems.at[3]),
        ]
        for copy in copies:
            copy.start()
        for copy in copies:
            copy.wait()


def decoder_qkv_back(half, order, dq, dk, dv, h, x, dx1, vecs, weights, normed, own, other):
    rows = lambda width: pl.BlockSpec((QKV_ROWS, width), lambda i: (i, 0))
    return pl.pallas_call(
        qkv_back_kernel,
        grid=(TUBES // QKV_ROWS,),
        in_specs=[pl.BlockSpec(memory_space=pltpu.SMEM), whole((1, VIS))]
        + [rows(DD)] * 6
        + [whole(vecs.shape), whole((3 * DD, DD)), whole((VIS, D)), any_spec(), any_spec()],
        out_specs=[whole((VIS, DD)), any_spec(), any_spec(), whole((8, DD))],
        out_shape=[
            jax.ShapeDtypeStruct((VIS, DD), bf16),
            jax.ShapeDtypeStruct((DEC_ROWS, DD), f32),
            jax.ShapeDtypeStruct((DEC_ROWS, DD), f32),
            jax.ShapeDtypeStruct((8, DD), f32),
        ],
        scratch_shapes=[
            pltpu.VMEM((2, 3 * DD // 2, DD), f32),
            pltpu.VMEM((2, D // 2, DD), f32),
            pltpu.VMEM((VIS, DD), f32),
            pltpu.SemaphoreType.DMA((4,)),
        ],
        input_output_aliases={11: 1, 12: 2},
        compiler_params=params(),
        name="decoder_qkv_back",
    )(half, order, dq, dk, dv, h, x, dx1, vecs, weights, normed, own, other)


HALF = D // 2
HALF_FF = FF // 2
LAYER_ROWS = 4 * HALF + 2 * HALF_FF
ENC_ROWS = D + 2 * LAYER_ROWS
AT_O, AT_D, AT_Q, AT_U = 0, HALF, HALF + HALF_FF, HALF + HALF_FF + 3 * HALF
STAGES = ((AT_Q, 3 * HALF), (AT_O, HALF), (AT_U, HALF_FF), (AT_D, HALF_FF))


def pieces_of(start, size, per):
    pieces = []
    at = start
    while at < start + size:
        many = min(start + size, (at // per + 1) * per) - at
        pieces.append((at // per, at % per, many, at - start))
        at += many
    return pieces


def stage_copies(sources, per, held, sems, stages):
    copies = []
    count = 0
    first = min(at for at, _ in stages)
    for at, size in stages:
        stage = []
        for shard, row, many, before in pieces_of(at, size, per):
            for group in range(2):
                stage.append(
                    pltpu.make_async_copy(
                        sources[group].at[shard, pl.ds(row, many)],
                        held.at[group, pl.ds(at - first + before, many)],
                        sems.at[count],
                    )
                )
                count += 1
        copies.append(stage)
    return copies


MOST_COPIES = 96


def layer_stages(layer):
    start = D + layer * LAYER_ROWS
    return [(start + at, size) for at, size in STAGES]


def encoder_kernel(per, *refs):
    pix_ref, pix_other_ref, pos_ref, proj_ref, vec_ref, split_own_ref, split_other_ref = refs[:7]
    splits = (split_own_ref, split_other_ref)
    own_ref, other_ref, normed_ref, latent_ref, out_ref = refs[7:12]
    kept = (refs[12:20], refs[20:28])
    held, sems = refs[28:]
    copies = stage_copies(
        (own_ref, other_ref), per, held, sems, [(0, D)] + layer_stages(0) + layer_stages(1)
    )
    for stage in copies:
        for copy in stage:
            copy.start()

    def wait(stage):
        for copy in copies[stage]:
            copy.wait()

    wait(0)
    x = pos_ref[...] + vec_ref[0:1]
    for group, pixels in enumerate((pix_ref, pix_other_ref)):
        x = x + nn(pixels[...], held[group, pl.ds(0, D)])
    for layer in range(2):
        stages = [1 + 4 * layer + index for index in range(4)]
        x = encoder_layer(layer, x, vec_ref, splits, held, lambda index: wait(stages[index]), kept[layer])
    out_ref[...] = x
    unit3, _ = norm_parts(x)
    normed = (unit3 * vec_ref[13:14] + vec_ref[14:15]).astype(bf16)
    normed_ref[...] = normed
    latent_ref[...] = nn(normed, proj_ref[...])


def encoder_layer(layer, x, vec_ref, splits, held, wait, kept):
    x_ref, h_ref, qkv_ref, a_ref, x1_ref, h2_ref, u_ref, slope_ref = kept
    base = 1 + 6 * layer
    biases = layer * (2 * HALF + HALF_FF)
    start = D + layer * LAYER_ROWS
    g1, b1, bo, g2, b2, bd = (vec_ref[base + index : base + index + 1] for index in range(6))
    x_ref[...] = x
    unit, _ = norm_parts(x)
    h = (unit * g1 + b1).astype(bf16)
    h_ref[...] = h
    wait(0)
    for kind in range(3):
        for group in range(2):
            part = pl.ds((2 * kind + group) * HALF, HALF)
            value = nt(h, held[group, pl.ds(start + AT_Q + kind * HALF, HALF)])
            if kind != 1:
                at = biases + kind // 2 * HALF
                value = value + splits[group][:, at : at + HALF]
            qkv_ref[:, part] = value.astype(bf16)
    for pair in range(D // 128):
        q, k, v = (qkv_ref[:, pl.ds(kind * D + pair * 128, 128)] for kind in range(3))
        v_one = jnp.concatenate([v, jnp.ones((VIS, 128), bf16)], 1)
        mixed = []
        for head in range(2):
            scores = nt(jnp.where(half_lane(head), q, jnp.zeros_like(q)), k)
            top = jnp.max(scores, 1, keepdims=True)
            expo = jnp.exp2((scores - top) * (SCORE * LOG2E)).astype(bf16)
            both = nn(expo, v_one)
            mixed.append(both[:, :128] / both[:, 128:])
        a_ref[:, pl.ds(pair * 128, 128)] = jnp.where(half_lane(0), mixed[0], mixed[1]).astype(bf16)
    wait(1)
    x1 = x + bo
    for group in range(2):
        x1 = x1 + nn(a_ref[:, pl.ds(group * HALF, HALF)], held[group, pl.ds(start + AT_O, HALF)])
    x1_ref[...] = x1
    unit2, _ = norm_parts(x1)
    h2 = (unit2 * g2 + b2).astype(bf16)
    h2_ref[...] = h2
    wait(2)
    wait(3)
    out = x1 + bd
    for group in range(2):
        rows_of = lambda chunk: pl.ds(start + AT_U + chunk * WIDE, WIDE)
        for chunk, before in ahead(HALF_FF // WIDE, lambda chunk: nt(h2, held[group, rows_of(chunk)])):
            part = pl.ds(group * HALF_FF + chunk * WIDE, WIDE)
            at = biases + 2 * HALF + chunk * WIDE
            value, slope = gelu_pair(before + splits[group][:, at : at + WIDE])
            slope_ref[:, part] = slope
            active = value.astype(bf16)
            u_ref[:, part] = active
            out = out + nn(active, held[group, pl.ds(start + AT_D + chunk * WIDE, WIDE)])
    return out


def encoder(per, pixels, pos, proj, vecs, splits, own, other):
    shapes = [((VIS, D), bf16), ((VIS, DD), f32), ((VIS, D), f32)] + 2 * [
        ((VIS, D), f32),
        ((VIS, D), bf16),
        ((VIS, 3 * D), bf16),
        ((VIS, D), bf16),
        ((VIS, D), f32),
        ((VIS, D), bf16),
        ((VIS, FF), bf16),
        ((VIS, FF), f32),
    ]
    result = pl.pallas_call(
        lambda *refs: encoder_kernel(per, *refs),
        in_specs=[vmem_spec()] * 7 + [any_spec()] * 2,
        out_specs=[vmem_spec()] * len(shapes),
        out_shape=[jax.ShapeDtypeStruct(shape, kind) for shape, kind in shapes],
        scratch_shapes=[
            pltpu.VMEM((2, ENC_ROWS, D), bf16),
            pltpu.SemaphoreType.DMA((MOST_COPIES,)),
        ],
        compiler_params=params(),
        name="encoder",
    )(*pixels, pos, proj, vecs, *splits, own, other)
    return result[:3], (result[3:11], result[11:])


RIGHT_AT = LAYER_ROWS


def encoder_back_kernel(per, *refs):
    (
        latent_ref, out_ref, proj_ref, vec_ref, pix_ref, pix_other_ref, start_ref, start_other_ref
    ) = refs[:8]
    kept = (refs[8:16], refs[16:24])
    own_ref, other_ref = refs[24:26]
    results = (refs[26:32], refs[32:38])
    held, sems, da, dqkv = refs[38:]
    order = (3, 2, 1, 0)
    stages = [layer_stages(layer)[index] for layer in (1, 0) for index in order]
    copies = stage_copies((own_ref, other_ref), per, held, sems, stages)
    for stage in copies:
        for copy in stage:
            copy.start()

    def wait(turn, index):
        for copy in copies[4 * turn + order.index(index)]:
            copy.wait()

    starts = jnp.concatenate([split3(ref[:, :D]) for ref in (start_ref, start_other_ref)], 0)
    grad = None
    for turn, layer in enumerate((1, 0)):
        grad = encoder_layer_back(
            layer, grad, latent_ref, out_ref, proj_ref, vec_ref, starts, (pix_ref, pix_other_ref),
            kept[layer], held, lambda index: wait(turn, index), da, dqkv, results[layer],
        )


def encoder_layer_back(
    layer, grad, latent_ref, out_ref, proj_ref, vec_ref, starts, pixels, kept, held, wait, da, dqkv, results
):
    last = layer == 1
    base = 1 + 6 * layer
    start = layer * LAYER_ROWS
    x_ref, h_ref, qkv_ref, a_ref, x1_ref, h2_ref, u_ref, slope_ref = kept
    mine_ref, other_pack_ref, left_ref, gvec_ref, gbu_ref, gbq_ref = results
    packs = (mine_ref, other_pack_ref)
    g1, b1, bo, g2, b2, bd = (vec_ref[base + index : base + index + 1] for index in range(6))
    gvec_ref[6:8] = jnp.zeros((2, D), f32)
    if last:
        unit3, rate3 = norm_parts(out_ref[...])
        grad_normed = nt(latent_ref[...], proj_ref[...])
        grad_out = norm_back(grad_normed, vec_ref[13:14], unit3, rate3)
        gvec_ref[6:7] = col_sum(grad_normed * unit3)
        gvec_ref[7:8] = col_sum(grad_normed)
    else:
        grad_out = grad
    out_low = grad_out.astype(bf16)
    unit2, rate2 = norm_parts(x1_ref[...])
    grad_h2 = jnp.zeros((VIS, D), f32)
    wait(3)
    wait(2)
    for group in range(2):
        for chunk in range(HALF_FF // WIDE):
            part = pl.ds(group * HALF_FF + chunk * WIDE, WIDE)
            grad_active = nt(out_low, held[group, pl.ds(start + AT_D + chunk * WIDE, WIDE)])
            grad_before = (slope_ref[:, part] * grad_active).astype(bf16)
            packs[group][:, pl.ds(AT_U + chunk * WIDE, WIDE)] = grad_before
            packs[group][:, pl.ds(AT_D + chunk * WIDE, WIDE)] = u_ref[:, part]
            gbu_ref[:, part] = col_sum(grad_before.astype(f32))
            grad_h2 = grad_h2 + nn(grad_before, held[group, pl.ds(start + AT_U + chunk * WIDE, WIDE)])
    grad_x1 = grad_out + norm_back(grad_h2, g2, unit2, rate2)
    x1_low = grad_x1.astype(bf16)
    wait(1)
    for group in range(2):
        part = pl.ds(group * HALF, HALF)
        da[:, part] = nt(x1_low, held[group, pl.ds(start + AT_O, HALF)]).astype(bf16)
        packs[group][:, pl.ds(AT_O, HALF)] = a_ref[:, part]
    zero = jnp.zeros((), bf16)
    for pair in range(D // 128):
        lanes = pl.ds(pair * 128, 128)
        q, k, v = (qkv_ref[:, pl.ds(kind * D + pair * 128, 128)] for kind in range(3))
        grad = da[:, lanes]
        dq = dk = dv = jnp.zeros((VIS, 128), f32)
        for head in range(2):
            mask = half_lane(head)
            q_head = jnp.where(mask, q, zero)
            grad_head = jnp.where(mask, grad, zero)
            scores = nt(q_head, k) * SCORE
            expo = jnp.exp(scores - jnp.max(scores, 1, keepdims=True))
            probs = expo / jnp.sum(expo, 1, keepdims=True)
            grad_probs = nt(grad_head, v)
            row_total = jnp.sum(probs * grad_probs, 1, keepdims=True)
            grad_scores = (probs * (grad_probs - row_total)).astype(bf16)
            dv = dv + tn(probs.astype(bf16), grad_head)
            dk = dk + tn(grad_scores, q_head)
            dq = dq + nn(grad_scores, jnp.where(mask, k, zero))
        dqkv[:, lanes] = (dq * SCORE).astype(bf16)
        dqkv[:, pl.ds(D + pair * 128, 128)] = (dk * SCORE).astype(bf16)
        dqkv[:, pl.ds(2 * D + pair * 128, 128)] = dv.astype(bf16)
    wait(0)
    grad_h = jnp.zeros((VIS, D), f32)
    for kind in range(3):
        for group in range(2):
            grad = dqkv[:, pl.ds((2 * kind + group) * HALF, HALF)]
            rows = pl.ds(AT_Q + kind * HALF, HALF)
            packs[group][:, rows] = grad
            grad_h = grad_h + nn(
                grad, held[group, pl.ds(start + AT_Q + kind * HALF, HALF)]
            )
    unit, rate = norm_parts(x_ref[...])
    grad_x = grad_x1 + norm_back(grad_h, g1, unit, rate)
    gbq_ref[0:1] = col_sum(dqkv[:, pl.ds(0, D)].astype(f32))
    gbq_ref[1:2] = col_sum(dqkv[:, pl.ds(2 * D, D)].astype(f32))
    gvec_ref[0:1] = col_sum(grad_h * unit)
    gvec_ref[1:2] = col_sum(grad_h)
    gvec_ref[2:3] = col_sum(x1_low.astype(f32))
    gvec_ref[3:4] = col_sum(grad_h2 * unit2)
    gvec_ref[4:5] = col_sum(grad_h2)
    gvec_ref[5:6] = col_sum(out_low.astype(f32))
    rights = [x1_low, out_low, h_ref[...], h2_ref[...]]
    spans = [(AT_O, HALF, 0), (AT_D, HALF_FF, 0), (AT_Q, 3 * HALF, 0), (AT_U, HALF_FF, 0)]
    if not last:
        embed_low = grad_x.astype(bf16)
        rights.append(embed_low)
        gvec_ref[6:7] = col_sum(embed_low.astype(f32))
    before = 0 if last else D
    for index, right in enumerate(rights):
        for pack in packs:
            pack[:, pl.ds(RIGHT_AT + index * D, D)] = right
        inner = nt(starts, right)
        for group in range(2):
            parts = split3(fold3(inner[3 * RANK * group : 3 * RANK * (group + 1)]))
            if index == 4:
                value = fold3(nn(parts, pixels[group][...]))
                left_ref[group, :, pl.ds(0, D)] = value
            else:
                at, size, _ = spans[index]
                value = fold3(nn(parts, packs[group][:, pl.ds(at, size)]))
                left_ref[group, :, pl.ds(before + at, size)] = value
    return grad_x


def encoder_back(per, latent, out, proj, vecs, pixels, starts, kept, own, other):
    shapes = []
    for layer in range(2):
        width = RIGHT_AT + (5 - layer) * D
        shapes += [
            ((VIS, width), bf16),
            ((VIS, width), bf16),
            ((2, RANK, LAYER_ROWS + (1 - layer) * D), f32),
            ((8, D), f32),
            ((1, FF), f32),
            ((2, D), f32),
        ]
    result = pl.pallas_call(
        lambda *refs: encoder_back_kernel(per, *refs),
        in_specs=[vmem_spec()] * 24 + [any_spec()] * 2,
        out_specs=[vmem_spec()] * len(shapes),
        out_shape=[jax.ShapeDtypeStruct(shape, kind) for shape, kind in shapes],
        scratch_shapes=[
            pltpu.VMEM((2, 2 * LAYER_ROWS, D), bf16),
            pltpu.SemaphoreType.DMA((MOST_COPIES,)),
            pltpu.VMEM((VIS, D), bf16),
            pltpu.VMEM((VIS, 3 * D), bf16),
        ],
        compiler_params=pltpu.CompilerParams(vmem_limit_bytes=60 << 20),
        name="encoder_back",
    )(latent, out, proj, vecs, *pixels, *starts, *kept[0], *kept[1], own, other)
    return result[:6], result[6:]


HALF_ROWS = 384


def error_factor_kernel(start_ref, error_ref, out_ref):
    turned = nt(error_ref[...], split3(start_ref[...]))
    out_ref[...] = fold3(turned.T)


def error_factor(start, error):
    rows, width = error.shape
    return pl.pallas_call(
        error_factor_kernel,
        grid=(rows // HALF_ROWS,),
        in_specs=[whole((RANK, width)), pl.BlockSpec((HALF_ROWS, width), lambda j: (j, 0))],
        out_specs=pl.BlockSpec((RANK, HALF_ROWS), lambda j: (0, j)),
        out_shape=jax.ShapeDtypeStruct((RANK, rows), f32),
        compiler_params=params(),
        name="error_factor",
    )(start, error)


def low_left(basis3):
    high, middle = basis3[:RANK], basis3[RANK : 2 * RANK]
    return jnp.concatenate([high, high, middle, jnp.zeros_like(high)], 0)


def low_right(factor3):
    high = factor3[:RANK]
    return jnp.concatenate([factor3[: 2 * RANK], high, jnp.zeros_like(high)], 0)


DEC_BLOCK = 1152


def dec_left_kernel(start_ref, start_other_ref, own_ref, other_ref, out_ref):
    for group, (begin_ref, ref) in enumerate(((start_ref, own_ref), (start_other_ref, other_ref))):
        start = split3(begin_ref[:, D:])
        grad = ref[...]
        high = grad.astype(bf16)
        rest = (grad - high.astype(f32)).astype(bf16)
        out_ref[group] = fold3(nt(start, high) + nt(start, rest))


def dec_left_factor(starts, own, other):
    rows = pl.BlockSpec((DEC_BLOCK, DD), lambda j: (j, 0))
    return pl.pallas_call(
        dec_left_kernel,
        grid=(DEC_ROWS // DEC_BLOCK,),
        in_specs=[whole((RANK, D + DD))] * 2 + [rows, rows],
        out_specs=pl.BlockSpec((2, RANK, DEC_BLOCK), lambda j: (0, 0, j)),
        out_shape=jax.ShapeDtypeStruct((2, RANK, DEC_ROWS), f32),
        compiler_params=params(),
        name="dec_left_factor",
    )(*starts, own, other)


MESH_ID = pl.DeviceIdType.MESH
PLANE = 4


def levels_of(workers):
    return (PLANE, workers // PLANE) if workers == 4 * PLANE else (workers,)


def peers_of(workers, me, level):
    counts = levels_of(workers)
    if len(counts) == 1:
        return [lax.rem(me + distance, workers) for distance in range(1, workers)]
    plane, column = me // PLANE, lax.rem(me, PLANE)
    if level == 0:
        return [plane * PLANE + lax.rem(column + d, PLANE) for d in range(1, counts[0])]
    return [lax.rem(plane + d, counts[1]) * PLANE + column for d in range(1, counts[1])]


def greet(workers, me, partner):
    barrier = pltpu.get_barrier_semaphore()
    count = 0
    for level in range(len(levels_of(workers))):
        for peer in peers_of(workers, me, level):
            pl.semaphore_signal(barrier, 1, device_id={"dp": peer}, device_id_type=MESH_ID)
            count += 1
    pl.semaphore_signal(barrier, 1, device_id={"tensor": partner}, device_id_type=MESH_ID)
    pl.semaphore_wait(barrier, count + 1)


def sum_workers(workers, me, lanes, local, slots, sums, sems, work=lambda turn: None):
    counts = levels_of(workers)
    deep = len(counts) == 2
    if deep:
        plane, column = me // PLANE, lax.rem(me, PLANE)
        own, inner = column, plane
        sizes = (lanes * counts[1], lanes)
    else:
        own, inner = me, 0
        sizes = (lanes, 0)

    def span(level, index, base=0):
        return pl.ds(pl.multiple_of(base + index * sizes[level], 128), sizes[level])

    base = own * sizes[0]
    peers = [peers_of(workers, me, level) for level in range(len(counts))]
    places = [
        [lax.rem(mine + d, count) for d in range(1, count)]
        for mine, count in zip((own, inner), counts)
    ]
    first_sem = [0, counts[0]]

    def exchange(turn, level, source, target):
        copies = []
        for index, peer in enumerate(peers[level]):
            sem = first_sem[level] + index
            copy = pltpu.make_async_remote_copy(
                src_ref=source(index),
                dst_ref=target(index),
                send_sem=sems.at[2 * turn, sem],
                recv_sem=sems.at[2 * turn + 1, sem],
                device_id={"dp": peer},
                device_id_type=MESH_ID,
            )
            copy.start()
            copies.append(copy)
        return copies

    def slot(level, index):
        at = index * sizes[0] if level == 0 else counts[0] * sizes[0] + index * sizes[1]
        return slots.at[:, pl.ds(at, sizes[level])]

    def gathered(level, copies, total):
        for index, copy in enumerate(copies):
            copy.wait_recv()
            total = total + slot(level, index)[...]
        return total

    sent = exchange(
        0, 0, lambda index: local.at[:, span(0, places[0][index])], lambda index: slot(0, index)
    )
    work(0)
    here = span(0, own)
    total = gathered(0, sent, local[:, here])
    if deep:
        local[:, here] = total
        more = exchange(
            0, 1, lambda index: local.at[:, span(1, places[1][index], base)],
            lambda index: slot(1, index),
        )
        work(1)
        share = span(1, inner, base)
        sums[:, share] = gathered(1, more, local[:, share])
        back = exchange(1, 1, lambda _: sums.at[:, share], lambda _: sums.at[:, share])
        work(2)
        for copy in more:
            copy.wait_send()
        for copy in back:
            copy.wait()
    else:
        sums[:, here] = total
        work(1)
        work(2)
    last = exchange(1, 0, lambda _: sums.at[:, here], lambda _: sums.at[:, here])
    work(3)
    for copy in sent:
        copy.wait_send()
    for copy in last:
        copy.wait()


def sum_small(workers, me, local, slots, sums, sems, work):
    width = local.shape[1]
    counts = levels_of(workers)
    if len(counts) == 1:
        work(0)
        work(1)
        sum_workers(workers, me, width // workers, local, slots, sums, sems)
        return
    places = (lax.rem(me, PLANE), me // PLANE)
    for level, count in enumerate(counts):
        base = 0 if level == 0 else counts[0]

        def slot(index):
            return slots.at[:, pl.ds(pl.multiple_of((base + index) * width, 128), width)]

        mine = slot(places[level])
        mine[...] = local[...] if level == 0 else sums[...]
        copies = []
        for index, peer in enumerate(peers_of(workers, me, level)):
            copy = pltpu.make_async_remote_copy(
                src_ref=mine,
                dst_ref=mine,
                send_sem=sems.at[2 * level, index],
                recv_sem=sems.at[2 * level + 1, index],
                device_id={"dp": peer},
                device_id_type=MESH_ID,
            )
            copy.start()
            copies.append(copy)
        work(level)
        for copy in copies:
            copy.wait()
        total = slot(0)[...]
        for index in range(1, count):
            total = total + slot(index)[...]
        sums[...] = total


def orthonormal(left):
    place = lax.broadcasted_iota(jnp.int32, (RANK, 1), 0)
    gram = lax.dot_general(
        left, left, (((1,), (1,)), ((), ())), precision=highest_precision,
        preferred_element_type=f32,
    )
    for index in range(RANK):
        scale = lax.rsqrt(gram[index : index + 1, index : index + 1])
        column = gram[:, index : index + 1] * scale
        below = jnp.where(place > index, column, 0.0)
        pivot = left[index : index + 1] * scale
        left = jnp.where(place == index, pivot, left - below * pivot)
        gram = gram - below * (gram[index : index + 1] * scale)
    return left


def lanes_for(width, workers):
    return pl.cdiv(width, 128 * workers) * 128


RANGES = [(0, D)] + [
    (D + layer * LAYER_ROWS + at, size)
    for layer in range(2)
    for at, size in ((AT_O, HALF), (AT_D, HALF_FF), (AT_Q, 3 * HALF), (AT_U, HALF_FF))
]
LOW = 4 * RANK
LOADS = 2 * (3 + len(RANGES)) + 4 + 3
ERROR_PARTS = 4


def compress_kernel(
    workers, lanes,
    first_ref, second_ref, dec_ref, error_part_ref, dec_error_part_ref,
    enc_vec0_ref, enc_bu0_ref, enc_bq0_ref, enc_vec1_ref, enc_bu1_ref, enc_bq1_ref,
    dec_vec_ref, dec_vec1_ref, dec_bu_ref, dec_bh_ref, loss_ref,
    error_ref, pix_ref, pack0_ref, pack1_ref, pix_came_ref, pack0_came_ref, pack1_came_ref,
    dec_own_ref, dec_came_ref, dec_error_ref,
    enc_basis, dec_basis, enc_factor, dec_factor, wide_out, narrow_out, split_out,
    turned_out, rights_out, comb_out,
    send, came, local, slots, sums, local2, slots2, sums2, parts, dec_parts,
    held, lefts, turned, rights, comb, dec_came, dec_held,
    sems, sems2, pair_sems, load_sems, out_sems,
):
    me = lax.axis_index("dp")
    half = lax.axis_index("tensor")
    first = first_ref.shape[2]
    factor_width = ENC_ROWS + DEC_ROWS
    width = factor_width + VEC_LANES
    clips = ((pix_ref, pack0_ref, pack1_ref), (pix_came_ref, pack0_came_ref, pack1_came_ref))

    left_loads, right_loads, error_loads, dec_loads = [], [], [], []

    def load(group, source, target):
        count = sum(len(loads) for loads in (left_loads, right_loads, error_loads, dec_loads))
        group.append(pltpu.make_async_copy(source, target, load_sems.at[count]))

    def begin(group):
        for copy in group:
            copy.start()

    for clip, (pixels, pack0, pack1) in enumerate(clips):
        load(left_loads, pixels, lefts.at[clip, :, pl.ds(0, D)])
        for layer, pack in enumerate((pack0, pack1)):
            target = lefts.at[clip, :, pl.ds(D + layer * LAYER_ROWS, LAYER_ROWS)]
            load(left_loads, pack.at[:, pl.ds(0, LAYER_ROWS)], target)
    size = ENC_ROWS // ERROR_PARTS
    for index in range(ERROR_PARTS):
        block = pl.ds(index * size, size)
        load(error_loads, error_ref.at[block], held.at[block])
    for clip, (_, pack0, pack1) in enumerate(clips):
        rows = pl.ds(clip * VIS, VIS)
        load(right_loads, pack0.at[:, pl.ds(RIGHT_AT + 4 * D, D)], rights.at[0, rows])
        for layer, pack in enumerate((pack0, pack1)):
            for kind in range(4):
                target = rights.at[1 + 4 * layer + kind, rows]
                load(right_loads, pack.at[:, pl.ds(RIGHT_AT + kind * D, D)], target)
    load(dec_loads, dec_own_ref, comb)
    load(dec_loads, dec_came_ref, dec_came)
    load(dec_loads, dec_error_ref, dec_held)

    spans = ((first_ref, 0, first), (second_ref, first, ENC_ROWS - first), (dec_ref, ENC_ROWS, DEC_ROWS))
    for ref, at, size in spans:
        send[:, at : at + size] = ref[1]
    shared_refs = (enc_vec0_ref, enc_vec1_ref, dec_vec_ref, dec_vec1_ref)
    for target in (send, local):
        at = factor_width
        for ref in shared_refs:
            target[:, at : at + ref.shape[1]] = ref[...]
            at += ref.shape[1]
    for group, target in ((1, send), (0, local)):
        pieces = []
        for bq_ref, bu_ref in ((enc_bq0_ref, enc_bu0_ref), (enc_bq1_ref, enc_bu1_ref)):
            for row in range(2):
                pieces.append(bq_ref[row : row + 1, group * HALF : (group + 1) * HALF])
            for index in range(HALF_FF // CHUNK):
                low = group * HALF_FF + index * CHUNK
                pieces.append(bu_ref[:, low : low + CHUNK])
        low = group * DD // 2
        pieces.append(
            jnp.concatenate([dec_vec1_ref[row : row + 1, low : low + DD // 2] for row in range(2)], 1)
        )
        for ref in (dec_bu_ref, dec_bh_ref):
            for index in range(2):
                low = (2 * group + index) * CHUNK
                pieces.append(ref[:, low : low + CHUNK])
        pieces.append(sum(loss_ref[:, index * CHUNK : (index + 1) * CHUNK] for index in range(CHUNKS)))
        pieces += [jnp.zeros((1, CHUNK), f32)] * (3 * RANK - len(pieces))
        for index in range(3):
            low = at + index * CHUNK
            target[:, low : low + CHUNK] = jnp.concatenate(pieces[RANK * index : RANK * (index + 1)], 0)
    if width < workers * lanes:
        tail = jnp.zeros((RANK, workers * lanes - width), f32)
        send[:, width:] = tail
    greet(workers, me, 1 - half)
    pair = pltpu.make_async_remote_copy(
        src_ref=send,
        dst_ref=came,
        send_sem=pair_sems.at[0],
        recv_sem=pair_sems.at[1],
        device_id={"tensor": 1 - half},
        device_id_type=MESH_ID,
    )
    pair.start()
    for ref, at, size in spans[:2]:
        local[:, at : at + size] = ref[0] + error_part_ref[:, at : at + size]
    local[:, ENC_ROWS:factor_width] = dec_ref[0] + dec_error_part_ref[...]
    if width < workers * lanes:
        local[:, width:] = tail
    pair.wait()
    local[...] += came[...]

    blocks = ENC_ROWS // HALF_ROWS
    dec_blocks = DEC_ROWS // HALF_ROWS

    def rows_of(index):
        return pl.ds(pl.multiple_of(index * HALF_ROWS, HALF_ROWS), HALF_ROWS)

    def turn(index, _):
        rows = rows_of(index)
        both = jnp.concatenate([lefts[0, :, rows], lefts[1, :, rows]], 0)
        turned[rows, 0 : 2 * VIS] = both.T
        return 0

    def combine(index, _):
        rows = rows_of(index)
        comb[rows] = comb[rows] + dec_came[rows] + dec_held[rows].astype(f32)
        return 0

    def meanwhile(phase):
        if phase == 0:
            begin(left_loads)
        elif phase == 1:
            begin(dec_loads)
            for copy in left_loads:
                copy.wait()
            lax.fori_loop(0, 10, turn, 0)
        elif phase == 2:
            begin(error_loads)
            lax.fori_loop(10, 18, turn, 0)
        else:
            begin(right_loads)
            lax.fori_loop(18, blocks, turn, 0)
            for copy in dec_loads:
                copy.wait()
            lax.fori_loop(0, dec_blocks, combine, 0)

    sum_workers(workers, me, lanes, local, slots, sums, sems, meanwhile)
    enc = orthonormal(sums[:, :ENC_ROWS])
    enc_basis[...] = enc
    parts[...] = split3(enc)
    dec = orthonormal(sums[:, ENC_ROWS:factor_width])
    dec_basis[...] = dec
    dec_parts[...] = split3(dec)

    for copy in error_loads + right_loads:
        copy.wait()
    stores = [
        pltpu.make_async_copy(source, target, out_sems.at[index])
        for index, (source, target) in enumerate(
            ((rights, rights_out), (comb, comb_out), (turned, turned_out))
        )
    ]
    begin(stores[:2])
    wide_rows = 2 * HALF_ROWS

    def add_error(index, total):
        rows = pl.ds(pl.multiple_of(index * wide_rows, wide_rows), wide_rows)
        return total + nn(parts[:, rows], held[rows])

    total = lax.fori_loop(0, ENC_ROWS // wide_rows, add_error, jnp.zeros((3 * RANK, D), f32))
    inners = [nn(parts[:, pl.ds(at, size)], turned[pl.ds(at, size), 0 : 2 * VIS]) for at, size in RANGES]
    inners = [split3(fold3(inner)) for inner in inners]
    for index, inner in enumerate(inners):
        total = total + nn(inner, rights[index])
    local2[:, :D] = fold3(total)

    def add_dec(index, total):
        rows = rows_of(index)
        block = comb[rows]
        high = block.astype(bf16)
        rest = (block - high.astype(f32)).astype(bf16)
        return total + nn(dec_parts[:, rows], high) + nn(dec_parts[:, rows], rest)

    local2[:, D : D + DD] = fold3(
        lax.fori_loop(0, dec_blocks, add_dec, jnp.zeros((3 * RANK, DD), f32))
    )
    if D + DD < local2.shape[1]:
        local2[:, D + DD :] = jnp.zeros((RANK, local2.shape[1] - D - DD), f32)
    mean = lambda at, size: sums[:, at : at + size] * (1.0 / workers)
    at = factor_width
    vec0, vec1 = mean(at, D), mean(at + D, D)
    dec0, dec1 = mean(at + 2 * D, DD), mean(at + 2 * D + DD, DD)
    wide_out[...] = jnp.concatenate([vec0[6:7], vec0[:6], vec1], 0)
    narrow_out[...] = jnp.concatenate([dec1[4:5], dec1[2:4], dec0[:6]], 0)
    for index in range(3):
        split_out[RANK * index : RANK * (index + 1)] = mean(at + 2 * D + 2 * DD + index * CHUNK, CHUNK)

    def turn_basis(index, _):
        rows = rows_of(index)
        turned[rows, 2 * VIS :] = low_left(parts[:, rows]).T
        return 0

    def meanwhile2(level):
        if level == 0:
            lax.fori_loop(0, blocks // 2, turn_basis, 0)
        else:
            lax.fori_loop(blocks // 2, blocks, turn_basis, 0)
            stores[2].start()

    sum_small(workers, me, local2, slots2, sums2, sems2, meanwhile2)
    for copy in stores:
        copy.wait()
    enc_factor[...] = sums2[:, :D] * (1.0 / workers)
    dec_factor[...] = sums2[:, D : D + DD] * (1.0 / workers)


VEC_LANES = 2 * D + 2 * DD + 3 * CHUNK


def compress(
    workers, first, second, dec, error_part, dec_error_part, vecs, error, mine, came, dec_own, dec_came,
    dec_error,
):
    lanes = lanes_for(ENC_ROWS + DEC_ROWS + VEC_LANES, workers)
    wide = pltpu.VMEM((RANK, workers * lanes), f32)
    small = D + DD if len(levels_of(workers)) == 2 else workers * lanes_for(D + DD, workers)
    wide2 = pltpu.VMEM((RANK, small), f32)
    return pl.pallas_call(
        lambda *refs: compress_kernel(workers, lanes, *refs),
        in_specs=[vmem_spec()] * (5 + len(vecs)) + [any_spec()] * 10,
        out_specs=[vmem_spec()] * 7 + [any_spec()] * 3,
        out_shape=[
            jax.ShapeDtypeStruct((RANK, ENC_ROWS), f32),
            jax.ShapeDtypeStruct((RANK, DEC_ROWS), f32),
            jax.ShapeDtypeStruct((RANK, D), f32),
            jax.ShapeDtypeStruct((RANK, DD), f32),
            jax.ShapeDtypeStruct((15, D), f32),
            jax.ShapeDtypeStruct((9, DD), f32),
            jax.ShapeDtypeStruct((3 * RANK, CHUNK), f32),
            jax.ShapeDtypeStruct((ENC_ROWS, 2 * VIS + LOW), bf16),
            jax.ShapeDtypeStruct((len(RANGES), 2 * VIS, D), bf16),
            jax.ShapeDtypeStruct((DEC_ROWS, DD), f32),
        ],
        scratch_shapes=[
            wide,
            wide,
            wide,
            pltpu.VMEM((RANK, (workers + 4) * lanes), f32),
            wide,
            wide2,
            pltpu.VMEM((RANK, 8 * small), f32),
            wide2,
            pltpu.VMEM((3 * RANK, ENC_ROWS), bf16),
            pltpu.VMEM((3 * RANK, DEC_ROWS), bf16),
            pltpu.VMEM((ENC_ROWS, D), bf16),
            pltpu.VMEM((2, VIS, ENC_ROWS), bf16),
            pltpu.VMEM((ENC_ROWS, 2 * VIS + LOW), bf16),
            pltpu.VMEM((len(RANGES), 2 * VIS, D), bf16),
            pltpu.VMEM((DEC_ROWS, DD), f32),
            pltpu.VMEM((DEC_ROWS, DD), f32),
            pltpu.VMEM((DEC_ROWS, DD), bf16),
            pltpu.SemaphoreType.DMA((4, workers)),
            pltpu.SemaphoreType.DMA((4, workers)),
            pltpu.SemaphoreType.DMA((2,)),
            pltpu.SemaphoreType.DMA((LOADS,)),
            pltpu.SemaphoreType.DMA((4,)),
        ],
        compiler_params=pltpu.CompilerParams(
            collective_id=1, has_side_effects=True, vmem_limit_bytes=60 << 20
        ),
        name="compress",
    )(
        first, second, dec, error_part, dec_error_part, *vecs, error, *mine, *came, dec_own, dec_came,
        dec_error,
    )


def new_errors_kernel(
    turned_ref, rights_ref, error_ref, comb_ref, enc_factor_ref, basis_ref, factor_ref,
    out_ref, dec_out_ref,
    turned, rights, held, comb, dec_held, in_sems, out_sems,
):
    blocks = ENC_ROWS // HALF_ROWS
    dec_blocks = DEC_ROWS // HALF_ROWS

    def rows_of(index):
        start = index * HALF_ROWS
        if not isinstance(index, int):
            start = pl.multiple_of(start, HALF_ROWS)
        return pl.ds(start, HALF_ROWS)

    def loads(index):
        rows = rows_of(index)
        return (
            pltpu.make_async_copy(error_ref.at[rows], held.at[rows], in_sems.at[0, index]),
            pltpu.make_async_copy(turned_ref.at[rows], turned.at[rows], in_sems.at[1, index]),
        )

    def right_load(kind):
        target = rights.at[kind, pl.ds(0, 2 * VIS)]
        return pltpu.make_async_copy(rights_ref.at[kind], target, in_sems.at[2, kind])

    def store(index):
        rows = rows_of(index)
        return pltpu.make_async_copy(held.at[rows], out_ref.at[rows], out_sems.at[index])

    comb_load = pltpu.make_async_copy(comb_ref, comb, in_sems.at[2, len(RANGES)])
    comb_load.start()
    for kind, (at, size) in enumerate(RANGES):
        right_load(kind).start()
        for index in range(at // HALF_ROWS, (at + size) // HALF_ROWS):
            for copy in loads(index):
                copy.start()
    comb_load.wait()
    dec_right = low_right(split3(-factor_ref[...]))
    enc_right = low_right(split3(-enc_factor_ref[...]))
    for kind in range(len(RANGES)):
        rights[kind, 2 * VIS :] = enc_right

    def dec_residue(index, _):
        rows = rows_of(index)
        left = low_left(split3(basis_ref[:, rows]))
        dec_held[rows] = (comb[rows] + tn(left, dec_right)).astype(bf16)
        return 0

    lax.fori_loop(0, dec_blocks, dec_residue, 0)
    dec_store = pltpu.make_async_copy(dec_held, dec_out_ref, out_sems.at[blocks])
    dec_store.start()
    for kind, (at, size) in enumerate(RANGES):
        right_load(kind).wait()

        def residue(index, _, kind=kind):
            for copy in loads(index):
                copy.wait()
            rows = rows_of(index)
            value = nn(turned[rows], rights[kind]) + held[rows].astype(f32)
            held[rows] = value.astype(bf16)
            store(index).start()
            return 0

        lax.fori_loop(at // HALF_ROWS, (at + size) // HALF_ROWS, residue, 0)
    for index in range(blocks):
        store(index).wait()
    dec_store.wait()


def new_errors(turned, rights, error, comb, bases):
    blocks = ENC_ROWS // HALF_ROWS
    return pl.pallas_call(
        new_errors_kernel,
        in_specs=[any_spec()] * 4 + [vmem_spec()] * 3,
        out_specs=[any_spec()] * 2,
        out_shape=[
            jax.ShapeDtypeStruct((ENC_ROWS, D), bf16),
            jax.ShapeDtypeStruct((DEC_ROWS, DD), bf16),
        ],
        scratch_shapes=[
            pltpu.VMEM(turned.shape, bf16),
            pltpu.VMEM((len(RANGES), 2 * VIS + LOW, D), bf16),
            pltpu.VMEM(error.shape, bf16),
            pltpu.VMEM(comb.shape, f32),
            pltpu.VMEM(comb.shape, bf16),
            pltpu.SemaphoreType.DMA((3, blocks)),
            pltpu.SemaphoreType.DMA((blocks + 1,)),
        ],
        compiler_params=params(),
        name="new_errors",
    )(turned, rights, error, comb, *bases)


PART_Z_X_Y, PART_Z_Y_X, PART_X_Y_Z, PART_DEC = range(4)
Z_X_Y_PARTS = (PART_DEC, PART_Z_X_Y)
WAY_X, WAY_Y, WAY_UP, WAY_DOWN = range(4)
ERROR_ROWS = 1248


def gather_kernel(
    parts, planes, weights_ref, dec_weights_ref, tubes_ref, error_ref, dec_error_ref, start_ref, order_ref,
    split_ref, mask_ref,
    own_ref, other_ref, pixels_ref, part_ref, dec_part_ref, picked_ref, picked_other_ref, pix_other_ref,
    start_other_ref, split_other_ref, visible_ref, bqkv_ref, bu_ref, bh_ref, pos_enc_ref, pos_dec_ref, scal_ref, proj_ref, wqkv_ref, wo_ref, wd_ref, wu_ref, wh_ref,
    held, dec_held, dec_own, dec_other, joined, pix_held, shard_ref, dec_shard_ref,
    send_sems, recv_sems, pair_sems, sems,
):
    me = lax.axis_index("dp")
    half = lax.axis_index("tensor")
    z = me // PLANE
    column = lax.rem(me, PLANE)
    column_x = column + 1 - 2 * lax.rem(column, 2)
    column_y = lax.rem(column + 2, PLANE)
    column_xy = lax.rem(column_x + 2, PLANE)
    up = z < planes - 1
    down = z > 0
    peers = (
        z * PLANE + column_x,
        z * PLANE + column_y,
        jnp.minimum(me + PLANE, PLANE * planes - 1),
        jnp.maximum(me - PLANE, 0),
    )
    rows = [pl.ds(at, size) for at, size in parts]

    def place(part, slot):
        return dec_own.at[slot] if part == PART_DEC else own_ref.at[slot, rows[part]]

    def copy(way, part, slot, mine=False):
        source = place(part, slot)
        if mine:
            source = dec_shard_ref if part == PART_DEC else shard_ref.at[rows[part]]
        return pltpu.make_async_remote_copy(
            src_ref=source,
            dst_ref=place(part, slot),
            send_sem=send_sems.at[way, part, slot],
            recv_sem=recv_sems.at[part, slot],
            device_id={"dp": peers[way]},
            device_id_type=MESH_ID,
        )

    def send(way, part, slot, mine=False):
        copy(way, part, slot, mine).start()

    def recv(part, slot):
        copy(WAY_X, part, slot).wait_recv()

    def pair(part, plane):
        block = pl.ds(plane * PLANE, PLANE)
        if part == PART_DEC:
            source, target = dec_own.at[block], dec_other.at[block]
        else:
            source, target = own_ref.at[block, rows[part]], other_ref.at[block, rows[part]]
        return pltpu.make_async_remote_copy(
            src_ref=source,
            dst_ref=target,
            send_sem=pair_sems.at[0, part, plane],
            recv_sem=pair_sems.at[1, part, plane],
            device_id={"tensor": 1 - half},
            device_id_type=MESH_ID,
        )

    def load(index):
        return pltpu.make_async_copy(
            error_ref.at[pl.ds(index * ERROR_ROWS, ERROR_ROWS)], held.at[index % 2], sems.at[index % 2]
        )

    load(0).start()
    load(1).start()
    dec_load = pltpu.make_async_copy(dec_error_ref, dec_held, sems.at[2])
    dec_load.start()

    shard_ref[...] = weights_ref[...].astype(bf16)
    spare = dec_shard_ref.shape[0] - dec_weights_ref.shape[0]
    count = jnp.zeros((spare, DD), f32) + (mask_ref[0] + mask_ref[1]).astype(f32)
    dec_shard_ref[...] = jnp.concatenate([dec_weights_ref[...], count], 0).astype(bf16)

    barrier = pltpu.get_barrier_semaphore()
    for way in (WAY_X, WAY_Y):
        pl.semaphore_signal(barrier, 1, device_id={"dp": peers[way]}, device_id_type=MESH_ID)
    pl.semaphore_signal(barrier, 1, device_id={"tensor": 1 - half}, device_id_type=MESH_ID)
    for ok, way in ((up, WAY_UP), (down, WAY_DOWN)):

        @pl.when(ok)
        def _(way=way):
            pl.semaphore_signal(barrier, 1, device_id={"dp": peers[way]}, device_id_type=MESH_ID)

    pl.semaphore_wait(barrier, 3 + up.astype(jnp.int32) + down.astype(jnp.int32))

    def both_z(part, slot, mine=False):
        @pl.when(up)
        def _():
            send(WAY_UP, part, slot, mine)

        @pl.when(down)
        def _():
            send(WAY_DOWN, part, slot, mine)

    def sides(distance):
        return [
            ((z + side * distance >= 0) & (z + side * distance < planes), z + side * distance, on, way)
            for side, on, way in ((-1, up, WAY_UP), (1, down, WAY_DOWN))
        ]

    def along(distance):
        for there, plane, on, way in sides(distance):

            @pl.when(there)
            def _(slot=plane * PLANE + column, on=on, way=way):
                for part in Z_X_Y_PARTS + (PART_Z_Y_X,):
                    recv(part, slot)

                    @pl.when(on)
                    def _():
                        send(way, part, slot)

                    send(WAY_Y if part == PART_Z_Y_X else WAY_X, part, slot)
                for part in Z_X_Y_PARTS:
                    send(WAY_Y, part, slot)
                send(WAY_X, PART_Z_Y_X, slot)

    def cross(distance):
        for there, plane, _, _ in sides(distance):

            @pl.when(there)
            def _(base=plane * PLANE):
                for part in Z_X_Y_PARTS:
                    recv(part, base + column_x)
                    send(WAY_Y, part, base + column_x)
                recv(PART_Z_Y_X, base + column_y)
                send(WAY_X, PART_Z_Y_X, base + column_y)

    def finish(distance):
        for there, plane, _, _ in sides(distance)[: 2 if distance else 1]:

            @pl.when(there)
            def _(plane=plane, base=plane * PLANE):
                recv(PART_Z_X_Y, base + column_y)
                recv(PART_Z_X_Y, base + column_xy)
                pair(PART_Z_X_Y, plane).start()
                recv(PART_Z_Y_X, base + column_x)
                recv(PART_Z_Y_X, base + column_xy)
                pair(PART_Z_Y_X, plane).start()

    def finish_dec(distance):
        for there, plane, _, _ in sides(distance)[: 2 if distance else 1]:

            @pl.when(there)
            def _(plane=plane, base=plane * PLANE):
                recv(PART_DEC, base + column_y)
                recv(PART_DEC, base + column_xy)
                pair(PART_DEC, plane).start()

    def whole_plane(distance):
        for there, plane, on, way in sides(distance):

            @pl.when(there)
            def _(plane=plane, on=on, way=way):
                for index in range(PLANE):
                    slot = plane * PLANE + index
                    recv(PART_X_Y_Z, slot)

                    @pl.when(on)
                    def _(slot=slot):
                        send(way, PART_X_Y_Z, slot)

                pair(PART_X_Y_Z, plane).start()

    workers = planes * PLANE
    start3 = split3(start_ref[:, :D])
    chunks = error_ref.shape[0] // ERROR_ROWS

    def work(index):
        load(index).wait()
        lanes = pl.ds(index * ERROR_ROWS, ERROR_ROWS)
        part_ref[:, lanes] = fold3(nt(start3, held[index % 2]))
        if index + 2 < chunks:
            load(index + 2).start()

    send(WAY_X, PART_X_Y_Z, me, True)
    send(WAY_Y, PART_X_Y_Z, me, True)
    for part in (PART_DEC, PART_Z_X_Y, PART_Z_Y_X):
        both_z(part, me, True)
    for part in Z_X_Y_PARTS:
        send(WAY_X, part, me, True)
    send(WAY_Y, PART_Z_Y_X, me, True)
    send(WAY_X, PART_Z_Y_X, me, True)
    for part in Z_X_Y_PARTS:
        send(WAY_Y, part, me, True)
    keeps = [
        pltpu.make_async_copy(shard_ref, own_ref.at[me], sems.at[3]),
        pltpu.make_async_copy(dec_shard_ref, dec_own.at[me], sems.at[6]),
    ]
    for keep in keeps:
        keep.start()
    swap_pixels = pltpu.make_async_remote_copy(
        src_ref=tubes_ref.at[1 - half],
        dst_ref=pixels_ref,
        send_sem=sems.at[4],
        recv_sem=sems.at[5],
        device_id={"tensor": 1 - half},
        device_id_type=MESH_ID,
    )
    swap_pixels.start()
    small_swaps = [
        pltpu.make_async_remote_copy(
            src_ref=source,
            dst_ref=target,
            send_sem=sems.at[11 + 2 * index],
            recv_sem=sems.at[12 + 2 * index],
            device_id={"tensor": 1 - half},
            device_id_type=MESH_ID,
        )
        for index, (source, target) in enumerate(
            ((start_ref, start_other_ref), (split_ref, split_other_ref))
        )
    ]
    for small in small_swaps:
        small.start()
    loads = [
        pltpu.make_async_copy(tubes_ref.at[index], pix_held.at[clip], sems.at[7 + clip])
        for clip, index in ((0, half), (1, 1 - half))
    ]
    for get in loads:
        get.start()
    work(0)
    near = z * PLANE
    recv(PART_X_Y_Z, near + column_x)
    send(WAY_Y, PART_X_Y_Z, near + column_x)
    for part in Z_X_Y_PARTS:
        recv(part, near + column_x)
        send(WAY_Y, part, near + column_x)
    recv(PART_Z_Y_X, near + column_y)
    send(WAY_X, PART_Z_Y_X, near + column_y)
    for keep in keeps:
        keep.wait()
    place_index = lax.broadcasted_iota(jnp.int32, (1, TUBES), 1)
    place_index = place_index.astype(f32)
    orders = []
    for clip, (index, out) in enumerate(((half, picked_ref), (1 - half, picked_other_ref))):
        row = order_ref[pl.ds(index, 1), :VIS]
        if clip == 0:
            visible_ref[...] = row
        orders.append(jnp.broadcast_to(row.astype(f32), (8, VIS)).T[:, :1])
        loads[clip].wait()
        hot = jnp.where(orders[clip] == place_index, 1.0, 0.0).astype(bf16)
        out[...] = nn(hot, pix_held[clip]).astype(bf16)
    swap_picked = pltpu.make_async_remote_copy(
        src_ref=picked_other_ref,
        dst_ref=pix_other_ref,
        send_sem=sems.at[9],
        recv_sem=sems.at[10],
        device_id={"tensor": 1 - half},
        device_id_type=MESH_ID,
    )
    swap_picked.start()
    work(1)
    along(1)
    recv(PART_X_Y_Z, near + column_y)
    recv(PART_X_Y_Z, near + column_xy)
    for index in range(PLANE):
        both_z(PART_X_Y_Z, near + index)
    pair(PART_X_Y_Z, z).start()
    work(2)
    cross(1)
    finish(0)
    pos_enc_ref[...] = sinusoid_of(orders[0], D)
    work(3)
    along(2)
    first_place = lax.broadcasted_iota(jnp.int32, (TUBES // 32, 1), 0).astype(f32) * 32.0
    second_place = lax.broadcasted_iota(jnp.int32, (32, 1), 0).astype(f32)
    rate, even = rates(DD)
    first = first_place * rate
    second = second_place * rate
    ahead = jnp.where(even, jnp.sin(first), jnp.cos(first))
    turned = jnp.where(even, jnp.cos(first), -jnp.sin(first))
    cos2, sin2 = jnp.cos(second), jnp.sin(second)
    for index in range(TUBES // 32):
        pos_dec_ref[pl.ds(32 * index, 32)] = (
            ahead[index : index + 1] * cos2 + turned[index : index + 1] * sin2
        )
    work(4)
    whole_plane(1)
    cross(2)
    work(5)
    finish(1)
    along(3)
    work(6)
    whole_plane(2)
    cross(3)
    work(7)
    finish(2)
    dec_load.wait()
    dec_part_ref[...] = fold3(nt(split3(start_ref[:, D:]), dec_held[...]))
    for distance in range(planes):
        finish_dec(distance)
    for plane in range(planes):
        pair(PART_DEC, plane).wait()
    total = jnp.zeros((1, 128), f32)
    per = joined.shape[1] // workers
    for index in range(workers):
        for group, ref in enumerate((dec_own, dec_other)):
            block = ref[index].astype(f32)
            joined[group, pl.ds(index * per, per)] = block[:per]
            if group == 0:
                total = total + block[per : per + 1, :128]
    for group in range(2):

        def matrix(at, size):
            return joined[group, pl.ds(at, size)].astype(bf16)

        wo_ref[pl.ds(group * DD // 2, DD // 2)] = matrix(DEC_O, DD // 2)
        for kind in range(3):
            wqkv_ref[pl.ds((2 * kind + group) * DD // 2, DD // 2)] = matrix(
                DEC_Q + kind * DD // 2, DD // 2
            )
        for ref, at in ((wd_ref, DEC_D), (wu_ref, DEC_U), (wh_ref, DEC_H)):
            ref[pl.ds(group * DFF // 2, DFF // 2)] = matrix(at, DFF // 2)
        proj_ref[half if group == 0 else 1 - half] = matrix(0, D // 2)
    counted = mask_ref[half].astype(f32)
    scal_ref[0:1] = jnp.zeros((1, 128), f32) + counted
    scal_ref[1:2] = counted * (2.0 * workers / PIX) / (MASKED * total)
    scal_ref[2:3] = MASKED * total
    scal_ref[3:8] = jnp.zeros((5, 128), f32)
    whole_plane(3)
    finish(3)
    swap_pixels.wait()
    swap_picked.wait()
    for small in small_swaps:
        small.wait()
    dec_at = 2 * (2 * HALF + HALF_FF)
    bqkv_ref[...] = jnp.zeros_like(bqkv_ref)
    for group, ref in enumerate((split_ref, split_other_ref)):
        for kind in range(2):
            low = 2 * kind * DD + group * DD // 2
            bqkv_ref[:, low : low + DD // 2] = ref[:, dec_at + kind * DD // 2 : dec_at + (kind + 1) * DD // 2]
        for out, at in ((bu_ref, dec_at + DD), (bh_ref, dec_at + DD + DFF // 2)):
            out[:, group * DFF // 2 : (group + 1) * DFF // 2] = ref[:, at : at + DFF // 2]
    for plane in range(planes):
        for part in range(3):
            pair(part, plane).wait()
        for index in range(PLANE):
            slot = plane * PLANE + index

            @pl.when(column == index)
            def _():
                for part in (PART_DEC, PART_Z_X_Y, PART_Z_Y_X):
                    copy(WAY_X, part, slot).wait_send()
                    copy(WAY_Y, part, slot).wait_send()

            @pl.when(column_x == index)
            def _():
                for part in Z_X_Y_PARTS:
                    copy(WAY_Y, part, slot).wait_send()

            @pl.when(column_y == index)
            def _():
                copy(WAY_X, PART_Z_Y_X, slot).wait_send()

            for part in range(4):
                sent = True if part == PART_X_Y_Z else column == index

                @pl.when(up & (plane <= z) & sent)
                def _():
                    copy(WAY_UP, part, slot).wait_send()

                @pl.when(down & (plane >= z) & sent)
                def _():
                    copy(WAY_DOWN, part, slot).wait_send()

    copy(WAY_X, PART_X_Y_Z, me).wait_send()
    copy(WAY_Y, PART_X_Y_Z, me).wait_send()
    copy(WAY_Y, PART_X_Y_Z, near + column_x).wait_send()


def spare_rows(rows):
    return -(rows + 1) % 16 + 1


def gather_weights(planes, weights, dec_weights, tubes, error, dec_error, start, order, split, mask):
    workers = planes * PLANE
    size = weights.shape[0]
    dec_size = dec_weights.shape[0] + spare_rows(dec_weights.shape[0])
    same = dec_size * DD // D
    long = (size + same) * 2 // 5 // 16 * 16 + 16
    parts = ((0, long - same), (long - same, long), (2 * long - same, size - 2 * long + same))
    shards = jax.ShapeDtypeStruct((workers,) + weights.shape, bf16)
    low = lambda *shape: jax.ShapeDtypeStruct(shape, bf16)
    wide = lambda *shape: jax.ShapeDtypeStruct(shape, f32)
    dec_shards = pltpu.VMEM((workers, dec_size, DD), bf16)
    return pl.pallas_call(
        lambda *refs: gather_kernel(parts, planes, *refs),
        in_specs=[vmem_spec()] * 2
        + [any_spec()] * 3
        + [vmem_spec()] * 3
        + [pl.BlockSpec(memory_space=pltpu.SMEM)],
        out_specs=[any_spec()] * 3 + [vmem_spec()] * 20,
        out_shape=[
            shards,
            shards,
            jax.ShapeDtypeStruct(tubes.shape[1:], tubes.dtype),
            wide(RANK, error.shape[0]),
            wide(RANK, dec_error.shape[0]),
            low(VIS, D),
            low(VIS, D),
            low(VIS, D),
            wide(*start.shape),
            wide(*split.shape),
            jax.ShapeDtypeStruct((1, VIS), jnp.int32),
            wide(1, 3 * DD),
            wide(1, DFF),
            wide(1, PIX),
            wide(VIS, D),
            wide(TUBES, DD),
            wide(8, 128),
            low(2, D // 2, DD),
            low(3 * DD, DD),
            low(DD, DD),
            low(DFF, DD),
            low(DFF, DD),
            low(PIX, DD),
        ],
        scratch_shapes=[
            pltpu.VMEM((2, ERROR_ROWS, D), bf16),
            pltpu.VMEM(dec_error.shape, bf16),
            dec_shards,
            dec_shards,
            pltpu.VMEM((2, DEC_ROWS, DD), f32),
            pltpu.VMEM((2, TUBES, D), bf16),
            pltpu.VMEM(weights.shape, bf16),
            pltpu.VMEM((dec_size, DD), bf16),
            pltpu.SemaphoreType.DMA((4, 4, workers)),
            pltpu.SemaphoreType.DMA((4, workers)),
            pltpu.SemaphoreType.DMA((2, 4, planes)),
            pltpu.SemaphoreType.DMA((15,)),
        ],
        compiler_params=pltpu.CompilerParams(
            collective_id=3, has_side_effects=True, vmem_limit_bytes=BIG_VMEM
        ),
        name="gather_weights",
    )(weights, dec_weights, tubes, error, dec_error, start, order, split, mask)


def cut(block, widths):
    pieces = []
    start = 0
    for width in widths:
        pieces.append(block[start : start + width])
        start = start + width
    return pieces


def swap(value):
    return lax.ppermute(value, "tensor", [(0, 1), (1, 0)])


def per_device(
    tubes,
    tube_order,
    clip_mask,
    enc_weights,
    dec_weights,
    vec_split,
    vec_shared,
    enc_moment,
    dec_moment,
    split_moment,
    shared_moment,
    enc_error,
    dec_error,
    factors,
):
    workers = lax.axis_size("dp")
    half = lax.axis_index("tensor")
    worker_index = lax.axis_index("dp")
    mine = lambda both: lax.dynamic_index_in_dim(both, half, 0, keepdims=False)
    which = half.astype(jnp.int32)[None]
    enc_per = enc_weights.shape[1]
    start_own = factors[0]
    wide = vec_shared[: 15 * D].reshape(15, D)
    narrow = vec_shared[15 * D :].reshape(9, DD)
    if workers == 4 * PLANE:
        per = enc_per
        (
            enc_own, enc_other, pixels, enc_error_part, dec_error_part, pix_vis, picked_other,
            pix_vis_other, start_other, split_other, visible, bqkv, bu, bh, pos_enc, pos_dec, scal, proj, d_qkv, d_out, d_down, d_up, head_rows,
        ) = gather_weights(
            workers // PLANE, enc_weights[0], dec_weights[0], tubes, enc_error[0, 0], dec_error[0, 0],
            start_own,
            tube_order, vec_split, clip_mask,
        )
        proj = proj.reshape(D, DD)
        loss_weight = scal[2, 0]
    else:
        visible = mine(tube_order)[None, :VIS]
        start_other = swap(start_own)
        split_other = swap(vec_split)
        counted_all = clip_mask.astype(f32)
        counted = mine(counted_all)
        picked = pick_visible(which, tube_order, tubes)
        pix_vis, picked_other = picked
        pix_vis_other = swap(picked_other)
        own = lax.all_gather(enc_weights[0].astype(bf16), "dp", axis=0)
        dec_all = lax.all_gather(dec_weights[0].astype(bf16), "dp", axis=0)
        loss_weight = MASKED * lax.psum(jnp.sum(counted_all), "dp")
        pixels = swap(lax.dynamic_index_in_dim(tubes, 1 - half, 0, keepdims=False))
        per = enc_per * workers
        enc_own = own.reshape(1, per, D)
        enc_other = swap(enc_own)
        enc_error_part = error_factor(start_own[:, :D], enc_error[0, 0])
        dec_error_part = error_factor(start_own[:, D:], dec_error[0, 0])
        dec_own = dec_all.reshape(DEC_ROWS, DD)
        dec_other = swap(dec_own)
        dec_widths = [D // 2, DD // 2, DFF // 2, 3 * DD // 2, DFF // 2, PIX // 2]
        own_parts = cut(dec_own, dec_widths)
        other_parts = cut(dec_other, dec_widths)
        proj = jnp.where(
            half == 0,
            jnp.concatenate([own_parts[0], other_parts[0]], 0),
            jnp.concatenate([other_parts[0], own_parts[0]], 0),
        )
        d_out, d_down, d_up, head_rows = (
            jnp.concatenate([own_parts[index], other_parts[index]], 0) for index in (1, 2, 4, 5)
        )
        kinds = lambda block: block.reshape(3, DD // 2, DD)
        d_qkv = jnp.concatenate([kinds(own_parts[3]), kinds(other_parts[3])], 1)
        d_qkv = d_qkv.reshape(3 * DD, DD)
        pos_enc = sinusoid_of(visible.reshape(VIS, 1).astype(f32), D)
        pos_dec = sinusoid_of(jnp.arange(TUBES).astype(f32)[:, None], DD)
        scal = jnp.broadcast_to(
            jnp.stack([counted, 2.0 * workers / (PIX * loss_weight) * counted] + [counted] * 6)[
                :, None
            ],
            (8, 128),
        )
        dec_at = 2 * (2 * HALF + HALF_FF)
        bq, bv, bu, bh = (
            jnp.concatenate([split[:, at : at + size] for split in (vec_split, split_other)], 1)
            for at, size in (
                (dec_at, DD // 2),
                (dec_at + DD // 2, DD // 2),
                (dec_at + DD, DFF // 2),
                (dec_at + DD + DFF // 2, PIX // 2),
            )
        )
        bqkv = jnp.concatenate([bq, jnp.zeros_like(bq), bv], 1)
    starts = (start_own, start_other)
    splits = (vec_split, split_other)

    (enc_normed, latent, enc_out), kept = encoder(
        per, (pix_vis, pix_vis_other), pos_enc, proj, wide, splits, enc_own, enc_other
    )

    dec_start, h, qkv, hidden = decoder_qkv(
        visible, pos_dec, latent, narrow, d_qkv, bqkv
    )
    mixed, logs = attend(qkv)
    grad_mixed, grad_middle, dec_grads, dec_sent, g_vec, g_bu, g_bh, loss_lanes = decoder_tokens(
        which, mixed, dec_start, tubes, pixels, hidden, scal, narrow, bu, bh, d_out, d_down, d_up,
        head_rows,
    )
    dq, dk, dv = attend_back(qkv, mixed, grad_mixed, logs)
    latent_low, dec_grads, dec_sent, g_vec1 = decoder_qkv_back(
        which, visible, dq, dk, dv, h, dec_start, grad_middle, narrow, d_qkv, enc_normed,
        dec_grads, dec_sent,
    )
    dec_left = dec_left_factor(starts, dec_grads, dec_sent)
    dec_came = swap(dec_sent)

    back = encoder_back(
        per, latent_low, enc_out, proj, wide, (pix_vis, pix_vis_other), starts, kept, enc_own, enc_other
    )
    packs, sent, enc_lefts = ([layer[index] for layer in back] for index in range(3))
    enc_vec_grads = [layer[3:] for layer in back]
    came = [swap(value) for value in sent]
    mine_packs = (pix_vis, packs[0], packs[1])
    their_packs = (picked_other, came[0], came[1])

    (
        enc_basis, dec_basis, enc_right, dec_right, g_wide, g_narrow, g_split, turned, rights, dec_comb
    ) = compress(
        workers, enc_lefts[0], enc_lefts[1], dec_left, enc_error_part, dec_error_part,
        (*enc_vec_grads[0], *enc_vec_grads[1], g_vec, g_vec1, g_bu, g_bh, loss_lanes),
        enc_error[0, 0], mine_packs, their_packs, dec_grads, dec_came, dec_error[0, 0],
    )
    enc_error_new, dec_error_new = new_errors(
        turned, rights, enc_error[0, 0], dec_comb, (enc_right, dec_basis, dec_right)
    )
    enc_rows = enc_basis.shape[1] // workers
    dec_rows = dec_basis.shape[1] // workers
    enc_owned = lax.dynamic_slice_in_dim(enc_basis, worker_index * enc_rows, enc_rows, 1)
    dec_owned = lax.dynamic_slice_in_dim(dec_basis, worker_index * dec_rows, dec_rows, 1)
    enc_mom = momentum_keep * enc_moment[0] + jnp.einsum(
        "rx,rc->xc", enc_owned, enc_right, precision=highest_precision
    )
    dec_mom = momentum_keep * dec_moment[0] + jnp.einsum(
        "rx,rc->xc", dec_owned, dec_right, precision=highest_precision
    )
    pieces = vec_split.shape[1] // CHUNK
    split_mom = momentum_keep * split_moment[0] + g_split[:pieces].reshape(-1)
    shared_mom = momentum_keep * shared_moment + jnp.concatenate(
        [g_wide.reshape(-1), g_narrow.reshape(-1)]
    )
    return (
        jnp.sum(g_split[pieces]) * (workers / PIX),
        loss_weight,
        (enc_weights[0] - step_rate * enc_mom)[None],
        enc_mom[None],
        enc_error_new[None, None],
        (dec_weights[0] - step_rate * dec_mom)[None],
        dec_mom[None],
        dec_error_new[None, None],
        jnp.concatenate([enc_right, dec_right], 1)[None],
        (vec_split[0] - step_rate * split_mom)[None],
        split_mom[None],
        vec_shared - step_rate * shared_mom,
        shared_mom,
    )


def solution(mesh):
    placed = (
        P("dp", None, "tensor"),
        P("dp", None),
        P("dp"),
        P("tensor", "dp", None),
        P("tensor", "dp", None),
        P("tensor", None),
        P(),
        P("tensor", "dp", None),
        P("tensor", "dp", None),
        P("tensor", None),
        P(),
        P("dp", "tensor", None, None),
        P("dp", "tensor", None, None),
        P("tensor", None, None),
    )
    return jax.shard_map(
        per_device,
        mesh=mesh,
        in_specs=placed,
        out_specs=(
            P(),
            P(),
            P("tensor", "dp", None),
            P("tensor", "dp", None),
            P("dp", "tensor", None, None),
            P("tensor", "dp", None),
            P("tensor", "dp", None),
            P("dp", "tensor", None, None),
            P("tensor", None, None),
            P("tensor", None),
            P("tensor", None),
            P(),
            P(),
        ),
        check_vma=False,
    )
```
